128 devices in a mesh: fsdp: 128 (over y, x, z, core).
Axes of the slice: x: 4, y: 4, z: 4, core: 2. Of those that a mesh axis runs over, the one named last changes fastest.
Arguments:
- tokens: bfloat16 [16384, 1024], P('fsdp'), may hold values from -6 to 6
- cotangent: bfloat16 [16384, 1024], P('fsdp'), may hold values from -6 to 6
- input_weight: bfloat16 [1024, 4120], P('fsdp'), may hold values from -0.1875 to 0.1875
- output_weight: bfloat16 [2048, 1024], P('fsdp'), as said below
- gate_up_weight: bfloat16 [1024, 4096], P('fsdp'), may hold values from -0.1875 to 0.1875
- down_weight: bfloat16 [2048, 1024], P('fsdp'), may hold values from -0.125 to 0.125
- norm_gains: bfloat16 [2, 1024], P(None, 'fsdp'), may hold values from 0.5 to 1.5
- conv_params: bfloat16 [5, 1792], P(None, 'fsdp'), may hold values from -3 to 3
- mixer_scale: bfloat16 [1, 1536], P(None, 'fsdp'), may hold values from 0.5 to 1.5
- decay_log: float32 [24], replicated, may hold values from -4 to 1
- step_bias: float32 [24], replicated, may hold values from -4 to -1
- mixer_skip_factor: float32 [24], replicated, may hold values from 0.5 to 1.5
Outputs:
- layer_output: bfloat16 [16384, 1024], P('fsdp')
- input_grad: bfloat16 [16384, 1024], P('fsdp')
- input_weight_grad: float32 [1024, 4120], P('fsdp')
- output_weight_grad: float32 [2048, 1024], P('fsdp')
- gate_up_weight_grad: float32 [1024, 4096], P('fsdp')
- down_weight_grad: float32 [2048, 1024], P('fsdp')
- norm_gains_grad: float32 [2, 1024], P(None, 'fsdp')
- conv_params_grad: float32 [5, 1792], P(None, 'fsdp')
- mixer_scale_grad: float32 [1, 1536], P(None, 'fsdp')
- decay_log_grad: float32 [24], replicated
- step_bias_grad: float32 [24], replicated
- skip_gain_grad: float32 [24], replicated
The draws below stay inside these ranges and needn't reach their ends.
Inputs may be any that keep to these rules, and one draw needn't show every extreme that they name: `output_weight`: independent entries, at most 20 / sqrt(2048) in magnitude in the first 512 rows and at most 5 / sqrt(2048) in the others.
All inputs are finite; a program needn't handle non-finite values.
Results may differ from the reference program's by a relative error of at most 0.022.
Values may be sent and summed in bfloat16 or wider, within the bound.
A program may use at most 192 MiB of HBM per device.

```python
import math
import jax
import jax.numpy as jnp
from jax import lax

D = 1024
FF = 2048
QH = 8
KVH = 2
HD = 64
MIXER_HEADS = 24
MIXER_HEAD_SIZE = 64
STATE = 128
CONVK = 4
TOK_DEV = 128
Q_WIDTH = 512
KV_WIDTH = 128
MIXER_FEATURES = 1536
CONV_WIDTH = 1792
IN_WIDTH = 4120
TOKENS = 16384
N_FSDP = 128


def draw_output_weight(key, part):
    key = jax.random.fold_in(key, 11)
    values = jnp.clip(jax.random.normal(key, (Q_WIDTH + MIXER_FEATURES, D), jnp.float32), -5.0, 5.0)
    row_index = lax.broadcasted_iota(jnp.int32, (Q_WIDTH + MIXER_FEATURES, 1), 0)
    factor = jnp.where(row_index < Q_WIDTH, 4.0, 1.0)
    return (values * factor / math.sqrt(Q_WIDTH + MIXER_FEATURES)).astype(jnp.bfloat16)


def block_scale(stream_key, extent, shards, low, top_value):
    loudness, own = 1.0, jax.random.fold_in(stream_key, 6)
    for dim, parts in shards:
        heights = jnp.exp(jax.random.uniform(jax.random.fold_in(own, dim), (parts,), jnp.float32, low / len(shards), top_value / len(shards)))
        loudness = loudness * jnp.repeat(heights, extent[dim] // parts).reshape([-1 if axis == dim else 1 for axis in range(len(extent))])
    return loudness


def bell_draw(stream_key, shape, width, bound, shards=(), held_as=jnp.bfloat16):
    level = block_scale(stream_key, shape, shards, -0.22, 0.18) if shards else 1.0
    array = jax.random.normal(stream_key, shape, jnp.float32) * width * level
    return jnp.minimum(jnp.maximum(array, -bound), bound).astype(held_as)


def setup_inputs(seed: int = 0) -> dict:
    arg_keys = jax.random.split(jax.random.key(seed), 13)
    tokens = bell_draw(arg_keys[0], (TOKENS, D), 1.0, 6.0, ((0, 128),))
    cotangent = bell_draw(arg_keys[1], (TOKENS, D), 1.0, 6.0, ((0, 128),))
    input_weight = bell_draw(arg_keys[2], (D, IN_WIDTH), D ** -0.5, 0.1875, ((0, 128),))
    output_weight = draw_output_weight(jax.random.fold_in(arg_keys[12], 71), 0)
    gate_up_weight = bell_draw(arg_keys[4], (D, 2 * FF), D ** -0.5, 0.1875, ((0, 128),))
    down_weight = bell_draw(arg_keys[5], (FF, D), FF ** -0.5, 0.125, ((0, 128),))
    norm_gains = jnp.clip(1.0 + 0.1 * jax.random.normal(arg_keys[6], (2, D), jnp.float32), 0.5, 1.5).astype(jnp.bfloat16)
    conv_params = bell_draw(arg_keys[7], (CONVK + 1, CONV_WIDTH), CONVK ** -0.5, 3.0, ((1, 128),))
    mixer_scale = jnp.clip(1.0 + 0.1 * jax.random.normal(arg_keys[8], (1, MIXER_FEATURES), jnp.float32), 0.5, 1.5).astype(jnp.bfloat16)
    decay_log = jnp.clip(jax.random.uniform(arg_keys[9], (MIXER_HEADS,), jnp.float32, -4.0, 1.0), -4.0, 1.0)
    step_bias = jnp.clip(jax.random.uniform(arg_keys[10], (MIXER_HEADS,), jnp.float32, -4.0, -1.0), -4.0, -1.0)
    mixer_skip_factor = jnp.clip(jax.random.uniform(arg_keys[11], (MIXER_HEADS,), jnp.float32, 0.5, 1.5), 0.5, 1.5)
    return dict(tokens=tokens, cotangent=cotangent, input_weight=input_weight, output_weight=output_weight, gate_up_weight=gate_up_weight, down_weight=down_weight, norm_gains=norm_gains, conv_params=conv_params, mixer_scale=mixer_scale, decay_log=decay_log, step_bias=step_bias, mixer_skip_factor=mixer_skip_factor)


norm_eps = 1e-05
rope_base = 10000.0
masked_value = -1e+30

@jax.custom_vjp
def reduced_precision(v):
    return lax.optimization_barrier(v.astype(jnp.bfloat16)).astype(jnp.float32)

@jax.custom_vjp
def reduced_backward(v):
    return v

def low_keep(v):
    return (reduced_precision(v), None)

def low_pass(kept, grad):
    return (grad,)

def back_keep(v):
    return (v, None)

def back_low(kept, grad):
    return (reduced_precision(grad),)
reduced_precision.defvjp(low_keep, low_pass)
reduced_backward.defvjp(back_keep, back_low)

def highest(left, right):
    return jnp.dot(left, right, precision=lax.Precision.HIGHEST, preferred_element_type=jnp.float32)

def rms_scale(values, gain):
    return values * lax.rsqrt(lax.optimization_barrier(jnp.mean(values * values, axis=-1, keepdims=True)) + norm_eps) * gain

def rope_tables(length_total):
    position = lax.broadcasted_iota(jnp.int32, (length_total, HD // 2), 0).astype(jnp.float32)
    column = lax.broadcasted_iota(jnp.int32, (length_total, HD // 2), 1).astype(jnp.float32)
    angle = position * jnp.exp(column * (-2.0 * math.log(rope_base) / HD))
    cosine_table = jnp.concatenate([jnp.cos(angle), jnp.cos(angle)], axis=1)
    sine_table = jnp.concatenate([jnp.sin(angle), jnp.sin(angle)], axis=1)
    return (cosine_table, sine_table)

def rotate(values, cosine_table, sine_table):
    half_size = values.shape[-1] // 2
    turned = jnp.concatenate([-values[..., half_size:], values[..., :half_size]], axis=-1)
    return values * cosine_table + turned * sine_table

def pre_mixer(projected, conv_all, step_bias, decay_log):
    length_total = projected.shape[0]
    cosine_table, sine_table = rope_tables(length_total)
    cosine_table = cosine_table[:, None, :]
    sine_table = sine_table[:, None, :]
    queries = projected[:, :Q_WIDTH].reshape(length_total, QH, HD)
    key_rows = projected[:, Q_WIDTH:Q_WIDTH + KV_WIDTH].reshape(length_total, KVH, HD)
    value_rows = projected[:, Q_WIDTH + KV_WIDTH:Q_WIDTH + 2 * KV_WIDTH]
    offset = Q_WIDTH + 2 * KV_WIDTH
    zgate = projected[:, offset:offset + MIXER_FEATURES]
    conv_in = projected[:, offset + MIXER_FEATURES:offset + MIXER_FEATURES + CONV_WIDTH]
    dt_raw = projected[:, offset + MIXER_FEATURES + CONV_WIDTH:]
    padded = jnp.concatenate([jnp.zeros((CONVK - 1, CONV_WIDTH), jnp.float32), conv_in], axis=0)
    summed = conv_all[CONVK]
    for tap_index in range(CONVK):
        summed = summed + conv_all[tap_index] * padded[tap_index:tap_index + length_total]
    active = jax.nn.silu(summed)
    step_sizes = jax.nn.softplus(dt_raw + step_bias)
    cumulative = jnp.cumsum(step_sizes * -jnp.exp(decay_log), axis=0)
    query_rot = rotate(queries, cosine_table, sine_table).reshape(length_total, Q_WIDTH)
    key_rot = rotate(key_rows, cosine_table, sine_table).reshape(length_total, KV_WIDTH)
    return (query_rot, key_rot, value_rows, zgate, active[:, :MIXER_FEATURES], active[:, MIXER_FEATURES:MIXER_FEATURES + STATE], active[:, MIXER_FEATURES + STATE:], step_sizes, cumulative)

def post_mixer(state_result, mixer_input_activated, zgate, mixer_skip_factor, scale_row):
    length_total = state_result.shape[0]
    central_output = state_result.reshape(length_total, MIXER_HEADS, MIXER_HEAD_SIZE) + mixer_skip_factor[:, None] * mixer_input_activated.reshape(length_total, MIXER_HEADS, MIXER_HEAD_SIZE)
    gated = central_output.reshape(length_total, MIXER_FEATURES) * jax.nn.silu(zgate)
    return rms_scale(gated, scale_row)

def swiglu(gate_up):
    return jax.nn.silu(gate_up[:, :FF]) * gate_up[:, FF:]

def layer_sequence(hidden, params):
    input_weight, output_weight, gate_up_weight, down_weight, norm_gains, conv_params, mixer_scale, decay_log, step_bias, mixer_skip_factor = params
    length_total = hidden.shape[0]
    score_scale = 1.0 / math.sqrt(HD)
    normed = reduced_precision(rms_scale(hidden, norm_gains[0]))
    projected = reduced_backward(highest(normed, input_weight))
    query_rot, key_rot, value_rows, zgate, mixer_input_activated, b_active, c_active, step_sizes, cumulative = pre_mixer(projected, conv_params, step_bias, decay_log)
    causal = lax.broadcasted_iota(jnp.int32, (length_total, length_total), 0) >= lax.broadcasted_iota(jnp.int32, (length_total, length_total), 1)
    query_group_rows = reduced_precision(query_rot).reshape(length_total, KVH, QH // KVH, HD)
    key_head_rows = reduced_precision(key_rot).reshape(length_total, KVH, HD)
    value_head_rows = reduced_precision(value_rows).reshape(length_total, KVH, HD)
    unscaled_scores = reduced_backward(jnp.einsum('ixnb,qxb->xniq', query_group_rows, key_head_rows, precision=lax.Precision.HIGHEST))
    scores = jnp.where(causal, unscaled_scores * score_scale, masked_value)
    probability_table = reduced_precision(jax.nn.softmax(scores, axis=-1))
    attention_result = jnp.einsum('mfbi,imq->bmfq', probability_table, value_head_rows, precision=lax.Precision.HIGHEST)
    attention_result = reduced_precision(reduced_backward(attention_result.reshape(length_total, Q_WIDTH)))
    inner_prod = reduced_backward(highest(reduced_precision(c_active), reduced_precision(b_active).T))
    gaps = cumulative[:, None, :] - cumulative[None, :, :]
    decay_table = jnp.exp(jnp.where(causal[:, :, None], gaps, masked_value))
    mixing = reduced_precision(inner_prod[:, :, None] * decay_table * step_sizes[None, :, :])
    mixer_input_heads = reduced_precision(mixer_input_activated).reshape(length_total, MIXER_HEADS, MIXER_HEAD_SIZE)
    state_result = reduced_backward(jnp.einsum('tsh,shp->thp', mixing, mixer_input_heads, precision=lax.Precision.HIGHEST))
    normed_state = post_mixer(state_result.reshape(length_total, MIXER_FEATURES), mixer_input_activated, zgate, mixer_skip_factor, mixer_scale[0])
    mixed = jnp.concatenate([attention_result, reduced_precision(normed_state)], axis=1)
    residual = hidden + reduced_backward(highest(mixed, output_weight))
    normed_ff = reduced_precision(rms_scale(residual, norm_gains[1]))
    gate_up = reduced_backward(highest(normed_ff, gate_up_weight))
    hidden_ff = reduced_precision(swiglu(gate_up))
    return residual + reduced_backward(highest(hidden_ff, down_weight))

def reference(tokens, cotangent, input_weight, output_weight, gate_up_weight, down_weight, norm_gains, conv_params, mixer_scale, decay_log, step_bias, mixer_skip_factor):
    params = tuple((weight.astype(jnp.float32) for weight in (input_weight, output_weight, gate_up_weight, down_weight, norm_gains, conv_params, mixer_scale, decay_log, step_bias, mixer_skip_factor)))
    sequences = tokens.astype(jnp.float32).reshape(N_FSDP, TOK_DEV, D)

    def forward(sequences, params):

        def one_step(carry, sequence):
            return (carry, layer_sequence(sequence, params))
        _, results = lax.scan(jax.checkpoint(one_step), jnp.zeros((), jnp.float32), sequences)
        return results
    results, pullback = jax.vjp(forward, sequences, params)
    d_sequences, d_params = pullback(cotangent.astype(jnp.float32).reshape(N_FSDP, TOK_DEV, D))
    return (results.reshape(TOKENS, D).astype(jnp.bfloat16), d_sequences.reshape(TOKENS, D).astype(jnp.bfloat16), d_params[0], d_params[1], d_params[2], d_params[3], d_params[4], d_params[5], d_params[6], d_params[7], d_params[8], d_params[9])
```

```python
import math

import jax
import jax.numpy as jnp
from jax import lax
from jax.experimental import pallas as pl
from jax.experimental.pallas import tpu as pltpu
from jax.sharding import PartitionSpec as P

FF = 2048
QH = 8
KVH = 2
HD = 64
MIXER_HEADS = 24
MIXER_HEAD_SIZE = 64
STATE = 128
CONVK = 4
Q_WIDTH = 512
KV_WIDTH = 128
MIXER_FEATURES = 1536
CONV_WIDTH = 1792


norm_eps = 1e-05
rope_base = 10000.0
masked_value = -1e30


AXES = ("y", "x", "z")
ORDERS = (("x", "y", "z"), ("y", "z", "x"), ("z", "x", "y"))
STEPS = (1, 3, 2)
WEIGHTS = ("small", "in", "out", "gu", "down")
ROWS = {"small": 16, "in": 16, "out": 32, "gu": 16, "down": 32}
COLS = {"small": 128, "in": 2048, "out": 512, "gu": 2048, "down": 512}
PARTS = {
    "small": ((0, 128),),
    "in": ((0, 768), (768, 1408), (1408, 2048)),
    "out": ((0, 128), (128, 256), (256, 512)),
    "gu": ((0, 640), (640, 1408), (1408, 2048)),
    "down": ((0, 256), (256, 384), (384, 512)),
}


class Place:
    def __init__(self):
        me = lax.axis_index("fsdp")
        self.me = me
        self.core = lax.rem(me, 2)
        self.at = {
            "y": lax.div(me, 32),
            "x": lax.rem(lax.div(me, 8), 4),
            "z": lax.rem(lax.div(me, 2), 4),
        }
        self.sibling = me + 1 - 2 * self.core

    def moved(self, axis, step):
        return lax.rem(self.at[axis] + step, 4)

    def peer(self, axis, step):
        at = dict(self.at)
        at[axis] = self.moved(axis, step)
        return ((at["y"] * 4 + at["x"]) * 4 + at["z"]) * 2 + self.core

    def partners(self):
        return [self.sibling] + [self.peer(axis, step) for axis in AXES for step in STEPS]


def meet(place):
    barrier = pltpu.get_barrier_semaphore()
    partners = place.partners()
    for partner in partners:
        pl.semaphore_signal(
            barrier, inc=1, device_id=(partner,), device_id_type=pl.DeviceIdType.MESH
        )
    pl.semaphore_wait(barrier, len(partners))


def push(src, dst, send_sem, recv_sem, device):
    return pltpu.make_async_remote_copy(
        src_ref=src,
        dst_ref=dst,
        send_sem=send_sem,
        recv_sem=recv_sem,
        device_id=(device,),
        device_id_type=pl.DeviceIdType.MESH,
    )


def block_index(where, low, high):
    return tuple(where.get(axis, slice(None)) for axis in AXES) + (
        slice(None),
        pl.ds(low, high - low),
    )


class Gather:
    def __init__(self, place, arrays, send_sem, recv_sem, pass_send, pass_recv):
        self.place, self.arrays = place, arrays
        self.send_sem, self.recv_sem = send_sem, recv_sem
        self.pass_send, self.pass_recv = pass_send, pass_recv
        self.slots, self.pass_slots = {}, {}
        for name in WEIGHTS:
            for part in range(len(PARTS[name])):
                for phase in range(3):
                    for step in STEPS:
                        self.slots[name, part, phase, step] = len(self.slots)
                if name != "small":
                    for piece in range(4):
                        self.pass_slots[name, part, piece] = len(self.pass_slots)

    def ref(self, name):
        if name == "small":
            return self.arrays[name]
        return self.arrays[name].at[self.place.core]

    def copy(self, name, part, phase, step):
        order = ORDERS[part]
        where = {axis: self.place.at[axis] for axis in order[phase:]}
        view = self.ref(name).at[block_index(where, *PARTS[name][part])]
        slot = self.slots[name, part, phase, step]
        return push(
            view,
            view,
            self.send_sem.at[slot],
            self.recv_sem.at[slot],
            self.place.peer(order[phase], step),
        )

    def start(self, name, phase):
        for step in STEPS:
            for part in range(len(PARTS[name])):
                self.copy(name, part, phase, step).start()

    def arrived(self, name, phase, step=None):
        for one in STEPS if step is None else (step,):
            for part in range(len(PARTS[name])):
                self.copy(name, part, phase, one).wait_recv()

    def pass_copy(self, name, part, piece):
        last = ORDERS[part][2]
        back = (0, 1, 3, 2)[piece]
        where = {last: self.place.moved(last, (4 - back) % 4)}
        view = self.ref(name).at[block_index(where, *PARTS[name][part])]
        slot = self.pass_slots[name, part, piece]
        return push(
            view, view, self.pass_send.at[slot], self.pass_recv.at[slot], self.place.sibling
        )

    def pass_on(self, name, piece):
        for part in range(len(PARTS[name])):
            self.pass_copy(name, part, piece).start()

    def passed(self, name):
        for piece in range(4):
            for part in range(len(PARTS[name])):
                self.pass_copy(name, part, piece).wait_recv()

    def finish(self):
        for key in self.slots:
            self.copy(*key).wait_send()
        for key in self.pass_slots:
            self.pass_copy(*key).wait_send()


def gather_counts():
    copies = sum(len(PARTS[name]) for name in WEIGHTS) * 9
    passes = sum(len(PARTS[name]) for name in WEIGHTS if name != "small") * 4
    return copies, passes


class Enter:
    def __init__(self, place, gather, pack, got, shards, sems):
        self.place, self.gather = place, gather
        self.pack, self.got, self.shards = pack, got, shards
        self.send_sem, self.recv_sem = sems

    def own(self, name, core):
        at = self.place.at
        return self.gather.arrays[name].at[core, at["y"], at["x"], at["z"]]

    def copies(self):
        core = self.place.core
        pairs = [(self.pack, self.got)]
        for name in ("out", "down"):
            shard = self.shards[name]
            columns = pl.ds(pl.multiple_of((1 - core) * 512, 512), 512)
            rows = pl.ds(pl.multiple_of(core * 16, 16), 16)
            pairs.append((shard.at[:, columns], self.own(name, 1 - core).at[rows, :]))
        return [
            push(src, dst, self.send_sem.at[i], self.recv_sem.at[i], self.place.sibling)
            for i, (src, dst) in enumerate(pairs)
        ]

    def run(self):
        core, at = self.place.core, self.place.at
        wide = jnp.float32
        rows_in, rows_gu = self.shards["in"], self.shards["gu"]
        for low, ref in ((0, rows_in), (2048, rows_gu)):
            both = jnp.concatenate(
                [ref[:, 0:2048].astype(wide), ref[:, 2048:4096].astype(wide)], axis=0
            )
            self.pack[:, low : low + 2048] = both.astype(jnp.bfloat16)
        small = self.shards["small"][...]
        self.pack[:, 4096:4224] = jnp.concatenate([small, small], axis=0).astype(jnp.bfloat16)
        copies = self.copies()
        for copy in copies:
            copy.start()
        for name in ("out", "down"):
            columns = pl.ds(pl.multiple_of(core * 512, 512), 512)
            rows = pl.ds(pl.multiple_of(core * 16, 16), 16)
            self.own(name, core)[rows, :] = self.shards[name][:, columns]
        copies[0].wait_recv()
        for name, low, size in (("small", 4096, 128), ("in", 0, 2048), ("gu", 2048, 2048)):
            mine = self.pack[:, low : low + size].astype(wide)
            other = self.got[:, low : low + size].astype(wide)
            other = jnp.concatenate([other[8:16], other[0:8]], axis=0)
            upper = lax.broadcasted_iota(jnp.int32, (16, size), 0) < 8
            take = upper == (core == 0)
            block = jnp.where(take, mine, other).astype(jnp.bfloat16)
            if name == "small":
                self.gather.arrays[name][at["y"], at["x"], at["z"]] = block
            else:
                self.own(name, core)[...] = block
        for copy in copies[1:]:
            copy.wait_recv()

    def finish(self):
        for copy in self.copies():
            copy.wait_send()


class Scatter:
    def __init__(self, place, grads, first, second, third, mid, low, send_sem, recv_sem):
        self.place, self.grads = place, grads
        self.got = (first, second, third)
        self.kept = (grads, mid, low)
        self.send_sem, self.recv_sem = send_sem, recv_sem
        self.slots = {}
        for name in WEIGHTS:
            for part in range(len(PARTS[name])):
                for phase in range(3):
                    for step in STEPS:
                        self.slots[name, part, phase, step] = len(self.slots)

    def view(self, ref, part, phase, where, low, high):
        order = ORDERS[part][::-1]
        left = [axis for axis in AXES if axis not in order[:phase]]
        return ref.at[
            tuple(where if axis == order[phase] else slice(None) for axis in left)
            + (slice(None), pl.ds(low, high - low))
        ]

    def copy(self, name, part, phase, step):
        axis = ORDERS[part][2 - phase]
        low, high = PARTS[name][part]
        src = self.view(
            self.kept[phase][name], part, phase, self.place.moved(axis, step), low, high
        )
        slot = STEPS.index(step)
        dst = self.got[phase][name].at[
            (slot,) + (slice(None),) * (2 - phase) + (slice(None), pl.ds(low, high - low))
        ]
        one = self.slots[name, part, phase, step]
        return push(
            src, dst, self.send_sem.at[one], self.recv_sem.at[one], self.place.peer(axis, step)
        )

    def start(self, name, part, phase):
        for step in STEPS:
            self.copy(name, part, phase, step).start()

    def add(self, name, part, phase):
        low, high = PARTS[name][part]
        axis = ORDERS[part][2 - phase]
        for step in STEPS:
            self.copy(name, part, phase, step).wait_recv()
        own = self.view(self.kept[phase][name], part, phase, self.place.at[axis], low, high)
        total = own[...].astype(jnp.float32)
        for slot in range(3):
            total = total + self.got[phase][name][
                (slot,) + (slice(None),) * (2 - phase) + (slice(None), pl.ds(low, high - low))
            ].astype(jnp.float32)
        return total

    def relay(self, name, part, phase):
        low, high = PARTS[name][part]
        total = self.add(name, part, phase)
        self.kept[phase + 1][name][
            (slice(None),) * (2 - phase) + (slice(None), pl.ds(low, high - low))
        ] = total.astype(jnp.bfloat16)
        self.start(name, part, phase + 1)

    def finish(self):
        for key in self.slots:
            self.copy(*key).wait_send()


class SumAll:
    def __init__(self, place, got, send_sem, recv_sem):
        self.place, self.got = place, got
        self.send_sem, self.recv_sem = send_sem, recv_sem

    def slot(self, stage):
        return self.place.core if stage == 0 else self.place.at[AXES[stage - 1]]

    def copies(self, stage):
        if stage == 0:
            devices = [self.place.sibling]
        else:
            devices = [self.place.peer(AXES[stage - 1], step) for step in STEPS]
        view = self.got.at[stage, self.slot(stage)]
        return [
            push(view, view, self.send_sem.at[stage * 3 + i], self.recv_sem.at[stage * 3 + i], device)
            for i, device in enumerate(devices)
        ]

    def start(self, stage, value):
        self.got[stage, self.slot(stage)] = value
        for copy in self.copies(stage):
            copy.start()

    def total(self, stage):
        for copy in self.copies(stage):
            copy.wait_recv()
        total = self.got[stage, 0]
        for slot in range(1, 2 if stage == 0 else 4):
            total = total + self.got[stage, slot]
        return total

    def finish(self):
        for stage in range(4):
            for copy in self.copies(stage):
                copy.wait_send()


def gather_kernel(
    small_ref, in_ref, out_ref, gu_ref, down_ref, g_small, g_in, g_out, g_gu, g_down,
    pack, got, enter_send, enter_recv, send_sem, recv_sem, pass_send, pass_recv,
):
    place = Place()
    meet(place)
    arrays = {"small": g_small, "in": g_in, "out": g_out, "gu": g_gu, "down": g_down}
    shards = {"small": small_ref, "in": in_ref, "out": out_ref, "gu": gu_ref, "down": down_ref}
    gather = Gather(place, arrays, send_sem, recv_sem, pass_send, pass_recv)
    enter = Enter(place, gather, pack, got, shards, (enter_send, enter_recv))
    enter.run()
    for name in WEIGHTS:
        gather.start(name, 0)
    for name in WEIGHTS:
        gather.arrived(name, 0)
        gather.start(name, 1)
    for name in WEIGHTS:
        gather.arrived(name, 1)
        gather.start(name, 2)
        if name != "small":
            gather.pass_on(name, 0)
    for name in WEIGHTS:
        for piece, step in enumerate(STEPS):
            gather.arrived(name, 2, step)
            if name != "small":
                gather.pass_on(name, piece + 1)
    for name in WEIGHTS[1:]:
        gather.passed(name)
    gather.finish()
    enter.finish()


def vmem(count):
    return [pl.BlockSpec(memory_space=pltpu.VMEM)] * count


def gather_weights(small, in_shard, out_shard, gu_shard, down_shard):
    copies, passes = gather_counts()
    shapes = [
        jax.ShapeDtypeStruct(
            (() if name == "small" else (2,)) + (4, 4, 4, ROWS[name], COLS[name]), jnp.bfloat16
        )
        for name in WEIGHTS
    ]
    return pl.pallas_call(
        gather_kernel,
        out_shape=shapes,
        in_specs=vmem(5),
        out_specs=vmem(5),
        scratch_shapes=[
            pltpu.VMEM((16, 4224), jnp.bfloat16),
            pltpu.VMEM((16, 4224), jnp.bfloat16),
            pltpu.SemaphoreType.DMA((3,)),
            pltpu.SemaphoreType.DMA((3,)),
            pltpu.SemaphoreType.DMA((copies,)),
            pltpu.SemaphoreType.DMA((copies,)),
            pltpu.SemaphoreType.DMA((passes,)),
            pltpu.SemaphoreType.DMA((passes,)),
        ],
        compiler_params=pltpu.CompilerParams(
            collective_id=0, has_side_effects=True, vmem_limit_bytes=58 * 2**20
        ),
        name="gather_weights",
    )(small, in_shard, out_shard, gu_shard, down_shard)


def scatter_kernel(*refs):
    g = dict(zip(WEIGHTS, refs[0:5]))
    vectors = refs[5]
    outs = dict(zip(WEIGHTS, refs[6:11]))
    vectors_out = refs[11]
    first = dict(zip(WEIGHTS, refs[12:17]))
    second = dict(zip(WEIGHTS, refs[17:22]))
    third = dict(zip(WEIGHTS, refs[22:27]))
    mid = dict(zip(WEIGHTS, refs[27:32]))
    low = dict(zip(WEIGHTS, refs[32:37]))
    sums, ends, end_got = refs[37], dict(zip(WEIGHTS[1:], refs[38:42])), dict(zip(WEIGHTS[1:], refs[42:46]))
    send_sem, recv_sem, sum_send, sum_recv, end_send, end_recv = refs[46:]
    place = Place()
    meet(place)
    scatter = Scatter(place, g, first, second, third, mid, low, send_sem, recv_sem)
    sum_all = SumAll(place, sums, sum_send, sum_recv)
    order = ("down", "gu", "out", "in", "small")
    sum_all.start(0, vectors[...])
    for name in order:
        for part in range(len(PARTS[name])):
            scatter.start(name, part, 0)
    for phase in range(2):
        sum_all.start(phase + 1, sum_all.total(phase))
        for name in order:
            for part in range(len(PARTS[name])):
                scatter.relay(name, part, phase)
    sum_all.start(3, sum_all.total(2))
    end = End(place, ends, end_got, outs, end_send, end_recv)
    for name in order:
        for part in range(len(PARTS[name])):
            value = scatter.add(name, part, 2)
            low_col, high_col = PARTS[name][part]
            if name == "small":
                outs[name][...] = jnp.where(place.core == 0, value[0:8], value[8:16])
            else:
                ends[name][:, low_col:high_col] = value
        if name != "small":
            end.start(name)
    for name in order[:4]:
        end.take(name)
    vectors_out[...] = sum_all.total(3)
    scatter.finish()
    sum_all.finish()
    end.finish()


class End:
    def __init__(self, place, ends, got, outs, send_sem, recv_sem):
        self.place, self.ends, self.got, self.outs = place, ends, got, outs
        self.send_sem, self.recv_sem = send_sem, recv_sem

    def rows(self, name, core):
        half = ROWS[name] // 2
        return pl.ds(pl.multiple_of(core * half, 8), half)

    def copy(self, name):
        slot = WEIGHTS.index(name) - 1
        return push(
            self.ends[name].at[self.rows(name, 1 - self.place.core), :],
            self.got[name],
            self.send_sem.at[slot],
            self.recv_sem.at[slot],
            self.place.sibling,
        )

    def columns(self, name, core):
        size = COLS[name]
        return pl.ds(pl.multiple_of(core * size, size), size)

    def start(self, name):
        self.copy(name).start()
        core = self.place.core
        self.outs[name][:, self.columns(name, core)] = self.ends[name][self.rows(name, core), :]

    def take(self, name):
        self.copy(name).wait_recv()
        self.outs[name][:, self.columns(name, 1 - self.place.core)] = self.got[name][...]

    def finish(self):
        for name in WEIGHTS[1:]:
            self.copy(name).wait_send()


def scatter_grads(grads, vectors):
    copies, _ = gather_counts()
    low, wide = jnp.bfloat16, jnp.float32
    out_shapes = [
        jax.ShapeDtypeStruct(
            (ROWS[name] // 2, COLS[name] * (1 if name == "small" else 2)), wide
        )
        for name in WEIGHTS
    ] + [jax.ShapeDtypeStruct(vectors.shape, wide)]

    def each(lead, kind=low, names=WEIGHTS, share=1):
        return [pltpu.VMEM(lead + (ROWS[n] // share, COLS[n]), kind) for n in names]

    sems = pltpu.SemaphoreType.DMA
    return pl.pallas_call(
        scatter_kernel,
        out_shape=out_shapes,
        in_specs=vmem(6),
        out_specs=vmem(6),
        scratch_shapes=each((3, 4, 4))
        + each((3, 4))
        + each((3,))
        + each((4, 4))
        + each((4,))
        + [pltpu.VMEM((4, 4) + vectors.shape, wide)]
        + each((), wide, WEIGHTS[1:])
        + each((), wide, WEIGHTS[1:], 2)
        + [sems((copies,)), sems((copies,)), sems((12,)), sems((12,)), sems((4,)), sems((4,))],
        compiler_params=pltpu.CompilerParams(
            collective_id=1, has_side_effects=True, vmem_limit_bytes=58 * 2**20
        ),
        name="scatter_grads",
    )(*grads, vectors)

def rms_scale(values, gain):
    return values * lax.rsqrt(jnp.mean(values * values, axis=-1, keepdims=True) + norm_eps) * gain


def rope_tables(length_total):
    position = lax.broadcasted_iota(jnp.int32, (length_total, HD // 2), 0).astype(jnp.float32)
    column = lax.broadcasted_iota(jnp.int32, (length_total, HD // 2), 1).astype(jnp.float32)
    angle = position * jnp.exp(column * (-2.0 * math.log(rope_base) / HD))
    cosine_table = jnp.concatenate([jnp.cos(angle), jnp.cos(angle)], axis=1)
    sine_table = jnp.concatenate([jnp.sin(angle), jnp.sin(angle)], axis=1)
    return (cosine_table, sine_table)


def rotate(values, cosine_table, sine_table):
    half_size = values.shape[-1] // 2
    turned = jnp.concatenate([-values[..., half_size:], values[..., :half_size]], axis=-1)
    return values * cosine_table + turned * sine_table


def pre_mixer(projected, conv_all, step_bias, decay_log):
    length_total = projected.shape[0]
    cosine_table, sine_table = rope_tables(length_total)
    cosine_table = cosine_table[:, None, :]
    sine_table = sine_table[:, None, :]
    queries = projected[:, :Q_WIDTH].reshape(length_total, QH, HD)
    key_rows = projected[:, Q_WIDTH : Q_WIDTH + KV_WIDTH].reshape(length_total, KVH, HD)
    value_rows = projected[:, Q_WIDTH + KV_WIDTH : Q_WIDTH + 2 * KV_WIDTH]
    offset = Q_WIDTH + 2 * KV_WIDTH
    zgate = projected[:, offset : offset + MIXER_FEATURES]
    conv_in = projected[:, offset + MIXER_FEATURES : offset + MIXER_FEATURES + CONV_WIDTH]
    dt_raw = projected[:, offset + MIXER_FEATURES + CONV_WIDTH :]
    padded = jnp.concatenate([jnp.zeros((CONVK - 1, CONV_WIDTH), jnp.float32), conv_in], axis=0)
    summed = conv_all[CONVK]
    for tap_index in range(CONVK):
        summed = summed + conv_all[tap_index] * padded[tap_index : tap_index + length_total]
    active = jax.nn.silu(summed)
    step_sizes = jax.nn.softplus(dt_raw + step_bias)
    cumulative = jnp.cumsum(step_sizes * -jnp.exp(decay_log), axis=0)
    query_rot = rotate(queries, cosine_table, sine_table).reshape(length_total, Q_WIDTH)
    key_rot = rotate(key_rows, cosine_table, sine_table).reshape(length_total, KV_WIDTH)
    return (
        query_rot,
        key_rot,
        value_rows,
        zgate,
        active[:, :MIXER_FEATURES],
        active[:, MIXER_FEATURES : MIXER_FEATURES + STATE],
        active[:, MIXER_FEATURES + STATE :],
        step_sizes,
        cumulative,
    )


def post_mixer(state_result, mixer_input_activated, zgate, mixer_skip_factor, scale_row):
    length_total = state_result.shape[0]
    central_output = state_result.reshape(
        length_total, MIXER_HEADS, MIXER_HEAD_SIZE
    ) + mixer_skip_factor[:, None] * mixer_input_activated.reshape(
        length_total, MIXER_HEADS, MIXER_HEAD_SIZE
    )
    gated = central_output.reshape(length_total, MIXER_FEATURES) * jax.nn.silu(zgate)
    return rms_scale(gated, scale_row)


def swiglu(gate_up):
    return jax.nn.silu(gate_up[:, :FF]) * gate_up[:, FF:]


def fold_rows(left_low, piece):
    return jnp.dot(left_low, piece, preferred_element_type=jnp.float32)


def back_rows(grad_low, piece):
    return lax.dot_general(
        grad_low, piece, (((1,), (1,)), ((), ())), preferred_element_type=jnp.float32
    )


def grad_rows(left_low, right_low):
    return lax.dot_general(
        left_low, right_low, (((0,), (0,)), ((), ())), preferred_element_type=jnp.float32
    )


def attend_scores(query_group_rows, key_head_rows, causal):
    unscaled_scores = jnp.einsum(
        "ixnb,qxb->xniq", query_group_rows, key_head_rows, preferred_element_type=jnp.float32
    )
    return jnp.where(causal, unscaled_scores * (1.0 / math.sqrt(HD)), masked_value)


def local(
    tokens,
    cotangent,
    input_weight,
    output_weight,
    gate_up_weight,
    down_weight,
    norm_gains,
    conv_params,
    mixer_scale,
    decay_log,
    step_bias,
    mixer_skip_factor,
):
    length_total = tokens.shape[0]
    hidden = tokens.astype(jnp.float32)
    core = lax.rem(lax.axis_index("fsdp"), 2)
    wide = jnp.float32
    packed = jnp.concatenate(
        [
            jnp.pad(norm_gains, ((0, 0), (0, 6))),
            conv_params,
            jnp.pad(mixer_scale, ((0, 0), (0, 2))),
        ],
        axis=0,
    )
    small = jnp.concatenate(
        [
            jnp.pad(input_weight[:, 4096:], ((0, 0), (0, 8))),
            jnp.pad(packed, ((0, 0), (0, 82))),
        ],
        axis=1,
    ).astype(wide)
    g_small, g_in, g_out, g_gu, g_down = gather_weights(
        small, input_weight, output_weight, gate_up_weight, down_weight
    )
    g_small = g_small.reshape(1024, 128)
    spread = g_small.reshape(128, 8, 128)[:, :, 32:46].astype(wide)
    gains_all = spread[:, 0:2, :8].transpose(1, 0, 2).reshape(2, 1024)
    conv_all = spread[:, 2:7, :].transpose(1, 0, 2).reshape(5, 1792)
    scale_all = spread[:, 7:8, :12].transpose(1, 0, 2).reshape(1, 1536)

    def whole(halves, rows, columns):
        return halves.reshape(2, rows, columns).transpose(1, 0, 2).reshape(rows, 2 * columns)

    in_full = jnp.concatenate([whole(g_in, 1024, 2048), g_small[:, :24]], axis=1)
    out_full = whole(g_out, 2048, 512)
    gu_full = whole(g_gu, 1024, 2048)
    down_full = whole(g_down, 2048, 512)
    causal = lax.broadcasted_iota(
        jnp.int32, (length_total, length_total), 0
    ) >= lax.broadcasted_iota(jnp.int32, (length_total, length_total), 1)
    normed, norm_in_back = jax.vjp(rms_scale, hidden, gains_all[0])
    normed_low = normed.astype(jnp.bfloat16)
    projected = fold_rows(normed_low, in_full)
    mixer_in, pre_back = jax.vjp(pre_mixer, projected, conv_all, step_bias, decay_log)
    (
        query_rot,
        key_rot,
        value_rows,
        zgate,
        mixer_input_activated,
        b_active,
        c_active,
        step_sizes,
        cumulative,
    ) = mixer_in
    query_group_rows = query_rot.astype(jnp.bfloat16).reshape(length_total, KVH, QH // KVH, HD)
    key_head_rows = key_rot.astype(jnp.bfloat16).reshape(length_total, KVH, HD)
    value_head_rows = value_rows.astype(jnp.bfloat16).reshape(length_total, KVH, HD)
    scores = attend_scores(query_group_rows, key_head_rows, causal)
    row_peak = jnp.max(scores, axis=-1, keepdims=True)
    exponent = jnp.exp(scores - row_peak)
    totals = jnp.sum(exponent, axis=-1, keepdims=True)
    log_total = row_peak + jnp.log(totals)
    probability_reduced = (exponent / totals).astype(jnp.bfloat16)
    attention_result = jnp.einsum(
        "mfbi,imq->bmfq", probability_reduced, value_head_rows, preferred_element_type=jnp.float32
    )
    attention_result = attention_result.reshape(length_total, Q_WIDTH).astype(jnp.bfloat16)
    c_low = c_active.astype(jnp.bfloat16)
    b_low = b_active.astype(jnp.bfloat16)
    mixer_input_reduced = mixer_input_activated.astype(jnp.bfloat16)
    inner_prod = lax.dot_general(
        c_low, b_low, (((1,), (1,)), ((), ())), preferred_element_type=jnp.float32
    )
    head_grouping = math.gcd(MIXER_HEADS, 8)
    head_block_list = MIXER_HEADS // head_grouping
    cum_heads = cumulative.T.reshape(head_block_list, head_grouping, length_total)
    step_heads = step_sizes.T.reshape(head_block_list, head_grouping, length_total)
    mixer_input_heads = (
        mixer_input_reduced.reshape(length_total, MIXER_HEADS, MIXER_HEAD_SIZE)
        .transpose(1, 0, 2)
        .reshape(head_block_list, head_grouping, length_total, MIXER_HEAD_SIZE)
    )

    def mixing_of(cum_block, step_block):
        gaps = cum_block[:, :, None] - cum_block[:, None, :]
        decay_table = jnp.exp(jnp.where(causal[None], gaps, masked_value))
        return (inner_prod[None] * decay_table * step_block[:, None, :], decay_table)

    def state_block(block_items):
        cum_block, step_block, x_block = block_items
        mixing, _ = mixing_of(cum_block, step_block)
        return jnp.einsum(
            "hts,hsp->htp", mixing.astype(jnp.bfloat16), x_block, preferred_element_type=jnp.float32
        )

    state_result = lax.map(state_block, (cum_heads, step_heads, mixer_input_heads))
    state_result = (
        state_result.reshape(MIXER_HEADS, length_total, MIXER_HEAD_SIZE)
        .transpose(1, 0, 2)
        .reshape(length_total, MIXER_FEATURES)
    )
    normed_state, post_back = jax.vjp(
        post_mixer, state_result, mixer_input_activated, zgate, mixer_skip_factor, scale_all[0]
    )
    mixed = jnp.concatenate([attention_result, normed_state.astype(jnp.bfloat16)], axis=1)
    branch = fold_rows(mixed, out_full)
    residual = hidden + branch
    normed_ff, norm_ff_back = jax.vjp(rms_scale, residual, gains_all[1])
    normed_ff_low = normed_ff.astype(jnp.bfloat16)
    gate_up = fold_rows(normed_ff_low, gu_full)
    hidden_ff, swiglu_back = jax.vjp(swiglu, gate_up)
    hidden_low = hidden_ff.astype(jnp.bfloat16)
    down_out = fold_rows(hidden_low, down_full)
    layer_output = (residual + down_out).astype(jnp.bfloat16)
    grad_out = cotangent.astype(jnp.float32)
    d_hidden_ff = back_rows(cotangent, down_full)
    (d_gate_up,) = swiglu_back(d_hidden_ff)
    d_gate_low = d_gate_up.astype(jnp.bfloat16)
    d_normed_ff = back_rows(d_gate_low, gu_full)
    d_resid_ff, d_gain_ff = norm_ff_back(d_normed_ff)
    d_residual = grad_out + d_resid_ff
    d_branch_low = d_residual.astype(jnp.bfloat16)
    d_mixed = back_rows(d_branch_low, out_full)
    d_attended = d_mixed[:, :Q_WIDTH].astype(jnp.bfloat16)
    d_state_out, d_x_skip, d_zgate, d_skip_gain, d_scale = post_back(d_mixed[:, Q_WIDTH:])
    state_gradient_reduced = d_state_out.astype(jnp.bfloat16)
    d_heads = (
        state_gradient_reduced.reshape(length_total, MIXER_HEADS, MIXER_HEAD_SIZE)
        .transpose(1, 0, 2)
        .reshape(head_block_list, head_grouping, length_total, MIXER_HEAD_SIZE)
    )

    def state_back(d_inner, block_items):
        cum_block, step_block, x_block, d_block = block_items
        mixing, decay_table = mixing_of(cum_block, step_block)
        d_mixing = jnp.einsum("htp,hsp->hts", d_block, x_block, preferred_element_type=jnp.float32)
        d_x_block = jnp.einsum(
            "hts,htp->hsp", mixing.astype(jnp.bfloat16), d_block, preferred_element_type=jnp.float32
        )
        scaled = d_mixing * step_block[:, None, :]
        d_inner = d_inner + jnp.sum(scaled * decay_table, axis=0)
        d_step = jnp.sum(d_mixing * (inner_prod[None] * decay_table), axis=1)
        flow = scaled * inner_prod[None] * decay_table
        d_cum = jnp.sum(flow, axis=2) - jnp.sum(flow, axis=1)
        return (d_inner, (d_x_block, d_step, d_cum))

    d_inner, (mixer_input_heads_gradient, d_step_heads, d_cum_heads) = lax.scan(
        state_back,
        jnp.zeros((length_total, length_total), jnp.float32),
        (cum_heads, step_heads, mixer_input_heads, d_heads),
    )
    mixer_input_state_gradient = (
        mixer_input_heads_gradient.reshape(MIXER_HEADS, length_total, MIXER_HEAD_SIZE)
        .transpose(1, 0, 2)
        .reshape(length_total, MIXER_FEATURES)
    )
    d_steps = d_step_heads.reshape(MIXER_HEADS, length_total).T
    d_cumulative = d_cum_heads.reshape(MIXER_HEADS, length_total).T
    d_inner_low = d_inner.astype(jnp.bfloat16)
    d_c_active = jnp.dot(d_inner_low, b_low, preferred_element_type=jnp.float32)
    d_b_active = lax.dot_general(
        d_inner_low, c_low, (((0,), (0,)), ((), ())), preferred_element_type=jnp.float32
    )
    output_heads_gradient = d_attended.reshape(length_total, KVH, QH // KVH, HD)
    probability_table = jnp.exp(attend_scores(query_group_rows, key_head_rows, causal) - log_total)
    d_probs = jnp.einsum(
        "ixnb,qxb->xniq", output_heads_gradient, value_head_rows, preferred_element_type=jnp.float32
    )
    d_scores = probability_table * (
        d_probs - jnp.sum(probability_table * d_probs, axis=-1, keepdims=True)
    )
    unscaled_gradient = (d_scores * (1.0 / math.sqrt(HD))).astype(jnp.bfloat16)
    d_query = jnp.einsum(
        "mfbi,imq->bmfq", unscaled_gradient, key_head_rows, preferred_element_type=jnp.float32
    ).reshape(length_total, Q_WIDTH)
    d_key = jnp.einsum(
        "mcnp,nmca->pma", unscaled_gradient, query_group_rows, preferred_element_type=jnp.float32
    ).reshape(length_total, KV_WIDTH)
    d_value = jnp.einsum(
        "mcnp,nmca->pma",
        probability_table.astype(jnp.bfloat16),
        output_heads_gradient,
        preferred_element_type=jnp.float32,
    ).reshape(length_total, KV_WIDTH)
    d_projected, d_conv, d_step_bias, d_decay_log = pre_back(
        (
            d_query,
            d_key,
            d_value,
            d_zgate,
            mixer_input_state_gradient + d_x_skip,
            d_b_active,
            d_c_active,
            d_steps,
            d_cumulative,
        )
    )
    d_proj_low = d_projected.astype(jnp.bfloat16)
    d_normed = back_rows(d_proj_low, in_full)
    d_hidden, d_gain_in = norm_in_back(d_normed)
    input_grad = (d_residual + d_hidden).astype(jnp.bfloat16)
    dt_low = jnp.pad(d_proj_low[:, 4096:], ((0, 0), (0, 104)))

    def half(value, which):
        size = value.shape[1] // 2
        return lax.dynamic_slice_in_dim(value, which * size, size, 1)

    rights = (d_proj_low[:, :4096], d_branch_low, d_gate_low, cotangent)
    lefts = (normed_low, mixed, normed_ff_low, hidden_low)
    swap = [(i, i ^ 1) for i in range(128)]
    sent = jnp.concatenate([*lefts, *(half(r, 1 - core) for r in rights), dt_low], axis=1)
    came = lax.ppermute(sent, "fsdp", swap)
    grads, at = [], 0
    left_pairs = []
    for left in lefts:
        left_pairs.append(jnp.concatenate([left, came[:, at : at + left.shape[1]]], axis=0))
        at += left.shape[1]
    for left, right in zip(left_pairs, rights):
        size = right.shape[1] // 2
        pair = jnp.concatenate([half(right, core), came[:, at : at + size]], axis=0)
        at += size
        grads.append(grad_rows(left, pair).astype(jnp.bfloat16))
    dt_pair = jnp.concatenate([dt_low, came[:, at:]], axis=0)
    grads = [grad_rows(left_pairs[0], dt_pair).astype(jnp.bfloat16)] + grads
    grads = [
        grad.reshape(4, 4, 4, ROWS[name], COLS[name]) for name, grad in zip(WEIGHTS, grads)
    ]
    heads = jnp.concatenate([d_decay_log, d_step_bias, d_skip_gain])
    vectors = jnp.concatenate(
        [
            jnp.pad(jnp.stack([d_gain_in, d_gain_ff]), ((0, 0), (0, 768))),
            d_conv,
            jnp.pad(jnp.concatenate([d_scale, heads]), (0, 184))[None],
        ],
        axis=0,
    )
    dt_grad, in_grad, output_weight_grad, gate_up_weight_grad, down_weight_grad, total = (
        scatter_grads(grads, vectors)
    )
    summed_rows = jnp.concatenate([in_grad, dt_grad[:, :24]], axis=1)
    full_gains, full_conv, full_scale = total[0:2, :1024], total[2:7], total[7:8, :1536]
    decay_log_grad, step_bias_grad, skip_gain_grad = (
        total[7, 1536:1560],
        total[7, 1560:1584],
        total[7, 1584:1608],
    )
    position = lax.axis_index("fsdp")
    norm_gains_grad = lax.dynamic_slice_in_dim(
        full_gains, position * norm_gains.shape[1], norm_gains.shape[1], 1
    )
    conv_params_grad = lax.dynamic_slice_in_dim(
        full_conv, position * conv_params.shape[1], conv_params.shape[1], 1
    )
    mixer_scale_grad = lax.dynamic_slice_in_dim(
        full_scale, position * mixer_scale.shape[1], mixer_scale.shape[1], 1
    )
    return (
        layer_output,
        input_grad,
        summed_rows,
        output_weight_grad,
        gate_up_weight_grad,
        down_weight_grad,
        norm_gains_grad,
        conv_params_grad,
        mixer_scale_grad,
        decay_log_grad,
        step_bias_grad,
        skip_gain_grad,
    )


def solution(mesh):
    in_specs = (
        P("fsdp", None),
        P("fsdp", None),
        P("fsdp", None),
        P("fsdp", None),
        P("fsdp", None),
        P("fsdp", None),
        P(None, "fsdp"),
        P(None, "fsdp"),
        P(None, "fsdp"),
        P(),
        P(),
        P(),
    )
    out_specs = (
        P("fsdp", None),
        P("fsdp", None),
        P("fsdp", None),
        P("fsdp", None),
        P("fsdp", None),
        P("fsdp", None),
        P(None, "fsdp"),
        P(None, "fsdp"),
        P(None, "fsdp"),
        P(),
        P(),
        P(),
    )
    return jax.shard_map(local, mesh=mesh, in_specs=in_specs, out_specs=out_specs, check_vma=False)
```

```python
import math

import jax
import jax.numpy as jnp
import numpy as np
from jax import lax
from jax.experimental import pallas as pl
from jax.experimental.pallas import tpu as pltpu
from jax.sharding import PartitionSpec as P

HD = 64
MIXER_HEADS = 24
MIXER_HEAD_SIZE = 64
CONVK = 4
MIXER_FEATURES = 1536
TOK = 128
norm_eps = 1e-05
rope_base = 10000.0
masked_value = -1e30

Y, X, Z = range(3)
AXES = (Y, X, Z)
ORDERS = ((X, Y, Z), (Y, Z, X), (Z, X, Y))
STEPS = (1, 3, 2)
SMALL, INA, INB, OUT, GU, DOWN = range(6)
WEIGHTS = (SMALL, INA, INB, OUT, GU, DOWN)
ROWS = (16, 16, 16, 32, 16, 32)
COLS = (128, 1024, 1024, 512, 2048, 512)
PARTS = (
    ((0, 128),),
    ((0, 384), (384, 768), (768, 1024)),
    ((0, 384), (384, 640), (640, 1024)),
    ((0, 128), (128, 384), (384, 512)),
    ((0, 768), (768, 1408), (1408, 2048)),
    ((0, 128), (128, 256), (256, 512)),
)


class Place:
    def __init__(self):
        me = lax.axis_index("fsdp")
        self.me = me
        self.core = lax.rem(me, 2)
        self.at = [lax.div(me, 32), lax.rem(lax.div(me, 8), 4), lax.rem(lax.div(me, 2), 4)]
        self.sibling = me + 1 - 2 * self.core

    def moved(self, axis, step):
        return lax.rem(self.at[axis] + step, 4)

    def peer(self, axis, step):
        at = list(self.at)
        at[axis] = self.moved(axis, step)
        return ((at[Y] * 4 + at[X]) * 4 + at[Z]) * 2 + self.core

    def partners(self):
        return [self.sibling] + [self.peer(axis, step) for axis in AXES for step in STEPS]


def arrive(place):
    for partner in place.partners():
        pl.semaphore_signal(
            pltpu.get_barrier_semaphore(),
            inc=1,
            device_id=(partner,),
            device_id_type=pl.DeviceIdType.MESH,
        )


def meet(place):
    pl.semaphore_wait(pltpu.get_barrier_semaphore(), len(place.partners()))


def push(src, dst, send_sem, recv_sem, device):
    return pltpu.make_async_remote_copy(
        src_ref=src,
        dst_ref=dst,
        send_sem=send_sem,
        recv_sem=recv_sem,
        device_id=(device,),
        device_id_type=pl.DeviceIdType.MESH,
    )


def block_index(where, low, high):
    return tuple(where.get(axis, slice(None)) for axis in AXES) + (
        slice(None),
        pl.ds(low, high - low),
    )


def some_blocks(ref, count):
    lead = {1: (0, 0, 0), 3: (0, 0, pl.ds(0, 3)), 4: (0, 0), 12: (0, pl.ds(0, 3)), 16: (0,)}
    lead |= {32: (pl.ds(0, 2),), 48: (pl.ds(0, 3),), 64: (slice(None),)}
    return ref.at[lead[count]]


def expect(ref, count, sem, place):
    view = some_blocks(ref, count)
    return push(view, view, sem, sem, place.sibling)


def halved(part, phase_axis, half, order):
    axis = min(one for one in order if one != phase_axis)
    return {axis: pl.ds(2 * half, 2)}


class Gather:
    COUNTS = (3, 12, 48)

    def __init__(self, place, arrays, send_sem, recv_sem):
        self.place, self.arrays = place, arrays
        self.send_sem, self.recv_sem = send_sem, recv_sem

    def ref(self, name):
        if name == SMALL:
            return self.arrays[name]
        return self.arrays[name].at[self.place.core]

    def send_slot(self, name, phase):
        return self.send_sem.at[4 * name + phase]

    def recv_slot(self, name, phase, kind):
        if name == SMALL:
            return self.recv_sem.at[phase]
        return self.recv_sem.at[8 * name - 5 + (0, 1, 4)[phase] + (min(kind, 2) if phase else 0)]

    def slab(self, name, part, phase, step, half=None):
        order = ORDERS[part]
        where = {axis: self.place.at[axis] for axis in order[phase:]}
        where[order[phase]] = self.place.moved(order[phase], step)
        if half is not None:
            where |= halved(part, order[phase], half, order[: phase + 1])
        return self.ref(name).at[block_index(where, *PARTS[name][part])]

    def copy(self, name, part, phase, kind):
        step, source, half = (
            ((1, 0, None), (3, 0, None), (2, 0, None))
            if phase == 0 or name == SMALL
            else ((1, 0, None), (3, 0, None), (1, 3, 0), (3, 1, 1))
        )[kind]
        view = self.slab(name, part, phase, source, half)
        return push(
            view,
            view,
            self.send_slot(name, phase),
            self.recv_slot(name, phase, kind),
            self.place.peer(ORDERS[part][phase], step),
        )

    def start(self, name, phase, kinds=(0, 1)):
        if phase == 0 or name == SMALL:
            kinds = (0, 1, 2)
        for kind in kinds:
            for part in range(len(PARTS[name])):
                self.copy(name, part, phase, kind).start()

    def arrived(self, name, phase, kind=0):
        count = self.COUNTS[phase]
        if phase and name != SMALL:
            count //= 3
        slot = self.recv_slot(name, phase, kind)
        expect(self.ref(name), count, slot, self.place).wait_recv()

    def hand_on(self, name, phase):
        for kind in (0, 1):
            self.arrived(name, phase, kind)
            self.start(name, phase, (kind + 2,))
            if phase == 2:
                self.pass_on(name, (3, 1)[kind])

    def pass_on(self, name, step):
        for part in range(len(PARTS[name])):
            view = self.slab(name, part, 2, step)
            push(
                view,
                view,
                self.send_slot(name, 3),
                self.recv_sem.at[8 * name + 2],
                self.place.sibling,
            ).start()

    def passed(self, name):
        expect(self.ref(name), 64, self.recv_sem.at[8 * name + 2], self.place).wait_recv()

    def finish(self, name):
        for phase in range(3 if name == SMALL else 4):
            count = (*self.COUNTS, 64)[phase]
            expect(self.ref(name), count, self.send_slot(name, phase), self.place).wait_send()


def each(count, body):
    def step(index, nothing):
        body(index)
        return nothing

    lax.fori_loop(0, count, step, 0)


class Enter:
    def __init__(self, place, gather, pack, got, shards, sems):
        self.place, self.gather = place, gather
        self.pack, self.got, self.shards = pack, got, shards
        self.send_sem, self.recv_sem = sems

    def own(self, name, core):
        at = self.place.at
        return self.gather.arrays[name].at[core, at[Y], at[X], at[Z]]

    def copies(self):
        core = self.place.core
        pairs = [(self.pack, self.got)]
        for name in (OUT, DOWN):
            shard = self.shards[name]
            columns = pl.ds(pl.multiple_of((1 - core) * 512, 512), 512)
            rows = pl.ds(pl.multiple_of(core * 16, 16), 16)
            pairs.append((shard.at[:, columns], self.own(name, 1 - core).at[rows, :]))
        return [
            push(src, dst, self.send_sem.at[i], self.recv_sem.at[i], self.place.sibling)
            for i, (src, dst) in enumerate(pairs)
        ]

    COLUMNS = ((INA, 0, 1024), (INB, 1024, 1024), (GU, 2048, 2048), (SMALL, 4096, 128))

    def run(self, greet):
        core, at = self.place.core, self.place.at
        wide = jnp.float32
        for name, low, size in self.COLUMNS[:3]:
            ref = self.shards[GU] if name == GU else self.shards[INA]
            first = 2048 if name == INB else 0
            both = jnp.concatenate(
                [
                    ref[:, first + size * half : first + size * half + size].astype(wide)
                    for half in range(2)
                ],
                axis=0,
            )
            self.pack[:, low : low + size] = both.astype(jnp.bfloat16)
        small = self.shards[SMALL][...]
        self.pack[:, 4096:4224] = jnp.concatenate([small, small], axis=0).astype(jnp.bfloat16)
        greet()
        copies = self.copies()
        for copy in copies:
            copy.start()
        for name in (OUT, DOWN):
            columns = pl.ds(pl.multiple_of(core * 512, 512), 512)
            rows = pl.ds(pl.multiple_of(core * 16, 16), 16)
            self.own(name, core)[rows, :] = self.shards[name][:, columns]
        copies[0].wait_recv()
        for name, low, size in self.COLUMNS:
            mine = self.pack[:, low : low + size].astype(wide)
            other = self.got[:, low : low + size].astype(wide)
            other = jnp.concatenate([other[8:16], other[0:8]], axis=0)
            upper = lax.broadcasted_iota(jnp.int32, (16, size), 0) < 8
            take = upper == (core == 0)
            block = jnp.where(take, mine, other).astype(jnp.bfloat16)
            if name == SMALL:
                self.gather.arrays[name][at[Y], at[X], at[Z]] = block
            else:
                self.own(name, core)[...] = block
        for copy in copies[1:]:
            copy.wait_recv()

    def finish(self):
        for copy in self.copies():
            copy.wait_send()


class Scatter:
    COUNTS = (48, 12, 3)

    def __init__(self, place, grads, first, second, third, send_sem, recv_sem):
        self.place, self.grads = place, grads
        self.got = (first, second, third)
        self.send_sem, self.recv_sem = send_sem, recv_sem

    def send_slot(self, name, phase):
        return self.send_sem.at[3 * name + phase]

    def recv_slot(self, name, phase, early=False):
        return self.recv_sem.at[4 * name + (3 if early else phase)]

    def slab(self, name, part, phase, step, half=None):
        order = ORDERS[part][::-1]
        where = {axis: self.place.at[axis] for axis in order[:phase]}
        where[order[phase]] = self.place.moved(order[phase], step)
        if half is not None:
            where |= halved(part, order[phase], half, order[phase:])
        return self.grads[name].at[block_index(where, *PARTS[name][part])]

    def landing(self, name, part, phase, slot, half=None):
        low, high = PARTS[name][part]
        lead = [slice(None)] * (2 - phase)
        if half is not None:
            lead[0] = pl.ds(2 * half, 2)
        return (slot, *lead, slice(None), pl.ds(low, high - low))

    def push(self, name, part, phase, to, source, half, slot, early=False):
        dst = self.got[phase][name].at[self.landing(name, part, phase, slot, half)]
        push(
            self.slab(name, part, phase, source, half),
            dst,
            self.send_slot(name, phase),
            self.recv_slot(name, phase, early),
            self.place.peer(ORDERS[part][2 - phase], to),
        ).start()

    def start(self, name, phase, parts=None):
        for part in range(len(PARTS[name])) if parts is None else parts:
            if phase or name == SMALL:
                for slot, step in enumerate(STEPS):
                    self.push(name, part, phase, step, step, None, slot)
            else:
                self.push(name, part, 0, 3, 2, 0, 2, True)
                self.push(name, part, 0, 1, 2, 1, 2, True)
                self.push(name, part, 0, 3, 3, 1, 0)
                self.push(name, part, 0, 1, 1, 0, 1)

    def arrived(self, name, phase, early=False):
        count = self.COUNTS[phase]
        if phase == 0 and name != SMALL:
            count = 16 if early else 32
        slot = self.recv_slot(name, phase, early)
        expect(self.grads[name], count, slot, self.place).wait_recv()

    def hand_on(self, name):
        self.arrived(name, 0, True)
        for part in range(len(PARTS[name])):
            for step, half, slot in ((3, 0, 0), (1, 1, 1)):
                own = self.slab(name, part, 0, step, half)
                came = self.got[0][name].at[self.landing(name, part, 0, 2, half)]

                def body(i):
                    own[i] = (own[i].astype(jnp.float32) + came[i].astype(jnp.float32)).astype(
                        jnp.bfloat16
                    )

                each(2, body)
                self.push(name, part, 0, step, step, half, slot)

    def add(self, name, part, phase, pick=()):
        total = self.slab(name, part, phase, 0)[(*pick, Ellipsis)].astype(jnp.float32)
        for slot in range(3 if phase or name == SMALL else 2):
            piece = self.got[phase][name].at[self.landing(name, part, phase, slot)]
            total = total + piece[(*pick, Ellipsis)].astype(jnp.float32)
        return total

    def relay(self, name, phase):
        self.arrived(name, phase)
        for part in range(len(PARTS[name])):
            own = self.slab(name, part, phase, 0)

            def body(i):
                own[i] = self.add(name, part, phase, (i,)).astype(jnp.bfloat16)

            each(4, body)
            self.start(name, phase + 1, (part,))

    def finish(self):
        for name in WEIGHTS:
            for phase, count in enumerate(self.COUNTS):
                slot = self.send_slot(name, phase)
                expect(self.grads[name], count, slot, self.place).wait_send()


class SumAll:
    def __init__(self, place, got, send_sem, recv_sem):
        self.place, self.got = place, got
        self.send_sem, self.recv_sem = send_sem, recv_sem

    def start(self, stage, value):
        if stage == 0:
            slot, devices = self.place.core, [self.place.sibling]
        else:
            axis = AXES[stage - 1]
            slot, devices = self.place.at[axis], [self.place.peer(axis, s) for s in STEPS]
        self.got[stage, slot] = value
        view = self.got.at[stage, slot]
        for device in devices:
            push(view, view, self.send_sem.at[stage], self.recv_sem.at[stage], device).start()

    def expect(self, stage):
        view = self.got.at[stage, pl.ds(0, 3 if stage else 1)]
        return push(
            view, view, self.send_sem.at[stage], self.recv_sem.at[stage], self.place.sibling
        )

    def total(self, stage):
        self.expect(stage).wait_recv()
        total = self.got[stage, 0]
        for slot in range(1, 4 if stage else 2):
            total = total + self.got[stage, slot]
        return total

    def finish(self):
        for stage in range(4):
            self.expect(stage).wait_send()


class End:
    def __init__(self, place, ends, got, outs, send_sem, recv_sem):
        self.place, self.ends, self.got, self.outs = place, ends, got, outs
        self.send_sem, self.recv_sem = send_sem, recv_sem

    def rows(self, name, core):
        half = ROWS[name] // 2
        return pl.ds(pl.multiple_of(core * half, 8), half)

    def copy(self, name):
        slot = name - 1
        return push(
            self.ends[name].at[self.rows(name, 1 - self.place.core), :],
            self.got[name],
            self.send_sem.at[slot],
            self.recv_sem.at[slot],
            self.place.sibling,
        )

    def columns(self, name, core):
        size = COLS[name]
        first = 2048 if name == INB else 0
        return pl.ds(pl.multiple_of(first + core * size, size), size)

    def start(self, name):
        self.copy(name).start()
        core = self.place.core
        self.outs[name][:, self.columns(name, core)] = self.ends[name][self.rows(name, core), :]

    def take(self, name):
        self.copy(name).wait_recv()
        self.outs[name][:, self.columns(name, 1 - self.place.core)] = self.got[name][...]

    def finish(self):
        for name in WEIGHTS[1:]:
            self.copy(name).wait_send()


LOW, WIDE = jnp.bfloat16, jnp.float32


def dot(left, right):
    return jnp.dot(left, right, preferred_element_type=WIDE)


def dot_back(left, right):
    return lax.dot_general(left, right, (((1,), (1,)), ((), ())), preferred_element_type=WIDE)


def dot_over_rows(left, right):
    return lax.dot_general(left, right, (((0,), (0,)), ((), ())), preferred_element_type=WIDE)


def exact_dot(left, right):
    return jnp.dot(left, right, precision=lax.Precision.HIGHEST, preferred_element_type=WIDE)


def sigmoid(v):
    return 1.0 / (1.0 + jnp.exp(-v))


def tile(index, size):
    return pl.ds(pl.multiple_of(index * size, size), size)


def lanes(shape):
    return lax.broadcasted_iota(jnp.int32, shape, len(shape) - 1)


def rows_of(shape):
    return lax.broadcasted_iota(jnp.int32, shape, 0)


def pair_stack(value):
    first = lanes(value.shape) < HD
    zero = jnp.zeros_like(value)
    return jnp.concatenate([jnp.where(first, value, zero), jnp.where(first, zero, value)], axis=0)


def pair_join(stacked):
    first = lanes((TOK, 128)) < HD
    return jnp.where(first, stacked[:TOK], stacked[TOK:])


def swap_halves(value):
    first = lax.rem(lanes(value.shape), HD) < HD // 2
    return jnp.where(first, pltpu.roll(value, 128 - HD // 2, 1), pltpu.roll(value, HD // 2, 1))


def doubled(value, which):
    first = lanes(value.shape) < HD
    turned = pltpu.roll(value, HD, 1)
    return jnp.where(first, value, turned) if which == 0 else jnp.where(first, turned, value)


class Layer:
    def __init__(self, refs):
        vars(self).update(refs)


    def enter(self):
        self.vectors[...] = jnp.zeros((8, 1792), WIDE)
        self.skip_sum[...] = jnp.zeros((8, 1536), WIDE)
        self.heads[...] = jnp.zeros((8, 128), WIDE)
        self.heads[0:1, 0:24] = self.decay_log[...]
        self.heads[1:2, 0:24] = self.step_bias[...]
        own = self.small_shard
        own[...] = jnp.zeros((8, 128), WIDE)
        own[0:2, 0:8] = self.norm_gains[...].astype(WIDE)
        own[2:7, 0:14] = self.conv_params[...].astype(WIDE)
        own[7:8, 0:12] = self.mixer_scale[...].astype(WIDE)
        moved = pltpu.roll(own[...], 32, 1)
        own[...] = jnp.zeros((8, 128), WIDE)
        own[:, 0:24] = self.in_shard[:, 4096:4120].astype(WIDE)
        own[...] = own[...] + moved

    def tables(self):
        position = rows_of((TOK, 128)).astype(WIDE)
        column = lax.rem(lanes((TOK, 128)), HD // 2).astype(WIDE)
        angle = position * jnp.exp(column * (-2.0 * math.log(rope_base) / HD))
        sine = jnp.sin(angle)
        first = lax.rem(lanes((TOK, 128)), HD) < HD // 2
        self.cosines[...] = jnp.cos(angle)
        self.sines[...] = jnp.where(first, -sine, sine)
        first = lanes((1, 128)) < HD
        for i in range(12):
            self.skip[0:1, 128 * i : 128 * i + 128] = jnp.where(
                first,
                self.mixer_skip[0:1, 2 * i : 2 * i + 1],
                self.mixer_skip[0:1, 2 * i + 1 : 2 * i + 2],
            )

    def spread(self):
        self.small_wide[...] = self.g_small[...].astype(WIDE).reshape(1024, 128)

        def turned(row):
            got = self.small_wide[pl.ds(row, 128, stride=8), :]
            return jnp.transpose(got)[32:48]

        for group, size, first, count, into in (
            (8, 1024, 0, 2, self.gains),
            (14, 1792, 2, 5, self.taps),
            (12, 1536, 7, 1, self.scale),
        ):
            stacked = jnp.concatenate([turned(first + i) for i in range(count)], axis=0)
            stacked = stacked.astype(LOW)
            for low in range(0, size, 256):
                start = rows_of((128, 256)) * group
                column = lanes((128, 256)) + low
                hot = (column >= start) & (column < start + group)
                index = jnp.sum(jnp.where(hot, start, 0).astype(WIDE), axis=0, keepdims=True)
                within = (lanes((1, 256)) + low).astype(WIDE) - index
                found = dot(stacked, jnp.where(hot, 1.0, 0.0).astype(LOW))
                mask = rows_of((16, 256)).astype(WIDE) == within
                for i in range(count):
                    into[i : i + 1, low : low + 256] = jnp.sum(
                        jnp.where(mask, found[16 * i : 16 * i + 16], 0.0), axis=0, keepdims=True
                    )


    def norm_in(self):
        x = self.tokens[...].astype(WIDE)
        self.inverse_in[...] = lax.rsqrt(jnp.mean(x * x, axis=-1, keepdims=True) + norm_eps)
        normed = x * self.inverse_in[...] * self.gains[0:1, :]
        self.normed[...] = normed.astype(LOW)
        self.left_in[:, 0:128] = jnp.transpose(normed).astype(LOW)

    def project(self):
        for weights, first in ((self.g_ina, 0), (self.g_inb, 2048)):

            def body(i):
                weight = weights[lax.div(i, 2), :, :, :, :, tile(lax.rem(i, 2), 512)]
                self.proj[:, pl.ds(pl.multiple_of(first + i * 512, 512), 512)] = dot(
                    self.normed[...], weight.reshape(1024, 512)
                )

            each(4, body)
        raw = dot(self.normed[...], self.g_small[...].reshape(1024, 128))
        self.step_raw[...] = jnp.where(lanes((TOK, 128)) < MIXER_HEADS, raw, 0.0)

    def convolved(self, i):
        low = 128 * i
        own = self.proj[:, 2304 + low : 2432 + low]
        row = rows_of((TOK, 128))
        shifted = [own] + [
            jnp.where(row >= k, pltpu.roll(own, k, 0), 0.0) for k in range(1, CONVK)
        ]
        total = self.taps[4:5, low : low + 128]
        for k in range(CONVK):
            total = total + self.taps[3 - k : 4 - k, low : low + 128] * shifted[k]
        return shifted, total

    def activate(self):
        for i in range(14):
            _, total = self.convolved(i)
            active = total * sigmoid(total)
            self.active[:, 128 * i : 128 * i + 128] = active
            self.active_low[:, 128 * i : 128 * i + 128] = active.astype(LOW)

    def steps(self):
        raw = self.step_raw[...] + self.heads[1:2, :]
        step = jnp.maximum(raw, 0.0) + jnp.log1p(jnp.exp(-jnp.abs(raw)))
        rate = -jnp.exp(self.heads[0:1, :])
        lower = jnp.where(rows_of((TOK, TOK)) >= lanes((TOK, TOK)), 1.0, 0.0)
        total = exact_dot(lower, step * rate)
        self.step[...] = step
        self.cum[...] = total
        self.step_rows[...] = jnp.transpose(step)
        self.cum_rows[...] = jnp.transpose(total)

    def causal(self):
        return rows_of((TOK, TOK)) >= lanes((TOK, TOK))

    def attend(self):
        for i in range(5):
            value = self.proj[:, 128 * i : 128 * i + 128]
            turned = value * self.cosines[...] + swap_halves(value) * self.sines[...]
            self.turned[:, 128 * i : 128 * i + 128] = turned.astype(LOW)
        key = self.turned[:, 512:640].astype(WIDE)
        values = self.proj[:, 640:768]
        for which in range(2):
            self.keys[which] = doubled(key, which).astype(LOW)
            self.values[which] = doubled(values, which).astype(LOW)
        causal = self.causal()
        causal = jnp.concatenate([causal, causal], axis=0)
        for i in range(4):
            queries = pair_stack(self.turned[:, 128 * i : 128 * i + 128])
            scores = dot_back(queries, self.keys[i // 2]) * (1.0 / math.sqrt(HD))
            scores = jnp.where(causal, scores, masked_value)
            power = jnp.exp(scores - jnp.max(scores, axis=-1, keepdims=True))
            probs = power / jnp.sum(power, axis=-1, keepdims=True)
            self.probs[i] = probs
            self.mixed[:, 128 * i : 128 * i + 128] = pair_join(
                dot(probs.astype(LOW), self.values[i // 2])
            ).astype(LOW)

    def decay(self, head):
        gaps = self.cum[:, head : head + 1] - self.cum_rows[head : head + 1, :]
        return jnp.exp(jnp.where(self.causal(), gaps, masked_value))

    def mix(self):
        self.inner[...] = dot_back(self.active_low[:, 1664:1792], self.active_low[:, 1536:1664])
        inner = self.inner[...]
        square = jnp.zeros((TOK, 1), WIDE)
        for i in range(12):
            mixing = jnp.concatenate(
                [
                    inner * self.decay(head) * self.step_rows[head : head + 1, :]
                    for head in (2 * i, 2 * i + 1)
                ],
                axis=0,
            ).astype(LOW)
            self.mixing[i] = mixing
            at = slice(128 * i, 128 * i + 128)
            state = pair_join(dot(mixing, self.active_low[:, at]))
            central = state + self.skip[0:1, at] * self.active[:, at]
            self.central[:, at] = central
            gate = self.proj[:, 768 + 128 * i : 896 + 128 * i]
            gated = central * (gate * sigmoid(gate))
            square = square + jnp.sum(gated * gated, axis=-1, keepdims=True)
        inverse = lax.rsqrt(square * (1.0 / MIXER_FEATURES) + norm_eps)
        self.inverse_state[...] = inverse
        for i in range(12):
            at = slice(128 * i, 128 * i + 128)
            gate = self.proj[:, 768 + 128 * i : 896 + 128 * i]
            gated = self.central[:, at] * (gate * sigmoid(gate))
            self.mixed[:, 512 + 128 * i : 640 + 128 * i] = (
                gated * inverse * self.scale[0:1, at]
            ).astype(LOW)

    def turn_left(self, source, into, count):
        for i in range(count):
            block = source[:, 128 * i : 128 * i + 128].astype(WIDE)
            into[128 * i : 128 * i + 128, 0:128] = jnp.transpose(block).astype(LOW)

    def branch(self):
        for half in range(2):
            at = slice(512 * half, 512 * half + 512)
            self.residual[:, at] = self.tokens[:, at].astype(WIDE) + dot(
                self.mixed[...], self.g_out[half].reshape(2048, 512)
            )
        x = self.residual[...]
        self.inverse_ff[...] = lax.rsqrt(jnp.mean(x * x, axis=-1, keepdims=True) + norm_eps)
        normed = x * self.inverse_ff[...] * self.gains[1:2, :]
        self.normed_ff[...] = normed.astype(LOW)
        self.left_gu[:, 0:128] = jnp.transpose(normed).astype(LOW)

    def feed(self):
        for half in range(2):

            def body(i):
                weight = self.g_gu[half, :, :, :, :, tile(i, 512)].reshape(1024, 512)
                self.gate_up[:, pl.ds(pl.multiple_of(half * 2048 + i * 512, 512), 512)] = dot(
                    self.normed_ff[...], weight
                )

            each(4, body)
        for i in range(16):
            at = slice(128 * i, 128 * i + 128)
            gate = self.gate_up[:, at]
            self.hidden[:, at] = (
                gate * sigmoid(gate) * self.gate_up[:, 2048 + 128 * i : 2176 + 128 * i]
            ).astype(LOW)

    def down(self):
        for half in range(2):
            at = slice(512 * half, 512 * half + 512)
            self.layer_output[:, at] = (
                self.residual[:, at] + dot(self.hidden[...], self.g_down[half].reshape(2048, 512))
            ).astype(LOW)


    def back_down(self):
        def body(y):
            grad = dot_back(
                self.cotangent[:, 0:512], self.g_down[0, y].reshape(512, 512)
            ) + dot_back(self.cotangent[:, 512:1024], self.g_down[1, y].reshape(512, 512))
            at = tile(y, 512)
            gate = self.gate_up[:, at]
            up = self.gate_up[:, pl.ds(pl.multiple_of(2048 + y * 512, 512), 512)]
            share = sigmoid(gate)
            self.d_gate[:, at] = (grad * up * (share * (1.0 + gate * (1.0 - share)))).astype(LOW)
            self.d_gate[:, pl.ds(pl.multiple_of(2048 + y * 512, 512), 512)] = (
                grad * (gate * share)
            ).astype(LOW)

        each(4, body)

    def norm_back(self, grad, x, inverse, gain):
        turned = x * inverse
        d_gain = jnp.sum(grad * turned, axis=0, keepdims=True)
        scaled = grad * gain
        d_x = inverse * (scaled - turned * jnp.mean(scaled * turned, axis=-1, keepdims=True))
        return d_x, d_gain

    def back_feed(self):
        def body(y):
            grad = dot_back(self.d_gate[:, 0:2048], self.g_gu[0, y].reshape(256, 2048)) + dot_back(
                self.d_gate[:, 2048:4096], self.g_gu[1, y].reshape(256, 2048)
            )
            self.d_wide[:, tile(y, 256)] = grad

        each(4, body)
        d_x, d_gain = self.norm_back(
            self.d_wide[:, 0:1024], self.residual[...], self.inverse_ff[...], self.gains[1:2, :]
        )
        self.vectors[1:2, 0:1024] = d_gain
        d_residual = self.cotangent[...].astype(WIDE) + d_x
        self.residual[...] = d_residual
        self.d_branch[...] = d_residual.astype(LOW)

    def back_branch(self):
        def body(y):
            self.d_wide[:, tile(y, 512)] = dot_back(
                self.d_branch[:, 0:512], self.g_out[0, y].reshape(512, 512)
            ) + dot_back(self.d_branch[:, 512:1024], self.g_out[1, y].reshape(512, 512))

        each(4, body)

    def back_gated(self):
        inverse = self.inverse_state[...]
        mean = jnp.zeros((TOK, 1), WIDE)
        for i in range(12):
            at = slice(128 * i, 128 * i + 128)
            gate = self.proj[:, 768 + 128 * i : 896 + 128 * i]
            gated = self.central[:, at] * (gate * sigmoid(gate))
            grad = self.d_wide[:, 512 + 128 * i : 640 + 128 * i]
            turned = gated * inverse
            self.vectors[7:8, at] = jnp.sum(grad * turned, axis=0, keepdims=True)
            mean = mean + jnp.sum(grad * self.scale[0:1, at] * turned, axis=-1, keepdims=True)
        mean = mean * (1.0 / MIXER_FEATURES)
        for i in range(12):
            at = slice(128 * i, 128 * i + 128)
            gate = self.proj[:, 768 + 128 * i : 896 + 128 * i]
            share = sigmoid(gate)
            open_gate = gate * share
            central = self.central[:, at]
            grad = self.d_wide[:, 512 + 128 * i : 640 + 128 * i]
            d_gated = inverse * (
                grad * self.scale[0:1, at] - central * open_gate * inverse * mean
            )
            d_central = d_gated * open_gate
            self.d_proj[:, 768 + 128 * i : 896 + 128 * i] = (
                d_gated * central * (share * (1.0 + gate * (1.0 - share)))
            ).astype(LOW)
            self.d_state[:, at] = d_central.astype(LOW)
            self.d_active[:, at] = d_central * self.skip[0:1, at]
            self.skip_sum[0:1, at] = jnp.sum(
                d_central * self.active[:, at], axis=0, keepdims=True
            )

    def back_mix(self):
        inner = self.inner[...]
        self.d_inner[...] = jnp.zeros((TOK, TOK), WIDE)
        self.d_cum[...] = jnp.zeros((TOK, TOK), WIDE)
        self.flow_rows[...] = jnp.zeros((TOK, TOK), WIDE)
        self.d_step_rows[...] = jnp.zeros((TOK, TOK), WIDE)
        lane = lanes((TOK, TOK))
        for i in range(12):
            at = slice(128 * i, 128 * i + 128)
            stacked = pair_stack(self.d_state[:, at])
            d_mixing = dot_back(stacked, self.active_low[:, at])
            self.d_active[:, at] += dot_over_rows(self.mixing[i], stacked)
            for which, head in enumerate((2 * i, 2 * i + 1)):
                grad = d_mixing[TOK * which : TOK * which + TOK]
                decay = self.decay(head)
                step = self.step_rows[head : head + 1, :]
                faded = grad * decay
                self.d_inner[...] += faded * step
                part = faded * inner
                d_step = jnp.sum(part, axis=0, keepdims=True)
                self.d_step_rows[head : head + 1, :] = d_step
                self.flow_rows[head : head + 1, :] = d_step * step
                over = jnp.sum(part * step, axis=-1, keepdims=True)
                self.d_cum[...] = jnp.where(lane == head, over, self.d_cum[...])
        d_inner = self.d_inner[...].astype(LOW)
        self.d_active[:, 1664:1792] = dot(d_inner, self.active_low[:, 1536:1664])
        self.d_active[:, 1536:1664] = dot_over_rows(d_inner, self.active_low[:, 1664:1792])
        d_cum = self.d_cum[...] - jnp.transpose(self.flow_rows[...])
        upper = jnp.where(rows_of((TOK, TOK)) <= lanes((TOK, TOK)), 1.0, 0.0)
        d_rated = exact_dot(upper, d_cum)
        rate = -jnp.exp(self.heads[0:1, :])
        d_step = jnp.transpose(self.d_step_rows[...]) + d_rated * rate
        self.vectors[7:8, 1536:1664] = (
            jnp.sum(d_rated * self.step[...], axis=0, keepdims=True) * rate
        )
        raw = self.step_raw[...] + self.heads[1:2, :]
        d_raw = jnp.where(lane < MIXER_HEADS, d_step * sigmoid(raw), 0.0)
        self.vectors[7:8, 1664:1792] = jnp.sum(d_raw, axis=0, keepdims=True)
        self.right_dt[0:128, :] = d_raw.astype(LOW)
        hot = jnp.where(
            lax.div(rows_of((1536, 128)), MIXER_HEAD_SIZE) == lanes((1536, 128)), 1.0, 0.0
        )
        self.vectors[0:1, 1024:1152] = exact_dot(self.skip_sum[...], hot)[0:1]

    def back_attend(self):
        d_keys, d_values = [], []
        for i in range(4):
            at = slice(128 * i, 128 * i + 128)
            which = i // 2
            d_out = pair_stack(self.d_wide[:, at].astype(LOW))
            d_probs = dot_back(d_out, self.values[which])
            probs = self.probs[i]
            d_scores = probs * (d_probs - jnp.sum(probs * d_probs, axis=-1, keepdims=True))
            d_raw = (d_scores * (1.0 / math.sqrt(HD))).astype(LOW)
            self.unturn(i, pair_join(dot(d_raw, self.keys[which])))
            d_keys.append(dot_over_rows(d_raw, pair_stack(self.turned[:, at])))
            d_values.append(dot_over_rows(probs.astype(LOW), d_out))
        first = lanes((TOK, 128)) < HD

        def joined(parts):
            one, two = parts[0] + parts[1], parts[2] + parts[3]
            return jnp.where(first, one + pltpu.roll(one, HD, 1), two + pltpu.roll(two, HD, 1))

        self.unturn(4, joined(d_keys))
        self.d_proj[:, 640:768] = joined(d_values).astype(LOW)

    def unturn(self, i, grad):
        self.d_proj[:, 128 * i : 128 * i + 128] = (
            grad * self.cosines[...] - swap_halves(grad) * self.sines[...]
        ).astype(LOW)

    def back_activate(self):
        row = rows_of((TOK, 128))
        for i in range(14):
            at = slice(128 * i, 128 * i + 128)
            shifted, total = self.convolved(i)
            share = sigmoid(total)
            grad = self.d_active[:, at] * (share * (1.0 + total * (1.0 - share)))
            self.vectors[6:7, at] = jnp.sum(grad, axis=0, keepdims=True)
            d_in = self.taps[3:4, at] * grad
            for k in range(CONVK):
                self.vectors[5 - k : 6 - k, at] = jnp.sum(grad * shifted[k], axis=0, keepdims=True)
                if k:
                    later = jnp.where(row < TOK - k, pltpu.roll(grad, TOK - k, 0), 0.0)
                    d_in = d_in + self.taps[3 - k : 4 - k, at] * later
            self.d_proj[:, 2304 + 128 * i : 2432 + 128 * i] = d_in.astype(LOW)

    def back_project(self):
        small = self.g_small[...].reshape(1024, 128)
        self.d_wide[:, 0:1024] = dot_back(self.right_dt[0:128, :], small)

        def body(y):
            total = self.d_wide[:, tile(y, 256)]
            for half in range(2):
                low = 1024 * half
                total = total + dot_back(
                    self.d_proj[:, low : low + 1024], self.g_ina[half, y].reshape(256, 1024)
                )
                total = total + dot_back(
                    self.d_proj[:, 2048 + low : 3072 + low], self.g_inb[half, y].reshape(256, 1024)
                )
            self.d_wide[:, tile(y, 256)] = total

        each(4, body)
        d_x, d_gain = self.norm_back(
            self.d_wide[:, 0:1024],
            self.tokens[...].astype(WIDE),
            self.inverse_in[...],
            self.gains[0:1, :],
        )
        self.vectors[0:1, 0:1024] = d_gain
        self.input_grad[...] = (self.residual[...] + d_x).astype(LOW)


    def grad_wide(self, left, right, into):
        width = right.shape[1]
        size = min(width, 512)

        def body(i):
            y, at = lax.rem(i, 4), tile(lax.div(i, 4), size)
            block = dot(left[tile(y, 256), :], right[:, at])
            into[y, :, :, :, at] = block.astype(LOW).reshape(4, 4, 16, size)

        each(4 * (width // size), body)

    def grad_tall(self, left, right, into):
        def body(y):
            block = dot(left[tile(y, 512), :], right[...])
            into[y] = block.astype(LOW).reshape(4, 4, 32, 512)

        each(4, body)


class Swap:
    def __init__(self, place, layer, send_sem, recv_sem):
        self.place, self.layer = place, layer
        self.send_sem, self.recv_sem = send_sem, recv_sem
        self.lefts = (
            None, layer.left_in, None, layer.left_out, layer.left_gu, layer.left_down,
        )
        self.rights = (
            layer.right_dt, layer.right_ina, layer.right_inb, layer.right_out, layer.right_gu,
            layer.right_down,
        )
        self.sources = (
            None, layer.d_proj, layer.d_proj, layer.d_branch, layer.d_gate, layer.cotangent,
        )

    def half(self, name, core):
        size = COLS[name]
        first = 2048 if name == INB else 0
        return pl.ds(pl.multiple_of(first + core * size, size), size)

    def left_copy(self, name):
        ref = self.lefts[name]
        src, dst = ref.at[:, pl.ds(0, 128)], ref.at[:, pl.ds(128, 128)]
        return push(
            src, dst, self.send_sem.at[name], self.recv_sem.at[name], self.place.sibling
        )

    def right_copy(self, name):
        ref, source = self.rights[name], self.sources[name]
        if source is None:
            src = ref.at[pl.ds(0, 128), :]
        else:
            src = source.at[:, self.half(name, 1 - self.place.core)]
        slot = 6 + name
        return push(
            src,
            ref.at[pl.ds(128, 128), :],
            self.send_sem.at[slot],
            self.recv_sem.at[slot],
            self.place.sibling,
        )

    def start_left(self, name):
        self.left_copy(name).start()

    def start_right(self, name):
        ref, source = self.rights[name], self.sources[name]
        if source is not None:
            ref[0:128, :] = source[:, self.half(name, self.place.core)]
        self.right_copy(name).start()

    def arrived(self, name):
        if self.lefts[name] is not None:
            self.left_copy(name).wait_recv()
        self.right_copy(name).wait_recv()

    def finish(self):
        for name in WEIGHTS:
            if name != GU:
                self.right_copy(name).wait_send()
            if self.lefts[name] is not None:
                self.left_copy(name).wait_send()


INS = dict(
    tokens=0, cotangent=1, in_shard=2, out_shard=3, gu_shard=4, down_shard=5, norm_gains=6,
    conv_params=7, mixer_scale=8, decay_log=9, step_bias=10, mixer_skip=11,
)
OUTS = dict(
    layer_output=((TOK, 1024), LOW),
    input_grad=((TOK, 1024), LOW),
    grad_in=((8, 4120), WIDE),
    grad_out=((16, 1024), WIDE),
    grad_gu=((8, 4096), WIDE),
    grad_down=((16, 1024), WIDE),
    total=((8, 1792), WIDE),
)
SCRATCH = dict(
    g_small=((4, 4, 4, 16, 128), LOW),
    g_ina=((2, 4, 4, 4, 16, 1024), LOW),
    g_inb=((2, 4, 4, 4, 16, 1024), LOW),
    g_out=((2, 4, 4, 4, 32, 512), LOW),
    g_gu=((2, 4, 4, 4, 16, 2048), LOW),
    g_down=((2, 4, 4, 4, 32, 512), LOW),
    grad_small=((4, 4, 4, 16, 128), LOW),
    grad_down_low=((4, 4, 4, 32, 512), LOW),
    small_shard=((8, 128), WIDE),
    heads=((8, 128), WIDE),
    skip=((8, 1536), WIDE),
    cosines=((TOK, 128), WIDE),
    sines=((TOK, 128), WIDE),
    pack=((16, 4224), LOW),
    got=((16, 4224), LOW),
    small_wide=((1024, 128), WIDE),
    gains=((8, 1024), WIDE),
    taps=((8, 1792), WIDE),
    scale=((8, 1536), WIDE),
    normed=((TOK, 1024), LOW),
    inverse_in=((TOK, 1), WIDE),
    proj=((TOK, 4096), WIDE),
    step_raw=((TOK, 128), WIDE),
    active=((TOK, 1792), WIDE),
    active_low=((TOK, 1792), LOW),
    step=((TOK, TOK), WIDE),
    cum=((TOK, TOK), WIDE),
    step_rows=((TOK, TOK), WIDE),
    cum_rows=((TOK, TOK), WIDE),
    turned=((TOK, 640), LOW),
    keys=((2, TOK, 128), LOW),
    values=((2, TOK, 128), LOW),
    probs=((4, 256, TOK), WIDE),
    mixed=((TOK, 2048), LOW),
    inner=((TOK, TOK), WIDE),
    mixing=((12, 256, TOK), LOW),
    central=((TOK, 1536), WIDE),
    inverse_state=((TOK, 1), WIDE),
    residual=((TOK, 1024), WIDE),
    inverse_ff=((TOK, 1), WIDE),
    gate_up=((TOK, 4096), WIDE),
    d_gate=((TOK, 4096), LOW),
    d_branch=((TOK, 1024), LOW),
    d_state=((TOK, 1536), LOW),
    skip_sum=((8, 1536), WIDE),
    d_inner=((TOK, TOK), WIDE),
    d_cum=((TOK, TOK), WIDE),
    flow_rows=((TOK, TOK), WIDE),
    d_step_rows=((TOK, TOK), WIDE),
    vectors=((8, 1792), WIDE),
    left_in=((1024, 256), LOW),
    left_out=((2048, 256), LOW),
    left_gu=((1024, 256), LOW),
    left_down=((2048, 256), LOW),
    right_ina=((256, 1024), LOW),
    right_inb=((256, 1024), LOW),
    right_out=((256, 512), LOW),
    right_gu=((256, 2048), LOW),
    right_down=((256, 512), LOW),
    right_dt=((256, 128), LOW),
    sums=((4, 4, 8, 1792), WIDE),
)
LANDINGS = ((3, 4, 4), (3, 4), (3,))
SEMS = dict(
    enter=3, gather=43, scatter=24, sums=4, end=5, swap=12,
)


class Plan:
    def __init__(self, refs):
        names = [*INS, *OUTS, *SCRATCH]
        layer = Layer(dict(zip(names, refs)))
        rest = list(refs[len(names) :])
        landings = [[rest.pop(0) for _ in WEIGHTS] for _ in LANDINGS]
        ends = [None] + [rest.pop(0) for _ in WEIGHTS[1:]]
        ends_got = [None] + [rest.pop(0) for _ in WEIGHTS[1:]]
        sems = {name: (rest.pop(0), rest.pop(0)) for name in SEMS}
        layer.normed_ff, layer.hidden = layer.normed, layer.mixed
        layer.d_proj = layer.d_gate
        layer.d_wide = layer.gate_up.at[:, pl.ds(0, 2048)]
        layer.d_active = layer.gate_up.at[:, pl.ds(2048, 1792)]
        place = Place()
        arrays = (layer.g_small, layer.g_ina, layer.g_inb, layer.g_out, layer.g_gu, layer.g_down)
        shards = (
            layer.small_shard, layer.in_shard, None, layer.out_shard, layer.gu_shard,
            layer.down_shard,
        )
        grads = (
            layer.grad_small,
            layer.g_gu.at[1, :, :, :, :, pl.ds(0, 1024)],
            layer.g_gu.at[1, :, :, :, :, pl.ds(1024, 1024)],
            layer.g_out.at[0],
            layer.g_gu.at[0],
            layer.grad_down_low,
        )
        outs = (None, layer.grad_in, layer.grad_in, layer.grad_out, layer.grad_gu, layer.grad_down)
        self.place, self.layer, self.grads = place, layer, grads
        self.gather = Gather(place, arrays, *sems["gather"])
        self.enter = Enter(place, self.gather, layer.pack, layer.got, shards, sems["enter"])
        self.scatter = Scatter(place, grads, *landings, *sems["scatter"])
        self.sum_all = SumAll(place, layer.sums, *sems["sums"])
        self.end = End(place, ends, ends_got, outs, *sems["end"])
        self.swap = Swap(place, layer, *sems["swap"])

    def last(self, name):
        self.scatter.arrived(name, 2)
        for part, (low, high) in enumerate(PARTS[name]):
            value = self.scatter.add(name, part, 2)
            if name == SMALL:
                mine = jnp.where(self.place.core == 0, value[0:8], value[8:16])
                self.layer.grad_in[:, 4096:4120] = mine[:, 0:24]
            else:
                self.end.ends[name][:, low:high] = value
        if name != SMALL:
            self.end.start(name)


def layer_kernel(*refs):
    plan = Plan(refs)
    place, layer, grads, gather = plan.place, plan.layer, plan.grads, plan.gather
    enter, scatter, sum_all, end, swap = (
        plan.enter, plan.scatter, plan.sum_all, plan.end, plan.swap,
    )

    def onward(name, phase):
        gather.arrived(name, phase, 2 if phase and name != SMALL else 0)
        gather.start(name, phase + 1)
        if phase == 1 and name != SMALL:
            gather.pass_on(name, 0)

    def landed(name):
        gather.arrived(name, 2, 2)
        gather.pass_on(name, 2)

    arrive(place)
    layer.enter()
    enter.run(lambda: meet(place))
    for name in WEIGHTS:
        gather.start(name, 0)
    swap.start_right(DOWN)
    onward(SMALL, 0)
    onward(INA, 0)
    onward(INB, 0)
    onward(OUT, 0)
    onward(SMALL, 1)
    gather.hand_on(INA, 1)
    gather.hand_on(INB, 1)
    onward(GU, 0)
    gather.hand_on(OUT, 1)
    onward(INA, 1)
    onward(INB, 1)
    onward(DOWN, 0)
    onward(OUT, 1)
    gather.hand_on(GU, 1)
    layer.tables()
    gather.arrived(SMALL, 2)
    layer.spread()
    layer.norm_in()
    swap.start_left(INA)
    gather.hand_on(DOWN, 1)
    gather.hand_on(INA, 2)
    gather.hand_on(INB, 2)
    onward(GU, 1)
    gather.hand_on(OUT, 2)
    landed(INA)
    landed(INB)
    onward(DOWN, 1)
    gather.passed(INA)
    gather.passed(INB)
    layer.project()
    landed(OUT)
    layer.activate()
    layer.steps()
    gather.hand_on(GU, 2)
    layer.attend()
    layer.mix()
    gather.hand_on(DOWN, 2)
    gather.passed(OUT)
    layer.branch()
    swap.start_left(GU)
    layer.turn_left(layer.mixed, layer.left_out, 16)
    swap.start_left(OUT)
    landed(GU)
    gather.passed(GU)
    layer.feed()
    layer.turn_left(layer.hidden, layer.left_down, 16)
    swap.start_left(DOWN)
    landed(DOWN)
    swap.arrived(DOWN)
    layer.grad_tall(layer.left_down, layer.right_down, grads[DOWN])
    scatter.start(DOWN, 0)
    gather.passed(DOWN)
    layer.back_down()
    swap.start_right(GU)
    scatter.hand_on(DOWN)
    layer.down()
    layer.back_feed()
    swap.start_right(OUT)
    gather.finish(GU)
    swap.arrived(GU)
    layer.grad_wide(layer.left_gu, layer.right_gu, grads[GU])
    scatter.start(GU, 0)
    layer.back_branch()
    gather.finish(OUT)
    swap.arrived(OUT)
    layer.grad_tall(layer.left_out, layer.right_out, grads[OUT])
    scatter.start(OUT, 0)
    scatter.relay(DOWN, 0)
    swap.right_copy(GU).wait_send()
    layer.back_gated()
    layer.back_attend()
    swap.start_right(INA)
    scatter.hand_on(GU)
    swap.arrived(INA)
    layer.grad_wide(layer.left_in, layer.right_ina, grads[INA])
    scatter.start(INA, 0)
    layer.back_mix()
    swap.start_right(SMALL)
    scatter.hand_on(OUT)
    layer.back_activate()
    swap.start_right(INB)
    swap.arrived(SMALL)
    layer.grad_wide(layer.left_in, layer.right_dt, grads[SMALL])
    scatter.start(SMALL, 0)
    swap.arrived(INB)
    layer.grad_wide(layer.left_in, layer.right_inb, grads[INB])
    scatter.start(INB, 0)
    scatter.relay(DOWN, 1)
    scatter.relay(GU, 0)
    layer.back_project()
    sum_all.start(0, layer.vectors[...])
    scatter.hand_on(INA)
    scatter.relay(SMALL, 0)
    scatter.relay(OUT, 0)
    sum_all.start(1, sum_all.total(0))
    scatter.hand_on(INB)
    plan.last(DOWN)
    scatter.relay(SMALL, 1)
    scatter.relay(GU, 1)
    scatter.relay(INA, 0)
    scatter.relay(OUT, 1)
    sum_all.start(2, sum_all.total(1))
    scatter.relay(INB, 0)
    plan.last(GU)
    plan.last(SMALL)
    scatter.relay(INA, 1)
    plan.last(OUT)
    sum_all.start(3, sum_all.total(2))
    scatter.relay(INB, 1)
    plan.last(INA)
    plan.last(INB)
    for name in (DOWN, GU, OUT, INA, INB):
        end.take(name)
    layer.total[...] = sum_all.total(3)
    for name in (SMALL, INA, INB, DOWN):
        gather.finish(name)
    scatter.finish()
    sum_all.finish()
    end.finish()
    swap.finish()
    enter.finish()


def finish_kernel(*refs):
    ins, outs = refs[:7], refs[7:]
    for ref, into in zip(ins[:6], outs[:6]):
        into[...] = ref[...]
    me = lax.axis_index("fsdp")
    total = ins[6][...]
    column = lanes((8, 1792))

    def share(size):
        start = me * size
        picked = jnp.where((column >= start) & (column < start + size), total, 0.0)
        folded = picked[:, 0:128]
        for i in range(1, 14):
            folded = folded + picked[:, 128 * i : 128 * i + 128]
        return pltpu.roll(folded, lax.rem(1792 - start, 128), 1)

    outs[6][...] = share(8)[0:2, 0:8]
    outs[7][...] = share(14)[2:7, 0:14]
    outs[8][...] = share(12)[7:8, 0:12]
    outs[9][...] = total[7:8, 1536:1560]
    outs[10][...] = total[7:8, 1664:1688]
    outs[11][...] = total[0:1, 1024:1048]


def local(
    tokens, cotangent, input_weight, output_weight, gate_up_weight, down_weight,
    norm_gains, conv_params, mixer_scale, decay_log, step_bias, mixer_skip_factor,
):
    ins = (
        tokens, cotangent, input_weight, output_weight, gate_up_weight, down_weight, norm_gains,
        conv_params, mixer_scale, decay_log[None], step_bias[None], mixer_skip_factor[None],
    )
    blocks = [(ROWS[name], COLS[name]) for name in WEIGHTS]
    scratch = [pltpu.VMEM(*one) for one in SCRATCH.values()]
    scratch += [pltpu.VMEM(lead + block, LOW) for lead in LANDINGS for block in blocks]
    scratch += [pltpu.VMEM(block, WIDE) for block in blocks[1:]]
    scratch += [pltpu.VMEM((block[0] // 2, block[1]), WIDE) for block in blocks[1:]]
    scratch += [pltpu.SemaphoreType.DMA((count,)) for count in SEMS.values() for _ in range(2)]
    whole = pl.BlockSpec(memory_space=pltpu.VMEM)
    results = pl.pallas_call(
        layer_kernel,
        out_shape=[jax.ShapeDtypeStruct(*one) for one in OUTS.values()],
        in_specs=[whole] * len(INS),
        out_specs=[whole] * len(OUTS),
        scratch_shapes=scratch,
        compiler_params=pltpu.CompilerParams(
            collective_id=0, has_side_effects=True, vmem_limit_bytes=63 * 2**20
        ),
        name="layer",
    )(*ins)
    shares = [(2, 8), (5, 14), (1, 12), (1, 24), (1, 24), (1, 24)]
    final = pl.pallas_call(
        finish_kernel,
        out_shape=[jax.ShapeDtypeStruct(*one) for one in list(OUTS.values())[:6]]
        + [jax.ShapeDtypeStruct(one, WIDE) for one in shares],
        in_specs=[whole] * len(OUTS),
        out_specs=[whole] * 12,
        name="finish",
    )(*results)
    return (*final[:9], *(one[0] for one in final[9:]))


def solution(mesh):
    in_specs = (
        P("fsdp", None),
        P("fsdp", None),
        P("fsdp", None),
        P("fsdp", None),
        P("fsdp", None),
        P("fsdp", None),
        P(None, "fsdp"),
        P(None, "fsdp"),
        P(None, "fsdp"),
        P(),
        P(),
        P(),
    )
    out_specs = (
        P("fsdp", None),
        P("fsdp", None),
        P("fsdp", None),
        P("fsdp", None),
        P("fsdp", None),
        P("fsdp", None),
        P(None, "fsdp"),
        P(None, "fsdp"),
        P(None, "fsdp"),
        P(),
        P(),
        P(),
    )
    return jax.shard_map(local, mesh=mesh, in_specs=in_specs, out_specs=out_specs, check_vma=False)
```

```python
import math

import jax
import jax.numpy as jnp
import numpy as np
from jax import lax
from jax.experimental import pallas as pl
from jax.experimental.pallas import tpu as pltpu
from jax.sharding import PartitionSpec as P

HD = 64
MIXER_HEADS = 24
MIXER_HEAD_SIZE = 64
CONVK = 4
MIXER_FEATURES = 1536
TOK = 128
norm_eps = 1e-05
rope_base = 10000.0
masked_value = -1e30

Y, X, Z = range(3)
AXES = (Y, X, Z)
ORDERS = ((X, Y, Z), (Y, Z, X), (Z, X, Y))
STEPS = (1, 3, 2)
SMALL, INA, INB, OUT, GUA, GUB, DOWN = range(7)
WEIGHTS = (SMALL, INA, INB, OUT, GUA, GUB, DOWN)
ROWS = (16, 16, 16, 32, 16, 16, 32)
COLS = (128, 1024, 1024, 512, 1024, 1024, 512)
FIRST = (0, 0, 2048, 0, 0, 1024, 0)
STRIDE = (0, 1024, 1024, 512, 2048, 2048, 512)
PARTS = (
    ((0, 128),),
    ((0, 384), (384, 768), (768, 1024)),
    ((0, 384), (384, 640), (640, 1024)),
    ((0, 128), (128, 384), (384, 512)),
    ((0, 384), (384, 768), (768, 1024)),
    ((0, 384), (384, 640), (640, 1024)),
    ((0, 128), (128, 256), (256, 512)),
)
DIRECT = {SMALL: 3, INA: 2}
BACK_DIRECT = {SMALL: 0, INB: 1}


def half_columns(name, core):
    return pl.ds(pl.multiple_of(FIRST[name] + core * STRIDE[name], 512), COLS[name])


class Place:
    def __init__(self):
        me = lax.axis_index("fsdp")
        self.me = me
        self.core = lax.rem(me, 2)
        self.at = [lax.div(me, 32), lax.rem(lax.div(me, 8), 4), lax.rem(lax.div(me, 2), 4)]
        self.sibling = me + 1 - 2 * self.core

    def moved(self, axis, step):
        return lax.rem(self.at[axis] + step, 4)

    def peer(self, axis, step):
        at = list(self.at)
        at[axis] = self.moved(axis, step)
        return ((at[Y] * 4 + at[X]) * 4 + at[Z]) * 2 + self.core

    def partners(self):
        return [self.sibling] + [self.peer(axis, step) for axis in AXES for step in STEPS]


def arrive(place):
    for partner in place.partners():
        pl.semaphore_signal(
            pltpu.get_barrier_semaphore(),
            inc=1,
            device_id=(partner,),
            device_id_type=pl.DeviceIdType.MESH,
        )


def meet(place):
    pl.semaphore_wait(pltpu.get_barrier_semaphore(), len(place.partners()))


def push(src, dst, send_sem, recv_sem, device):
    return pltpu.make_async_remote_copy(
        src_ref=src,
        dst_ref=dst,
        send_sem=send_sem,
        recv_sem=recv_sem,
        device_id=(device,),
        device_id_type=pl.DeviceIdType.MESH,
    )


def block_index(where, low, high):
    return tuple(where.get(axis, slice(None)) for axis in AXES) + (
        slice(None),
        pl.ds(low, high - low),
    )


def some_blocks(ref, count):
    lead = {1: (0, 0, 0), 3: (0, 0, pl.ds(0, 3)), 4: (0, 0), 12: (0, pl.ds(0, 3)), 16: (0,)}
    lead |= {2: (0, 0, pl.ds(0, 2)), 8: (0, pl.ds(0, 2)), 32: (pl.ds(0, 2),), 48: (pl.ds(0, 3),), 64: (slice(None),)}
    return ref.at[lead[count]]


def expect(ref, count, sem, place):
    view = some_blocks(ref, count)
    return push(view, view, sem, sem, place.sibling)


def halved(part, phase_axis, half, order):
    axis = min(one for one in order if one != phase_axis)
    return {axis: pl.ds(2 * half, 2)}


class Gather:
    COUNTS = (3, 12, 48)

    def __init__(self, place, arrays, send_sem, recv_sem):
        self.place, self.arrays = place, arrays
        self.send_sem, self.recv_sem = send_sem, recv_sem

    def ref(self, name):
        if name == SMALL:
            return self.arrays[name]
        return self.arrays[name].at[self.place.core]

    def send_slot(self, name, phase):
        return self.send_sem.at[4 * name + phase]

    def recv_slot(self, name, phase, kind):
        if name == SMALL:
            return self.recv_sem.at[phase]
        if phase < DIRECT.get(name, 1):
            kind = 0
        elif kind > 1:
            kind = 2
        return self.recv_sem.at[10 * name - 7 + (0, 1, 4)[phase] + kind]

    def slab(self, name, part, phase, step, half=None):
        order = ORDERS[part]
        where = {axis: self.place.at[axis] for axis in order[phase:]}
        where[order[phase]] = self.place.moved(order[phase], step)
        if half is not None:
            where |= halved(part, order[phase], half, order[: phase + 1])
        return self.ref(name).at[block_index(where, *PARTS[name][part])]

    def copy(self, name, part, phase, kind, half=None, slot=None):
        step, source, handed = (
            ((1, 0, None), (3, 0, None), (2, 0, None))
            if phase < DIRECT.get(name, 1)
            else ((1, 0, None), (3, 0, None), (1, 3, 0), (3, 1, 1))
        )[kind]
        view = self.slab(name, part, phase, source, handed if half is None else half)
        return push(
            view,
            view,
            self.send_slot(name, phase),
            self.recv_slot(name, phase, kind) if slot is None else slot,
            self.place.peer(ORDERS[part][phase], step),
        )

    def start(self, name, phase, kinds=(0, 1)):
        if phase < DIRECT.get(name, 1):
            kinds = (0, 1, 2)
        for kind in kinds:
            for part in range(len(PARTS[name])):
                self.copy(name, part, phase, kind).start()

    def late_slot(self, name, kind):
        return self.recv_sem.at[10 * name + kind]

    def start_early(self, name):
        for kind in (0, 1):
            for part in range(len(PARTS[name])):
                self.copy(name, part, 2, kind, kind).start()

    def start_late(self, name):
        for kind in (0, 1):
            slot = self.late_slot(name, kind)
            for part in range(len(PARTS[name])):
                self.copy(name, part, 2, kind, 1 - kind, slot).start()

    def arrived(self, name, phase, kind=0):
        count = self.COUNTS[phase]
        if phase >= DIRECT.get(name, 1):
            count //= 3
            if phase == 2 and kind < 2:
                count //= 2
        slot = self.recv_slot(name, phase, kind)
        expect(self.ref(name), count, slot, self.place).wait_recv()

    def hand_on(self, name, phase, kinds=(0, 1)):
        for kind in kinds:
            self.arrived(name, phase, kind)
            self.start(name, phase, (kind + 2,))

    def arrived_late(self, name, kinds=(0, 1)):
        for kind in kinds:
            slot = self.late_slot(name, kind)
            expect(self.ref(name), 8, slot, self.place).wait_recv()
            self.pass_on(name, (3, 1)[kind])

    def pass_on(self, name, step):
        for part in range(len(PARTS[name])):
            view = self.slab(name, part, 2, step)
            push(
                view,
                view,
                self.send_slot(name, 3),
                self.recv_sem.at[10 * name + 2],
                self.place.sibling,
            ).start()

    def passed(self, name):
        expect(self.ref(name), 64, self.recv_sem.at[10 * name + 2], self.place).wait_recv()

    def finish(self, name):
        for phase in range(3 if name == SMALL else 4):
            count = (*self.COUNTS, 64)[phase]
            expect(self.ref(name), count, self.send_slot(name, phase), self.place).wait_send()


def each(count, body):
    for index in range(count):
        body(index)


class Enter:
    def __init__(self, place, gather, pack, got, shards, sems):
        self.place, self.gather = place, gather
        self.pack, self.got, self.shards = pack, got, shards
        self.send_sem, self.recv_sem = sems

    def own(self, name, core):
        at = self.place.at
        return self.gather.arrays[name].at[core, at[Y], at[X], at[Z]]

    def copies(self):
        core = self.place.core
        pairs = [(self.pack, self.got)]
        for name in (OUT, DOWN):
            shard = self.shards[name]
            columns = half_columns(name, 1 - core)
            rows = pl.ds(pl.multiple_of(core * 16, 16), 16)
            pairs.append((shard.at[:, columns], self.own(name, 1 - core).at[rows, :]))
        return [
            push(src, dst, self.send_sem.at[i], self.recv_sem.at[i], self.place.sibling)
            for i, (src, dst) in enumerate(pairs)
        ]

    COLUMNS = (
        (INA, 0, 1024), (INB, 1024, 1024), (GUA, 2048, 1024), (GUB, 3072, 1024), (SMALL, 4096, 128),
    )

    def run(self, greet):
        core, at = self.place.core, self.place.at
        wide = jnp.float32
        for name, low, size in self.COLUMNS[:4]:
            both = [
                self.shards[name][:, half_columns(name, half)].astype(wide) for half in range(2)
            ]
            self.pack[:, low : low + size] = jnp.concatenate(both, axis=0).astype(jnp.bfloat16)
        small = self.shards[SMALL][...]
        self.pack[:, 4096:4224] = jnp.concatenate([small, small], axis=0).astype(jnp.bfloat16)
        greet()
        copies = self.copies()
        for copy in copies:
            copy.start()
        for name in (OUT, DOWN):
            columns = half_columns(name, core)
            rows = pl.ds(pl.multiple_of(core * 16, 16), 16)
            self.own(name, core)[rows, :] = self.shards[name][:, columns]
        copies[0].wait_recv()
        for name, low, size in self.COLUMNS:
            mine = self.pack[:, low : low + size].astype(wide)
            other = self.got[:, low : low + size].astype(wide)
            other = jnp.concatenate([other[8:16], other[0:8]], axis=0)
            upper = lax.broadcasted_iota(jnp.int32, (16, size), 0) < 8
            take = upper == (core == 0)
            block = jnp.where(take, mine, other).astype(jnp.bfloat16)
            if name == SMALL:
                self.gather.arrays[name][at[Y], at[X], at[Z]] = block
            else:
                self.own(name, core)[...] = block
        for copy in copies[1:]:
            copy.wait_recv()

    def finish(self):
        for copy in self.copies():
            copy.wait_send()


class Scatter:
    COUNTS = (48, 12, 3)

    def __init__(self, place, grads, first, second, third, send_sem, recv_sem):
        self.place, self.grads = place, grads
        self.got = (first, second, third)
        self.send_sem, self.recv_sem = send_sem, recv_sem

    def send_slot(self, name, phase):
        return self.send_sem.at[3 * name + phase]

    def recv_slot(self, name, phase, early=False):
        return self.recv_sem.at[5 * name + phase + (3 if early else 0)]

    def direct(self, name, phase):
        return phase >= BACK_DIRECT.get(name, 2)

    def slab(self, name, part, phase, step, half=None):
        order = ORDERS[part][::-1]
        where = {axis: self.place.at[axis] for axis in order[:phase]}
        where[order[phase]] = self.place.moved(order[phase], step)
        if half is not None:
            where |= halved(part, order[phase], half, order[phase:])
        return self.grads[name].at[block_index(where, *PARTS[name][part])]

    def landing(self, name, part, phase, slot, half=None):
        low, high = PARTS[name][part]
        lead = [slice(None)] * (2 - phase)
        if half is not None:
            lead[0] = pl.ds(2 * half, 2)
        return (slot, *lead, slice(None), pl.ds(low, high - low))

    def push(self, name, part, phase, to, source, half, slot, early=False):
        dst = self.got[phase][name].at[self.landing(name, part, phase, slot, half)]
        push(
            self.slab(name, part, phase, source, half),
            dst,
            self.send_slot(name, phase),
            self.recv_slot(name, phase, early),
            self.place.peer(ORDERS[part][2 - phase], to),
        ).start()

    def start(self, name, phase, parts=None):
        for part in range(len(PARTS[name])) if parts is None else parts:
            if self.direct(name, phase):
                for slot, step in enumerate(STEPS):
                    self.push(name, part, phase, step, step, None, slot)
            else:
                self.push(name, part, phase, 3, 2, 0, 2, True)
                self.push(name, part, phase, 1, 2, 1, 2, True)
                self.push(name, part, phase, 3, 3, 1, 0)
                self.push(name, part, phase, 1, 1, 0, 1)

    def arrived(self, name, phase, early=False):
        count = self.COUNTS[phase]
        if not self.direct(name, phase):
            count = count // 3 * (1 if early else 2)
        slot = self.recv_slot(name, phase, early)
        expect(self.grads[name], count, slot, self.place).wait_recv()

    def hand_on(self, name, phase):
        self.arrived(name, phase, True)
        for part in range(len(PARTS[name])):
            for step, half, slot in ((3, 0, 0), (1, 1, 1)):
                own = self.slab(name, part, phase, step, half)
                came = self.got[phase][name].at[self.landing(name, part, phase, 2, half)]

                def body(i):
                    own[i] = (own[i].astype(jnp.float32) + came[i].astype(jnp.float32)).astype(
                        jnp.bfloat16
                    )

                each(2, body)
                self.push(name, part, phase, step, step, half, slot)

    def add(self, name, part, phase, pick=()):
        total = self.slab(name, part, phase, 0)[(*pick, Ellipsis)].astype(jnp.float32)
        for slot in range(3 if self.direct(name, phase) else 2):
            piece = self.got[phase][name].at[self.landing(name, part, phase, slot)]
            total = total + piece[(*pick, Ellipsis)].astype(jnp.float32)
        return total

    def relay(self, name, phase):
        self.arrived(name, phase)
        for part in range(len(PARTS[name])):
            own = self.slab(name, part, phase, 0)

            def body(i):
                own[i] = self.add(name, part, phase, (i,)).astype(jnp.bfloat16)

            each(4, body)
            self.start(name, phase + 1, (part,))

    def finish(self):
        for name in WEIGHTS:
            for phase, count in enumerate(self.COUNTS):
                slot = self.send_slot(name, phase)
                expect(self.grads[name], count, slot, self.place).wait_send()


class SumAll:
    def __init__(self, place, got, send_sem, recv_sem):
        self.place, self.got = place, got
        self.send_sem, self.recv_sem = send_sem, recv_sem

    def start(self, stage, value):
        if stage == 0:
            slot, devices = self.place.core, [self.place.sibling]
        else:
            axis = AXES[stage - 1]
            slot, devices = self.place.at[axis], [self.place.peer(axis, s) for s in STEPS]
        self.got[stage, slot] = value
        view = self.got.at[stage, slot]
        for device in devices:
            push(view, view, self.send_sem.at[stage], self.recv_sem.at[stage], device).start()

    def expect(self, stage):
        view = self.got.at[stage, pl.ds(0, 3 if stage else 1)]
        return push(
            view, view, self.send_sem.at[stage], self.recv_sem.at[stage], self.place.sibling
        )

    def total(self, stage):
        self.expect(stage).wait_recv()
        total = self.got[stage, 0]
        for slot in range(1, 4 if stage else 2):
            total = total + self.got[stage, slot]
        return total

    def finish(self):
        for stage in range(4):
            self.expect(stage).wait_send()


class End:
    def __init__(self, place, ends, got, outs, send_sem, recv_sem):
        self.place, self.ends, self.got, self.outs = place, ends, got, outs
        self.send_sem, self.recv_sem = send_sem, recv_sem

    def rows(self, name, core):
        half = ROWS[name] // 2
        return pl.ds(pl.multiple_of(core * half, 8), half)

    def copy(self, name):
        slot = name - 1
        return push(
            self.ends[name].at[self.rows(name, 1 - self.place.core), :],
            self.got[name],
            self.send_sem.at[slot],
            self.recv_sem.at[slot],
            self.place.sibling,
        )

    def start(self, name):
        self.copy(name).start()
        core = self.place.core
        self.outs[name][:, half_columns(name, core)] = self.ends[name][self.rows(name, core), :]

    def take(self, name):
        self.copy(name).wait_recv()
        self.outs[name][:, half_columns(name, 1 - self.place.core)] = self.got[name][...]

    def finish(self):
        for name in WEIGHTS[1:]:
            self.copy(name).wait_send()


LOW, WIDE = jnp.bfloat16, jnp.float32


def dot(left, right):
    return jnp.dot(left, right, preferred_element_type=WIDE)


def dot_back(left, right):
    return lax.dot_general(left, right, (((1,), (1,)), ((), ())), preferred_element_type=WIDE)


def dot_over_rows(left, right):
    return lax.dot_general(left, right, (((0,), (0,)), ((), ())), preferred_element_type=WIDE)


def exact_dot(left, right):
    return jnp.dot(left, right, precision=lax.Precision.HIGHEST, preferred_element_type=WIDE)


def sigmoid(v):
    return 1.0 / (1.0 + jnp.exp(-v))


def tile(index, size):
    return pl.ds(index * size, size)


def lanes(shape):
    return lax.broadcasted_iota(jnp.int32, shape, len(shape) - 1)


def rows_of(shape):
    return lax.broadcasted_iota(jnp.int32, shape, 0)


def pair_stack(value):
    first = lanes(value.shape) < HD
    zero = jnp.zeros_like(value)
    return jnp.concatenate([jnp.where(first, value, zero), jnp.where(first, zero, value)], axis=0)


def pair_join(stacked):
    first = lanes((TOK, 128)) < HD
    return jnp.where(first, stacked[:TOK], stacked[TOK:])


def swap_halves(value):
    first = lax.rem(lanes(value.shape), HD) < HD // 2
    return jnp.where(first, pltpu.roll(value, 128 - HD // 2, 1), pltpu.roll(value, HD // 2, 1))


def doubled(value, which):
    first = lanes(value.shape) < HD
    turned = pltpu.roll(value, HD, 1)
    return jnp.where(first, value, turned) if which == 0 else jnp.where(first, turned, value)


class Layer:
    def __init__(self, refs):
        vars(self).update(refs)


    def enter(self):
        self.vectors[...] = jnp.zeros((8, 1792), WIDE)
        self.skip_sum[...] = jnp.zeros((8, 1536), WIDE)
        self.heads[...] = jnp.zeros((8, 128), WIDE)
        self.heads[0:1, 0:24] = self.decay_log[...]
        self.heads[1:2, 0:24] = self.step_bias[...]
        own = self.small_shard
        own[...] = jnp.zeros((8, 128), WIDE)
        own[0:2, 0:8] = self.norm_gains[...].astype(WIDE)
        own[2:7, 0:14] = self.conv_params[...].astype(WIDE)
        own[7:8, 0:12] = self.mixer_scale[...].astype(WIDE)
        moved = pltpu.roll(own[...], 32, 1)
        own[...] = jnp.zeros((8, 128), WIDE)
        own[:, 0:24] = self.in_shard[:, 4096:4120].astype(WIDE)
        own[...] = own[...] + moved

    def tables(self):
        position = rows_of((TOK, 128)).astype(WIDE)
        column = lax.rem(lanes((TOK, 128)), HD // 2).astype(WIDE)
        angle = position * jnp.exp(column * (-2.0 * math.log(rope_base) / HD))
        sine = jnp.sin(angle)
        first = lax.rem(lanes((TOK, 128)), HD) < HD // 2
        self.cosines[...] = jnp.cos(angle)
        self.sines[...] = jnp.where(first, -sine, sine)
        first = lanes((1, 128)) < HD
        for i in range(12):
            self.skip[0:1, 128 * i : 128 * i + 128] = jnp.where(
                first,
                self.mixer_skip[0:1, 2 * i : 2 * i + 1],
                self.mixer_skip[0:1, 2 * i + 1 : 2 * i + 2],
            )

    def spread(self):
        self.small_wide[...] = self.g_small[...].astype(WIDE).reshape(1024, 128)

        def turned(row):
            got = self.small_wide[pl.ds(row, 128, stride=8), :]
            return jnp.transpose(got)[32:48]

        for group, size, first, count, into in (
            (8, 1024, 0, 2, self.gains),
            (14, 1792, 2, 5, self.taps),
            (12, 1536, 7, 1, self.scale),
        ):
            stacked = jnp.concatenate([turned(first + i) for i in range(count)], axis=0)
            stacked = stacked.astype(LOW)
            for low in range(0, size, 256):
                start = rows_of((128, 256)) * group
                column = lanes((128, 256)) + low
                hot = (column >= start) & (column < start + group)
                index = jnp.sum(jnp.where(hot, start, 0).astype(WIDE), axis=0, keepdims=True)
                within = (lanes((1, 256)) + low).astype(WIDE) - index
                found = dot(stacked, jnp.where(hot, 1.0, 0.0).astype(LOW))
                mask = rows_of((16, 256)).astype(WIDE) == within
                for i in range(count):
                    into[i : i + 1, low : low + 256] = jnp.sum(
                        jnp.where(mask, found[16 * i : 16 * i + 16], 0.0), axis=0, keepdims=True
                    )


    def norm_in(self):
        x = self.tokens[...].astype(WIDE)
        self.inverse_in[...] = lax.rsqrt(jnp.mean(x * x, axis=-1, keepdims=True) + norm_eps)
        normed = x * self.inverse_in[...] * self.gains[0:1, :]
        self.normed[...] = normed.astype(LOW)
        self.left_in[:, 0:128] = jnp.transpose(normed).astype(LOW)

    def project_first(self):
        for i in range(4):
            weight = self.g_ina[i // 2, :, :, :, :, tile(i % 2, 512)]
            self.proj[:, tile(i, 512)] = dot(self.normed[...], weight.reshape(1024, 512))

    def project_last(self):
        for i in range(4):
            weight = self.g_inb[i // 2, :, :, :, :, tile(i % 2, 512)]
            self.proj[:, tile(4 + i, 512)] = dot(self.normed[...], weight.reshape(1024, 512))
        raw = dot(self.normed[...], self.g_small[...].reshape(1024, 128))
        self.step_raw[...] = jnp.where(lanes((TOK, 128)) < MIXER_HEADS, raw, 0.0)

    def convolved(self, i):
        low = 128 * i
        own = self.proj[:, 2304 + low : 2432 + low]
        row = rows_of((TOK, 128))
        shifted = [own] + [
            jnp.where(row >= k, pltpu.roll(own, k, 0), 0.0) for k in range(1, CONVK)
        ]
        total = self.taps[4:5, low : low + 128]
        for k in range(CONVK):
            total = total + self.taps[3 - k : 4 - k, low : low + 128] * shifted[k]
        return shifted, total

    def activate(self):
        for i in range(14):
            _, total = self.convolved(i)
            active = total * sigmoid(total)
            self.active[:, 128 * i : 128 * i + 128] = active

    def steps(self):
        raw = self.step_raw[...] + self.heads[1:2, :]
        step = jnp.maximum(raw, 0.0) + jnp.log1p(jnp.exp(-jnp.abs(raw)))
        rate = -jnp.exp(self.heads[0:1, :])
        lower = jnp.where(rows_of((TOK, TOK)) >= lanes((TOK, TOK)), 1.0, 0.0)
        total = exact_dot(lower, step * rate)
        self.step[...] = step
        self.cum[...] = total
        self.step_rows[...] = jnp.transpose(step)
        self.cum_rows[...] = jnp.transpose(total)

    def causal(self):
        return rows_of((TOK, TOK)) >= lanes((TOK, TOK))

    def attend(self):
        for i in range(5):
            value = self.proj[:, 128 * i : 128 * i + 128]
            turned = value * self.cosines[...] + swap_halves(value) * self.sines[...]
            self.turned[:, 128 * i : 128 * i + 128] = turned.astype(LOW)
        key = self.turned[:, 512:640].astype(WIDE)
        values = self.proj[:, 640:768]
        for which in range(2):
            self.keys[which] = doubled(key, which).astype(LOW)
            self.values[which] = doubled(values, which).astype(LOW)
        causal = self.causal()
        causal = jnp.concatenate([causal, causal], axis=0)
        for i in range(4):
            queries = pair_stack(self.turned[:, 128 * i : 128 * i + 128])
            scores = dot_back(queries, self.keys[i // 2]) * (1.0 / math.sqrt(HD))
            scores = jnp.where(causal, scores, masked_value)
            power = jnp.exp(scores - jnp.max(scores, axis=-1, keepdims=True))
            probs = power / jnp.sum(power, axis=-1, keepdims=True)
            self.small_wide[tile(i, 256), :] = probs
            self.mixed[:, 128 * i : 128 * i + 128] = pair_join(
                dot(probs.astype(LOW), self.values[i // 2])
            ).astype(LOW)

    def decay(self, head):
        gaps = self.cum[:, head : head + 1] - self.cum_rows[head : head + 1, :]
        return jnp.exp(jnp.where(self.causal(), gaps, masked_value))

    def mix(self):
        self.inner[...] = dot_back(self.active[:, 1664:1792].astype(LOW), self.active[:, 1536:1664].astype(LOW))
        inner = self.inner[...]
        square = jnp.zeros((TOK, 1), WIDE)
        for i in range(12):
            mixing = jnp.concatenate(
                [
                    inner * self.decay(head) * self.step_rows[head : head + 1, :]
                    for head in (2 * i, 2 * i + 1)
                ],
                axis=0,
            ).astype(LOW)
            self.mixing[i] = mixing
            at = slice(128 * i, 128 * i + 128)
            state = pair_join(dot(mixing, self.active[:, at].astype(LOW)))
            central = state + self.skip[0:1, at] * self.active[:, at]
            self.central[:, at] = central
            gate = self.proj[:, 768 + 128 * i : 896 + 128 * i]
            gated = central * (gate * sigmoid(gate))
            square = square + jnp.sum(gated * gated, axis=-1, keepdims=True)
        inverse = lax.rsqrt(square * (1.0 / MIXER_FEATURES) + norm_eps)
        self.inverse_state[...] = inverse
        for i in range(12):
            at = slice(128 * i, 128 * i + 128)
            gate = self.proj[:, 768 + 128 * i : 896 + 128 * i]
            gated = self.central[:, at] * (gate * sigmoid(gate))
            self.mixed[:, 512 + 128 * i : 640 + 128 * i] = (
                gated * inverse * self.scale[0:1, at]
            ).astype(LOW)

    def turn_left(self, source, into, count):
        for i in range(count):
            block = source[:, 128 * i : 128 * i + 128].astype(WIDE)
            into[128 * i : 128 * i + 128, 0:128] = jnp.transpose(block).astype(LOW)

    def branch(self):
        for half in range(2):
            at = slice(512 * half, 512 * half + 512)
            self.residual[:, at] = self.tokens[:, at].astype(WIDE) + dot(
                self.mixed[...], self.g_out[half].reshape(2048, 512)
            )
        x = self.residual[...]
        self.inverse_ff[...] = lax.rsqrt(jnp.mean(x * x, axis=-1, keepdims=True) + norm_eps)
        normed = x * self.inverse_ff[...] * self.gains[1:2, :]
        self.normed_ff[...] = normed.astype(LOW)
        self.left_gu[:, 0:128] = jnp.transpose(normed).astype(LOW)

    def feed(self, weights, first):
        for i in range(2):
            for half in range(2):
                weight = weights[half, :, :, :, :, tile(i, 512)].reshape(1024, 512)
                low = 2048 * half + first + 512 * i
                self.gate_up[:, low : low + 512] = dot(self.normed_ff[...], weight)
        for i in range(first // 128, first // 128 + 8):
            at = slice(128 * i, 128 * i + 128)
            gate = self.gate_up[:, at]
            hidden = gate * sigmoid(gate) * self.gate_up[:, 2048 + 128 * i : 2176 + 128 * i]
            self.hidden[:, at] = hidden.astype(LOW)
            self.left_down[at, 0:128] = jnp.transpose(hidden).astype(LOW)

    def down(self):
        for half in range(2):
            at = slice(512 * half, 512 * half + 512)
            self.layer_output[:, at] = (
                self.residual[:, at] + dot(self.hidden[...], self.g_down[half].reshape(2048, 512))
            ).astype(LOW)


    def back_down(self, first):
        for y in (first, first + 1):
            grad = dot_back(
                self.cotangent[:, 0:512], self.g_down[0, y].reshape(512, 512)
            ) + dot_back(self.cotangent[:, 512:1024], self.g_down[1, y].reshape(512, 512))
            for i in range(4):
                low = 512 * y + 128 * i
                part = grad[:, 128 * i : 128 * i + 128]
                gate = self.gate_up[:, low : low + 128]
                up = self.gate_up[:, 2048 + low : 2176 + low]
                share = sigmoid(gate)
                self.d_gate[:, low : low + 128] = (
                    part * up * (share * (1.0 + gate * (1.0 - share)))
                ).astype(LOW)
                self.d_gate[:, 2048 + low : 2176 + low] = (part * (gate * share)).astype(LOW)

    def norm_back(self, grad, x, inverse, gain):
        turned = x * inverse
        d_gain = jnp.sum(grad * turned, axis=0, keepdims=True)
        scaled = grad * gain
        d_x = inverse * (scaled - turned * jnp.mean(scaled * turned, axis=-1, keepdims=True))
        return d_x, d_gain

    def back_feed(self, weights, first):
        for y in range(4):
            total = None if first == 0 else self.d_wide[:, tile(y, 256)]
            for half in range(2):
                low = 2048 * half + first
                part = dot_back(
                    self.d_gate[:, low : low + 1024], weights[half, y].reshape(256, 1024)
                )
                total = part if total is None else total + part
            self.d_wide[:, tile(y, 256)] = total

    def back_residual(self):
        d_x, d_gain = self.norm_back(
            self.d_wide[:, 0:1024], self.residual[...], self.inverse_ff[...], self.gains[1:2, :]
        )
        self.vectors[1:2, 0:1024] = d_gain
        d_residual = self.cotangent[...].astype(WIDE) + d_x
        self.proj[:, 0:768] = d_residual[:, 0:768]
        self.gate_up[:, 3840:4096] = d_residual[:, 768:1024]
        self.d_branch[...] = d_residual.astype(LOW)

    def back_branch(self):
        def body(y):
            self.d_wide[:, tile(y, 512)] = dot_back(
                self.d_branch[:, 0:512], self.g_out[0, y].reshape(512, 512)
            ) + dot_back(self.d_branch[:, 512:1024], self.g_out[1, y].reshape(512, 512))

        each(4, body)

    def back_gated(self):
        inverse = self.inverse_state[...]
        mean = jnp.zeros((TOK, 1), WIDE)
        for i in range(12):
            at = slice(128 * i, 128 * i + 128)
            gate = self.proj[:, 768 + 128 * i : 896 + 128 * i]
            gated = self.central[:, at] * (gate * sigmoid(gate))
            grad = self.d_wide[:, 512 + 128 * i : 640 + 128 * i]
            turned = gated * inverse
            self.vectors[7:8, at] = jnp.sum(grad * turned, axis=0, keepdims=True)
            mean = mean + jnp.sum(grad * self.scale[0:1, at] * turned, axis=-1, keepdims=True)
        mean = mean * (1.0 / MIXER_FEATURES)
        for i in range(12):
            at = slice(128 * i, 128 * i + 128)
            gate = self.proj[:, 768 + 128 * i : 896 + 128 * i]
            share = sigmoid(gate)
            open_gate = gate * share
            central = self.central[:, at]
            grad = self.d_wide[:, 512 + 128 * i : 640 + 128 * i]
            d_gated = inverse * (
                grad * self.scale[0:1, at] - central * open_gate * inverse * mean
            )
            d_central = d_gated * open_gate
            self.d_proj[:, 768 + 128 * i : 896 + 128 * i] = (
                d_gated * central * (share * (1.0 + gate * (1.0 - share)))
            ).astype(LOW)
            self.d_state[:, at] = d_central.astype(LOW)
            self.d_active[:, at] = d_central * self.skip[0:1, at]
            self.skip_sum[0:1, at] = jnp.sum(
                d_central * self.active[:, at], axis=0, keepdims=True
            )

    def back_mix(self):
        inner = self.inner[...]
        self.d_inner[...] = jnp.zeros((TOK, TOK), WIDE)
        self.d_cum[...] = jnp.zeros((TOK, TOK), WIDE)
        self.flow_rows[...] = jnp.zeros((TOK, TOK), WIDE)
        self.d_step_rows[...] = jnp.zeros((TOK, TOK), WIDE)
        lane = lanes((TOK, TOK))
        for i in range(12):
            at = slice(128 * i, 128 * i + 128)
            stacked = pair_stack(self.d_state[:, at])
            d_mixing = dot_back(stacked, self.active[:, at].astype(LOW))
            self.d_active[:, at] += dot_over_rows(self.mixing[i], stacked)
            for which, head in enumerate((2 * i, 2 * i + 1)):
                grad = d_mixing[TOK * which : TOK * which + TOK]
                decay = self.decay(head)
                step = self.step_rows[head : head + 1, :]
                faded = grad * decay
                self.d_inner[...] += faded * step
                part = faded * inner
                d_step = jnp.sum(part, axis=0, keepdims=True)
                self.d_step_rows[head : head + 1, :] = d_step
                self.flow_rows[head : head + 1, :] = d_step * step
                over = jnp.sum(part * step, axis=-1, keepdims=True)
                self.d_cum[...] = jnp.where(lane == head, over, self.d_cum[...])
        d_inner = self.d_inner[...].astype(LOW)
        self.d_active[:, 1664:1792] = dot(d_inner, self.active[:, 1536:1664].astype(LOW))
        self.d_active[:, 1536:1664] = dot_over_rows(d_inner, self.active[:, 1664:1792].astype(LOW))
        d_cum = self.d_cum[...] - jnp.transpose(self.flow_rows[...])
        upper = jnp.where(rows_of((TOK, TOK)) <= lanes((TOK, TOK)), 1.0, 0.0)
        d_rated = exact_dot(upper, d_cum)
        rate = -jnp.exp(self.heads[0:1, :])
        d_step = jnp.transpose(self.d_step_rows[...]) + d_rated * rate
        self.vectors[7:8, 1536:1664] = (
            jnp.sum(d_rated * self.step[...], axis=0, keepdims=True) * rate
        )
        raw = self.step_raw[...] + self.heads[1:2, :]
        d_raw = jnp.where(lane < MIXER_HEADS, d_step * sigmoid(raw), 0.0)
        self.vectors[7:8, 1664:1792] = jnp.sum(d_raw, axis=0, keepdims=True)
        self.right_dt[0:128, :] = d_raw.astype(LOW)
        hot = jnp.where(
            lax.div(rows_of((1536, 128)), MIXER_HEAD_SIZE) == lanes((1536, 128)), 1.0, 0.0
        )
        self.vectors[0:1, 1024:1152] = exact_dot(self.skip_sum[...], hot)[0:1]

    def back_attend(self):
        d_keys, d_values = [], []
        for i in range(4):
            at = slice(128 * i, 128 * i + 128)
            which = i // 2
            d_out = pair_stack(self.d_wide[:, at].astype(LOW))
            d_probs = dot_back(d_out, self.values[which])
            probs = self.small_wide[tile(i, 256), :]
            d_scores = probs * (d_probs - jnp.sum(probs * d_probs, axis=-1, keepdims=True))
            d_raw = (d_scores * (1.0 / math.sqrt(HD))).astype(LOW)
            self.unturn(i, pair_join(dot(d_raw, self.keys[which])))
            d_keys.append(dot_over_rows(d_raw, pair_stack(self.turned[:, at])))
            d_values.append(dot_over_rows(probs.astype(LOW), d_out))
        first = lanes((TOK, 128)) < HD

        def joined(parts):
            one, two = parts[0] + parts[1], parts[2] + parts[3]
            return jnp.where(first, one + pltpu.roll(one, HD, 1), two + pltpu.roll(two, HD, 1))

        self.unturn(4, joined(d_keys))
        self.d_proj[:, 640:768] = joined(d_values).astype(LOW)

    def unturn(self, i, grad):
        self.d_proj[:, 128 * i : 128 * i + 128] = (
            grad * self.cosines[...] - swap_halves(grad) * self.sines[...]
        ).astype(LOW)

    def back_activate(self):
        row = rows_of((TOK, 128))
        for i in range(14):
            at = slice(128 * i, 128 * i + 128)
            shifted, total = self.convolved(i)
            share = sigmoid(total)
            grad = self.d_active[:, at] * (share * (1.0 + total * (1.0 - share)))
            self.vectors[6:7, at] = jnp.sum(grad, axis=0, keepdims=True)
            d_in = self.taps[3:4, at] * grad
            for k in range(CONVK):
                self.vectors[5 - k : 6 - k, at] = jnp.sum(grad * shifted[k], axis=0, keepdims=True)
                if k:
                    later = jnp.where(row < TOK - k, pltpu.roll(grad, TOK - k, 0), 0.0)
                    d_in = d_in + self.taps[3 - k : 4 - k, at] * later
            self.d_proj[:, 2304 + 128 * i : 2432 + 128 * i] = d_in.astype(LOW)

    def back_project(self):
        small = self.g_small[...].reshape(1024, 128)
        self.d_wide[:, 0:1024] = dot_back(self.right_dt[0:128, :], small)

        def body(y):
            total = self.d_wide[:, tile(y, 256)]
            for half in range(2):
                low = 1024 * half
                total = total + dot_back(
                    self.d_proj[:, low : low + 1024], self.g_ina[half, y].reshape(256, 1024)
                )
                total = total + dot_back(
                    self.d_proj[:, 2048 + low : 3072 + low], self.g_inb[half, y].reshape(256, 1024)
                )
            self.d_wide[:, tile(y, 256)] = total

        each(4, body)
        d_x, d_gain = self.norm_back(
            self.d_wide[:, 0:1024],
            self.tokens[...].astype(WIDE),
            self.inverse_in[...],
            self.gains[0:1, :],
        )
        self.vectors[0:1, 0:1024] = d_gain
        d_residual = jnp.concatenate([self.proj[:, 0:768], self.gate_up[:, 3840:4096]], axis=1)
        self.input_grad[...] = (d_residual + d_x).astype(LOW)


    def grad_wide(self, left, right, into):
        width = right.shape[1]
        size = min(width, 512)
        for n in range(width // size):
            for y in range(4):
                block = dot(left[tile(y, 256), :], right[:, tile(n, size)])
                into[y, :, :, :, tile(n, size)] = block.astype(LOW).reshape(4, 4, 16, size)

    def grad_tall(self, left, right, into):
        for y in range(4):
            block = dot(left[tile(y, 512), :], right[...])
            into[y] = block.astype(LOW).reshape(4, 4, 32, 512)


class Swap:
    def __init__(self, place, layer, send_sem, recv_sem):
        self.place, self.layer = place, layer
        self.send_sem, self.recv_sem = send_sem, recv_sem
        self.lefts = (
            None, layer.left_in, None, layer.left_out, layer.left_gu, None, layer.left_down,
        )
        self.rights = (
            layer.right_dt, layer.right_ina, layer.right_inb, layer.right_out, layer.right_gua,
            layer.right_gub, layer.right_down,
        )
        self.sources = (
            None, layer.d_proj, layer.d_proj, layer.d_branch, layer.d_gate, layer.d_gate,
            layer.cotangent,
        )

    def left_copy(self, name):
        ref = self.lefts[name]
        src, dst = ref.at[:, pl.ds(0, 128)], ref.at[:, pl.ds(128, 128)]
        return push(
            src, dst, self.send_sem.at[name], self.recv_sem.at[name], self.place.sibling
        )

    def right_copy(self, name):
        ref, source = self.rights[name], self.sources[name]
        if source is None:
            src = ref.at[pl.ds(0, 128), :]
        else:
            src = source.at[:, half_columns(name, 1 - self.place.core)]
        slot = 7 + name
        return push(
            src,
            ref.at[pl.ds(128, 128), :],
            self.send_sem.at[slot],
            self.recv_sem.at[slot],
            self.place.sibling,
        )

    def start_left(self, name):
        self.left_copy(name).start()

    def start_right(self, name):
        ref, source = self.rights[name], self.sources[name]
        if source is not None:
            ref[0:128, :] = source[:, half_columns(name, self.place.core)]
        self.right_copy(name).start()

    def arrived(self, name):
        if self.lefts[name] is not None:
            self.left_copy(name).wait_recv()
        self.right_copy(name).wait_recv()

    def finish(self):
        for name in WEIGHTS:
            if name not in (GUA, GUB):
                self.right_copy(name).wait_send()
            if self.lefts[name] is not None:
                self.left_copy(name).wait_send()


INS = dict(
    tokens=0, cotangent=1, in_shard=2, out_shard=3, gu_shard=4, down_shard=5, norm_gains=6,
    conv_params=7, mixer_scale=8, decay_log=9, step_bias=10, mixer_skip=11,
)
OUTS = dict(
    layer_output=((TOK, 1024), LOW),
    input_grad=((TOK, 1024), LOW),
    grad_in=((8, 4120), WIDE),
    grad_out=((16, 1024), WIDE),
    grad_gu=((8, 4096), WIDE),
    grad_down=((16, 1024), WIDE),
    total=((8, 1792), WIDE),
)
SCRATCH = dict(
    g_small=((4, 4, 4, 16, 128), LOW),
    g_ina=((2, 4, 4, 4, 16, 1024), LOW),
    g_inb=((2, 4, 4, 4, 16, 1024), LOW),
    g_out=((2, 4, 4, 4, 32, 512), LOW),
    g_gua=((2, 4, 4, 4, 16, 1024), LOW),
    g_gub=((2, 4, 4, 4, 16, 1024), LOW),
    g_down=((2, 4, 4, 4, 32, 512), LOW),
    grad_small=((4, 4, 4, 16, 128), LOW),
    grad_down_low=((4, 4, 4, 32, 512), LOW),
    small_shard=((8, 128), WIDE),
    heads=((8, 128), WIDE),
    skip=((8, 1536), WIDE),
    cosines=((TOK, 128), WIDE),
    sines=((TOK, 128), WIDE),
    pack=((16, 4224), LOW),
    got=((16, 4224), LOW),
    small_wide=((1024, 128), WIDE),
    gains=((8, 1024), WIDE),
    taps=((8, 1792), WIDE),
    scale=((8, 1536), WIDE),
    normed=((TOK, 1024), LOW),
    inverse_in=((TOK, 1), WIDE),
    proj=((TOK, 4096), WIDE),
    step_raw=((TOK, 128), WIDE),
    active=((TOK, 1792), WIDE),
    step=((TOK, TOK), WIDE),
    cum=((TOK, TOK), WIDE),
    step_rows=((TOK, TOK), WIDE),
    cum_rows=((TOK, TOK), WIDE),
    turned=((TOK, 640), LOW),
    keys=((2, TOK, 128), LOW),
    values=((2, TOK, 128), LOW),
    mixed=((TOK, 2048), LOW),
    inner=((TOK, TOK), WIDE),
    mixing=((12, 256, TOK), LOW),
    central=((TOK, 1536), WIDE),
    inverse_state=((TOK, 1), WIDE),
    residual=((TOK, 1024), WIDE),
    inverse_ff=((TOK, 1), WIDE),
    gate_up=((TOK, 4096), WIDE),
    d_gate=((TOK, 4096), LOW),
    d_branch=((TOK, 1024), LOW),
    d_state=((TOK, 1536), LOW),
    skip_sum=((8, 1536), WIDE),
    d_inner=((TOK, TOK), WIDE),
    d_cum=((TOK, TOK), WIDE),
    flow_rows=((TOK, TOK), WIDE),
    d_step_rows=((TOK, TOK), WIDE),
    vectors=((8, 1792), WIDE),
    left_in=((1024, 256), LOW),
    left_out=((2048, 256), LOW),
    left_gu=((1024, 256), LOW),
    left_down=((2048, 256), LOW),
    right_ina=((256, 1024), LOW),
    right_inb=((256, 1024), LOW),
    right_out=((256, 512), LOW),
    right_gua=((256, 1024), LOW),
    right_gub=((256, 1024), LOW),
    right_down=((256, 512), LOW),
    right_dt=((256, 128), LOW),
    sums=((4, 4, 8, 1792), WIDE),
)
LANDINGS = ((3, 4, 4), (3, 4), (3,))
SEMS = dict(
    enter=3, gather=63, scatter=35, sums=4, end=6, swap=14,
)


class Plan:
    def __init__(self, refs):
        names = [*INS, *OUTS, *SCRATCH]
        layer = Layer(dict(zip(names, refs)))
        rest = list(refs[len(names) :])
        landings = [[rest.pop(0) for _ in WEIGHTS] for _ in LANDINGS]
        ends = [None] + [rest.pop(0) for _ in WEIGHTS[1:]]
        ends_got = [None] + [rest.pop(0) for _ in WEIGHTS[1:]]
        sems = {name: (rest.pop(0), rest.pop(0)) for name in SEMS}
        layer.normed_ff, layer.hidden = layer.normed, layer.mixed
        layer.d_proj = layer.d_gate
        layer.d_wide = layer.gate_up.at[:, pl.ds(0, 2048)]
        layer.d_active = layer.gate_up.at[:, pl.ds(2048, 1792)]
        place = Place()
        arrays = (
            layer.g_small, layer.g_ina, layer.g_inb, layer.g_out, layer.g_gua, layer.g_gub,
            layer.g_down,
        )
        shards = (
            layer.small_shard, layer.in_shard, layer.in_shard, layer.out_shard, layer.gu_shard,
            layer.gu_shard, layer.down_shard,
        )
        grads = (
            layer.grad_small,
            layer.g_gua.at[1],
            layer.g_gub.at[1],
            layer.g_out.at[0],
            layer.g_gua.at[0],
            layer.g_gub.at[0],
            layer.grad_down_low,
        )
        outs = (
            None, layer.grad_in, layer.grad_in, layer.grad_out, layer.grad_gu, layer.grad_gu,
            layer.grad_down,
        )
        self.place, self.layer, self.grads = place, layer, grads
        self.gather = Gather(place, arrays, *sems["gather"])
        self.enter = Enter(place, self.gather, layer.pack, layer.got, shards, sems["enter"])
        self.scatter = Scatter(place, grads, *landings, *sems["scatter"])
        self.sum_all = SumAll(place, layer.sums, *sems["sums"])
        self.end = End(place, ends, ends_got, outs, *sems["end"])
        self.swap = Swap(place, layer, *sems["swap"])

    def last(self, name):
        self.scatter.arrived(name, 2)
        for part, (low, high) in enumerate(PARTS[name]):
            value = self.scatter.add(name, part, 2)
            if name == SMALL:
                mine = jnp.where(self.place.core == 0, value[0:8], value[8:16])
                self.layer.grad_in[:, 4096:4120] = mine[:, 0:24]
            else:
                self.end.ends[name][:, low:high] = value
        if name != SMALL:
            self.end.start(name)


def layer_kernel(*refs):
    plan = Plan(refs)
    place, layer, grads, gather = plan.place, plan.layer, plan.grads, plan.gather
    enter, scatter, sum_all, end, swap = (
        plan.enter, plan.scatter, plan.sum_all, plan.end, plan.swap,
    )

    def onward(name, phase):
        gather.arrived(name, phase, 0 if phase < DIRECT.get(name, 1) else 2)
        if phase == 0 or name == SMALL:
            gather.start(name, phase + 1)
        else:
            gather.start_early(name)

    def onward_late(name):
        gather.start_late(name)
        gather.pass_on(name, 0)

    def landed(name):
        gather.arrived(name, 2, 2)
        gather.pass_on(name, 2)

    arrive(place)
    layer.enter()
    enter.run(lambda: meet(place))
    gather.start(SMALL, 0)
    gather.start(INA, 0)
    gather.start(INB, 0)
    gather.start(OUT, 0)
    gather.start(GUA, 0)
    gather.start(DOWN, 0)
    gather.start(GUB, 0)
    swap.start_right(DOWN)
    layer.tables()
    onward(SMALL, 0)
    onward(INA, 0)
    onward(INB, 0)
    onward(OUT, 0)
    onward(GUA, 0)
    onward(DOWN, 0)
    onward(GUB, 0)
    onward(SMALL, 1)
    gather.hand_on(INB, 1, (0,))
    gather.hand_on(INB, 1, (1,))
    onward(INA, 1)
    onward_late(INA)
    gather.hand_on(OUT, 1, (0,))
    gather.hand_on(OUT, 1, (1,))
    gather.hand_on(GUA, 1, (0,))
    gather.hand_on(GUA, 1, (1,))
    gather.hand_on(DOWN, 1, (0,))
    gather.hand_on(DOWN, 1, (1,))
    gather.hand_on(GUB, 1, (0,))
    gather.hand_on(GUB, 1, (1,))
    onward(INB, 1)
    gather.arrived(SMALL, 2)
    layer.spread()
    layer.norm_in()
    swap.start_left(INA)
    gather.hand_on(INA, 2, (0,))
    gather.hand_on(INA, 2, (1,))
    onward_late(INB)
    gather.arrived_late(INA, (0,))
    gather.arrived_late(INA, (1,))
    onward(OUT, 1)
    onward(GUA, 1)
    gather.hand_on(INB, 2, (0,))
    gather.hand_on(INB, 2, (1,))
    onward_late(OUT)
    landed(INA)
    gather.passed(INA)
    layer.project_first()
    gather.arrived_late(INB, (0,))
    gather.arrived_late(INB, (1,))
    onward(DOWN, 1)
    layer.attend()
    gather.hand_on(OUT, 2, (0,))
    gather.hand_on(OUT, 2, (1,))
    onward_late(GUA)
    gather.hand_on(GUA, 2, (0,))
    gather.hand_on(GUA, 2, (1,))
    onward_late(DOWN)
    landed(INB)
    gather.arrived_late(OUT, (0,))
    gather.arrived_late(OUT, (1,))
    gather.passed(INB)
    layer.project_last()
    layer.activate()
    layer.steps()
    gather.hand_on(DOWN, 2, (0,))
    gather.hand_on(DOWN, 2, (1,))
    layer.mix()
    landed(OUT)
    onward(GUB, 1)
    onward_late(GUB)
    gather.arrived_late(GUA, (0,))
    gather.arrived_late(GUA, (1,))
    gather.passed(OUT)
    layer.branch()
    swap.start_left(GUA)
    layer.turn_left(layer.mixed, layer.left_out, 16)
    swap.start_left(OUT)
    landed(GUA)
    gather.arrived_late(DOWN, (0,))
    gather.arrived_late(DOWN, (1,))
    landed(DOWN)
    gather.passed(GUA)
    layer.feed(layer.g_gua, 0)
    gather.hand_on(GUB, 2, (0,))
    gather.hand_on(GUB, 2, (1,))
    gather.passed(DOWN)
    layer.back_down(0)
    swap.start_right(GUA)
    gather.arrived_late(GUB, (0,))
    gather.arrived_late(GUB, (1,))
    layer.back_feed(layer.g_gua, 0)
    gather.finish(GUA)
    swap.arrived(GUA)
    layer.grad_wide(layer.left_gu, layer.right_gua, grads[GUA])
    scatter.start(GUA, 0)
    landed(GUB)
    gather.passed(GUB)
    layer.feed(layer.g_gub, 1024)
    swap.start_left(DOWN)
    layer.back_down(2)
    swap.start_right(GUB)
    layer.back_feed(layer.g_gub, 1024)
    layer.back_residual()
    swap.start_right(OUT)
    scatter.hand_on(GUA, 0)
    swap.arrived(DOWN)
    layer.grad_tall(layer.left_down, layer.right_down, grads[DOWN])
    scatter.start(DOWN, 0)
    gather.finish(GUB)
    swap.arrived(GUB)
    layer.grad_wide(layer.left_gu, layer.right_gub, grads[GUB])
    scatter.start(GUB, 0)
    layer.back_branch()
    swap.right_copy(GUA).wait_send()
    swap.right_copy(GUB).wait_send()
    layer.back_gated()
    layer.back_attend()
    swap.start_right(INA)
    scatter.relay(GUA, 0)
    scatter.hand_on(DOWN, 0)
    layer.back_mix()
    swap.start_right(SMALL)
    gather.finish(OUT)
    swap.arrived(OUT)
    layer.grad_tall(layer.left_out, layer.right_out, grads[OUT])
    scatter.start(OUT, 0)
    scatter.hand_on(GUB, 0)
    swap.arrived(INA)
    layer.grad_wide(layer.left_in, layer.right_ina, grads[INA])
    scatter.start(INA, 0)
    layer.back_activate()
    swap.start_right(INB)
    scatter.hand_on(GUA, 1)
    swap.arrived(SMALL)
    layer.grad_wide(layer.left_in, layer.right_dt, grads[SMALL])
    scatter.start(SMALL, 0)
    layer.down()
    swap.arrived(INB)
    layer.grad_wide(layer.left_in, layer.right_inb, grads[INB])
    scatter.start(INB, 0)
    layer.back_project()
    sum_all.start(0, layer.vectors[...])
    scatter.relay(DOWN, 0)
    scatter.hand_on(OUT, 0)
    sum_all.start(1, sum_all.total(0))
    scatter.relay(GUB, 0)
    scatter.hand_on(INA, 0)
    scatter.relay(GUA, 1)
    scatter.relay(SMALL, 0)
    scatter.hand_on(INB, 0)
    scatter.hand_on(DOWN, 1)
    scatter.relay(OUT, 0)
    scatter.hand_on(GUB, 1)
    sum_all.start(2, sum_all.total(1))
    scatter.relay(INA, 0)
    plan.last(GUA)
    scatter.relay(SMALL, 1)
    end.take(GUA)
    scatter.relay(INB, 0)
    scatter.relay(DOWN, 1)
    scatter.hand_on(OUT, 1)
    scatter.relay(GUB, 1)
    scatter.hand_on(INA, 1)
    sum_all.start(3, sum_all.total(2))
    plan.last(SMALL)
    scatter.relay(OUT, 1)
    scatter.relay(INB, 1)
    scatter.relay(INA, 1)
    plan.last(DOWN)
    plan.last(GUB)
    end.take(DOWN)
    end.take(GUB)
    layer.total[...] = sum_all.total(3)
    plan.last(OUT)
    plan.last(INB)
    plan.last(INA)
    end.take(OUT)
    end.take(INB)
    end.take(INA)
    for name in (SMALL, INA, INB, DOWN):
        gather.finish(name)
    scatter.finish()
    sum_all.finish()
    end.finish()
    swap.finish()
    enter.finish()


def finish_kernel(*refs):
    ins, outs = refs[:7], refs[7:]
    for ref, into in zip(ins[:6], outs[:6]):
        into[...] = ref[...]
    me = lax.axis_index("fsdp")
    total = ins[6][...]
    column = lanes((8, 1792))

    def share(size):
        start = me * size
        picked = jnp.where((column >= start) & (column < start + size), total, 0.0)
        folded = picked[:, 0:128]
        for i in range(1, 14):
            folded = folded + picked[:, 128 * i : 128 * i + 128]
        return pltpu.roll(folded, lax.rem(1792 - start, 128), 1)

    outs[6][...] = share(8)[0:2, 0:8]
    outs[7][...] = share(14)[2:7, 0:14]
    outs[8][...] = share(12)[7:8, 0:12]
    outs[9][...] = total[7:8, 1536:1560]
    outs[10][...] = total[7:8, 1664:1688]
    outs[11][...] = total[0:1, 1024:1048]


def local(
    tokens, cotangent, input_weight, output_weight, gate_up_weight, down_weight,
    norm_gains, conv_params, mixer_scale, decay_log, step_bias, mixer_skip_factor,
):
    ins = (
        tokens, cotangent, input_weight, output_weight, gate_up_weight, down_weight, norm_gains,
        conv_params, mixer_scale, decay_log[None], step_bias[None], mixer_skip_factor[None],
    )
    blocks = [(ROWS[name], COLS[name]) for name in WEIGHTS]
    scratch = [pltpu.VMEM(*one) for one in SCRATCH.values()]
    scratch += [pltpu.VMEM(lead + block, LOW) for lead in LANDINGS for block in blocks]
    scratch += [pltpu.VMEM(block, WIDE) for block in blocks[1:]]
    scratch += [pltpu.VMEM((block[0] // 2, block[1]), WIDE) for block in blocks[1:]]
    scratch += [pltpu.SemaphoreType.DMA((count,)) for count in SEMS.values() for _ in range(2)]
    whole = pl.BlockSpec(memory_space=pltpu.VMEM)
    results = pl.pallas_call(
        layer_kernel,
        out_shape=[jax.ShapeDtypeStruct(*one) for one in OUTS.values()],
        in_specs=[whole] * len(INS),
        out_specs=[whole] * len(OUTS),
        scratch_shapes=scratch,
        compiler_params=pltpu.CompilerParams(
            collective_id=0, has_side_effects=True, vmem_limit_bytes=127 * 2**19
        ),
        name="layer",
    )(*ins)
    shares = [(2, 8), (5, 14), (1, 12), (1, 24), (1, 24), (1, 24)]
    final = pl.pallas_call(
        finish_kernel,
        out_shape=[jax.ShapeDtypeStruct(*one) for one in list(OUTS.values())[:6]]
        + [jax.ShapeDtypeStruct(one, WIDE) for one in shares],
        in_specs=[whole] * len(OUTS),
        out_specs=[whole] * 12,
        name="finish",
    )(*results)
    return (*final[:9], *(one[0] for one in final[9:]))


def solution(mesh):
    in_specs = (
        P("fsdp", None),
        P("fsdp", None),
        P("fsdp", None),
        P("fsdp", None),
        P("fsdp", None),
        P("fsdp", None),
        P(None, "fsdp"),
        P(None, "fsdp"),
        P(None, "fsdp"),
        P(),
        P(),
        P(),
    )
    out_specs = (
        P("fsdp", None),
        P("fsdp", None),
        P("fsdp", None),
        P("fsdp", None),
        P("fsdp", None),
        P("fsdp", None),
        P(None, "fsdp"),
        P(None, "fsdp"),
        P(None, "fsdp"),
        P(),
        P(),
        P(),
    )
    return jax.shard_map(local, mesh=mesh, in_specs=in_specs, out_specs=out_specs, check_vma=False)
```

```python
import math

import jax
import jax.numpy as jnp
import numpy as np
from jax import lax
from jax.experimental import pallas as pl
from jax.experimental.pallas import tpu as pltpu
from jax.sharding import PartitionSpec as P

HD = 64
MIXER_HEADS = 24
MIXER_HEAD_SIZE = 64
CONVK = 4
MIXER_FEATURES = 1536
TOK = 128
norm_eps = 1e-05
rope_base = 10000.0
masked_value = -1e30

Y, X, Z = range(3)
AXES = (Y, X, Z)
STEPS = (1, 3, 2)
SMALL, INA, INB, OUT, GU, DOWN = range(6)
WEIGHTS = (SMALL, INA, INB, OUT, GU, DOWN)
PAIRED = (GU, DOWN)
ROWS = (16, 16, 16, 32, 16, 32)
COLS = (128, 1024, 1024, 512, 1024, 512)
FIRST = (0, 0, 2048, 0, 0, 0)
DEPTH = (4, 4, 4, 4, 4, 2)
ORDERS = ((X, Y, Z), (Y, Z, X), (Z, X, Y))
PAIR_ORDERS = ((Y, X, Z), (Y, Z, X))
PARTS = (
    ((0, 128),),
    ((0, 256), (256, 512), (512, 1024)),
    ((0, 384), (384, 768), (768, 1024)),
    ((0, 128), (128, 256), (256, 512)),
    ((0, 512), (512, 1024)),
    ((0, 256), (256, 512)),
)
DIRECT = {SMALL: 3, INA: 2, INB: 2, OUT: 2}
BACK_DIRECT = {SMALL: 0, INB: 1, OUT: 1}


def order_of(name, part):
    return (PAIR_ORDERS if name in PAIRED else ORDERS)[part]


def extent(name, axis):
    return DEPTH[name] if axis == Y else 4


def steps_of(name, axis):
    return (2,) if name in PAIRED and axis == Y else STEPS


def half_columns(name, core):
    return pl.ds(pl.multiple_of(FIRST[name] + core * COLS[name], 512), COLS[name])


class Place:
    def __init__(self):
        me = lax.axis_index("fsdp")
        self.me = me
        self.core = lax.rem(me, 2)
        self.at = [lax.div(me, 32), lax.rem(lax.div(me, 8), 4), lax.rem(lax.div(me, 2), 4)]
        self.sibling = me + 1 - 2 * self.core
        self.parity = lax.rem(self.at[Y], 2)
        self.pair = lax.div(self.at[Y], 2)
        self.mate = me + 32 - 64 * self.parity

    def moved(self, axis, step):
        return lax.rem(self.at[axis] + step, 4)

    def spot(self, name, axis, step):
        if name in PAIRED and axis == Y:
            pair = lax.rem(self.pair + step // 2, 2)
            return pl.ds(2 * pair, 2) if name == GU else pair
        return self.moved(axis, step)

    def peer(self, axis, step):
        at = list(self.at)
        at[axis] = self.moved(axis, step)
        return ((at[Y] * 4 + at[X]) * 4 + at[Z]) * 2 + self.core

    def partners(self):
        return [self.sibling] + [self.peer(axis, step) for axis in AXES for step in STEPS]


def arrive(place):
    for partner in place.partners():
        pl.semaphore_signal(
            pltpu.get_barrier_semaphore(),
            inc=1,
            device_id=(partner,),
            device_id_type=pl.DeviceIdType.MESH,
        )


def meet(place):
    pl.semaphore_wait(pltpu.get_barrier_semaphore(), len(place.partners()))


def push(src, dst, send_sem, recv_sem, device):
    return pltpu.make_async_remote_copy(
        src_ref=src,
        dst_ref=dst,
        send_sem=send_sem,
        recv_sem=recv_sem,
        device_id=(device,),
        device_id_type=pl.DeviceIdType.MESH,
    )


def block_index(where, low, high):
    return tuple(where.get(axis, slice(None)) for axis in AXES) + (
        slice(None),
        pl.ds(low, high - low),
    )


def expect(ref, count, sem, place):
    sizes = [
        (i, j, k)
        for i in range(1, ref.shape[0] + 1)
        for j in range(1, 5)
        for k in range(1, 5)
        if i * j * k == count
    ][0]
    view = ref.at[tuple(pl.ds(0, size) for size in sizes)]
    return push(view, view, sem, sem, place.sibling)


def halved(name, axes, half):
    axis = min(axes)
    size = extent(name, axis) // 2
    return {axis: pl.ds(size * half, size)}


def slab_blocks(name, axes, axis):
    count = 2 if name == GU and axis == Y else 1
    for one in axes:
        count *= extent(name, one)
    return count


class Gather:
    def __init__(self, place, arrays, send_sem, recv_sem):
        self.place, self.arrays = place, arrays
        self.send_sem, self.recv_sem = send_sem, recv_sem

    def ref(self, name):
        if name == SMALL:
            return self.arrays[name]
        return self.arrays[name].at[self.place.core]

    def direct(self, name, phase):
        return phase < DIRECT.get(name, 1)

    def blocks(self, name, phase):
        order = order_of(name, 0)
        return slab_blocks(name, order[:phase], order[phase])

    def send_slot(self, name, phase):
        return self.send_sem.at[4 * name + phase]

    def recv_slot(self, name, phase, kind):
        if self.direct(name, phase):
            kind = 0
        elif kind > 1:
            kind = 2
        if name == SMALL:
            return self.recv_sem.at[phase]
        return self.recv_sem.at[10 * name - 7 + (0, 1, 4)[phase] + kind]

    def slab(self, name, part, phase, step, half=None):
        order = order_of(name, part)
        where = {axis: self.place.spot(name, axis, 0) for axis in order[phase:]}
        where[order[phase]] = self.place.spot(name, order[phase], step)
        if half is not None:
            where |= halved(name, order[:phase], half)
        return self.ref(name).at[block_index(where, *PARTS[name][part])]

    def copy(self, name, part, phase, kind, half=None, slot=None):
        axis = order_of(name, part)[phase]
        step, source, handed = (
            [(one, 0, None) for one in steps_of(name, axis)]
            if self.direct(name, phase)
            else ((1, 0, None), (3, 0, None), (1, 3, 0), (3, 1, 1))
        )[kind]
        view = self.slab(name, part, phase, source, handed if half is None else half)
        return push(
            view,
            view,
            self.send_slot(name, phase),
            self.recv_slot(name, phase, kind) if slot is None else slot,
            self.place.peer(axis, step),
        )

    def start(self, name, phase, kinds=(0, 1)):
        if self.direct(name, phase):
            kinds = range(len(steps_of(name, order_of(name, 0)[phase])))
        for kind in kinds:
            for part in range(len(PARTS[name])):
                self.copy(name, part, phase, kind).start()

    def late_slot(self, name, kind):
        return self.recv_sem.at[10 * name + kind]

    def start_early(self, name):
        for kind in (0, 1):
            for part in range(len(PARTS[name])):
                self.copy(name, part, 2, kind, kind).start()

    def start_late(self, name):
        for kind in (0, 1):
            slot = self.late_slot(name, kind)
            for part in range(len(PARTS[name])):
                self.copy(name, part, 2, kind, 1 - kind, slot).start()

    def arrived(self, name, phase, kind=0):
        count = self.blocks(name, phase)
        if self.direct(name, phase):
            count *= len(steps_of(name, order_of(name, 0)[phase]))
        elif phase == 2 and kind < 2:
            count //= 2
        slot = self.recv_slot(name, phase, kind)
        expect(self.ref(name), count, slot, self.place).wait_recv()

    def hand_on(self, name, phase, kinds=(0, 1)):
        for kind in kinds:
            self.arrived(name, phase, kind)
            self.start(name, phase, (kind + 2,))

    def arrived_late(self, name, kinds=(0, 1)):
        for kind in kinds:
            slot = self.late_slot(name, kind)
            expect(self.ref(name), self.blocks(name, 2) // 2, slot, self.place).wait_recv()
            self.pass_on(name, (3, 1)[kind])

    def pass_on(self, name, step):
        for part in range(len(PARTS[name])):
            view = self.slab(name, part, 2, step)
            push(
                view,
                view,
                self.send_slot(name, 3),
                self.recv_sem.at[10 * name + 2],
                self.place.sibling,
            ).start()

    def passed(self, name):
        count = 16 * DEPTH[name]
        expect(self.ref(name), count, self.recv_sem.at[10 * name + 2], self.place).wait_recv()

    def finish(self, name):
        for phase in range(3):
            count = self.blocks(name, phase)
            if self.direct(name, phase):
                count *= len(steps_of(name, order_of(name, 0)[phase]))
            else:
                count *= 3
            expect(self.ref(name), count, self.send_slot(name, phase), self.place).wait_send()
        if name != SMALL:
            slot = self.send_slot(name, 3)
            expect(self.ref(name), 16 * DEPTH[name], slot, self.place).wait_send()


def each(count, body):
    for index in range(count):
        body(index)


class Enter:
    COLUMNS = ((INA, 0, 1024), (INB, 1024, 1024), (GU, 2048, 2048), (SMALL, 4096, 128))

    def __init__(self, place, gather, pack, got, stage, shards, sems):
        self.place, self.gather = place, gather
        self.pack, self.got, self.stage, self.shards = pack, got, stage, shards
        self.send_sem, self.recv_sem = sems

    def own(self, name, core):
        at = self.place.at
        first = self.place.pair if name == DOWN else at[Y]
        return self.gather.arrays[name].at[core, first, at[X], at[Z]]

    def copies(self):
        core = self.place.core
        pairs = [(self.pack, self.got)]
        for name in (OUT, DOWN):
            rows = pl.ds(pl.multiple_of(core * 16, 16), 16)
            src = self.shards[name].at[:, half_columns(name, 1 - core)]
            pairs.append((src, self.own(name, 1 - core).at[rows, :]))
        return [
            push(src, dst, self.send_sem.at[i], self.recv_sem.at[i], self.place.sibling)
            for i, (src, dst) in enumerate(pairs)
        ]

    def mate_copy(self):
        return push(
            self.stage,
            self.own(GU, self.place.core),
            self.send_sem.at[3],
            self.recv_sem.at[3],
            self.place.mate,
        )

    def run(self, greet):
        core, at = self.place.core, self.place.at
        wide = jnp.float32
        for name, low, size in self.COLUMNS[:3]:
            first = FIRST[name]
            both = [
                self.shards[name][:, first + size * half : first + size * half + size]
                for half in range(2)
            ]
            both = [one.astype(wide) for one in both]
            self.pack[:, low : low + size] = jnp.concatenate(both, axis=0).astype(jnp.bfloat16)
        small = self.shards[SMALL][...]
        self.pack[:, 4096:4224] = jnp.concatenate([small, small], axis=0).astype(jnp.bfloat16)
        greet()
        copies = self.copies()
        for copy in copies:
            copy.start()
        for name in (OUT, DOWN):
            rows = pl.ds(pl.multiple_of(core * 16, 16), 16)
            self.own(name, core)[rows, :] = self.shards[name][:, half_columns(name, core)]
        copies[0].wait_recv()
        for name, low, size in self.COLUMNS:
            mine = self.pack[:, low : low + size].astype(wide)
            other = self.got[:, low : low + size].astype(wide)
            other = jnp.concatenate([other[8:16], other[0:8]], axis=0)
            upper = lax.broadcasted_iota(jnp.int32, (16, size), 0) < 8
            take = upper == (core == 0)
            block = jnp.where(take, mine, other)
            if name == SMALL:
                self.gather.arrays[name][at[Y], at[X], at[Z]] = block.astype(jnp.bfloat16)
            elif name == GU:
                even = jnp.concatenate([block[:, 0:512], block[:, 1024:1536]], axis=1)
                odd = jnp.concatenate([block[:, 512:1024], block[:, 1536:2048]], axis=1)
                first = self.place.parity == 0
                own = jnp.where(first, even, odd).astype(jnp.bfloat16)
                self.own(GU, core)[...] = own
                self.stage[...] = jnp.where(first, odd, even).astype(jnp.bfloat16)
                self.mate_copy().start()
            else:
                self.own(name, core)[...] = block.astype(jnp.bfloat16)
        for copy in copies[1:]:
            copy.wait_recv()

    def finish(self):
        for copy in self.copies():
            copy.wait_send()
        self.mate_copy().wait_send()


class Scatter:
    def __init__(self, place, grads, first, second, third, send_sem, recv_sem):
        self.place, self.grads = place, grads
        self.got = (first, second, third)
        self.send_sem, self.recv_sem = send_sem, recv_sem

    def send_slot(self, name, phase):
        return self.send_sem.at[3 * name + phase]

    def recv_slot(self, name, phase, early=False):
        return self.recv_sem.at[5 * name + phase + (3 if early else 0)]

    def direct(self, name, phase):
        return phase >= BACK_DIRECT.get(name, 2)

    def order(self, name, part):
        return order_of(name, part)[::-1]

    def blocks(self, name, phase):
        order = self.order(name, 0)
        return slab_blocks(name, order[phase + 1 :], order[phase])

    def steps(self, name, phase):
        return steps_of(name, self.order(name, 0)[phase])

    def slab(self, name, part, phase, step, half=None):
        order = self.order(name, part)
        where = {axis: self.place.spot(name, axis, 0) for axis in order[:phase]}
        where[order[phase]] = self.place.spot(name, order[phase], step)
        if half is not None:
            where |= halved(name, order[phase + 1 :], half)
        return self.grads[name].at[block_index(where, *PARTS[name][part])]

    def landing(self, name, part, phase, slot, half=None):
        low, high = PARTS[name][part]
        left = self.order(name, part)[phase + 1 :]
        lead = [slice(None)] * len(left)
        if half is not None:
            lead[0] = halved(name, left, half)[min(left)]
        if name == GU and phase == 2:
            lead = [slice(None)]
        return (slot, *lead, slice(None), pl.ds(low, high - low))

    def push(self, name, part, phase, to, source, half, slot, early=False):
        dst = self.got[phase][name].at[self.landing(name, part, phase, slot, half)]
        push(
            self.slab(name, part, phase, source, half),
            dst,
            self.send_slot(name, phase),
            self.recv_slot(name, phase, early),
            self.place.peer(self.order(name, part)[phase], to),
        ).start()

    def start(self, name, phase, parts=None):
        for part in range(len(PARTS[name])) if parts is None else parts:
            if self.direct(name, phase):
                for slot, step in enumerate(self.steps(name, phase)):
                    self.push(name, part, phase, step, step, None, slot)
            else:
                self.push(name, part, phase, 3, 2, 0, 2, True)
                self.push(name, part, phase, 1, 2, 1, 2, True)
                self.push(name, part, phase, 3, 3, 1, 0)
                self.push(name, part, phase, 1, 1, 0, 1)

    def arrived(self, name, phase, early=False):
        count = self.blocks(name, phase)
        if self.direct(name, phase):
            count *= len(self.steps(name, phase))
        elif not early:
            count *= 2
        slot = self.recv_slot(name, phase, early)
        expect(self.grads[name], count, slot, self.place).wait_recv()

    def hand_on(self, name, phase):
        self.arrived(name, phase, True)
        for part in range(len(PARTS[name])):
            for step, half, slot in ((3, 0, 0), (1, 1, 1)):
                own = self.slab(name, part, phase, step, half)
                came = self.got[phase][name].at[self.landing(name, part, phase, 2, half)]

                def body(i):
                    own[i] = (own[i].astype(jnp.float32) + came[i].astype(jnp.float32)).astype(
                        jnp.bfloat16
                    )

                each(own.shape[0], body)
                self.push(name, part, phase, step, step, half, slot)

    def add(self, name, part, phase, pick=()):
        total = self.slab(name, part, phase, 0)[(*pick, Ellipsis)].astype(jnp.float32)
        for slot in range(len(self.steps(name, phase)) if self.direct(name, phase) else 2):
            piece = self.got[phase][name].at[self.landing(name, part, phase, slot)]
            total = total + piece[(*pick, Ellipsis)].astype(jnp.float32)
        return total

    def relay(self, name, phase):
        self.arrived(name, phase)
        for part in range(len(PARTS[name])):
            own = self.slab(name, part, phase, 0)

            def body(i):
                own[i] = self.add(name, part, phase, (i,)).astype(jnp.bfloat16)

            each(own.shape[0], body)
            self.start(name, phase + 1, (part,))

    def finish(self):
        for name in WEIGHTS:
            for phase in range(3):
                times = len(self.steps(name, phase)) if self.direct(name, phase) else 3
                count = self.blocks(name, phase) * times
                slot = self.send_slot(name, phase)
                expect(self.grads[name], count, slot, self.place).wait_send()


class SumAll:
    def __init__(self, place, got, send_sem, recv_sem):
        self.place, self.got = place, got
        self.send_sem, self.recv_sem = send_sem, recv_sem

    def start(self, stage, value):
        if stage == 0:
            slot, devices = self.place.core, [self.place.sibling]
        else:
            axis = AXES[stage - 1]
            slot, devices = self.place.at[axis], [self.place.peer(axis, s) for s in STEPS]
        self.got[stage, slot] = value
        view = self.got.at[stage, slot]
        for device in devices:
            push(view, view, self.send_sem.at[stage], self.recv_sem.at[stage], device).start()

    def expect(self, stage):
        view = self.got.at[stage, pl.ds(0, 3 if stage else 1)]
        return push(
            view, view, self.send_sem.at[stage], self.recv_sem.at[stage], self.place.sibling
        )

    def total(self, stage):
        self.expect(stage).wait_recv()
        total = self.got[stage, 0]
        for slot in range(1, 4 if stage else 2):
            total = total + self.got[stage, slot]
        return total

    def finish(self):
        for stage in range(4):
            self.expect(stage).wait_send()


class Mate:
    COTANGENT, NORMED, DOWN_PART, BACK_PART, GRAD = range(5)

    def __init__(self, place, layer, send_sem, recv_sem):
        self.place, self.layer = place, layer
        self.send_sem, self.recv_sem = send_sem, recv_sem

    def copy(self, which):
        layer = self.layer
        src, dst = (
            (layer.both_cotangent.at[pl.ds(0, 128)], layer.both_cotangent.at[pl.ds(128, 128)]),
            (layer.both_normed.at[pl.ds(0, 128)], layer.both_normed.at[pl.ds(128, 128)]),
            (layer.down_part, layer.down_got),
            (layer.back_part, layer.back_got),
            (layer.gu_sum.at[1 - self.place.parity], layer.gu_got),
        )[which]
        return push(
            src, dst, self.send_sem.at[which], self.recv_sem.at[which], self.place.mate
        )

    def start(self, which):
        self.copy(which).start()

    def start_columns(self, y):
        at = pl.ds(256 * y, 256)
        push(
            self.layer.back_part.at[:, at],
            self.layer.back_got.at[:, at],
            self.send_sem.at[self.BACK_PART],
            self.recv_sem.at[self.BACK_PART],
            self.place.mate,
        ).start()

    def arrived(self, which):
        self.copy(which).wait_recv()

    def finish(self):
        for which in range(5):
            self.copy(which).wait_send()


class End:
    def __init__(self, place, ends, got, outs, send_sem, recv_sem):
        self.place, self.ends, self.got, self.outs = place, ends, got, outs
        self.send_sem, self.recv_sem = send_sem, recv_sem

    def rows(self, name, core):
        half = ROWS[name] // 2
        return pl.ds(pl.multiple_of(core * half, 8), half)

    def columns(self, name, core):
        if name == GU:
            return pl.ds(pl.multiple_of(core * 2048, 512), 2048)
        return half_columns(name, core)

    def copy(self, name):
        slot = name - 1
        return push(
            self.ends[name].at[self.rows(name, 1 - self.place.core), :],
            self.got[name],
            self.send_sem.at[slot],
            self.recv_sem.at[slot],
            self.place.sibling,
        )

    def start(self, name):
        self.copy(name).start()
        core = self.place.core
        self.outs[name][:, self.columns(name, core)] = self.ends[name][self.rows(name, core), :]

    def take(self, name):
        self.copy(name).wait_recv()
        self.outs[name][:, self.columns(name, 1 - self.place.core)] = self.got[name][...]

    def finish(self):
        for name in WEIGHTS[1:]:
            self.copy(name).wait_send()


LOW, WIDE = jnp.bfloat16, jnp.float32


def dot(left, right):
    return jnp.dot(left, right, preferred_element_type=WIDE)


def dot_back(left, right):
    return lax.dot_general(left, right, (((1,), (1,)), ((), ())), preferred_element_type=WIDE)


def dot_over_rows(left, right):
    return lax.dot_general(left, right, (((0,), (0,)), ((), ())), preferred_element_type=WIDE)


def exact_dot(left, right):
    return jnp.dot(left, right, precision=lax.Precision.HIGHEST, preferred_element_type=WIDE)


def sigmoid(v):
    return 1.0 / (1.0 + jnp.exp(-v))


def tile(index, size):
    return pl.ds(index * size, size)


def lanes(shape):
    return lax.broadcasted_iota(jnp.int32, shape, len(shape) - 1)


def rows_of(shape):
    return lax.broadcasted_iota(jnp.int32, shape, 0)


def pair_stack(value):
    first = lanes(value.shape) < HD
    zero = jnp.zeros_like(value)
    return jnp.concatenate([jnp.where(first, value, zero), jnp.where(first, zero, value)], axis=0)


def pair_join(stacked):
    first = lanes((TOK, 128)) < HD
    return jnp.where(first, stacked[:TOK], stacked[TOK:])


def swap_halves(value):
    first = lax.rem(lanes(value.shape), HD) < HD // 2
    return jnp.where(first, pltpu.roll(value, 128 - HD // 2, 1), pltpu.roll(value, HD // 2, 1))


def doubled(value, which):
    first = lanes(value.shape) < HD
    turned = pltpu.roll(value, HD, 1)
    return jnp.where(first, value, turned) if which == 0 else jnp.where(first, turned, value)


class Layer:
    def __init__(self, refs):
        vars(self).update(refs)


    def enter(self):
        self.vectors[...] = jnp.zeros((8, 1792), WIDE)
        self.skip_sum[...] = jnp.zeros((8, 1536), WIDE)
        self.heads[...] = jnp.zeros((8, 128), WIDE)
        self.heads[0:1, 0:24] = self.decay_log[...]
        self.heads[1:2, 0:24] = self.step_bias[...]
        own = self.small_shard
        own[...] = jnp.zeros((8, 128), WIDE)
        own[0:2, 0:8] = self.norm_gains[...].astype(WIDE)
        own[2:7, 0:14] = self.conv_params[...].astype(WIDE)
        own[7:8, 0:12] = self.mixer_scale[...].astype(WIDE)
        moved = pltpu.roll(own[...], 32, 1)
        own[...] = jnp.zeros((8, 128), WIDE)
        own[:, 0:24] = self.in_shard[:, 4096:4120].astype(WIDE)
        own[...] = own[...] + moved

    def tables(self):
        position = rows_of((TOK, 128)).astype(WIDE)
        column = lax.rem(lanes((TOK, 128)), HD // 2).astype(WIDE)
        angle = position * jnp.exp(column * (-2.0 * math.log(rope_base) / HD))
        sine = jnp.sin(angle)
        first = lax.rem(lanes((TOK, 128)), HD) < HD // 2
        self.cosines[...] = jnp.cos(angle)
        self.sines[...] = jnp.where(first, -sine, sine)
        first = lanes((1, 128)) < HD
        for i in range(12):
            self.skip[0:1, 128 * i : 128 * i + 128] = jnp.where(
                first,
                self.mixer_skip[0:1, 2 * i : 2 * i + 1],
                self.mixer_skip[0:1, 2 * i + 1 : 2 * i + 2],
            )

    def spread(self):
        self.small_wide[...] = self.g_small[...].astype(WIDE).reshape(1024, 128)

        def turned(row):
            got = self.small_wide[pl.ds(row, 128, stride=8), :]
            return jnp.transpose(got)[32:48]

        for group, size, first, count, into in (
            (8, 1024, 0, 2, self.gains),
            (14, 1792, 2, 5, self.taps),
            (12, 1536, 7, 1, self.scale),
        ):
            stacked = jnp.concatenate([turned(first + i) for i in range(count)], axis=0)
            stacked = stacked.astype(LOW)
            for low in range(0, size, 256):
                start = rows_of((128, 256)) * group
                column = lanes((128, 256)) + low
                hot = (column >= start) & (column < start + group)
                index = jnp.sum(jnp.where(hot, start, 0).astype(WIDE), axis=0, keepdims=True)
                within = (lanes((1, 256)) + low).astype(WIDE) - index
                found = dot(stacked, jnp.where(hot, 1.0, 0.0).astype(LOW))
                mask = rows_of((16, 256)).astype(WIDE) == within
                for i in range(count):
                    into[i : i + 1, low : low + 256] = jnp.sum(
                        jnp.where(mask, found[16 * i : 16 * i + 16], 0.0), axis=0, keepdims=True
                    )


    def norm_in(self):
        x = self.tokens[...].astype(WIDE)
        self.inverse_in[...] = lax.rsqrt(jnp.mean(x * x, axis=-1, keepdims=True) + norm_eps)
        normed = x * self.inverse_in[...] * self.gains[0:1, :]
        self.normed[...] = normed.astype(LOW)
        self.left_in[:, 0:128] = jnp.transpose(normed).astype(LOW)

    def project_first(self):
        for i in range(4):
            weight = self.g_ina[i // 2, :, :, :, :, tile(i % 2, 512)]
            self.proj[:, tile(i, 512)] = dot(self.normed[...], weight.reshape(1024, 512))

    def project_last(self):
        for i in range(4):
            weight = self.g_inb[i // 2, :, :, :, :, tile(i % 2, 512)]
            self.proj[:, tile(4 + i, 512)] = dot(self.normed[...], weight.reshape(1024, 512))
        raw = dot(self.normed[...], self.g_small[...].reshape(1024, 128))
        self.step_raw[...] = jnp.where(lanes((TOK, 128)) < MIXER_HEADS, raw, 0.0)

    def convolved(self, i):
        low = 128 * i
        own = self.proj[:, 2304 + low : 2432 + low]
        row = rows_of((TOK, 128))
        shifted = [own] + [
            jnp.where(row >= k, pltpu.roll(own, k, 0), 0.0) for k in range(1, CONVK)
        ]
        total = self.taps[4:5, low : low + 128]
        for k in range(CONVK):
            total = total + self.taps[3 - k : 4 - k, low : low + 128] * shifted[k]
        return shifted, total

    def activate(self):
        for i in range(14):
            _, total = self.convolved(i)
            active = total * sigmoid(total)
            self.active[:, 128 * i : 128 * i + 128] = active

    def steps(self):
        raw = self.step_raw[...] + self.heads[1:2, :]
        step = jnp.maximum(raw, 0.0) + jnp.log1p(jnp.exp(-jnp.abs(raw)))
        rate = -jnp.exp(self.heads[0:1, :])
        lower = jnp.where(rows_of((TOK, TOK)) >= lanes((TOK, TOK)), 1.0, 0.0)
        total = exact_dot(lower, step * rate)
        self.step[...] = step
        self.cum[...] = total
        self.step_rows[...] = jnp.transpose(step)
        self.cum_rows[...] = jnp.transpose(total)

    def causal(self):
        return rows_of((TOK, TOK)) >= lanes((TOK, TOK))

    def attend(self):
        for i in range(5):
            value = self.proj[:, 128 * i : 128 * i + 128]
            turned = value * self.cosines[...] + swap_halves(value) * self.sines[...]
            self.turned[:, 128 * i : 128 * i + 128] = turned.astype(LOW)
        key = self.turned[:, 512:640].astype(WIDE)
        values = self.proj[:, 640:768]
        for which in range(2):
            self.keys[which] = doubled(key, which).astype(LOW)
            self.values[which] = doubled(values, which).astype(LOW)
        causal = self.causal()
        causal = jnp.concatenate([causal, causal], axis=0)
        for i in range(4):
            queries = pair_stack(self.turned[:, 128 * i : 128 * i + 128])
            scores = dot_back(queries, self.keys[i // 2]) * (1.0 / math.sqrt(HD))
            scores = jnp.where(causal, scores, masked_value)
            power = jnp.exp(scores - jnp.max(scores, axis=-1, keepdims=True))
            probs = power / jnp.sum(power, axis=-1, keepdims=True)
            self.small_wide[tile(i, 256), :] = probs
            self.mixed[:, 128 * i : 128 * i + 128] = pair_join(
                dot(probs.astype(LOW), self.values[i // 2])
            ).astype(LOW)

    def decay(self, head):
        gaps = self.cum[:, head : head + 1] - self.cum_rows[head : head + 1, :]
        return jnp.exp(jnp.where(self.causal(), gaps, masked_value))

    def mix(self, low, high):
        if low == 0:
            self.inner[...] = dot_back(
                self.active[:, 1664:1792].astype(LOW), self.active[:, 1536:1664].astype(LOW)
            )
        inner = self.inner[...]
        square = jnp.zeros((TOK, 1), WIDE) if low == 0 else self.inverse_state[...]
        for i in range(low, high):
            mixing = jnp.concatenate(
                [
                    inner * self.decay(head) * self.step_rows[head : head + 1, :]
                    for head in (2 * i, 2 * i + 1)
                ],
                axis=0,
            ).astype(LOW)
            self.mixing[i] = mixing
            at = slice(128 * i, 128 * i + 128)
            state = pair_join(dot(mixing, self.active[:, at].astype(LOW)))
            central = state + self.skip[0:1, at] * self.active[:, at]
            self.central[:, at] = central
            gate = self.proj[:, 768 + 128 * i : 896 + 128 * i]
            gated = central * (gate * sigmoid(gate))
            square = square + jnp.sum(gated * gated, axis=-1, keepdims=True)
        self.inverse_state[...] = square

    def mix_norm(self):
        inverse = lax.rsqrt(self.inverse_state[...] * (1.0 / MIXER_FEATURES) + norm_eps)
        self.inverse_state[...] = inverse
        for i in range(12):
            at = slice(128 * i, 128 * i + 128)
            gate = self.proj[:, 768 + 128 * i : 896 + 128 * i]
            gated = self.central[:, at] * (gate * sigmoid(gate))
            self.mixed[:, 512 + 128 * i : 640 + 128 * i] = (
                gated * inverse * self.scale[0:1, at]
            ).astype(LOW)

    def turn_left(self, source, into, count):
        for i in range(count):
            block = source[:, 128 * i : 128 * i + 128].astype(WIDE)
            into[128 * i : 128 * i + 128, 0:128] = jnp.transpose(block).astype(LOW)

    def branch(self):
        for half in range(2):
            at = slice(512 * half, 512 * half + 512)
            self.residual[:, at] = self.tokens[:, at].astype(WIDE) + dot(
                self.mixed[...], self.g_out[half].reshape(2048, 512)
            )
        x = self.residual[...]
        self.inverse_ff[...] = lax.rsqrt(jnp.mean(x * x, axis=-1, keepdims=True) + norm_eps)
        normed = x * self.inverse_ff[...] * self.gains[1:2, :]
        self.both_normed[0:128, :] = normed.astype(LOW)
        self.left_gu[:, 0:128] = jnp.transpose(normed).astype(LOW)

    def turn_other(self):
        other = self.both_normed[128:256, :].astype(WIDE)
        self.left_gu[:, 128:256] = jnp.transpose(other).astype(LOW)

    def feed(self):
        for i in range(2):
            for half in range(2):
                weight = self.g_gu[half, :, :, :, :, tile(i, 512)].reshape(1024, 512)
                self.gate_up[:, tile(2 * half + i, 512)] = dot(self.both_normed[...], weight)
        for i in range(8):
            at = tile(i, 128)
            gate = self.gate_up[:, at]
            hidden = gate * sigmoid(gate) * self.gate_up[:, tile(8 + i, 128)]
            self.hidden[:, at] = hidden.astype(LOW)
            self.left_down[at, 0:256] = jnp.transpose(hidden).astype(LOW)

    def down(self):
        for half in range(2):
            at = tile(half, 512)
            part = dot(self.hidden[...], self.g_down[half].reshape(1024, 512))
            self.down_own[:, at] = self.residual[:, at] + part[0:128]
            self.down_part[:, at] = part[128:256].astype(LOW)

    def down_sum(self):
        self.layer_output[...] = (self.down_own[...] + self.down_got[...].astype(WIDE)).astype(LOW)


    def back_down(self):
        for q in range(2):
            grad = dot_back(
                self.both_cotangent[:, 0:512], self.g_down[0, q].reshape(512, 512)
            ) + dot_back(self.both_cotangent[:, 512:1024], self.g_down[1, q].reshape(512, 512))
            for i in range(4):
                part = grad[:, 128 * i : 128 * i + 128]
                at, up_at = tile(4 * q + i, 128), tile(8 + 4 * q + i, 128)
                gate = self.gate_up[:, at]
                share = sigmoid(gate)
                self.d_gate[:, at] = (
                    part * self.gate_up[:, up_at] * (share * (1.0 + gate * (1.0 - share)))
                ).astype(LOW)
                self.d_gate[:, up_at] = (part * (gate * share)).astype(LOW)

    def norm_back(self, grad, x, inverse, gain):
        turned = x * inverse
        d_gain = jnp.sum(grad * turned, axis=0, keepdims=True)
        scaled = grad * gain
        d_x = inverse * (scaled - turned * jnp.mean(scaled * turned, axis=-1, keepdims=True))
        return d_x, d_gain

    def back_feed(self, y):
        total = dot_back(self.d_gate[:, 0:1024], self.g_gu[0, y].reshape(256, 1024)) + dot_back(
            self.d_gate[:, 1024:2048], self.g_gu[1, y].reshape(256, 1024)
        )
        self.d_wide[:, tile(y, 256)] = total[0:128]
        self.back_part[:, tile(y, 256)] = total[128:256].astype(LOW)

    def back_residual(self):
        grad = self.d_wide[:, 0:1024] + self.back_got[...].astype(WIDE)
        d_x, d_gain = self.norm_back(
            grad, self.residual[...], self.inverse_ff[...], self.gains[1:2, :]
        )
        self.vectors[1:2, 0:1024] = d_gain
        d_residual = self.cotangent[...].astype(WIDE) + d_x
        self.d_residual[...] = d_residual
        self.d_branch[...] = d_residual.astype(LOW)

    def back_branch(self):
        def body(y):
            self.d_wide[:, tile(y, 512)] = dot_back(
                self.d_branch[:, 0:512], self.g_out[0, y].reshape(512, 512)
            ) + dot_back(self.d_branch[:, 512:1024], self.g_out[1, y].reshape(512, 512))

        each(4, body)

    def back_gated(self):
        inverse = self.inverse_state[...]
        mean = jnp.zeros((TOK, 1), WIDE)
        for i in range(12):
            at = slice(128 * i, 128 * i + 128)
            gate = self.proj[:, 768 + 128 * i : 896 + 128 * i]
            gated = self.central[:, at] * (gate * sigmoid(gate))
            grad = self.d_wide[:, 512 + 128 * i : 640 + 128 * i]
            turned = gated * inverse
            self.vectors[7:8, at] = jnp.sum(grad * turned, axis=0, keepdims=True)
            mean = mean + jnp.sum(grad * self.scale[0:1, at] * turned, axis=-1, keepdims=True)
        mean = mean * (1.0 / MIXER_FEATURES)
        for i in range(12):
            at = slice(128 * i, 128 * i + 128)
            gate = self.proj[:, 768 + 128 * i : 896 + 128 * i]
            share = sigmoid(gate)
            open_gate = gate * share
            central = self.central[:, at]
            grad = self.d_wide[:, 512 + 128 * i : 640 + 128 * i]
            d_gated = inverse * (
                grad * self.scale[0:1, at] - central * open_gate * inverse * mean
            )
            d_central = d_gated * open_gate
            self.d_proj[:, 768 + 128 * i : 896 + 128 * i] = (
                d_gated * central * (share * (1.0 + gate * (1.0 - share)))
            ).astype(LOW)
            self.d_state[:, at] = d_central.astype(LOW)
            self.d_active[:, at] = d_central * self.skip[0:1, at]
            self.skip_sum[0:1, at] = jnp.sum(
                d_central * self.active[:, at], axis=0, keepdims=True
            )

    def back_mix(self, low, high):
        inner = self.inner[...]
        lane = lanes((TOK, TOK))
        zero = jnp.zeros((TOK, TOK), WIDE)
        d_inner, d_cum = (zero, zero) if low == 0 else (self.d_inner[...], self.d_cum[...])
        if low == 0:
            self.flow_rows[...] = zero
            self.d_step_rows[...] = zero
        for i in range(low, high):
            at = slice(128 * i, 128 * i + 128)
            stacked = pair_stack(self.d_state[:, at])
            d_mixing = dot_back(stacked, self.active[:, at].astype(LOW))
            self.d_active[:, at] += dot_over_rows(self.mixing[i], stacked)
            for which, head in enumerate((2 * i, 2 * i + 1)):
                grad = d_mixing[TOK * which : TOK * which + TOK]
                decay = self.decay(head)
                step = self.step_rows[head : head + 1, :]
                faded = grad * decay
                d_inner = d_inner + faded * step
                part = faded * inner
                d_step = jnp.sum(part, axis=0, keepdims=True)
                self.d_step_rows[head : head + 1, :] = d_step
                self.flow_rows[head : head + 1, :] = d_step * step
                over = jnp.sum(part * step, axis=-1, keepdims=True)
                d_cum = jnp.where(lane == head, over, d_cum)
        self.d_inner[...] = d_inner
        self.d_cum[...] = d_cum

    def back_steps(self):
        lane = lanes((TOK, TOK))
        d_inner = self.d_inner[...].astype(LOW)
        self.d_active[:, 1664:1792] = dot(d_inner, self.active[:, 1536:1664].astype(LOW))
        self.d_active[:, 1536:1664] = dot_over_rows(d_inner, self.active[:, 1664:1792].astype(LOW))
        d_cum = self.d_cum[...] - jnp.transpose(self.flow_rows[...])
        upper = jnp.where(rows_of((TOK, TOK)) <= lanes((TOK, TOK)), 1.0, 0.0)
        d_rated = exact_dot(upper, d_cum)
        rate = -jnp.exp(self.heads[0:1, :])
        d_step = jnp.transpose(self.d_step_rows[...]) + d_rated * rate
        self.vectors[7:8, 1536:1664] = (
            jnp.sum(d_rated * self.step[...], axis=0, keepdims=True) * rate
        )
        raw = self.step_raw[...] + self.heads[1:2, :]
        d_raw = jnp.where(lane < MIXER_HEADS, d_step * sigmoid(raw), 0.0)
        self.vectors[7:8, 1664:1792] = jnp.sum(d_raw, axis=0, keepdims=True)
        self.right_dt[0:128, :] = d_raw.astype(LOW)
        hot = jnp.where(
            lax.div(rows_of((1536, 128)), MIXER_HEAD_SIZE) == lanes((1536, 128)), 1.0, 0.0
        )
        self.vectors[0:1, 1024:1152] = exact_dot(self.skip_sum[...], hot)[0:1]

    def back_attend(self):
        d_keys, d_values = [], []
        for i in range(4):
            at = slice(128 * i, 128 * i + 128)
            which = i // 2
            d_out = pair_stack(self.d_wide[:, at].astype(LOW))
            d_probs = dot_back(d_out, self.values[which])
            probs = self.small_wide[tile(i, 256), :]
            d_scores = probs * (d_probs - jnp.sum(probs * d_probs, axis=-1, keepdims=True))
            d_raw = (d_scores * (1.0 / math.sqrt(HD))).astype(LOW)
            self.unturn(i, pair_join(dot(d_raw, self.keys[which])))
            d_keys.append(dot_over_rows(d_raw, pair_stack(self.turned[:, at])))
            d_values.append(dot_over_rows(probs.astype(LOW), d_out))
        first = lanes((TOK, 128)) < HD

        def joined(parts):
            one, two = parts[0] + parts[1], parts[2] + parts[3]
            return jnp.where(first, one + pltpu.roll(one, HD, 1), two + pltpu.roll(two, HD, 1))

        self.unturn(4, joined(d_keys))
        self.d_proj[:, 640:768] = joined(d_values).astype(LOW)

    def unturn(self, i, grad):
        self.d_proj[:, 128 * i : 128 * i + 128] = (
            grad * self.cosines[...] - swap_halves(grad) * self.sines[...]
        ).astype(LOW)

    def back_activate(self):
        row = rows_of((TOK, 128))
        for i in range(14):
            at = slice(128 * i, 128 * i + 128)
            shifted, total = self.convolved(i)
            share = sigmoid(total)
            grad = self.d_active[:, at] * (share * (1.0 + total * (1.0 - share)))
            self.vectors[6:7, at] = jnp.sum(grad, axis=0, keepdims=True)
            d_in = self.taps[3:4, at] * grad
            for k in range(CONVK):
                self.vectors[5 - k : 6 - k, at] = jnp.sum(grad * shifted[k], axis=0, keepdims=True)
                if k:
                    later = jnp.where(row < TOK - k, pltpu.roll(grad, TOK - k, 0), 0.0)
                    d_in = d_in + self.taps[3 - k : 4 - k, at] * later
            self.d_proj[:, 2304 + 128 * i : 2432 + 128 * i] = d_in.astype(LOW)

    def back_project(self, low, high):
        small = self.g_small[...].reshape(1024, 128)
        for y in range(low, high):
            total = dot_back(self.right_dt[0:128, :], small[256 * y : 256 * y + 256])
            for half in range(2):
                at = tile(half, 1024)
                total = total + dot_back(self.d_proj[:, at], self.g_ina[half, y].reshape(256, 1024))
                at = tile(2 + half, 1024)
                total = total + dot_back(self.d_proj[:, at], self.g_inb[half, y].reshape(256, 1024))
            self.d_wide[:, tile(y, 256)] = total

    def back_input(self):
        d_x, d_gain = self.norm_back(
            self.d_wide[:, 0:1024],
            self.tokens[...].astype(WIDE),
            self.inverse_in[...],
            self.gains[0:1, :],
        )
        self.vectors[0:1, 0:1024] = d_gain
        self.input_grad[...] = (self.d_residual[...] + d_x).astype(LOW)


    def grad_wide(self, left, right, into):
        width = right.shape[1]
        size = min(width, 512)
        for n in range(width // size):
            for y in range(4):
                block = dot(left[tile(y, 256), :], right[:, tile(n, size)])
                into[y, :, :, :, tile(n, size)] = block.astype(LOW).reshape(4, 4, 16, size)

    def grad_tall(self, left, right, into):
        for y in range(into.shape[0]):
            block = dot(left[tile(y, 512), :], right[...])
            into[y] = block.astype(LOW).reshape(4, 4, 32, 512)


class Swap:
    def __init__(self, place, layer, send_sem, recv_sem):
        self.place, self.layer = place, layer
        self.send_sem, self.recv_sem = send_sem, recv_sem
        self.lefts = (
            None, layer.left_in, None, layer.left_out, layer.left_gu, layer.left_down,
        )
        self.rights = (
            layer.right_dt, layer.right_ina, layer.right_inb, layer.right_out, layer.right_gu,
            layer.right_down,
        )
        self.sources = (
            None, layer.d_proj, layer.d_proj, layer.d_branch, layer.d_gate, layer.both_cotangent,
        )

    def left_copy(self, name):
        ref = self.lefts[name]
        size = ref.shape[1] // 2
        src, dst = ref.at[:, pl.ds(0, size)], ref.at[:, pl.ds(size, size)]
        return push(
            src, dst, self.send_sem.at[name], self.recv_sem.at[name], self.place.sibling
        )

    def right_copy(self, name):
        ref, source = self.rights[name], self.sources[name]
        size = ref.shape[0] // 2
        if source is None:
            src = ref.at[pl.ds(0, size), :]
        else:
            src = source.at[:, half_columns(name, 1 - self.place.core)]
        slot = 6 + name
        return push(
            src,
            ref.at[pl.ds(size, size), :],
            self.send_sem.at[slot],
            self.recv_sem.at[slot],
            self.place.sibling,
        )

    def start_left(self, name):
        self.left_copy(name).start()

    def start_right(self, name):
        ref, source = self.rights[name], self.sources[name]
        if source is not None:
            size = ref.shape[0] // 2
            ref[0:size, :] = source[:, half_columns(name, self.place.core)]
        self.right_copy(name).start()

    def arrived(self, name):
        if self.lefts[name] is not None:
            self.left_copy(name).wait_recv()
        self.right_copy(name).wait_recv()

    def finish(self):
        for name in WEIGHTS:
            self.right_copy(name).wait_send()
            if self.lefts[name] is not None:
                self.left_copy(name).wait_send()


INS = dict(
    tokens=0, cotangent=1, in_shard=2, out_shard=3, gu_shard=4, down_shard=5, norm_gains=6,
    conv_params=7, mixer_scale=8, decay_log=9, step_bias=10, mixer_skip=11,
)
OUTS = dict(
    layer_output=((TOK, 1024), LOW),
    input_grad=((TOK, 1024), LOW),
    grad_in=((8, 4120), WIDE),
    grad_out=((16, 1024), WIDE),
    grad_gu=((8, 4096), WIDE),
    grad_down=((16, 1024), WIDE),
    total=((8, 1792), WIDE),
)
SCRATCH = dict(
    g_small=((4, 4, 4, 16, 128), LOW),
    g_ina=((2, 4, 4, 4, 16, 1024), LOW),
    g_inb=((2, 4, 4, 4, 16, 1024), LOW),
    g_out=((2, 4, 4, 4, 32, 512), LOW),
    g_gu=((2, 4, 4, 4, 16, 1024), LOW),
    g_down=((2, 2, 4, 4, 32, 512), LOW),
    low_small=((4, 4, 4, 16, 128), LOW),
    low_gu=((4, 4, 4, 16, 1024), LOW),
    low_down=((2, 4, 4, 32, 512), LOW),
    small_shard=((8, 128), WIDE),
    heads=((8, 128), WIDE),
    skip=((8, 1536), WIDE),
    cosines=((TOK, 128), WIDE),
    sines=((TOK, 128), WIDE),
    pack=((16, 4224), LOW),
    got=((16, 4224), LOW),
    stage=((16, 1024), LOW),
    small_wide=((1024, 128), WIDE),
    gains=((8, 1024), WIDE),
    taps=((8, 1792), WIDE),
    scale=((8, 1536), WIDE),
    normed=((TOK, 1024), LOW),
    inverse_in=((TOK, 1), WIDE),
    proj=((TOK, 4096), WIDE),
    step_raw=((TOK, 128), WIDE),
    active=((TOK, 1792), WIDE),
    step=((TOK, TOK), WIDE),
    cum=((TOK, TOK), WIDE),
    step_rows=((TOK, TOK), WIDE),
    cum_rows=((TOK, TOK), WIDE),
    turned=((TOK, 640), LOW),
    keys=((2, TOK, 128), LOW),
    values=((2, TOK, 128), LOW),
    mixed=((TOK, 2048), LOW),
    inner=((TOK, TOK), WIDE),
    mixing=((12, 256, TOK), LOW),
    central=((TOK, 1536), WIDE),
    inverse_state=((TOK, 1), WIDE),
    residual=((TOK, 1024), WIDE),
    d_residual=((TOK, 1024), WIDE),
    inverse_ff=((TOK, 1), WIDE),
    both_normed=((256, 1024), LOW),
    both_cotangent=((256, 1024), LOW),
    gate_up=((256, 2048), WIDE),
    hidden=((256, 1024), LOW),
    down_own=((TOK, 1024), WIDE),
    down_part=((TOK, 1024), LOW),
    down_got=((TOK, 1024), LOW),
    back_part=((TOK, 1024), LOW),
    back_got=((TOK, 1024), LOW),
    gu_sum=((2, 16, 1024), WIDE),
    gu_got=((16, 1024), WIDE),
    d_gate=((256, 2048), LOW),
    d_branch=((TOK, 1024), LOW),
    d_state=((TOK, 1536), LOW),
    d_proj=((TOK, 4096), LOW),
    skip_sum=((8, 1536), WIDE),
    d_inner=((TOK, TOK), WIDE),
    d_cum=((TOK, TOK), WIDE),
    flow_rows=((TOK, TOK), WIDE),
    d_step_rows=((TOK, TOK), WIDE),
    vectors=((8, 1792), WIDE),
    left_in=((1024, 256), LOW),
    left_out=((2048, 256), LOW),
    left_gu=((1024, 512), LOW),
    left_down=((1024, 512), LOW),
    right_ina=((256, 1024), LOW),
    right_inb=((256, 1024), LOW),
    right_out=((256, 512), LOW),
    right_gu=((512, 1024), LOW),
    right_down=((512, 512), LOW),
    right_dt=((256, 128), LOW),
    sums=((4, 4, 8, 1792), WIDE),
)
BLOCKS = tuple((ROWS[name], COLS[name]) for name in WEIGHTS)
LANDINGS = tuple((3, DEPTH[name], 4) for name in WEIGHTS)
LANDINGS += tuple((3, DEPTH[name]) for name in WEIGHTS)
LANDINGS += tuple({GU: (1, 2), DOWN: (1,)}.get(name, (3,)) for name in WEIGHTS)
ENDS = tuple((ROWS[name], 2048 if name == GU else COLS[name]) for name in WEIGHTS[1:])
SEMS = dict(
    enter=4, gather=53, scatter=30, sums=4, end=5, swap=12, mate=5,
)


class Plan:
    def __init__(self, refs):
        names = [*INS, *OUTS, *SCRATCH]
        layer = Layer(dict(zip(names, refs)))
        rest = list(refs[len(names) :])
        landings = [[rest.pop(0) for _ in WEIGHTS] for _ in range(3)]
        ends = [None] + [rest.pop(0) for _ in WEIGHTS[1:]]
        ends_got = [None] + [rest.pop(0) for _ in WEIGHTS[1:]]
        sems = {name: (rest.pop(0), rest.pop(0)) for name in SEMS}
        layer.d_wide = layer.gate_up.at[pl.ds(0, 128), :]
        layer.d_active = layer.gate_up.at[pl.ds(128, 128), pl.ds(0, 1792)]
        place = Place()
        arrays = (layer.g_small, layer.g_ina, layer.g_inb, layer.g_out, layer.g_gu, layer.g_down)
        shards = (
            layer.small_shard, layer.in_shard, layer.in_shard, layer.out_shard, layer.gu_shard,
            layer.down_shard,
        )
        grads = (
            layer.low_small, layer.g_gu.at[0], layer.g_gu.at[1], layer.g_out.at[0], layer.low_gu,
            layer.low_down,
        )
        outs = (
            None, layer.grad_in, layer.grad_in, layer.grad_out, layer.grad_gu, layer.grad_down,
        )
        self.place, self.layer, self.grads = place, layer, grads
        self.gather = Gather(place, arrays, *sems["gather"])
        self.enter = Enter(
            place, self.gather, layer.pack, layer.got, layer.stage, shards, sems["enter"]
        )
        self.scatter = Scatter(place, grads, *landings, *sems["scatter"])
        self.sum_all = SumAll(place, layer.sums, *sems["sums"])
        self.end = End(place, ends, ends_got, outs, *sems["end"])
        self.swap = Swap(place, layer, *sems["swap"])
        self.mate = Mate(place, layer, *sems["mate"])

    def last(self, name):
        self.scatter.arrived(name, 2)
        for part, (low, high) in enumerate(PARTS[name]):
            value = self.scatter.add(name, part, 2)
            if name == SMALL:
                mine = jnp.where(self.place.core == 0, value[0:8], value[8:16])
                self.layer.grad_in[:, 4096:4120] = mine[:, 0:24]
            elif name == GU:
                self.layer.gu_sum[:, :, low:high] = value
            else:
                self.end.ends[name][:, low:high] = value
        if name == GU:
            self.mate.start(Mate.GRAD)
        elif name != SMALL:
            self.end.start(name)

    def last_gu(self):
        self.mate.arrived(Mate.GRAD)
        layer, parity, into = self.layer, self.place.parity, self.end.ends[GU]
        for which, value in ((parity, layer.gu_sum[parity]), (1 - parity, layer.gu_got[...])):
            for q in range(2):
                at = pl.ds(pl.multiple_of(1024 * q + 512 * which, 512), 512)
                into[:, at] = value[:, 512 * q : 512 * q + 512]
        self.end.start(GU)


def layer_kernel(*refs):
    plan = Plan(refs)
    place, layer, grads, gather = plan.place, plan.layer, plan.grads, plan.gather
    enter, scatter, sum_all, end, swap = (
        plan.enter, plan.scatter, plan.sum_all, plan.end, plan.swap,
    )
    mate = plan.mate

    def onward(name, phase):
        gather.arrived(name, phase, 0 if gather.direct(name, phase) else 2)
        if phase == 0 or name == SMALL:
            gather.start(name, phase + 1)
        else:
            gather.start_early(name)

    def onward_late(name):
        gather.start_late(name)
        gather.pass_on(name, 0)

    def landed(name):
        gather.arrived(name, 2, 2)
        gather.pass_on(name, 2)

    arrive(place)
    layer.enter()
    enter.run(lambda: meet(place))
    gather.start(INA, 0)
    gather.start(INB, 0)
    gather.start(DOWN, 0)
    gather.start(OUT, 0)
    gather.start(SMALL, 0)
    layer.tables()
    enter.mate_copy().wait_recv()
    gather.start(GU, 0)
    onward(INA, 0)
    onward(INB, 0)
    onward(SMALL, 0)
    onward(DOWN, 0)
    onward(OUT, 0)
    onward(GU, 0)
    onward(INA, 1)
    onward_late(INA)
    gather.hand_on(DOWN, 1, (0,))
    onward(SMALL, 1)
    gather.hand_on(DOWN, 1, (1,))
    onward(INB, 1)
    onward_late(INB)
    onward(OUT, 1)
    gather.hand_on(GU, 1, (0,))
    gather.hand_on(GU, 1, (1,))
    gather.hand_on(INA, 2, (0,))
    gather.hand_on(INA, 2, (1,))
    gather.arrived_late(INA, (0,))
    gather.arrived_late(INA, (1,))
    onward(DOWN, 1)
    gather.arrived(SMALL, 2)
    layer.spread()
    layer.norm_in()
    swap.start_left(INA)
    gather.hand_on(INB, 2, (0,))
    gather.hand_on(INB, 2, (1,))
    onward_late(OUT)
    gather.arrived_late(INB, (0,))
    gather.arrived_late(INB, (1,))
    gather.hand_on(OUT, 2, (0,))
    gather.hand_on(OUT, 2, (1,))
    layer.both_cotangent[0:128, :] = layer.cotangent[...]
    mate.start(Mate.COTANGENT)
    onward(GU, 1)
    onward_late(GU)
    landed(INA)
    gather.hand_on(DOWN, 2, (0,))
    gather.hand_on(DOWN, 2, (1,))
    gather.passed(INA)
    layer.project_first()
    layer.attend()
    landed(INB)
    gather.arrived_late(OUT, (0,))
    gather.arrived_late(OUT, (1,))
    gather.passed(INB)
    layer.project_last()
    layer.activate()
    layer.steps()
    landed(OUT)
    layer.mix(0, 6)
    layer.mix(6, 12)
    layer.mix_norm()
    gather.passed(OUT)
    layer.branch()
    mate.start(Mate.NORMED)
    layer.turn_left(layer.mixed, layer.left_out, 16)
    swap.start_left(OUT)
    gather.hand_on(GU, 2, (1,))
    gather.hand_on(GU, 2, (0,))
    onward_late(DOWN)
    gather.arrived_late(GU, (0,))
    gather.arrived_late(GU, (1,))
    mate.arrived(Mate.COTANGENT)
    swap.start_right(DOWN)
    landed(GU)
    gather.arrived_late(DOWN, (0,))
    gather.arrived_late(DOWN, (1,))
    landed(DOWN)
    mate.arrived(Mate.NORMED)
    layer.turn_other()
    swap.start_left(GU)
    gather.passed(GU)
    layer.feed()
    swap.start_left(DOWN)
    gather.passed(DOWN)
    layer.back_down()
    swap.start_right(GU)
    for y in range(4):
        layer.back_feed(y)
        mate.start_columns(y)
    swap.arrived(DOWN)
    layer.grad_tall(layer.left_down, layer.right_down, grads[DOWN])
    scatter.start(DOWN, 0)
    swap.arrived(GU)
    layer.grad_wide(layer.left_gu, layer.right_gu, grads[GU])
    scatter.start(GU, 0)
    layer.down()
    mate.start(Mate.DOWN_PART)
    scatter.hand_on(DOWN, 0)
    mate.arrived(Mate.BACK_PART)
    layer.back_residual()
    swap.start_right(OUT)
    layer.back_branch()
    gather.finish(OUT)
    swap.arrived(OUT)
    layer.grad_tall(layer.left_out, layer.right_out, grads[OUT])
    scatter.start(OUT, 0)
    scatter.hand_on(GU, 0)
    layer.back_gated()
    layer.back_attend()
    swap.start_right(INA)
    layer.back_mix(0, 6)
    layer.back_mix(6, 12)
    gather.finish(GU)
    swap.arrived(INA)
    layer.grad_wide(layer.left_in, layer.right_ina, grads[INA])
    scatter.start(INA, 0)
    scatter.relay(DOWN, 0)
    layer.back_steps()
    swap.start_right(SMALL)
    scatter.hand_on(OUT, 0)
    layer.back_activate()
    swap.start_right(INB)
    swap.arrived(SMALL)
    layer.grad_wide(layer.left_in, layer.right_dt, grads[SMALL])
    scatter.start(SMALL, 0)
    mate.arrived(Mate.DOWN_PART)
    layer.down_sum()
    scatter.relay(GU, 0)
    swap.arrived(INB)
    layer.grad_wide(layer.left_in, layer.right_inb, grads[INB])
    scatter.start(INB, 0)
    scatter.hand_on(INA, 0)
    layer.back_project(0, 2)
    scatter.hand_on(DOWN, 1)
    layer.back_project(2, 4)
    layer.back_input()
    sum_all.start(0, layer.vectors[...])
    sum_all.start(1, sum_all.total(0))
    scatter.relay(OUT, 0)
    scatter.hand_on(GU, 1)
    scatter.relay(SMALL, 0)
    scatter.hand_on(INB, 0)
    scatter.relay(INA, 0)
    scatter.relay(DOWN, 1)
    sum_all.start(2, sum_all.total(1))
    scatter.relay(GU, 1)
    scatter.relay(OUT, 1)
    scatter.relay(SMALL, 1)
    scatter.relay(INB, 0)
    scatter.hand_on(INA, 1)
    plan.last(DOWN)
    end.take(DOWN)
    sum_all.start(3, sum_all.total(2))
    plan.last(GU)
    plan.last(OUT)
    plan.last(SMALL)
    end.take(OUT)
    scatter.relay(INA, 1)
    scatter.relay(INB, 1)
    plan.last_gu()
    end.take(GU)
    layer.total[...] = sum_all.total(3)
    plan.last(INA)
    plan.last(INB)
    end.take(INA)
    end.take(INB)
    for name in (SMALL, INA, INB, DOWN):
        gather.finish(name)
    scatter.finish()
    sum_all.finish()
    end.finish()
    swap.finish()
    mate.finish()
    enter.finish()


def finish_kernel(*refs):
    ins, outs = refs[:7], refs[7:]
    for ref, into in zip(ins[:6], outs[:6]):
        into[...] = ref[...]
    me = lax.axis_index("fsdp")
    total = ins[6][...]
    column = lanes((8, 1792))

    def share(size):
        start = me * size
        picked = jnp.where((column >= start) & (column < start + size), total, 0.0)
        folded = picked[:, 0:128]
        for i in range(1, 14):
            folded = folded + picked[:, 128 * i : 128 * i + 128]
        return pltpu.roll(folded, lax.rem(1792 - start, 128), 1)

    outs[6][...] = share(8)[0:2, 0:8]
    outs[7][...] = share(14)[2:7, 0:14]
    outs[8][...] = share(12)[7:8, 0:12]
    outs[9][...] = total[7:8, 1536:1560]
    outs[10][...] = total[7:8, 1664:1688]
    outs[11][...] = total[0:1, 1024:1048]


def local(
    tokens, cotangent, input_weight, output_weight, gate_up_weight, down_weight,
    norm_gains, conv_params, mixer_scale, decay_log, step_bias, mixer_skip_factor,
):
    ins = (
        tokens, cotangent, input_weight, output_weight, gate_up_weight, down_weight, norm_gains,
        conv_params, mixer_scale, decay_log[None], step_bias[None], mixer_skip_factor[None],
    )
    scratch = [pltpu.VMEM(*one) for one in SCRATCH.values()]
    scratch += [pltpu.VMEM(lead + block, LOW) for lead, block in zip(LANDINGS, BLOCKS * 3)]
    scratch += [pltpu.VMEM(block, WIDE) for block in ENDS]
    scratch += [pltpu.VMEM((block[0] // 2, block[1]), WIDE) for block in ENDS]
    scratch += [pltpu.SemaphoreType.DMA((count,)) for count in SEMS.values() for _ in range(2)]
    whole = pl.BlockSpec(memory_space=pltpu.VMEM)
    results = pl.pallas_call(
        layer_kernel,
        out_shape=[jax.ShapeDtypeStruct(*one) for one in OUTS.values()],
        in_specs=[whole] * len(INS),
        out_specs=[whole] * len(OUTS),
        scratch_shapes=scratch,
        compiler_params=pltpu.CompilerParams(
            collective_id=0, has_side_effects=True, vmem_limit_bytes=127 * 2**19
        ),
        name="layer",
    )(*ins)
    shares = [(2, 8), (5, 14), (1, 12), (1, 24), (1, 24), (1, 24)]
    final = pl.pallas_call(
        finish_kernel,
        out_shape=[jax.ShapeDtypeStruct(*one) for one in list(OUTS.values())[:6]]
        + [jax.ShapeDtypeStruct(one, WIDE) for one in shares],
        in_specs=[whole] * len(OUTS),
        out_specs=[whole] * 12,
        name="finish",
    )(*results)
    return (*final[:9], *(one[0] for one in final[9:]))


def solution(mesh):
    in_specs = (
        P("fsdp", None),
        P("fsdp", None),
        P("fsdp", None),
        P("fsdp", None),
        P("fsdp", None),
        P("fsdp", None),
        P(None, "fsdp"),
        P(None, "fsdp"),
        P(None, "fsdp"),
        P(),
        P(),
        P(),
    )
    out_specs = (
        P("fsdp", None),
        P("fsdp", None),
        P("fsdp", None),
        P("fsdp", None),
        P("fsdp", None),
        P("fsdp", None),
        P(None, "fsdp"),
        P(None, "fsdp"),
        P(None, "fsdp"),
        P(),
        P(),
        P(),
    )
    return jax.shard_map(local, mesh=mesh, in_specs=in_specs, out_specs=out_specs, check_vma=False)
```

```python
import math

import jax
import jax.numpy as jnp
import numpy as np
from jax import lax
from jax.experimental import pallas as pl
from jax.experimental.pallas import tpu as pltpu
from jax.sharding import PartitionSpec as P

HD = 64
MIXER_HEADS = 24
MIXER_HEAD_SIZE = 64
CONVK = 4
MIXER_FEATURES = 1536
TOK = 128
norm_eps = 1e-05
rope_base = 10000.0
masked_value = -1e30

Y, X, Z = range(3)
AXES = (Y, X, Z)
STEPS = (1, 3, 2)
SMALL, INA, INB, OUT, GU, DOWN = range(6)
WEIGHTS = (SMALL, INA, INB, OUT, GU, DOWN)
PAIRED = (GU, DOWN)
ROWS = (16, 16, 16, 32, 16, 32)
COLS = (128, 1024, 1024, 512, 1024, 512)
FIRST = (0, 0, 2048, 0, 0, 0)
DEPTH = (4, 4, 4, 4, 4, 2)
ORDERS = ((X, Y, Z), (Y, Z, X), (Z, X, Y))
PAIR_ORDERS = ((Y, X, Z), (Y, Z, X))
PARTS = (
    ((0, 128),),
    ((0, 256), (256, 640), (640, 1024)),
    ((0, 384), (384, 768), (768, 1024)),
    ((0, 128), (128, 256), (256, 512)),
    ((0, 512), (512, 1024)),
    ((0, 256), (256, 512)),
)
DIRECT = {SMALL: 3, INA: 2}
BACK_DIRECT = {SMALL: 0, INB: 1}


def order_of(name, part):
    return (PAIR_ORDERS if name in PAIRED else ORDERS)[part]


def extent(name, axis):
    return DEPTH[name] if axis == Y else 4


def steps_of(name, axis):
    return (2,) if name in PAIRED and axis == Y else STEPS


def half_columns(name, core):
    return pl.ds(pl.multiple_of(FIRST[name] + core * COLS[name], 512), COLS[name])


class Place:
    def __init__(self):
        me = lax.axis_index("fsdp")
        self.me = me
        self.core = lax.rem(me, 2)
        self.at = [lax.div(me, 32), lax.rem(lax.div(me, 8), 4), lax.rem(lax.div(me, 2), 4)]
        self.sibling = me + 1 - 2 * self.core
        self.parity = lax.rem(self.at[Y], 2)
        self.pair = lax.div(self.at[Y], 2)
        self.mate = me + 32 - 64 * self.parity

    def moved(self, axis, step):
        return lax.rem(self.at[axis] + step, 4)

    def spot(self, name, axis, step):
        if name in PAIRED and axis == Y:
            pair = lax.rem(self.pair + step // 2, 2)
            return pl.ds(2 * pair, 2) if name == GU else pair
        return self.moved(axis, step)

    def peer(self, axis, step):
        at = list(self.at)
        at[axis] = self.moved(axis, step)
        return ((at[Y] * 4 + at[X]) * 4 + at[Z]) * 2 + self.core

    def partners(self):
        return [self.sibling] + [self.peer(axis, step) for axis in AXES for step in STEPS]


def arrive(place):
    for partner in place.partners():
        pl.semaphore_signal(
            pltpu.get_barrier_semaphore(),
            inc=1,
            device_id=(partner,),
            device_id_type=pl.DeviceIdType.MESH,
        )


def meet(place):
    pl.semaphore_wait(pltpu.get_barrier_semaphore(), len(place.partners()))


def push(src, dst, send_sem, recv_sem, device):
    return pltpu.make_async_remote_copy(
        src_ref=src,
        dst_ref=dst,
        send_sem=send_sem,
        recv_sem=recv_sem,
        device_id=(device,),
        device_id_type=pl.DeviceIdType.MESH,
    )


def block_index(where, low, high):
    return tuple(where.get(axis, slice(None)) for axis in AXES) + (
        slice(None),
        pl.ds(low, high - low),
    )


def expect(ref, count, sem, place):
    sizes = [
        (i, j, k)
        for i in range(1, ref.shape[0] + 1)
        for j in range(1, 5)
        for k in range(1, 5)
        if i * j * k == count
    ][0]
    view = ref.at[tuple(pl.ds(0, size) for size in sizes)]
    return push(view, view, sem, sem, place.sibling)


def halved(name, axes, half):
    axis = min(axes)
    size = extent(name, axis) // 2
    return {axis: pl.ds(size * half, size)}


def slab_blocks(name, axes, axis):
    count = 2 if name == GU and axis == Y else 1
    for one in axes:
        count *= extent(name, one)
    return count


class Gather:
    def __init__(self, place, arrays, send_sem, recv_sem):
        self.place, self.arrays = place, arrays
        self.send_sem, self.recv_sem = send_sem, recv_sem

    def ref(self, name):
        if name == SMALL:
            return self.arrays[name]
        return self.arrays[name].at[self.place.core]

    def direct(self, name, phase):
        return phase < DIRECT.get(name, 1)

    def blocks(self, name, phase):
        order = order_of(name, 0)
        return slab_blocks(name, order[:phase], order[phase])

    def send_slot(self, name, phase):
        return self.send_sem.at[4 * name + phase]

    def recv_slot(self, name, phase, kind):
        if self.direct(name, phase):
            kind = 0
        elif kind > 1:
            kind = 2
        if name == SMALL:
            return self.recv_sem.at[phase]
        return self.recv_sem.at[10 * name - 7 + (0, 1, 4)[phase] + kind]

    def slab(self, name, part, phase, step, half=None):
        order = order_of(name, part)
        where = {axis: self.place.spot(name, axis, 0) for axis in order[phase:]}
        where[order[phase]] = self.place.spot(name, order[phase], step)
        if half is not None:
            where |= halved(name, order[:phase], half)
        return self.ref(name).at[block_index(where, *PARTS[name][part])]

    def copy(self, name, part, phase, kind, half=None, slot=None):
        axis = order_of(name, part)[phase]
        step, source, handed = (
            [(one, 0, None) for one in steps_of(name, axis)]
            if self.direct(name, phase)
            else ((1, 0, None), (3, 0, None), (1, 3, 0), (3, 1, 1))
        )[kind]
        view = self.slab(name, part, phase, source, handed if half is None else half)
        return push(
            view,
            view,
            self.send_slot(name, phase),
            self.recv_slot(name, phase, kind) if slot is None else slot,
            self.place.peer(axis, step),
        )

    def start(self, name, phase, kinds=(0, 1)):
        if self.direct(name, phase):
            kinds = range(len(steps_of(name, order_of(name, 0)[phase])))
        for kind in kinds:
            for part in range(len(PARTS[name])):
                self.copy(name, part, phase, kind).start()

    def late_slot(self, name, kind):
        return self.recv_sem.at[10 * name + kind]

    def start_early(self, name):
        for kind in (0, 1):
            for part in range(len(PARTS[name])):
                self.copy(name, part, 2, kind, kind).start()

    def start_late(self, name):
        for kind in (0, 1):
            slot = self.late_slot(name, kind)
            for part in range(len(PARTS[name])):
                self.copy(name, part, 2, kind, 1 - kind, slot).start()

    def arrived(self, name, phase, kind=0):
        count = self.blocks(name, phase)
        if self.direct(name, phase):
            count *= len(steps_of(name, order_of(name, 0)[phase]))
        elif phase == 2 and kind < 2:
            count //= 2
        slot = self.recv_slot(name, phase, kind)
        expect(self.ref(name), count, slot, self.place).wait_recv()

    def hand_on(self, name, phase, kinds=(0, 1)):
        for kind in kinds:
            self.arrived(name, phase, kind)
            self.start(name, phase, (kind + 2,))

    def arrived_late(self, name, kinds=(0, 1)):
        for kind in kinds:
            slot = self.late_slot(name, kind)
            expect(self.ref(name), self.blocks(name, 2) // 2, slot, self.place).wait_recv()
            self.pass_on(name, (3, 1)[kind])

    def pass_on(self, name, step):
        for part in range(len(PARTS[name])):
            view = self.slab(name, part, 2, step)
            push(
                view,
                view,
                self.send_slot(name, 3),
                self.recv_sem.at[10 * name + 2],
                self.place.sibling,
            ).start()

    def passed(self, name):
        count = 16 * DEPTH[name]
        expect(self.ref(name), count, self.recv_sem.at[10 * name + 2], self.place).wait_recv()

    def finish(self, name):
        for phase in range(3):
            count = self.blocks(name, phase)
            if self.direct(name, phase):
                count *= len(steps_of(name, order_of(name, 0)[phase]))
            else:
                count *= 3
            expect(self.ref(name), count, self.send_slot(name, phase), self.place).wait_send()
        if name != SMALL:
            slot = self.send_slot(name, 3)
            expect(self.ref(name), 16 * DEPTH[name], slot, self.place).wait_send()


def each(count, body):
    for index in range(count):
        body(index)


class Enter:
    COLUMNS = ((INA, 0, 1024), (INB, 1024, 1024), (GU, 2048, 2048), (SMALL, 4096, 128))

    def __init__(self, place, gather, pack, got, stage, shards, sems):
        self.place, self.gather = place, gather
        self.pack, self.got, self.stage, self.shards = pack, got, stage, shards
        self.send_sem, self.recv_sem = sems

    def own(self, name, core):
        at = self.place.at
        first = self.place.pair if name == DOWN else at[Y]
        return self.gather.arrays[name].at[core, first, at[X], at[Z]]

    def copies(self):
        core = self.place.core
        pairs = [(self.pack, self.got)]
        for name in (OUT, DOWN):
            rows = pl.ds(pl.multiple_of(core * 16, 16), 16)
            src = self.shards[name].at[:, half_columns(name, 1 - core)]
            pairs.append((src, self.own(name, 1 - core).at[rows, :]))
        return [
            push(src, dst, self.send_sem.at[i], self.recv_sem.at[i], self.place.sibling)
            for i, (src, dst) in enumerate(pairs)
        ]

    def mate_copy(self):
        return push(
            self.stage,
            self.own(GU, self.place.core),
            self.send_sem.at[3],
            self.recv_sem.at[3],
            self.place.mate,
        )

    def run(self, greet, begin):
        core, at = self.place.core, self.place.at
        wide = jnp.float32
        for name, low, size in self.COLUMNS[:3]:
            first = FIRST[name]
            both = [
                self.shards[name][:, first + size * half : first + size * half + size]
                for half in range(2)
            ]
            both = [one.astype(wide) for one in both]
            self.pack[:, low : low + size] = jnp.concatenate(both, axis=0).astype(jnp.bfloat16)
        small = self.shards[SMALL][...]
        self.pack[:, 4096:4224] = jnp.concatenate([small, small], axis=0).astype(jnp.bfloat16)
        greet()
        copies = self.copies()
        for copy in copies:
            copy.start()
        copies[0].wait_recv()
        for name, low, size in self.COLUMNS:
            mine = self.pack[:, low : low + size].astype(wide)
            other = self.got[:, low : low + size].astype(wide)
            other = jnp.concatenate([other[8:16], other[0:8]], axis=0)
            upper = lax.broadcasted_iota(jnp.int32, (16, size), 0) < 8
            take = upper == (core == 0)
            block = jnp.where(take, mine, other)
            if name == SMALL:
                self.gather.arrays[name][at[Y], at[X], at[Z]] = block.astype(jnp.bfloat16)
            elif name == GU:
                even = jnp.concatenate([block[:, 0:512], block[:, 1024:1536]], axis=1)
                odd = jnp.concatenate([block[:, 512:1024], block[:, 1536:2048]], axis=1)
                first = self.place.parity == 0
                own = jnp.where(first, even, odd).astype(jnp.bfloat16)
                self.own(GU, core)[...] = own
                self.stage[...] = jnp.where(first, odd, even).astype(jnp.bfloat16)
                self.mate_copy().start()
            else:
                self.own(name, core)[...] = block.astype(jnp.bfloat16)
                begin(name)
        for name in (OUT, DOWN):
            rows = pl.ds(pl.multiple_of(core * 16, 16), 16)
            self.own(name, core)[rows, :] = self.shards[name][:, half_columns(name, core)]
        for copy in copies[1:]:
            copy.wait_recv()

    def finish(self):
        for copy in self.copies():
            copy.wait_send()
        self.mate_copy().wait_send()


class Scatter:
    def __init__(self, place, grads, first, second, third, send_sem, recv_sem):
        self.place, self.grads = place, grads
        self.got = (first, second, third)
        self.send_sem, self.recv_sem = send_sem, recv_sem

    def send_slot(self, name, phase):
        return self.send_sem.at[3 * name + phase]

    def recv_slot(self, name, phase, early=False):
        return self.recv_sem.at[5 * name + phase + (3 if early else 0)]

    def direct(self, name, phase):
        return phase >= BACK_DIRECT.get(name, 2)

    def order(self, name, part):
        return order_of(name, part)[::-1]

    def blocks(self, name, phase):
        order = self.order(name, 0)
        return slab_blocks(name, order[phase + 1 :], order[phase])

    def steps(self, name, phase):
        return steps_of(name, self.order(name, 0)[phase])

    def slab(self, name, part, phase, step, half=None):
        order = self.order(name, part)
        where = {axis: self.place.spot(name, axis, 0) for axis in order[:phase]}
        where[order[phase]] = self.place.spot(name, order[phase], step)
        if half is not None:
            where |= halved(name, order[phase + 1 :], half)
        return self.grads[name].at[block_index(where, *PARTS[name][part])]

    def landing(self, name, part, phase, slot, half=None):
        low, high = PARTS[name][part]
        left = self.order(name, part)[phase + 1 :]
        lead = [slice(None)] * len(left)
        if half is not None:
            lead[0] = halved(name, left, half)[min(left)]
        if name == GU and phase == 2:
            lead = [slice(None)]
        return (slot, *lead, slice(None), pl.ds(low, high - low))

    def push(self, name, part, phase, to, source, half, slot, early=False):
        dst = self.got[phase][name].at[self.landing(name, part, phase, slot, half)]
        push(
            self.slab(name, part, phase, source, half),
            dst,
            self.send_slot(name, phase),
            self.recv_slot(name, phase, early),
            self.place.peer(self.order(name, part)[phase], to),
        ).start()

    def start(self, name, phase, parts=None):
        for part in range(len(PARTS[name])) if parts is None else parts:
            if self.direct(name, phase):
                for slot, step in enumerate(self.steps(name, phase)):
                    self.push(name, part, phase, step, step, None, slot)
            else:
                self.push(name, part, phase, 3, 2, 0, 2, True)
                self.push(name, part, phase, 1, 2, 1, 2, True)
                self.push(name, part, phase, 3, 3, 1, 0)
                self.push(name, part, phase, 1, 1, 0, 1)

    def arrived(self, name, phase, early=False):
        count = self.blocks(name, phase)
        if self.direct(name, phase):
            count *= len(self.steps(name, phase))
        elif not early:
            count *= 2
        slot = self.recv_slot(name, phase, early)
        expect(self.grads[name], count, slot, self.place).wait_recv()

    def hand_on(self, name, phase):
        self.arrived(name, phase, True)
        for part in range(len(PARTS[name])):
            for step, half, slot in ((3, 0, 0), (1, 1, 1)):
                own = self.slab(name, part, phase, step, half)
                came = self.got[phase][name].at[self.landing(name, part, phase, 2, half)]

                def body(i):
                    own[i] = (own[i].astype(jnp.float32) + came[i].astype(jnp.float32)).astype(
                        jnp.bfloat16
                    )

                each(own.shape[0], body)
                self.push(name, part, phase, step, step, half, slot)

    def add(self, name, part, phase, pick=()):
        total = self.slab(name, part, phase, 0)[(*pick, Ellipsis)].astype(jnp.float32)
        for slot in range(len(self.steps(name, phase)) if self.direct(name, phase) else 2):
            piece = self.got[phase][name].at[self.landing(name, part, phase, slot)]
            total = total + piece[(*pick, Ellipsis)].astype(jnp.float32)
        return total

    def relay(self, name, phase):
        self.arrived(name, phase)
        for part in range(len(PARTS[name])):
            own = self.slab(name, part, phase, 0)

            def body(i):
                own[i] = self.add(name, part, phase, (i,)).astype(jnp.bfloat16)

            each(own.shape[0], body)
            self.start(name, phase + 1, (part,))

    def finish(self):
        for name in WEIGHTS:
            for phase in range(3):
                times = len(self.steps(name, phase)) if self.direct(name, phase) else 3
                count = self.blocks(name, phase) * times
                slot = self.send_slot(name, phase)
                expect(self.grads[name], count, slot, self.place).wait_send()


class SumAll:
    def __init__(self, place, got, send_sem, recv_sem):
        self.place, self.got = place, got
        self.send_sem, self.recv_sem = send_sem, recv_sem

    def start(self, stage, value):
        if stage == 0:
            slot, devices = self.place.core, [self.place.sibling]
        else:
            axis = AXES[stage - 1]
            slot, devices = self.place.at[axis], [self.place.peer(axis, s) for s in STEPS]
        self.got[stage, slot] = value
        view = self.got.at[stage, slot]
        for device in devices:
            push(view, view, self.send_sem.at[stage], self.recv_sem.at[stage], device).start()

    def expect(self, stage):
        view = self.got.at[stage, pl.ds(0, 3 if stage else 1)]
        return push(
            view, view, self.send_sem.at[stage], self.recv_sem.at[stage], self.place.sibling
        )

    def total(self, stage):
        self.expect(stage).wait_recv()
        total = self.got[stage, 0]
        for slot in range(1, 4 if stage else 2):
            total = total + self.got[stage, slot]
        return total

    def finish(self):
        for stage in range(4):
            self.expect(stage).wait_send()


class Mate:
    COTANGENT, NORMED, DOWN_PART, BACK_PART, GRAD = range(5)

    def __init__(self, place, layer, send_sem, recv_sem):
        self.place, self.layer = place, layer
        self.send_sem, self.recv_sem = send_sem, recv_sem

    def copy(self, which):
        layer = self.layer
        src, dst = (
            (layer.both_cotangent.at[pl.ds(0, 128)], layer.both_cotangent.at[pl.ds(128, 128)]),
            (layer.both_normed.at[pl.ds(0, 128)], layer.both_normed.at[pl.ds(128, 128)]),
            (layer.down_part, layer.down_got),
            (layer.back_part, layer.back_got),
            (layer.gu_sum.at[1 - self.place.parity], layer.gu_got),
        )[which]
        return push(
            src, dst, self.send_sem.at[which], self.recv_sem.at[which], self.place.mate
        )

    def start(self, which):
        self.copy(which).start()

    def start_columns(self, y):
        at = pl.ds(256 * y, 256)
        push(
            self.layer.back_part.at[:, at],
            self.layer.back_got.at[:, at],
            self.send_sem.at[self.BACK_PART],
            self.recv_sem.at[self.BACK_PART],
            self.place.mate,
        ).start()

    def arrived(self, which):
        self.copy(which).wait_recv()

    def finish(self):
        for which in range(5):
            self.copy(which).wait_send()


class End:
    def __init__(self, place, ends, got, outs, send_sem, recv_sem):
        self.place, self.ends, self.got, self.outs = place, ends, got, outs
        self.send_sem, self.recv_sem = send_sem, recv_sem

    def rows(self, name, core):
        half = ROWS[name] // 2
        return pl.ds(pl.multiple_of(core * half, 8), half)

    def columns(self, name, core):
        if name == GU:
            return pl.ds(pl.multiple_of(core * 2048, 512), 2048)
        return half_columns(name, core)

    def copy(self, name):
        slot = name - 1
        return push(
            self.ends[name].at[self.rows(name, 1 - self.place.core), :],
            self.got[name],
            self.send_sem.at[slot],
            self.recv_sem.at[slot],
            self.place.sibling,
        )

    def start(self, name):
        self.copy(name).start()
        core = self.place.core
        self.outs[name][:, self.columns(name, core)] = self.ends[name][self.rows(name, core), :]

    def take(self, name):
        self.copy(name).wait_recv()
        self.outs[name][:, self.columns(name, 1 - self.place.core)] = self.got[name][...]

    def finish(self):
        for name in WEIGHTS[1:]:
            self.copy(name).wait_send()


LOW, WIDE = jnp.bfloat16, jnp.float32


def dot(left, right):
    return jnp.dot(left, right, preferred_element_type=WIDE)


def dot_back(left, right):
    return lax.dot_general(left, right, (((1,), (1,)), ((), ())), preferred_element_type=WIDE)


def dot_over_rows(left, right):
    return lax.dot_general(left, right, (((0,), (0,)), ((), ())), preferred_element_type=WIDE)


def exact_dot(left, right):
    return jnp.dot(left, right, precision=lax.Precision.HIGHEST, preferred_element_type=WIDE)


def sigmoid(v):
    return 1.0 / (1.0 + jnp.exp(-v))


def tile(index, size):
    return pl.ds(index * size, size)


def lanes(shape):
    return lax.broadcasted_iota(jnp.int32, shape, len(shape) - 1)


def rows_of(shape):
    return lax.broadcasted_iota(jnp.int32, shape, 0)


def pair_stack(value):
    first = lanes(value.shape) < HD
    zero = jnp.zeros_like(value)
    return jnp.concatenate([jnp.where(first, value, zero), jnp.where(first, zero, value)], axis=0)


def pair_join(stacked):
    first = lanes((TOK, 128)) < HD
    return jnp.where(first, stacked[:TOK], stacked[TOK:])


def swap_halves(value):
    first = lax.rem(lanes(value.shape), HD) < HD // 2
    return jnp.where(first, pltpu.roll(value, 128 - HD // 2, 1), pltpu.roll(value, HD // 2, 1))


def doubled(value, which):
    first = lanes(value.shape) < HD
    turned = pltpu.roll(value, HD, 1)
    return jnp.where(first, value, turned) if which == 0 else jnp.where(first, turned, value)


class Layer:
    def __init__(self, refs):
        vars(self).update(refs)


    def enter(self):
        self.vectors[...] = jnp.zeros((8, 1792), WIDE)
        self.skip_sum[...] = jnp.zeros((8, 1536), WIDE)
        self.heads[...] = jnp.zeros((8, 128), WIDE)
        self.heads[0:1, 0:24] = self.decay_log[...]
        self.heads[1:2, 0:24] = self.step_bias[...]
        own = self.small_shard
        own[...] = jnp.zeros((8, 128), WIDE)
        own[0:2, 0:8] = self.norm_gains[...].astype(WIDE)
        own[2:7, 0:14] = self.conv_params[...].astype(WIDE)
        own[7:8, 0:12] = self.mixer_scale[...].astype(WIDE)
        moved = pltpu.roll(own[...], 32, 1)
        own[...] = jnp.zeros((8, 128), WIDE)
        own[:, 0:24] = self.in_shard[:, 4096:4120].astype(WIDE)
        own[...] = own[...] + moved

    def tables(self):
        position = rows_of((TOK, 128)).astype(WIDE)
        column = lax.rem(lanes((TOK, 128)), HD // 2).astype(WIDE)
        angle = position * jnp.exp(column * (-2.0 * math.log(rope_base) / HD))
        sine = jnp.sin(angle)
        first = lax.rem(lanes((TOK, 128)), HD) < HD // 2
        self.cosines[...] = jnp.cos(angle)
        self.sines[...] = jnp.where(first, -sine, sine)
        first = lanes((1, 128)) < HD
        for i in range(12):
            self.skip[0:1, 128 * i : 128 * i + 128] = jnp.where(
                first,
                self.mixer_skip[0:1, 2 * i : 2 * i + 1],
                self.mixer_skip[0:1, 2 * i + 1 : 2 * i + 2],
            )

    def spread(self):
        self.small_wide[...] = self.g_small[...].astype(WIDE).reshape(1024, 128)

        def turned(row):
            got = self.small_wide[pl.ds(row, 128, stride=8), :]
            return jnp.transpose(got)[32:48]

        for group, size, first, count, into in (
            (8, 1024, 0, 2, self.gains),
            (14, 1792, 2, 5, self.taps),
            (12, 1536, 7, 1, self.scale),
        ):
            stacked = jnp.concatenate([turned(first + i) for i in range(count)], axis=0)
            stacked = stacked.astype(LOW)
            for low in range(0, size, 256):
                start = rows_of((128, 256)) * group
                column = lanes((128, 256)) + low
                hot = (column >= start) & (column < start + group)
                index = jnp.sum(jnp.where(hot, start, 0).astype(WIDE), axis=0, keepdims=True)
                within = (lanes((1, 256)) + low).astype(WIDE) - index
                found = dot(stacked, jnp.where(hot, 1.0, 0.0).astype(LOW))
                mask = rows_of((16, 256)).astype(WIDE) == within
                for i in range(count):
                    into[i : i + 1, low : low + 256] = jnp.sum(
                        jnp.where(mask, found[16 * i : 16 * i + 16], 0.0), axis=0, keepdims=True
                    )


    def norm_in(self):
        x = self.tokens[...].astype(WIDE)
        self.inverse_in[...] = lax.rsqrt(jnp.mean(x * x, axis=-1, keepdims=True) + norm_eps)
        normed = x * self.inverse_in[...] * self.gains[0:1, :]
        self.normed[...] = normed.astype(LOW)
        self.left_in[:, 0:128] = jnp.transpose(normed).astype(LOW)

    def project(self, weights, first, half):
        for i in range(2):
            weight = weights[half, :, :, :, :, tile(i, 512)].reshape(1024, 512)
            at = pl.ds(pl.multiple_of(first + half * 1024 + 512 * i, 512), 512)
            self.proj[:, at] = dot(self.normed[...], weight)

    def project_steps(self):
        raw = dot(self.normed[...], self.g_small[...].reshape(1024, 128))
        self.step_raw[...] = jnp.where(lanes((TOK, 128)) < MIXER_HEADS, raw, 0.0)

    def convolved(self, i):
        low = 128 * i
        own = self.proj[:, 2304 + low : 2432 + low]
        row = rows_of((TOK, 128))
        shifted = [own] + [
            jnp.where(row >= k, pltpu.roll(own, k, 0), 0.0) for k in range(1, CONVK)
        ]
        total = self.taps[4:5, low : low + 128]
        for k in range(CONVK):
            total = total + self.taps[3 - k : 4 - k, low : low + 128] * shifted[k]
        return shifted, total

    def activate(self):
        for i in range(14):
            _, total = self.convolved(i)
            active = total * sigmoid(total)
            self.active[:, 128 * i : 128 * i + 128] = active

    def steps(self):
        raw = self.step_raw[...] + self.heads[1:2, :]
        step = jnp.maximum(raw, 0.0) + jnp.log1p(jnp.exp(-jnp.abs(raw)))
        rate = -jnp.exp(self.heads[0:1, :])
        lower = jnp.where(rows_of((TOK, TOK)) >= lanes((TOK, TOK)), 1.0, 0.0)
        total = exact_dot(lower, step * rate)
        self.step[...] = step
        self.cum[...] = total
        self.step_rows[...] = jnp.transpose(step)
        self.cum_rows[...] = jnp.transpose(total)

    def causal(self):
        return rows_of((TOK, TOK)) >= lanes((TOK, TOK))

    def attend(self):
        for i in range(5):
            value = self.proj[:, 128 * i : 128 * i + 128]
            turned = value * self.cosines[...] + swap_halves(value) * self.sines[...]
            self.turned[:, 128 * i : 128 * i + 128] = turned.astype(LOW)
        key = self.turned[:, 512:640].astype(WIDE)
        values = self.proj[:, 640:768]
        for which in range(2):
            self.keys[which] = doubled(key, which).astype(LOW)
            self.values[which] = doubled(values, which).astype(LOW)
        causal = self.causal()
        causal = jnp.concatenate([causal, causal], axis=0)
        for i in range(4):
            queries = pair_stack(self.turned[:, 128 * i : 128 * i + 128])
            scores = dot_back(queries, self.keys[i // 2]) * (1.0 / math.sqrt(HD))
            scores = jnp.where(causal, scores, masked_value)
            power = jnp.exp(scores - jnp.max(scores, axis=-1, keepdims=True))
            probs = power / jnp.sum(power, axis=-1, keepdims=True)
            self.small_wide[tile(i, 256), :] = probs
            self.mixed[:, 128 * i : 128 * i + 128] = pair_join(
                dot(probs.astype(LOW), self.values[i // 2])
            ).astype(LOW)

    def decay(self, head):
        gaps = self.cum[:, head : head + 1] - self.cum_rows[head : head + 1, :]
        return jnp.exp(jnp.where(self.causal(), gaps, masked_value))

    def mix(self, low, high):
        if low == 0:
            self.inner[...] = dot_back(
                self.active[:, 1664:1792].astype(LOW), self.active[:, 1536:1664].astype(LOW)
            )
        inner = self.inner[...]
        square = jnp.zeros((TOK, 1), WIDE) if low == 0 else self.inverse_state[...]
        for i in range(low, high):
            mixing = jnp.concatenate(
                [
                    inner * self.decay(head) * self.step_rows[head : head + 1, :]
                    for head in (2 * i, 2 * i + 1)
                ],
                axis=0,
            ).astype(LOW)
            self.mixing[i] = mixing
            at = slice(128 * i, 128 * i + 128)
            state = pair_join(dot(mixing, self.active[:, at].astype(LOW)))
            central = state + self.skip[0:1, at] * self.active[:, at]
            self.central[:, at] = central
            gate = self.proj[:, 768 + 128 * i : 896 + 128 * i]
            gated = central * (gate * sigmoid(gate))
            square = square + jnp.sum(gated * gated, axis=-1, keepdims=True)
        self.inverse_state[...] = square

    def mix_norm(self):
        inverse = lax.rsqrt(self.inverse_state[...] * (1.0 / MIXER_FEATURES) + norm_eps)
        self.inverse_state[...] = inverse
        for i in range(12):
            at = slice(128 * i, 128 * i + 128)
            gate = self.proj[:, 768 + 128 * i : 896 + 128 * i]
            gated = self.central[:, at] * (gate * sigmoid(gate))
            self.mixed[:, 512 + 128 * i : 640 + 128 * i] = (
                gated * inverse * self.scale[0:1, at]
            ).astype(LOW)

    def turn_left(self, source, into, count):
        for i in range(count):
            block = source[:, 128 * i : 128 * i + 128].astype(WIDE)
            into[128 * i : 128 * i + 128, 0:128] = jnp.transpose(block).astype(LOW)

    def branch_half(self, half):
        at = pl.ds(pl.multiple_of(512 * half, 512), 512)
        self.residual[:, at] = self.tokens[:, at].astype(WIDE) + dot(
            self.mixed[...], self.g_out[half].reshape(2048, 512)
        )

    def branch(self):
        x = self.residual[...]
        self.inverse_ff[...] = lax.rsqrt(jnp.mean(x * x, axis=-1, keepdims=True) + norm_eps)
        normed = x * self.inverse_ff[...] * self.gains[1:2, :]
        self.both_normed[0:128, :] = normed.astype(LOW)
        self.left_gu[:, 0:128] = jnp.transpose(normed).astype(LOW)

    def turn_other(self):
        other = self.both_normed[128:256, :].astype(WIDE)
        self.left_gu[:, 128:256] = jnp.transpose(other).astype(LOW)

    def feed_half(self, half):
        for i in range(2):
            weight = self.g_gu[half, :, :, :, :, tile(i, 512)].reshape(1024, 512)
            at = pl.ds(pl.multiple_of(half * 1024 + 512 * i, 512), 512)
            self.gate_up[:, at] = dot(self.both_normed[...], weight)

    def feed(self, send):
        for i in range(8):
            at = tile(i, 128)
            gate = self.gate_up[:, at]
            hidden = gate * sigmoid(gate) * self.gate_up[:, tile(8 + i, 128)]
            self.hidden[:, at] = hidden.astype(LOW)
            self.left_down[at, 0:256] = jnp.transpose(hidden).astype(LOW)
            if i % 4 == 3:
                send(i // 4)

    def down(self):
        for half in range(2):
            at = tile(half, 512)
            part = dot(self.hidden[...], self.g_down[half].reshape(1024, 512))
            self.down_own[:, at] = self.residual[:, at] + part[0:128]
            self.down_part[:, at] = part[128:256].astype(LOW)

    def down_sum(self):
        self.layer_output[...] = (self.down_own[...] + self.down_got[...].astype(WIDE)).astype(LOW)


    def back_down(self):
        for q in range(2):
            grad = dot_back(
                self.both_cotangent[:, 0:512], self.g_down[0, q].reshape(512, 512)
            ) + dot_back(self.both_cotangent[:, 512:1024], self.g_down[1, q].reshape(512, 512))
            for i in range(4):
                part = grad[:, 128 * i : 128 * i + 128]
                at, up_at = tile(4 * q + i, 128), tile(8 + 4 * q + i, 128)
                gate = self.gate_up[:, at]
                share = sigmoid(gate)
                self.d_gate[:, at] = (
                    part * self.gate_up[:, up_at] * (share * (1.0 + gate * (1.0 - share)))
                ).astype(LOW)
                self.d_gate[:, up_at] = (part * (gate * share)).astype(LOW)

    def norm_back(self, grad, x, inverse, gain):
        turned = x * inverse
        d_gain = jnp.sum(grad * turned, axis=0, keepdims=True)
        scaled = grad * gain
        d_x = inverse * (scaled - turned * jnp.mean(scaled * turned, axis=-1, keepdims=True))
        return d_x, d_gain

    def back_feed(self, y):
        total = dot_back(self.d_gate[:, 0:1024], self.g_gu[0, y].reshape(256, 1024)) + dot_back(
            self.d_gate[:, 1024:2048], self.g_gu[1, y].reshape(256, 1024)
        )
        self.d_wide[:, tile(y, 256)] = total[0:128]
        self.back_part[:, tile(y, 256)] = total[128:256].astype(LOW)

    def back_residual(self):
        grad = self.d_wide[:, 0:1024] + self.back_got[...].astype(WIDE)
        d_x, d_gain = self.norm_back(
            grad, self.residual[...], self.inverse_ff[...], self.gains[1:2, :]
        )
        self.vectors[1:2, 0:1024] = d_gain
        d_residual = self.cotangent[...].astype(WIDE) + d_x
        self.d_residual[...] = d_residual
        self.d_branch[...] = d_residual.astype(LOW)

    def back_branch(self):
        def body(y):
            self.d_wide[:, tile(y, 512)] = dot_back(
                self.d_branch[:, 0:512], self.g_out[0, y].reshape(512, 512)
            ) + dot_back(self.d_branch[:, 512:1024], self.g_out[1, y].reshape(512, 512))

        each(4, body)

    def back_gated(self):
        inverse = self.inverse_state[...]
        mean = jnp.zeros((TOK, 1), WIDE)
        for i in range(12):
            at = slice(128 * i, 128 * i + 128)
            gate = self.proj[:, 768 + 128 * i : 896 + 128 * i]
            gated = self.central[:, at] * (gate * sigmoid(gate))
            grad = self.d_wide[:, 512 + 128 * i : 640 + 128 * i]
            turned = gated * inverse
            self.vectors[7:8, at] = jnp.sum(grad * turned, axis=0, keepdims=True)
            mean = mean + jnp.sum(grad * self.scale[0:1, at] * turned, axis=-1, keepdims=True)
        mean = mean * (1.0 / MIXER_FEATURES)
        for i in range(12):
            at = slice(128 * i, 128 * i + 128)
            gate = self.proj[:, 768 + 128 * i : 896 + 128 * i]
            share = sigmoid(gate)
            open_gate = gate * share
            central = self.central[:, at]
            grad = self.d_wide[:, 512 + 128 * i : 640 + 128 * i]
            d_gated = inverse * (
                grad * self.scale[0:1, at] - central * open_gate * inverse * mean
            )
            d_central = d_gated * open_gate
            self.d_proj[:, 768 + 128 * i : 896 + 128 * i] = (
                d_gated * central * (share * (1.0 + gate * (1.0 - share)))
            ).astype(LOW)
            self.d_state[:, at] = d_central.astype(LOW)
            self.d_active[:, at] = d_central * self.skip[0:1, at]
            self.skip_sum[0:1, at] = jnp.sum(
                d_central * self.active[:, at], axis=0, keepdims=True
            )

    def back_mix(self, low, high):
        inner = self.inner[...]
        lane = lanes((TOK, TOK))
        zero = jnp.zeros((TOK, TOK), WIDE)
        d_inner, d_cum = (zero, zero) if low == 0 else (self.d_inner[...], self.d_cum[...])
        if low == 0:
            self.flow_rows[...] = zero
            self.d_step_rows[...] = zero
        for i in range(low, high):
            at = slice(128 * i, 128 * i + 128)
            stacked = pair_stack(self.d_state[:, at])
            d_mixing = dot_back(stacked, self.active[:, at].astype(LOW))
            self.d_active[:, at] += dot_over_rows(self.mixing[i], stacked)
            for which, head in enumerate((2 * i, 2 * i + 1)):
                grad = d_mixing[TOK * which : TOK * which + TOK]
                decay = self.decay(head)
                step = self.step_rows[head : head + 1, :]
                faded = grad * decay
                d_inner = d_inner + faded * step
                part = faded * inner
                d_step = jnp.sum(part, axis=0, keepdims=True)
                self.d_step_rows[head : head + 1, :] = d_step
                self.flow_rows[head : head + 1, :] = d_step * step
                over = jnp.sum(part * step, axis=-1, keepdims=True)
                d_cum = jnp.where(lane == head, over, d_cum)
        self.d_inner[...] = d_inner
        self.d_cum[...] = d_cum

    def back_steps(self):
        lane = lanes((TOK, TOK))
        d_inner = self.d_inner[...].astype(LOW)
        self.d_active[:, 1664:1792] = dot(d_inner, self.active[:, 1536:1664].astype(LOW))
        self.d_active[:, 1536:1664] = dot_over_rows(d_inner, self.active[:, 1664:1792].astype(LOW))
        d_cum = self.d_cum[...] - jnp.transpose(self.flow_rows[...])
        upper = jnp.where(rows_of((TOK, TOK)) <= lanes((TOK, TOK)), 1.0, 0.0)
        d_rated = exact_dot(upper, d_cum)
        rate = -jnp.exp(self.heads[0:1, :])
        d_step = jnp.transpose(self.d_step_rows[...]) + d_rated * rate
        self.vectors[7:8, 1536:1664] = (
            jnp.sum(d_rated * self.step[...], axis=0, keepdims=True) * rate
        )
        raw = self.step_raw[...] + self.heads[1:2, :]
        d_raw = jnp.where(lane < MIXER_HEADS, d_step * sigmoid(raw), 0.0)
        self.vectors[7:8, 1664:1792] = jnp.sum(d_raw, axis=0, keepdims=True)
        self.right_dt[0:128, :] = d_raw.astype(LOW)
        hot = jnp.where(
            lax.div(rows_of((1536, 128)), MIXER_HEAD_SIZE) == lanes((1536, 128)), 1.0, 0.0
        )
        self.vectors[0:1, 1024:1152] = exact_dot(self.skip_sum[...], hot)[0:1]

    def back_attend(self):
        d_keys, d_values = [], []
        for i in range(4):
            at = slice(128 * i, 128 * i + 128)
            which = i // 2
            d_out = pair_stack(self.d_wide[:, at].astype(LOW))
            d_probs = dot_back(d_out, self.values[which])
            probs = self.small_wide[tile(i, 256), :]
            d_scores = probs * (d_probs - jnp.sum(probs * d_probs, axis=-1, keepdims=True))
            d_raw = (d_scores * (1.0 / math.sqrt(HD))).astype(LOW)
            self.unturn(i, pair_join(dot(d_raw, self.keys[which])))
            d_keys.append(dot_over_rows(d_raw, pair_stack(self.turned[:, at])))
            d_values.append(dot_over_rows(probs.astype(LOW), d_out))
        first = lanes((TOK, 128)) < HD

        def joined(parts):
            one, two = parts[0] + parts[1], parts[2] + parts[3]
            return jnp.where(first, one + pltpu.roll(one, HD, 1), two + pltpu.roll(two, HD, 1))

        self.unturn(4, joined(d_keys))
        self.d_proj[:, 640:768] = joined(d_values).astype(LOW)

    def unturn(self, i, grad):
        self.d_proj[:, 128 * i : 128 * i + 128] = (
            grad * self.cosines[...] - swap_halves(grad) * self.sines[...]
        ).astype(LOW)

    def back_activate(self):
        row = rows_of((TOK, 128))
        for i in range(14):
            at = slice(128 * i, 128 * i + 128)
            shifted, total = self.convolved(i)
            share = sigmoid(total)
            grad = self.d_active[:, at] * (share * (1.0 + total * (1.0 - share)))
            self.vectors[6:7, at] = jnp.sum(grad, axis=0, keepdims=True)
            d_in = self.taps[3:4, at] * grad
            for k in range(CONVK):
                self.vectors[5 - k : 6 - k, at] = jnp.sum(grad * shifted[k], axis=0, keepdims=True)
                if k:
                    later = jnp.where(row < TOK - k, pltpu.roll(grad, TOK - k, 0), 0.0)
                    d_in = d_in + self.taps[3 - k : 4 - k, at] * later
            self.d_proj[:, 2304 + 128 * i : 2432 + 128 * i] = d_in.astype(LOW)

    def back_project(self, low, high):
        small = self.g_small[...].reshape(1024, 128)
        for y in range(low, high):
            total = dot_back(self.right_dt[0:128, :], small[256 * y : 256 * y + 256])
            for half in range(2):
                at = tile(half, 1024)
                total = total + dot_back(self.d_proj[:, at], self.g_ina[half, y].reshape(256, 1024))
                at = tile(2 + half, 1024)
                total = total + dot_back(self.d_proj[:, at], self.g_inb[half, y].reshape(256, 1024))
            self.d_wide[:, tile(y, 256)] = total

    def back_input(self):
        d_x, d_gain = self.norm_back(
            self.d_wide[:, 0:1024],
            self.tokens[...].astype(WIDE),
            self.inverse_in[...],
            self.gains[0:1, :],
        )
        self.vectors[0:1, 0:1024] = d_gain
        self.input_grad[...] = (self.d_residual[...] + d_x).astype(LOW)


    def grad_wide(self, left, right, into):
        width = right.shape[1]
        size = min(width, 512)
        for n in range(width // size):
            for y in range(4):
                block = dot(left[tile(y, 256), :], right[:, tile(n, size)])
                into[y, :, :, :, tile(n, size)] = block.astype(LOW).reshape(4, 4, 16, size)

    def grad_tall(self, left, right, into):
        for y in range(into.shape[0]):
            block = dot(left[tile(y, 512), :], right[...])
            into[y] = block.astype(LOW).reshape(4, 4, 32, 512)


class Swap:
    def __init__(self, place, layer, send_sem, recv_sem):
        self.place, self.layer = place, layer
        self.send_sem, self.recv_sem = send_sem, recv_sem
        self.lefts = (
            None, layer.left_in, None, layer.left_out, layer.left_gu, layer.left_down,
        )
        self.rights = (
            layer.right_dt, layer.right_ina, layer.right_inb, layer.right_out, layer.right_gu,
            layer.right_down,
        )
        self.sources = (
            None, layer.d_proj, layer.d_proj, layer.d_branch, layer.d_gate, layer.both_cotangent,
        )

    def left_copy(self, name):
        ref = self.lefts[name]
        size = ref.shape[1] // 2
        src, dst = ref.at[:, pl.ds(0, size)], ref.at[:, pl.ds(size, size)]
        return push(
            src, dst, self.send_sem.at[name], self.recv_sem.at[name], self.place.sibling
        )

    def right_copy(self, name):
        ref, source = self.rights[name], self.sources[name]
        size = ref.shape[0] // 2
        if source is None:
            src = ref.at[pl.ds(0, size), :]
        else:
            src = source.at[:, half_columns(name, 1 - self.place.core)]
        slot = 6 + name
        return push(
            src,
            ref.at[pl.ds(size, size), :],
            self.send_sem.at[slot],
            self.recv_sem.at[slot],
            self.place.sibling,
        )

    def start_left(self, name):
        self.left_copy(name).start()

    def start_left_rows(self, q):
        ref, rows = self.lefts[DOWN], tile(q, 512)
        push(
            ref.at[rows, pl.ds(0, 256)],
            ref.at[rows, pl.ds(256, 256)],
            self.send_sem.at[DOWN],
            self.recv_sem.at[DOWN],
            self.place.sibling,
        ).start()

    def start_right(self, name):
        ref, source = self.rights[name], self.sources[name]
        if source is not None:
            size = ref.shape[0] // 2
            ref[0:size, :] = source[:, half_columns(name, self.place.core)]
        self.right_copy(name).start()

    def arrived(self, name):
        if self.lefts[name] is not None:
            self.left_copy(name).wait_recv()
        self.right_copy(name).wait_recv()

    def finish(self):
        for name in WEIGHTS:
            self.right_copy(name).wait_send()
            if self.lefts[name] is not None:
                self.left_copy(name).wait_send()


INS = dict(
    tokens=0, cotangent=1, in_shard=2, out_shard=3, gu_shard=4, down_shard=5, norm_gains=6,
    conv_params=7, mixer_scale=8, decay_log=9, step_bias=10, mixer_skip=11,
)
OUTS = dict(
    layer_output=((TOK, 1024), LOW),
    input_grad=((TOK, 1024), LOW),
    grad_in=((8, 4120), WIDE),
    grad_out=((16, 1024), WIDE),
    grad_gu=((8, 4096), WIDE),
    grad_down=((16, 1024), WIDE),
    total=((8, 1792), WIDE),
)
SCRATCH = dict(
    g_small=((4, 4, 4, 16, 128), LOW),
    g_ina=((2, 4, 4, 4, 16, 1024), LOW),
    g_inb=((2, 4, 4, 4, 16, 1024), LOW),
    g_out=((2, 4, 4, 4, 32, 512), LOW),
    g_gu=((2, 4, 4, 4, 16, 1024), LOW),
    g_down=((2, 2, 4, 4, 32, 512), LOW),
    low_small=((4, 4, 4, 16, 128), LOW),
    low_gu=((4, 4, 4, 16, 1024), LOW),
    low_down=((2, 4, 4, 32, 512), LOW),
    small_shard=((8, 128), WIDE),
    heads=((8, 128), WIDE),
    skip=((8, 1536), WIDE),
    cosines=((TOK, 128), WIDE),
    sines=((TOK, 128), WIDE),
    pack=((16, 4224), LOW),
    got=((16, 4224), LOW),
    stage=((16, 1024), LOW),
    small_wide=((1024, 128), WIDE),
    gains=((8, 1024), WIDE),
    taps=((8, 1792), WIDE),
    scale=((8, 1536), WIDE),
    normed=((TOK, 1024), LOW),
    inverse_in=((TOK, 1), WIDE),
    proj=((TOK, 4096), WIDE),
    step_raw=((TOK, 128), WIDE),
    active=((TOK, 1792), WIDE),
    step=((TOK, TOK), WIDE),
    cum=((TOK, TOK), WIDE),
    step_rows=((TOK, TOK), WIDE),
    cum_rows=((TOK, TOK), WIDE),
    turned=((TOK, 640), LOW),
    keys=((2, TOK, 128), LOW),
    values=((2, TOK, 128), LOW),
    mixed=((TOK, 2048), LOW),
    inner=((TOK, TOK), WIDE),
    mixing=((12, 256, TOK), LOW),
    central=((TOK, 1536), WIDE),
    inverse_state=((TOK, 1), WIDE),
    residual=((TOK, 1024), WIDE),
    d_residual=((TOK, 1024), WIDE),
    inverse_ff=((TOK, 1), WIDE),
    both_normed=((256, 1024), LOW),
    both_cotangent=((256, 1024), LOW),
    gate_up=((256, 2048), WIDE),
    hidden=((256, 1024), LOW),
    down_own=((TOK, 1024), WIDE),
    down_part=((TOK, 1024), LOW),
    down_got=((TOK, 1024), LOW),
    back_part=((TOK, 1024), LOW),
    back_got=((TOK, 1024), LOW),
    gu_sum=((2, 16, 1024), WIDE),
    gu_got=((16, 1024), WIDE),
    d_gate=((256, 2048), LOW),
    d_branch=((TOK, 1024), LOW),
    d_state=((TOK, 1536), LOW),
    d_proj=((TOK, 4096), LOW),
    skip_sum=((8, 1536), WIDE),
    d_inner=((TOK, TOK), WIDE),
    d_cum=((TOK, TOK), WIDE),
    flow_rows=((TOK, TOK), WIDE),
    d_step_rows=((TOK, TOK), WIDE),
    vectors=((8, 1792), WIDE),
    left_in=((1024, 256), LOW),
    left_out=((2048, 256), LOW),
    left_gu=((1024, 512), LOW),
    left_down=((1024, 512), LOW),
    right_ina=((256, 1024), LOW),
    right_inb=((256, 1024), LOW),
    right_out=((256, 512), LOW),
    right_gu=((512, 1024), LOW),
    right_down=((512, 512), LOW),
    right_dt=((256, 128), LOW),
    sums=((4, 4, 8, 1792), WIDE),
)
BLOCKS = tuple((ROWS[name], COLS[name]) for name in WEIGHTS)
LANDINGS = tuple((3, DEPTH[name], 4) for name in WEIGHTS)
LANDINGS += tuple((3, DEPTH[name]) for name in WEIGHTS)
LANDINGS += tuple({GU: (1, 2), DOWN: (1,)}.get(name, (3,)) for name in WEIGHTS)
ENDS = tuple((ROWS[name], 2048 if name == GU else COLS[name]) for name in WEIGHTS[1:])
SEMS = dict(
    enter=(4, 4), gather=(24, 53), scatter=(18, 30), sums=(4, 4), end=(5, 5), swap=(12, 12), mate=(5, 5),
)


class Plan:
    def __init__(self, refs):
        names = [*INS, *OUTS, *SCRATCH]
        layer = Layer(dict(zip(names, refs)))
        rest = list(refs[len(names) :])
        landings = [[rest.pop(0) for _ in WEIGHTS] for _ in range(3)]
        ends = [None] + [rest.pop(0) for _ in WEIGHTS[1:]]
        ends_got = [None] + [rest.pop(0) for _ in WEIGHTS[1:]]
        sems = {name: (rest.pop(0), rest.pop(0)) for name in SEMS}
        layer.d_wide = layer.gate_up.at[pl.ds(0, 128), :]
        layer.d_active = layer.gate_up.at[pl.ds(128, 128), pl.ds(0, 1792)]
        place = Place()
        arrays = (layer.g_small, layer.g_ina, layer.g_inb, layer.g_out, layer.g_gu, layer.g_down)
        shards = (
            layer.small_shard, layer.in_shard, layer.in_shard, layer.out_shard, layer.gu_shard,
            layer.down_shard,
        )
        grads = (
            layer.low_small, layer.g_gu.at[0], layer.g_gu.at[1], layer.g_out.at[0], layer.low_gu,
            layer.low_down,
        )
        outs = (
            None, layer.grad_in, layer.grad_in, layer.grad_out, layer.grad_gu, layer.grad_down,
        )
        self.place, self.layer, self.grads = place, layer, grads
        self.gather = Gather(place, arrays, *sems["gather"])
        self.enter = Enter(
            place, self.gather, layer.pack, layer.got, layer.stage, shards, sems["enter"]
        )
        self.scatter = Scatter(place, grads, *landings, *sems["scatter"])
        self.sum_all = SumAll(place, layer.sums, *sems["sums"])
        self.end = End(place, ends, ends_got, outs, *sems["end"])
        self.swap = Swap(place, layer, *sems["swap"])
        self.mate = Mate(place, layer, *sems["mate"])

    def last(self, name):
        self.scatter.arrived(name, 2)
        for part, (low, high) in enumerate(PARTS[name]):
            value = self.scatter.add(name, part, 2)
            if name == SMALL:
                mine = jnp.where(self.place.core == 0, value[0:8], value[8:16])
                self.layer.grad_in[:, 4096:4120] = mine[:, 0:24]
            elif name == GU:
                self.layer.gu_sum[:, :, low:high] = value
            else:
                self.end.ends[name][:, low:high] = value
        if name == GU:
            self.mate.start(Mate.GRAD)
        elif name != SMALL:
            self.end.start(name)

    def last_gu(self):
        self.mate.arrived(Mate.GRAD)
        layer, parity, into = self.layer, self.place.parity, self.end.ends[GU]
        for which, value in ((parity, layer.gu_sum[parity]), (1 - parity, layer.gu_got[...])):
            for q in range(2):
                at = pl.ds(pl.multiple_of(1024 * q + 512 * which, 512), 512)
                into[:, at] = value[:, 512 * q : 512 * q + 512]
        self.end.start(GU)


def layer_kernel(*refs):
    plan = Plan(refs)
    place, layer, grads, gather = plan.place, plan.layer, plan.grads, plan.gather
    enter, scatter, sum_all, end, swap = (
        plan.enter, plan.scatter, plan.sum_all, plan.end, plan.swap,
    )
    mate, core = plan.mate, place.core

    def onward(name, phase):
        gather.arrived(name, phase, 0 if gather.direct(name, phase) else 2)
        if phase == 0 or name == SMALL:
            gather.start(name, phase + 1)
        else:
            gather.start_early(name)

    def onward_late(name):
        gather.start_late(name)
        gather.pass_on(name, 0)

    def landed(name):
        gather.arrived(name, 2, 2)
        gather.pass_on(name, 2)

    arrive(place)
    layer.enter()
    enter.run(lambda: meet(place), lambda name: gather.start(name, 0))
    gather.start(SMALL, 0)
    gather.start(OUT, 0)
    gather.start(DOWN, 0)
    layer.tables()
    enter.mate_copy().wait_recv()
    gather.start(GU, 0)
    onward(SMALL, 0)
    onward(INB, 0)
    onward(OUT, 0)
    onward(INA, 0)
    onward(DOWN, 0)
    onward(GU, 0)
    onward(SMALL, 1)
    gather.hand_on(INB, 1, (0,))
    gather.hand_on(INB, 1, (1,))
    gather.hand_on(OUT, 1, (0,))
    gather.hand_on(OUT, 1, (1,))
    gather.hand_on(DOWN, 1, (0,))
    gather.hand_on(DOWN, 1, (1,))
    onward(INA, 1)
    onward_late(INA)
    gather.hand_on(GU, 1, (0,))
    gather.hand_on(GU, 1, (1,))
    onward(INB, 1)
    onward_late(INB)
    gather.arrived(SMALL, 2)
    layer.spread()
    layer.norm_in()
    swap.start_left(INA)
    layer.project_steps()
    gather.hand_on(INA, 2, (0,))
    gather.hand_on(INA, 2, (1,))
    gather.arrived_late(INA, (0,))
    onward(OUT, 1)
    onward_late(OUT)
    gather.arrived_late(INA, (1,))
    gather.hand_on(INB, 2, (0,))
    gather.hand_on(INB, 2, (1,))
    gather.arrived_late(INB, (0,))
    gather.arrived_late(INB, (1,))
    onward(DOWN, 1)
    landed(INA)
    layer.project(layer.g_ina, 0, core)
    gather.hand_on(OUT, 2, (0,))
    gather.hand_on(OUT, 2, (1,))
    onward(GU, 1)
    onward_late(GU)
    gather.passed(INA)
    layer.project(layer.g_ina, 0, 1 - core)
    layer.attend()
    gather.arrived_late(OUT, (0,))
    gather.arrived_late(OUT, (1,))
    layer.both_cotangent[0:128, :] = layer.cotangent[...]
    mate.start(Mate.COTANGENT)
    landed(INB)
    layer.project(layer.g_inb, 2048, core)
    gather.hand_on(DOWN, 2, (0,))
    gather.hand_on(DOWN, 2, (1,))
    gather.passed(INB)
    layer.project(layer.g_inb, 2048, 1 - core)
    layer.activate()
    layer.steps()
    landed(OUT)
    layer.mix(0, 6)
    layer.mix(6, 12)
    layer.mix_norm()
    layer.branch_half(core)
    gather.hand_on(GU, 2, (1,))
    gather.passed(OUT)
    layer.branch_half(1 - core)
    layer.branch()
    mate.start(Mate.NORMED)
    layer.turn_left(layer.mixed, layer.left_out, 16)
    swap.start_left(OUT)
    gather.hand_on(GU, 2, (0,))
    onward_late(DOWN)
    mate.arrived(Mate.COTANGENT)
    swap.start_right(DOWN)
    gather.arrived_late(GU, (1,))
    gather.arrived_late(GU, (0,))
    landed(GU)
    gather.arrived_late(DOWN, (0,))
    gather.arrived_late(DOWN, (1,))
    landed(DOWN)
    mate.arrived(Mate.NORMED)
    layer.turn_other()
    swap.start_left(GU)
    layer.feed_half(core)
    gather.passed(GU)
    layer.feed_half(1 - core)
    layer.feed(swap.start_left_rows)
    gather.passed(DOWN)
    layer.back_down()
    swap.start_right(GU)
    layer.back_feed(0)
    mate.start_columns(0)
    layer.back_feed(1)
    mate.start_columns(1)
    swap.arrived(DOWN)
    layer.grad_tall(layer.left_down, layer.right_down, grads[DOWN])
    scatter.start(DOWN, 0)
    layer.back_feed(2)
    mate.start_columns(2)
    layer.back_feed(3)
    mate.start_columns(3)
    swap.arrived(GU)
    layer.grad_wide(layer.left_gu, layer.right_gu, grads[GU])
    scatter.start(GU, 0)
    layer.down()
    mate.start(Mate.DOWN_PART)
    scatter.hand_on(DOWN, 0)
    mate.arrived(Mate.BACK_PART)
    layer.back_residual()
    swap.start_right(OUT)
    layer.back_branch()
    scatter.hand_on(GU, 0)
    gather.finish(OUT)
    swap.arrived(OUT)
    layer.grad_tall(layer.left_out, layer.right_out, grads[OUT])
    scatter.start(OUT, 0)
    layer.back_gated()
    layer.back_attend()
    swap.start_right(INA)
    layer.back_mix(0, 6)
    scatter.relay(DOWN, 0)
    layer.back_mix(6, 12)
    gather.finish(GU)
    swap.arrived(INA)
    layer.grad_wide(layer.left_in, layer.right_ina, grads[INA])
    scatter.start(INA, 0)
    scatter.relay(GU, 0)
    scatter.hand_on(OUT, 0)
    layer.back_steps()
    swap.start_right(SMALL)
    scatter.hand_on(DOWN, 1)
    layer.back_activate()
    swap.start_right(INB)
    mate.arrived(Mate.DOWN_PART)
    layer.down_sum()
    swap.arrived(SMALL)
    layer.grad_wide(layer.left_in, layer.right_dt, grads[SMALL])
    scatter.start(SMALL, 0)
    swap.arrived(INB)
    layer.grad_wide(layer.left_in, layer.right_inb, grads[INB])
    scatter.start(INB, 0)
    layer.back_project(0, 2)
    layer.back_project(2, 4)
    layer.back_input()
    sum_all.start(0, layer.vectors[...])
    scatter.hand_on(GU, 1)
    scatter.hand_on(INA, 0)
    scatter.relay(OUT, 0)
    sum_all.start(1, sum_all.total(0))
    scatter.relay(DOWN, 1)
    scatter.relay(SMALL, 0)
    scatter.hand_on(INB, 0)
    scatter.relay(GU, 1)
    scatter.relay(INA, 0)
    scatter.hand_on(OUT, 1)
    sum_all.start(2, sum_all.total(1))
    plan.last(DOWN)
    scatter.relay(SMALL, 1)
    end.take(DOWN)
    scatter.relay(INB, 0)
    scatter.hand_on(INA, 1)
    plan.last(GU)
    scatter.relay(OUT, 1)
    sum_all.start(3, sum_all.total(2))
    plan.last(SMALL)
    scatter.relay(INA, 1)
    plan.last_gu()
    scatter.relay(INB, 1)
    plan.last(OUT)
    end.take(GU)
    end.take(OUT)
    layer.total[...] = sum_all.total(3)
    plan.last(INA)
    plan.last(INB)
    end.take(INA)
    end.take(INB)
    for name in (SMALL, INA, INB, DOWN):
        gather.finish(name)
    scatter.finish()
    sum_all.finish()
    end.finish()
    swap.finish()
    mate.finish()
    enter.finish()


def finish_kernel(*refs):
    ins, outs = refs[:7], refs[7:]
    for ref, into in zip(ins[:6], outs[:6]):
        into[...] = ref[...]
    me = lax.axis_index("fsdp")
    total = ins[6][...]
    column = lanes((8, 1792))

    def share(size):
        start = me * size
        picked = jnp.where((column >= start) & (column < start + size), total, 0.0)
        folded = picked[:, 0:128]
        for i in range(1, 14):
            folded = folded + picked[:, 128 * i : 128 * i + 128]
        return pltpu.roll(folded, lax.rem(1792 - start, 128), 1)

    outs[6][...] = share(8)[0:2, 0:8]
    outs[7][...] = share(14)[2:7, 0:14]
    outs[8][...] = share(12)[7:8, 0:12]
    outs[9][...] = total[7:8, 1536:1560]
    outs[10][...] = total[7:8, 1664:1688]
    outs[11][...] = total[0:1, 1024:1048]


def local(
    tokens, cotangent, input_weight, output_weight, gate_up_weight, down_weight,
    norm_gains, conv_params, mixer_scale, decay_log, step_bias, mixer_skip_factor,
):
    ins = (
        tokens, cotangent, input_weight, output_weight, gate_up_weight, down_weight, norm_gains,
        conv_params, mixer_scale, decay_log[None], step_bias[None], mixer_skip_factor[None],
    )
    scratch = [pltpu.VMEM(*one) for one in SCRATCH.values()]
    scratch += [pltpu.VMEM(lead + block, LOW) for lead, block in zip(LANDINGS, BLOCKS * 3)]
    scratch += [pltpu.VMEM(block, WIDE) for block in ENDS]
    scratch += [pltpu.VMEM((block[0] // 2, block[1]), WIDE) for block in ENDS]
    scratch += [pltpu.SemaphoreType.DMA((n,)) for counts in SEMS.values() for n in counts]
    whole = pl.BlockSpec(memory_space=pltpu.VMEM)
    results = pl.pallas_call(
        layer_kernel,
        out_shape=[jax.ShapeDtypeStruct(*one) for one in OUTS.values()],
        in_specs=[whole] * len(INS),
        out_specs=[whole] * len(OUTS),
        scratch_shapes=scratch,
        compiler_params=pltpu.CompilerParams(
            collective_id=0, has_side_effects=True, vmem_limit_bytes=127 * 2**19
        ),
        name="layer",
    )(*ins)
    shares = [(2, 8), (5, 14), (1, 12), (1, 24), (1, 24), (1, 24)]
    final = pl.pallas_call(
        finish_kernel,
        out_shape=[jax.ShapeDtypeStruct(*one) for one in list(OUTS.values())[:6]]
        + [jax.ShapeDtypeStruct(one, WIDE) for one in shares],
        in_specs=[whole] * len(OUTS),
        out_specs=[whole] * 12,
        name="finish",
    )(*results)
    return (*final[:9], *(one[0] for one in final[9:]))


def solution(mesh):
    in_specs = (
        P("fsdp", None),
        P("fsdp", None),
        P("fsdp", None),
        P("fsdp", None),
        P("fsdp", None),
        P("fsdp", None),
        P(None, "fsdp"),
        P(None, "fsdp"),
        P(None, "fsdp"),
        P(),
        P(),
        P(),
    )
    out_specs = (
        P("fsdp", None),
        P("fsdp", None),
        P("fsdp", None),
        P("fsdp", None),
        P("fsdp", None),
        P("fsdp", None),
        P(None, "fsdp"),
        P(None, "fsdp"),
        P(None, "fsdp"),
        P(),
        P(),
        P(),
    )
    return jax.shard_map(local, mesh=mesh, in_specs=in_specs, out_specs=out_specs, check_vma=False)
```

```python
import math

import jax
import jax.numpy as jnp
import numpy as np
from jax import lax
from jax.experimental import pallas as pl
from jax.experimental.pallas import tpu as pltpu
from jax.sharding import PartitionSpec as P

HD = 64
MIXER_HEADS = 24
MIXER_HEAD_SIZE = 64
CONVK = 4
MIXER_FEATURES = 1536
TOK = 128
norm_eps = 1e-05
rope_base = 10000.0
masked_value = -1e30

Y, X, Z = range(3)
AXES = (Y, X, Z)
STEPS = (1, 3, 2)
SMALL, INA, INB, OUT, GU, DOWN = range(6)
WEIGHTS = (SMALL, INA, INB, OUT, GU, DOWN)
PAIRED = (GU, DOWN)
ROWS = (16, 16, 16, 32, 16, 32)
COLS = (128, 1024, 1024, 512, 1024, 512)
FIRST = (0, 0, 2048, 0, 0, 0)
DEPTH = (4, 4, 4, 4, 4, 2)
ORDERS = ((X, Y, Z), (Y, Z, X), (Z, X, Y))
PAIR_ORDERS = ((Y, X, Z), (Y, Z, X))
PARTS = (
    ((0, 128),),
    ((0, 256), (256, 640), (640, 1024)),
    ((0, 384), (384, 768), (768, 1024)),
    ((0, 128), (128, 256), (256, 512)),
    ((0, 512), (512, 1024)),
    ((0, 256), (256, 512)),
)
DIRECT = {SMALL: 3, INA: 2}
BACK_DIRECT = {SMALL: 0, INB: 1}


def order_of(name, part):
    return (PAIR_ORDERS if name in PAIRED else ORDERS)[part]


def extent(name, axis):
    return DEPTH[name] if axis == Y else 4


def steps_of(name, axis):
    return (2,) if name in PAIRED and axis == Y else STEPS


def half_columns(name, core):
    return pl.ds(pl.multiple_of(FIRST[name] + core * COLS[name], 512), COLS[name])


class Place:
    def __init__(self):
        me = lax.axis_index("fsdp")
        self.me = me
        self.core = lax.rem(me, 2)
        self.at = [lax.div(me, 32), lax.rem(lax.div(me, 8), 4), lax.rem(lax.div(me, 2), 4)]
        self.sibling = me + 1 - 2 * self.core
        self.parity = lax.rem(self.at[Y], 2)
        self.pair = lax.div(self.at[Y], 2)
        self.mate = me + 32 - 64 * self.parity

    def moved(self, axis, step):
        return lax.rem(self.at[axis] + step, 4)

    def spot(self, name, axis, step):
        if name in PAIRED and axis == Y:
            pair = lax.rem(self.pair + step // 2, 2)
            return pl.ds(2 * pair, 2) if name == GU else pair
        return self.moved(axis, step)

    def peer(self, axis, step):
        at = list(self.at)
        at[axis] = self.moved(axis, step)
        return ((at[Y] * 4 + at[X]) * 4 + at[Z]) * 2 + self.core

    def partners(self):
        return [self.sibling] + [self.peer(axis, step) for axis in AXES for step in STEPS]


def arrive(place):
    for partner in place.partners():
        pl.semaphore_signal(
            pltpu.get_barrier_semaphore(),
            inc=1,
            device_id=(partner,),
            device_id_type=pl.DeviceIdType.MESH,
        )


def meet(place):
    pl.semaphore_wait(pltpu.get_barrier_semaphore(), len(place.partners()))


def push(src, dst, send_sem, recv_sem, device):
    return pltpu.make_async_remote_copy(
        src_ref=src,
        dst_ref=dst,
        send_sem=send_sem,
        recv_sem=recv_sem,
        device_id=(device,),
        device_id_type=pl.DeviceIdType.MESH,
    )


def block_index(where, low, high):
    return tuple(where.get(axis, slice(None)) for axis in AXES) + (
        slice(None),
        pl.ds(low, high - low),
    )


def expect(ref, count, sem, place):
    sizes = [
        (i, j, k)
        for i in range(1, ref.shape[0] + 1)
        for j in range(1, 5)
        for k in range(1, 5)
        if i * j * k == count
    ][0]
    view = ref.at[tuple(pl.ds(0, size) for size in sizes)]
    return push(view, view, sem, sem, place.sibling)


def halved(name, axes, half):
    axis = min(axes)
    size = extent(name, axis) // 2
    return {axis: pl.ds(size * half, size)}


def slab_blocks(name, axes, axis):
    count = 2 if name == GU and axis == Y else 1
    for one in axes:
        count *= extent(name, one)
    return count


class Gather:
    def __init__(self, place, arrays, send_sem, recv_sem):
        self.place, self.arrays = place, arrays
        self.send_sem, self.recv_sem = send_sem, recv_sem

    def ref(self, name):
        if name == SMALL:
            return self.arrays[name]
        return self.arrays[name].at[self.place.core]

    def direct(self, name, phase):
        return phase < DIRECT.get(name, 1)

    def blocks(self, name, phase):
        order = order_of(name, 0)
        if name == SMALL and phase == 2:
            return 8
        return slab_blocks(name, order[:phase], order[phase])

    def send_slot(self, name, phase):
        return self.send_sem.at[4 * name + phase]

    def recv_slot(self, name, phase, kind):
        if self.direct(name, phase):
            kind = 0
        elif kind > 1:
            kind = 2
        if name == SMALL:
            return self.recv_sem.at[phase]
        return self.recv_sem.at[10 * name - 7 + (0, 1, 4)[phase] + kind]

    def slab(self, name, part, phase, step, half=None):
        order = order_of(name, part)
        where = {axis: self.place.spot(name, axis, 0) for axis in order[phase:]}
        where[order[phase]] = self.place.spot(name, order[phase], step)
        if half is not None:
            where |= halved(name, order[:phase], half)
        if name == SMALL and phase == 2:
            where[X] = pl.ds(2 * self.place.core, 2)
        return self.ref(name).at[block_index(where, *PARTS[name][part])]

    def copy(self, name, part, phase, kind, half=None, slot=None):
        axis = order_of(name, part)[phase]
        step, source, handed = (
            [(one, 0, None) for one in steps_of(name, axis)]
            if self.direct(name, phase)
            else ((1, 0, None), (3, 0, None), (1, 3, 0), (3, 1, 1))
        )[kind]
        view = self.slab(name, part, phase, source, handed if half is None else half)
        return push(
            view,
            view,
            self.send_slot(name, phase),
            self.recv_slot(name, phase, kind) if slot is None else slot,
            self.place.peer(axis, step),
        )

    def start(self, name, phase, kinds=(0, 1)):
        if self.direct(name, phase):
            kinds = range(len(steps_of(name, order_of(name, 0)[phase])))
        for kind in kinds:
            for part in range(len(PARTS[name])):
                self.copy(name, part, phase, kind).start()

    def late_slot(self, name, kind):
        return self.recv_sem.at[10 * name + kind]

    def start_early(self, name):
        for kind in (0, 1):
            for part in range(len(PARTS[name])):
                self.copy(name, part, 2, kind, kind).start()

    def start_late(self, name):
        for kind in (0, 1):
            slot = self.late_slot(name, kind)
            for part in range(len(PARTS[name])):
                self.copy(name, part, 2, kind, 1 - kind, slot).start()

    def arrived(self, name, phase, kind=0):
        count = self.blocks(name, phase)
        if self.direct(name, phase):
            count *= len(steps_of(name, order_of(name, 0)[phase]))
        elif phase == 2 and kind < 2:
            count //= 2
        slot = self.recv_slot(name, phase, kind)
        expect(self.ref(name), count, slot, self.place).wait_recv()

    def hand_on(self, name, phase, kinds=(0, 1)):
        for kind in kinds:
            self.arrived(name, phase, kind)
            self.start(name, phase, (kind + 2,))

    def arrived_late(self, name, kinds=(0, 1)):
        for kind in kinds:
            slot = self.late_slot(name, kind)
            expect(self.ref(name), self.blocks(name, 2) // 2, slot, self.place).wait_recv()
            self.pass_on(name, (3, 1)[kind])

    def pass_on(self, name, step):
        for part in range(len(PARTS[name])):
            view = self.slab(name, part, 2, step)
            push(
                view,
                view,
                self.send_slot(name, 3),
                self.recv_sem.at[10 * name + 2],
                self.place.sibling,
            ).start()

    def share_small(self):
        self.arrived(SMALL, 2)
        for step in STEPS:
            view = self.slab(SMALL, 0, 2, step)
            push(
                view, view, self.send_slot(SMALL, 3), self.recv_sem.at[53], self.place.sibling
            ).start()

    def shared_small(self):
        expect(self.ref(SMALL), 24, self.recv_sem.at[53], self.place).wait_recv()

    def passed(self, name):
        count = 16 * DEPTH[name]
        expect(self.ref(name), count, self.recv_sem.at[10 * name + 2], self.place).wait_recv()

    def finish(self, name):
        for phase in range(3):
            count = self.blocks(name, phase)
            if self.direct(name, phase):
                count *= len(steps_of(name, order_of(name, 0)[phase]))
            else:
                count *= 3
            expect(self.ref(name), count, self.send_slot(name, phase), self.place).wait_send()
        slot = self.send_slot(name, 3)
        count = 24 if name == SMALL else 16 * DEPTH[name]
        expect(self.ref(name), count, slot, self.place).wait_send()


def each(count, body):
    for index in range(count):
        body(index)


class Enter:
    COLUMNS = ((INA, 0, 1024), (INB, 1024, 1024), (GU, 2048, 2048), (SMALL, 4096, 128))

    def __init__(self, place, gather, pack, got, stage, shards, sems):
        self.place, self.gather = place, gather
        self.pack, self.got, self.stage, self.shards = pack, got, stage, shards
        self.send_sem, self.recv_sem = sems

    def own(self, name, core):
        at = self.place.at
        first = self.place.pair if name == DOWN else at[Y]
        return self.gather.arrays[name].at[core, first, at[X], at[Z]]

    def copies(self):
        core = self.place.core
        pairs = [(self.pack, self.got)]
        for name in (OUT, DOWN):
            rows = pl.ds(pl.multiple_of(core * 16, 16), 16)
            src = self.shards[name].at[:, half_columns(name, 1 - core)]
            pairs.append((src, self.own(name, 1 - core).at[rows, :]))
        return [
            push(src, dst, self.send_sem.at[i], self.recv_sem.at[i], self.place.sibling)
            for i, (src, dst) in enumerate(pairs)
        ]

    def mate_copy(self):
        return push(
            self.stage,
            self.own(GU, self.place.core),
            self.send_sem.at[3],
            self.recv_sem.at[3],
            self.place.mate,
        )

    def run(self, greet, begin):
        core, at = self.place.core, self.place.at
        wide = jnp.float32
        for name, low, size in self.COLUMNS[:3]:
            first = FIRST[name]
            both = [
                self.shards[name][:, first + size * half : first + size * half + size]
                for half in range(2)
            ]
            both = [one.astype(wide) for one in both]
            self.pack[:, low : low + size] = jnp.concatenate(both, axis=0).astype(jnp.bfloat16)
        small = self.shards[SMALL][...]
        self.pack[:, 4096:4224] = jnp.concatenate([small, small], axis=0).astype(jnp.bfloat16)
        greet()
        copies = self.copies()
        for copy in copies:
            copy.start()
        copies[0].wait_recv()
        for name, low, size in self.COLUMNS:
            mine = self.pack[:, low : low + size].astype(wide)
            other = self.got[:, low : low + size].astype(wide)
            other = jnp.concatenate([other[8:16], other[0:8]], axis=0)
            upper = lax.broadcasted_iota(jnp.int32, (16, size), 0) < 8
            take = upper == (core == 0)
            block = jnp.where(take, mine, other)
            if name == SMALL:
                self.gather.arrays[name][at[Y], at[X], at[Z]] = block.astype(jnp.bfloat16)
            elif name == GU:
                even = jnp.concatenate([block[:, 0:512], block[:, 1024:1536]], axis=1)
                odd = jnp.concatenate([block[:, 512:1024], block[:, 1536:2048]], axis=1)
                first = self.place.parity == 0
                own = jnp.where(first, even, odd).astype(jnp.bfloat16)
                self.own(GU, core)[...] = own
                self.stage[...] = jnp.where(first, odd, even).astype(jnp.bfloat16)
                self.mate_copy().start()
            else:
                self.own(name, core)[...] = block.astype(jnp.bfloat16)
                begin(name)
        for name in (OUT, DOWN):
            rows = pl.ds(pl.multiple_of(core * 16, 16), 16)
            self.own(name, core)[rows, :] = self.shards[name][:, half_columns(name, core)]
        for copy in copies[1:]:
            copy.wait_recv()

    def finish(self):
        for copy in self.copies():
            copy.wait_send()
        self.mate_copy().wait_send()


class Scatter:
    def __init__(self, place, grads, first, second, third, send_sem, recv_sem):
        self.place, self.grads = place, grads
        self.got = (first, second, third)
        self.send_sem, self.recv_sem = send_sem, recv_sem

    def send_slot(self, name, phase):
        return self.send_sem.at[3 * name + phase]

    def recv_slot(self, name, phase, early=False):
        return self.recv_sem.at[5 * name + phase + (3 if early else 0)]

    def direct(self, name, phase):
        return phase >= BACK_DIRECT.get(name, 2)

    def order(self, name, part):
        return order_of(name, part)[::-1]

    def blocks(self, name, phase):
        order = self.order(name, 0)
        return slab_blocks(name, order[phase + 1 :], order[phase])

    def steps(self, name, phase):
        return steps_of(name, self.order(name, 0)[phase])

    def slab(self, name, part, phase, step, half=None):
        order = self.order(name, part)
        where = {axis: self.place.spot(name, axis, 0) for axis in order[:phase]}
        where[order[phase]] = self.place.spot(name, order[phase], step)
        if half is not None:
            where |= halved(name, order[phase + 1 :], half)
        return self.grads[name].at[block_index(where, *PARTS[name][part])]

    def landing(self, name, part, phase, slot, half=None):
        low, high = PARTS[name][part]
        left = self.order(name, part)[phase + 1 :]
        lead = [slice(None)] * len(left)
        if half is not None:
            lead[0] = halved(name, left, half)[min(left)]
        if name == GU and phase == 2:
            lead = [slice(None)]
        return (slot, *lead, slice(None), pl.ds(low, high - low))

    def push(self, name, part, phase, to, source, half, slot, early=False):
        dst = self.got[phase][name].at[self.landing(name, part, phase, slot, half)]
        push(
            self.slab(name, part, phase, source, half),
            dst,
            self.send_slot(name, phase),
            self.recv_slot(name, phase, early),
            self.place.peer(self.order(name, part)[phase], to),
        ).start()

    def start(self, name, phase, parts=None):
        for part in range(len(PARTS[name])) if parts is None else parts:
            if self.direct(name, phase):
                for slot, step in enumerate(self.steps(name, phase)):
                    self.push(name, part, phase, step, step, None, slot)
            else:
                self.push(name, part, phase, 3, 2, 0, 2, True)
                self.push(name, part, phase, 1, 2, 1, 2, True)
                self.push(name, part, phase, 3, 3, 1, 0)
                self.push(name, part, phase, 1, 1, 0, 1)

    def arrived(self, name, phase, early=False):
        count = self.blocks(name, phase)
        if self.direct(name, phase):
            count *= len(self.steps(name, phase))
        elif not early:
            count *= 2
        slot = self.recv_slot(name, phase, early)
        expect(self.grads[name], count, slot, self.place).wait_recv()

    def hand_on(self, name, phase):
        self.arrived(name, phase, True)
        for part in range(len(PARTS[name])):
            for step, half, slot in ((3, 0, 0), (1, 1, 1)):
                own = self.slab(name, part, phase, step, half)
                came = self.got[phase][name].at[self.landing(name, part, phase, 2, half)]

                def body(i):
                    own[i] = (own[i].astype(jnp.float32) + came[i].astype(jnp.float32)).astype(
                        jnp.bfloat16
                    )

                each(own.shape[0], body)
                self.push(name, part, phase, step, step, half, slot)

    def add(self, name, part, phase, pick=()):
        total = self.slab(name, part, phase, 0)[(*pick, Ellipsis)].astype(jnp.float32)
        for slot in range(len(self.steps(name, phase)) if self.direct(name, phase) else 2):
            piece = self.got[phase][name].at[self.landing(name, part, phase, slot)]
            total = total + piece[(*pick, Ellipsis)].astype(jnp.float32)
        return total

    def relay(self, name, phase):
        self.arrived(name, phase)
        for part in range(len(PARTS[name])):
            own = self.slab(name, part, phase, 0)

            def body(i):
                own[i] = self.add(name, part, phase, (i,)).astype(jnp.bfloat16)

            each(own.shape[0], body)
            self.start(name, phase + 1, (part,))

    def finish(self):
        for name in WEIGHTS:
            for phase in range(3):
                times = len(self.steps(name, phase)) if self.direct(name, phase) else 3
                count = self.blocks(name, phase) * times
                slot = self.send_slot(name, phase)
                expect(self.grads[name], count, slot, self.place).wait_send()


class SumAll:
    def __init__(self, place, got, send_sem, recv_sem):
        self.place, self.got = place, got
        self.send_sem, self.recv_sem = send_sem, recv_sem

    def push(self, src, stage, slot, device):
        dst = self.got.at[stage, slot]
        push(src, dst, self.send_sem.at[stage], self.recv_sem.at[stage], device).start()

    def begin(self, values):
        core, size = self.place.core, self.got.shape[3]
        own = pl.ds(pl.multiple_of(core * size, size), size)
        other = pl.ds(pl.multiple_of((1 - core) * size, size), size)
        self.push(values.at[:, other], 0, core, self.place.sibling)
        self.got[0, core] = values[:, own]

    def start(self, stage, value):
        if stage == 4:
            slot, devices = self.place.core, [self.place.sibling]
        else:
            axis = AXES[stage - 1]
            slot, devices = self.place.at[axis], [self.place.peer(axis, s) for s in STEPS]
        self.got[stage, slot] = value
        for device in devices:
            self.push(self.got.at[stage, slot], stage, slot, device)

    def expect(self, stage):
        view = self.got.at[stage, pl.ds(0, 3 if 0 < stage < 4 else 1)]
        return push(
            view, view, self.send_sem.at[stage], self.recv_sem.at[stage], self.place.sibling
        )

    def total(self, stage):
        self.expect(stage).wait_recv()
        total = self.got[stage, 0]
        for slot in range(1, 4 if stage else 2):
            total = total + self.got[stage, slot]
        return total

    def into(self, ref):
        self.expect(4).wait_recv()
        size = self.got.shape[3]
        for half in range(2):
            ref[:, size * half : size * half + size] = self.got[4, half]

    def finish(self):
        for stage in range(5):
            self.expect(stage).wait_send()


class Mate:
    COTANGENT, NORMED, DOWN_PART, BACK_PART, GRAD = range(5)

    def __init__(self, place, layer, send_sem, recv_sem):
        self.place, self.layer = place, layer
        self.send_sem, self.recv_sem = send_sem, recv_sem

    def copy(self, which):
        layer = self.layer
        src, dst = (
            (layer.both_cotangent.at[pl.ds(0, 128)], layer.both_cotangent.at[pl.ds(128, 128)]),
            (layer.both_normed.at[pl.ds(0, 128)], layer.both_normed.at[pl.ds(128, 128)]),
            (layer.down_part, layer.down_got),
            (layer.back_part, layer.back_got),
            (layer.gu_sum.at[1 - self.place.parity], layer.gu_got),
        )[which]
        return push(
            src, dst, self.send_sem.at[which], self.recv_sem.at[which], self.place.mate
        )

    def start(self, which):
        self.copy(which).start()

    def start_columns(self, y):
        at = pl.ds(256 * y, 256)
        push(
            self.layer.back_part.at[:, at],
            self.layer.back_got.at[:, at],
            self.send_sem.at[self.BACK_PART],
            self.recv_sem.at[self.BACK_PART],
            self.place.mate,
        ).start()

    def arrived(self, which):
        self.copy(which).wait_recv()

    def finish(self):
        for which in range(5):
            self.copy(which).wait_send()


class End:
    def __init__(self, place, ends, got, outs, send_sem, recv_sem):
        self.place, self.ends, self.got, self.outs = place, ends, got, outs
        self.send_sem, self.recv_sem = send_sem, recv_sem

    def rows(self, name, core):
        half = ROWS[name] // 2
        return pl.ds(pl.multiple_of(core * half, 8), half)

    def columns(self, name, core):
        if name == GU:
            return pl.ds(pl.multiple_of(core * 2048, 512), 2048)
        return half_columns(name, core)

    def copy(self, name):
        slot = name - 1
        return push(
            self.ends[name].at[self.rows(name, 1 - self.place.core), :],
            self.got[name],
            self.send_sem.at[slot],
            self.recv_sem.at[slot],
            self.place.sibling,
        )

    def start(self, name):
        self.copy(name).start()
        core = self.place.core
        self.outs[name][:, self.columns(name, core)] = self.ends[name][self.rows(name, core), :]

    def take(self, name):
        self.copy(name).wait_recv()
        self.outs[name][:, self.columns(name, 1 - self.place.core)] = self.got[name][...]

    def finish(self):
        for name in WEIGHTS[1:]:
            self.copy(name).wait_send()


LOW, WIDE = jnp.bfloat16, jnp.float32


def dot(left, right):
    return jnp.dot(left, right, preferred_element_type=WIDE)


def dot_back(left, right):
    return lax.dot_general(left, right, (((1,), (1,)), ((), ())), preferred_element_type=WIDE)


def dot_over_rows(left, right):
    return lax.dot_general(left, right, (((0,), (0,)), ((), ())), preferred_element_type=WIDE)


def exact_dot(left, right):
    return jnp.dot(left, right, precision=lax.Precision.HIGHEST, preferred_element_type=WIDE)


def sigmoid(v):
    return 1.0 / (1.0 + jnp.exp(-v))


def tile(index, size):
    return pl.ds(index * size, size)


def lanes(shape):
    return lax.broadcasted_iota(jnp.int32, shape, len(shape) - 1)


def rows_of(shape):
    return lax.broadcasted_iota(jnp.int32, shape, 0)


def pair_stack(value):
    first = lanes(value.shape) < HD
    zero = jnp.zeros_like(value)
    return jnp.concatenate([jnp.where(first, value, zero), jnp.where(first, zero, value)], axis=0)


def pair_join(stacked):
    first = lanes((TOK, 128)) < HD
    return jnp.where(first, stacked[:TOK], stacked[TOK:])


def swap_halves(value):
    first = lax.rem(lanes(value.shape), HD) < HD // 2
    return jnp.where(first, pltpu.roll(value, 128 - HD // 2, 1), pltpu.roll(value, HD // 2, 1))


def doubled(value, which):
    first = lanes(value.shape) < HD
    turned = pltpu.roll(value, HD, 1)
    return jnp.where(first, value, turned) if which == 0 else jnp.where(first, turned, value)


class Layer:
    def __init__(self, refs):
        vars(self).update(refs)


    def enter(self):
        self.vectors[...] = jnp.zeros((8, 1792), WIDE)
        self.skip_sum[...] = jnp.zeros((8, 1536), WIDE)
        self.heads[...] = jnp.zeros((8, 128), WIDE)
        self.heads[0:1, 0:24] = self.decay_log[...]
        self.heads[1:2, 0:24] = self.step_bias[...]
        own = self.small_shard
        own[...] = jnp.zeros((8, 128), WIDE)
        own[0:2, 0:8] = self.norm_gains[...].astype(WIDE)
        own[2:7, 0:14] = self.conv_params[...].astype(WIDE)
        own[7:8, 0:12] = self.mixer_scale[...].astype(WIDE)
        moved = pltpu.roll(own[...], 32, 1)
        own[...] = jnp.zeros((8, 128), WIDE)
        own[:, 0:24] = self.in_shard[:, 4096:4120].astype(WIDE)
        own[...] = own[...] + moved

    def tables(self):
        position = rows_of((TOK, 128)).astype(WIDE)
        column = lax.rem(lanes((TOK, 128)), HD // 2).astype(WIDE)
        angle = position * jnp.exp(column * (-2.0 * math.log(rope_base) / HD))
        sine = jnp.sin(angle)
        first = lax.rem(lanes((TOK, 128)), HD) < HD // 2
        self.cosines[...] = jnp.cos(angle)
        self.sines[...] = jnp.where(first, -sine, sine)
        first = lanes((1, 128)) < HD
        for i in range(12):
            self.skip[0:1, 128 * i : 128 * i + 128] = jnp.where(
                first,
                self.mixer_skip[0:1, 2 * i : 2 * i + 1],
                self.mixer_skip[0:1, 2 * i + 1 : 2 * i + 2],
            )

    def spread(self):
        self.small_wide[...] = self.g_small[...].astype(WIDE).reshape(1024, 128)

        def turned(row):
            got = self.small_wide[pl.ds(row, 128, stride=8), :]
            return jnp.transpose(got)[32:48]

        for group, size, first, count, into in (
            (8, 1024, 0, 2, self.gains),
            (14, 1792, 2, 5, self.taps),
            (12, 1536, 7, 1, self.scale),
        ):
            stacked = jnp.concatenate([turned(first + i) for i in range(count)], axis=0)
            stacked = stacked.astype(LOW)
            for low in range(0, size, 256):
                start = rows_of((128, 256)) * group
                column = lanes((128, 256)) + low
                hot = (column >= start) & (column < start + group)
                index = jnp.sum(jnp.where(hot, start, 0).astype(WIDE), axis=0, keepdims=True)
                within = (lanes((1, 256)) + low).astype(WIDE) - index
                found = dot(stacked, jnp.where(hot, 1.0, 0.0).astype(LOW))
                mask = rows_of((16, 256)).astype(WIDE) == within
                for i in range(count):
                    into[i : i + 1, low : low + 256] = jnp.sum(
                        jnp.where(mask, found[16 * i : 16 * i + 16], 0.0), axis=0, keepdims=True
                    )


    def norm_in(self):
        x = self.tokens[...].astype(WIDE)
        self.inverse_in[...] = lax.rsqrt(jnp.mean(x * x, axis=-1, keepdims=True) + norm_eps)
        normed = x * self.inverse_in[...] * self.gains[0:1, :]
        self.normed[...] = normed.astype(LOW)
        self.left_in[:, 0:128] = jnp.transpose(normed).astype(LOW)

    def project(self, weights, first, half):
        for i in range(2):
            weight = weights[half, :, :, :, :, tile(i, 512)].reshape(1024, 512)
            at = pl.ds(pl.multiple_of(first + half * 1024 + 512 * i, 512), 512)
            self.proj[:, at] = dot(self.normed[...], weight)

    def project_steps(self):
        raw = dot(self.normed[...], self.g_small[...].reshape(1024, 128))
        self.step_raw[...] = jnp.where(lanes((TOK, 128)) < MIXER_HEADS, raw, 0.0)

    def convolved(self, i):
        low = 128 * i
        own = self.proj[:, 2304 + low : 2432 + low]
        row = rows_of((TOK, 128))
        shifted = [own] + [
            jnp.where(row >= k, pltpu.roll(own, k, 0), 0.0) for k in range(1, CONVK)
        ]
        total = self.taps[4:5, low : low + 128]
        for k in range(CONVK):
            total = total + self.taps[3 - k : 4 - k, low : low + 128] * shifted[k]
        return shifted, total

    def activate(self):
        for i in range(14):
            _, total = self.convolved(i)
            active = total * sigmoid(total)
            self.active[:, 128 * i : 128 * i + 128] = active

    def steps(self):
        raw = self.step_raw[...] + self.heads[1:2, :]
        step = jnp.maximum(raw, 0.0) + jnp.log1p(jnp.exp(-jnp.abs(raw)))
        rate = -jnp.exp(self.heads[0:1, :])
        lower = jnp.where(rows_of((TOK, TOK)) >= lanes((TOK, TOK)), 1.0, 0.0)
        total = exact_dot(lower, step * rate)
        self.step[...] = step
        self.cum[...] = total
        self.step_rows[...] = jnp.transpose(step)
        self.cum_rows[...] = jnp.transpose(total)

    def causal(self):
        return rows_of((TOK, TOK)) >= lanes((TOK, TOK))

    def attend(self):
        for i in range(5):
            value = self.proj[:, 128 * i : 128 * i + 128]
            turned = value * self.cosines[...] + swap_halves(value) * self.sines[...]
            self.turned[:, 128 * i : 128 * i + 128] = turned.astype(LOW)
        key = self.turned[:, 512:640].astype(WIDE)
        values = self.proj[:, 640:768]
        for which in range(2):
            self.keys[which] = doubled(key, which).astype(LOW)
            self.values[which] = doubled(values, which).astype(LOW)
        causal = self.causal()
        causal = jnp.concatenate([causal, causal], axis=0)
        for i in range(4):
            queries = pair_stack(self.turned[:, 128 * i : 128 * i + 128])
            scores = dot_back(queries, self.keys[i // 2]) * (1.0 / math.sqrt(HD))
            scores = jnp.where(causal, scores, masked_value)
            power = jnp.exp(scores - jnp.max(scores, axis=-1, keepdims=True))
            probs = power / jnp.sum(power, axis=-1, keepdims=True)
            self.small_wide[tile(i, 256), :] = probs
            self.mixed[:, 128 * i : 128 * i + 128] = pair_join(
                dot(probs.astype(LOW), self.values[i // 2])
            ).astype(LOW)

    def decay(self, head):
        gaps = self.cum[:, head : head + 1] - self.cum_rows[head : head + 1, :]
        return jnp.exp(jnp.where(self.causal(), gaps, masked_value))

    def mix(self, low, high):
        if low == 0:
            self.inner[...] = dot_back(
                self.active[:, 1664:1792].astype(LOW), self.active[:, 1536:1664].astype(LOW)
            )
        inner = self.inner[...]
        square = jnp.zeros((TOK, 1), WIDE) if low == 0 else self.inverse_state[...]
        for i in range(low, high):
            mixing = jnp.concatenate(
                [
                    inner * self.decay(head) * self.step_rows[head : head + 1, :]
                    for head in (2 * i, 2 * i + 1)
                ],
                axis=0,
            ).astype(LOW)
            self.mixing[i] = mixing
            at = slice(128 * i, 128 * i + 128)
            state = pair_join(dot(mixing, self.active[:, at].astype(LOW)))
            central = state + self.skip[0:1, at] * self.active[:, at]
            self.central[:, at] = central
            gate = self.proj[:, 768 + 128 * i : 896 + 128 * i]
            gated = central * (gate * sigmoid(gate))
            square = square + jnp.sum(gated * gated, axis=-1, keepdims=True)
        self.inverse_state[...] = square

    def mix_norm(self):
        inverse = lax.rsqrt(self.inverse_state[...] * (1.0 / MIXER_FEATURES) + norm_eps)
        self.inverse_state[...] = inverse
        for i in range(12):
            at = slice(128 * i, 128 * i + 128)
            gate = self.proj[:, 768 + 128 * i : 896 + 128 * i]
            gated = self.central[:, at] * (gate * sigmoid(gate))
            self.mixed[:, 512 + 128 * i : 640 + 128 * i] = (
                gated * inverse * self.scale[0:1, at]
            ).astype(LOW)

    def turn_left(self, source, into, count):
        for i in range(count):
            block = source[:, 128 * i : 128 * i + 128].astype(WIDE)
            into[128 * i : 128 * i + 128, 0:128] = jnp.transpose(block).astype(LOW)

    def branch_half(self, half):
        at = pl.ds(pl.multiple_of(512 * half, 512), 512)
        self.residual[:, at] = self.tokens[:, at].astype(WIDE) + dot(
            self.mixed[...], self.g_out[half].reshape(2048, 512)
        )

    def branch(self):
        x = self.residual[...]
        self.inverse_ff[...] = lax.rsqrt(jnp.mean(x * x, axis=-1, keepdims=True) + norm_eps)
        normed = x * self.inverse_ff[...] * self.gains[1:2, :]
        self.both_normed[0:128, :] = normed.astype(LOW)
        self.left_gu[:, 0:128] = jnp.transpose(normed).astype(LOW)

    def turn_other(self):
        other = self.both_normed[128:256, :].astype(WIDE)
        self.left_gu[:, 128:256] = jnp.transpose(other).astype(LOW)

    def feed_half(self, half):
        for i in range(2):
            weight = self.g_gu[half, :, :, :, :, tile(i, 512)].reshape(1024, 512)
            at = pl.ds(pl.multiple_of(half * 1024 + 512 * i, 512), 512)
            self.gate_up[:, at] = dot(self.both_normed[...], weight)

    def feed(self, send):
        for i in range(8):
            at = tile(i, 128)
            gate = self.gate_up[:, at]
            hidden = gate * sigmoid(gate) * self.gate_up[:, tile(8 + i, 128)]
            self.hidden[:, at] = hidden.astype(LOW)
            self.left_down[at, 0:256] = jnp.transpose(hidden).astype(LOW)
            if i % 4 == 3:
                send(i // 4)

    def down(self):
        for half in range(2):
            at = tile(half, 512)
            part = dot(self.hidden[...], self.g_down[half].reshape(1024, 512))
            self.down_own[:, at] = self.residual[:, at] + part[0:128]
            self.down_part[:, at] = part[128:256].astype(LOW)

    def down_sum(self):
        self.layer_output[...] = (self.down_own[...] + self.down_got[...].astype(WIDE)).astype(LOW)


    def back_down(self):
        for q in range(2):
            grad = dot_back(
                self.both_cotangent[:, 0:512], self.g_down[0, q].reshape(512, 512)
            ) + dot_back(self.both_cotangent[:, 512:1024], self.g_down[1, q].reshape(512, 512))
            for i in range(4):
                part = grad[:, 128 * i : 128 * i + 128]
                at, up_at = tile(4 * q + i, 128), tile(8 + 4 * q + i, 128)
                gate = self.gate_up[:, at]
                share = sigmoid(gate)
                self.d_gate[:, at] = (
                    part * self.gate_up[:, up_at] * (share * (1.0 + gate * (1.0 - share)))
                ).astype(LOW)
                self.d_gate[:, up_at] = (part * (gate * share)).astype(LOW)

    def norm_back(self, grad, x, inverse, gain):
        turned = x * inverse
        d_gain = jnp.sum(grad * turned, axis=0, keepdims=True)
        scaled = grad * gain
        d_x = inverse * (scaled - turned * jnp.mean(scaled * turned, axis=-1, keepdims=True))
        return d_x, d_gain

    def back_feed(self, y):
        total = dot_back(self.d_gate[:, 0:1024], self.g_gu[0, y].reshape(256, 1024)) + dot_back(
            self.d_gate[:, 1024:2048], self.g_gu[1, y].reshape(256, 1024)
        )
        self.d_wide[:, tile(y, 256)] = total[0:128]
        self.back_part[:, tile(y, 256)] = total[128:256].astype(LOW)

    def back_residual(self):
        grad = self.d_wide[:, 0:1024] + self.back_got[...].astype(WIDE)
        d_x, d_gain = self.norm_back(
            grad, self.residual[...], self.inverse_ff[...], self.gains[1:2, :]
        )
        self.vectors[1:2, 0:1024] = d_gain
        d_residual = self.cotangent[...].astype(WIDE) + d_x
        self.d_residual[...] = d_residual
        self.d_branch[...] = d_residual.astype(LOW)

    def back_branch(self):
        def body(y):
            self.d_wide[:, tile(y, 512)] = dot_back(
                self.d_branch[:, 0:512], self.g_out[0, y].reshape(512, 512)
            ) + dot_back(self.d_branch[:, 512:1024], self.g_out[1, y].reshape(512, 512))

        each(4, body)

    def back_gated(self):
        inverse = self.inverse_state[...]
        mean = jnp.zeros((TOK, 1), WIDE)
        for i in range(12):
            at = slice(128 * i, 128 * i + 128)
            gate = self.proj[:, 768 + 128 * i : 896 + 128 * i]
            gated = self.central[:, at] * (gate * sigmoid(gate))
            grad = self.d_wide[:, 512 + 128 * i : 640 + 128 * i]
            turned = gated * inverse
            self.vectors[7:8, at] = jnp.sum(grad * turned, axis=0, keepdims=True)
            mean = mean + jnp.sum(grad * self.scale[0:1, at] * turned, axis=-1, keepdims=True)
        mean = mean * (1.0 / MIXER_FEATURES)
        for i in range(12):
            at = slice(128 * i, 128 * i + 128)
            gate = self.proj[:, 768 + 128 * i : 896 + 128 * i]
            share = sigmoid(gate)
            open_gate = gate * share
            central = self.central[:, at]
            grad = self.d_wide[:, 512 + 128 * i : 640 + 128 * i]
            d_gated = inverse * (
                grad * self.scale[0:1, at] - central * open_gate * inverse * mean
            )
            d_central = d_gated * open_gate
            self.d_proj[:, 768 + 128 * i : 896 + 128 * i] = (
                d_gated * central * (share * (1.0 + gate * (1.0 - share)))
            ).astype(LOW)
            self.d_state[:, at] = d_central.astype(LOW)
            self.d_active[:, at] = d_central * self.skip[0:1, at]
            self.skip_sum[0:1, at] = jnp.sum(
                d_central * self.active[:, at], axis=0, keepdims=True
            )

    def back_mix(self, low, high):
        inner = self.inner[...]
        lane = lanes((TOK, TOK))
        zero = jnp.zeros((TOK, TOK), WIDE)
        d_inner, d_cum = (zero, zero) if low == 0 else (self.d_inner[...], self.d_cum[...])
        if low == 0:
            self.flow_rows[...] = zero
            self.d_step_rows[...] = zero
        for i in range(low, high):
            at = slice(128 * i, 128 * i + 128)
            stacked = pair_stack(self.d_state[:, at])
            d_mixing = dot_back(stacked, self.active[:, at].astype(LOW))
            self.d_active[:, at] += dot_over_rows(self.mixing[i], stacked)
            for which, head in enumerate((2 * i, 2 * i + 1)):
                grad = d_mixing[TOK * which : TOK * which + TOK]
                decay = self.decay(head)
                step = self.step_rows[head : head + 1, :]
                faded = grad * decay
                d_inner = d_inner + faded * step
                part = faded * inner
                d_step = jnp.sum(part, axis=0, keepdims=True)
                self.d_step_rows[head : head + 1, :] = d_step
                self.flow_rows[head : head + 1, :] = d_step * step
                over = jnp.sum(part * step, axis=-1, keepdims=True)
                d_cum = jnp.where(lane == head, over, d_cum)
        self.d_inner[...] = d_inner
        self.d_cum[...] = d_cum

    def back_steps(self):
        lane = lanes((TOK, TOK))
        d_inner = self.d_inner[...].astype(LOW)
        self.d_active[:, 1664:1792] = dot(d_inner, self.active[:, 1536:1664].astype(LOW))
        self.d_active[:, 1536:1664] = dot_over_rows(d_inner, self.active[:, 1664:1792].astype(LOW))
        d_cum = self.d_cum[...] - jnp.transpose(self.flow_rows[...])
        upper = jnp.where(rows_of((TOK, TOK)) <= lanes((TOK, TOK)), 1.0, 0.0)
        d_rated = exact_dot(upper, d_cum)
        rate = -jnp.exp(self.heads[0:1, :])
        d_step = jnp.transpose(self.d_step_rows[...]) + d_rated * rate
        self.vectors[7:8, 1536:1664] = (
            jnp.sum(d_rated * self.step[...], axis=0, keepdims=True) * rate
        )
        raw = self.step_raw[...] + self.heads[1:2, :]
        d_raw = jnp.where(lane < MIXER_HEADS, d_step * sigmoid(raw), 0.0)
        self.vectors[7:8, 1664:1792] = jnp.sum(d_raw, axis=0, keepdims=True)
        self.right_dt[0:128, :] = d_raw.astype(LOW)
        hot = jnp.where(
            lax.div(rows_of((1536, 128)), MIXER_HEAD_SIZE) == lanes((1536, 128)), 1.0, 0.0
        )
        self.vectors[0:1, 1024:1152] = exact_dot(self.skip_sum[...], hot)[0:1]

    def back_attend(self):
        d_keys, d_values = [], []
        for i in range(4):
            at = slice(128 * i, 128 * i + 128)
            which = i // 2
            d_out = pair_stack(self.d_wide[:, at].astype(LOW))
            d_probs = dot_back(d_out, self.values[which])
            probs = self.small_wide[tile(i, 256), :]
            d_scores = probs * (d_probs - jnp.sum(probs * d_probs, axis=-1, keepdims=True))
            d_raw = (d_scores * (1.0 / math.sqrt(HD))).astype(LOW)
            self.unturn(i, pair_join(dot(d_raw, self.keys[which])))
            d_keys.append(dot_over_rows(d_raw, pair_stack(self.turned[:, at])))
            d_values.append(dot_over_rows(probs.astype(LOW), d_out))
        first = lanes((TOK, 128)) < HD

        def joined(parts):
            one, two = parts[0] + parts[1], parts[2] + parts[3]
            return jnp.where(first, one + pltpu.roll(one, HD, 1), two + pltpu.roll(two, HD, 1))

        self.unturn(4, joined(d_keys))
        self.d_proj[:, 640:768] = joined(d_values).astype(LOW)

    def unturn(self, i, grad):
        self.d_proj[:, 128 * i : 128 * i + 128] = (
            grad * self.cosines[...] - swap_halves(grad) * self.sines[...]
        ).astype(LOW)

    def back_activate(self):
        row = rows_of((TOK, 128))
        for i in range(14):
            at = slice(128 * i, 128 * i + 128)
            shifted, total = self.convolved(i)
            share = sigmoid(total)
            grad = self.d_active[:, at] * (share * (1.0 + total * (1.0 - share)))
            self.vectors[6:7, at] = jnp.sum(grad, axis=0, keepdims=True)
            d_in = self.taps[3:4, at] * grad
            for k in range(CONVK):
                self.vectors[5 - k : 6 - k, at] = jnp.sum(grad * shifted[k], axis=0, keepdims=True)
                if k:
                    later = jnp.where(row < TOK - k, pltpu.roll(grad, TOK - k, 0), 0.0)
                    d_in = d_in + self.taps[3 - k : 4 - k, at] * later
            self.d_proj[:, 2304 + 128 * i : 2432 + 128 * i] = d_in.astype(LOW)

    def back_project(self, low, high):
        small = self.g_small[...].reshape(1024, 128)
        for y in range(low, high):
            total = dot_back(self.right_dt[0:128, :], small[256 * y : 256 * y + 256])
            for half in range(2):
                at = tile(half, 1024)
                total = total + dot_back(self.d_proj[:, at], self.g_ina[half, y].reshape(256, 1024))
                at = tile(2 + half, 1024)
                total = total + dot_back(self.d_proj[:, at], self.g_inb[half, y].reshape(256, 1024))
            self.d_wide[:, tile(y, 256)] = total

    def back_input(self):
        d_x, d_gain = self.norm_back(
            self.d_wide[:, 0:1024],
            self.tokens[...].astype(WIDE),
            self.inverse_in[...],
            self.gains[0:1, :],
        )
        self.vectors[0:1, 0:1024] = d_gain
        self.input_grad[...] = (self.d_residual[...] + d_x).astype(LOW)


    def grad_wide(self, left, right, into):
        width = right.shape[1]
        size = min(width, 512)
        for n in range(width // size):
            for y in range(4):
                block = dot(left[tile(y, 256), :], right[:, tile(n, size)])
                into[y, :, :, :, tile(n, size)] = block.astype(LOW).reshape(4, 4, 16, size)

    def grad_tall(self, left, right, into):
        for y in range(into.shape[0]):
            block = dot(left[tile(y, 512), :], right[...])
            into[y] = block.astype(LOW).reshape(4, 4, 32, 512)


class Swap:
    def __init__(self, place, layer, send_sem, recv_sem):
        self.place, self.layer = place, layer
        self.send_sem, self.recv_sem = send_sem, recv_sem
        self.lefts = (
            None, layer.left_in, None, layer.left_out, layer.left_gu, layer.left_down,
        )
        self.rights = (
            layer.right_dt, layer.right_ina, layer.right_inb, layer.right_out, layer.right_gu,
            layer.right_down,
        )
        self.sources = (
            None, layer.d_proj, layer.d_proj, layer.d_branch, layer.d_gate, layer.both_cotangent,
        )

    def left_copy(self, name):
        ref = self.lefts[name]
        size = ref.shape[1] // 2
        src, dst = ref.at[:, pl.ds(0, size)], ref.at[:, pl.ds(size, size)]
        return push(
            src, dst, self.send_sem.at[name], self.recv_sem.at[name], self.place.sibling
        )

    def right_copy(self, name):
        ref, source = self.rights[name], self.sources[name]
        size = ref.shape[0] // 2
        if source is None:
            src = ref.at[pl.ds(0, size), :]
        else:
            src = source.at[:, half_columns(name, 1 - self.place.core)]
        slot = 6 + name
        return push(
            src,
            ref.at[pl.ds(size, size), :],
            self.send_sem.at[slot],
            self.recv_sem.at[slot],
            self.place.sibling,
        )

    def start_left(self, name):
        self.left_copy(name).start()

    def start_left_rows(self, q):
        ref, rows = self.lefts[DOWN], tile(q, 512)
        push(
            ref.at[rows, pl.ds(0, 256)],
            ref.at[rows, pl.ds(256, 256)],
            self.send_sem.at[DOWN],
            self.recv_sem.at[DOWN],
            self.place.sibling,
        ).start()

    def start_right(self, name):
        ref, source = self.rights[name], self.sources[name]
        if source is not None:
            size = ref.shape[0] // 2
            ref[0:size, :] = source[:, half_columns(name, self.place.core)]
        self.right_copy(name).start()

    def arrived(self, name):
        if self.lefts[name] is not None:
            self.left_copy(name).wait_recv()
        self.right_copy(name).wait_recv()

    def finish(self):
        for name in WEIGHTS:
            self.right_copy(name).wait_send()
            if self.lefts[name] is not None:
                self.left_copy(name).wait_send()


INS = dict(
    tokens=0, cotangent=1, in_shard=2, out_shard=3, gu_shard=4, down_shard=5, norm_gains=6,
    conv_params=7, mixer_scale=8, decay_log=9, step_bias=10, mixer_skip=11,
)
OUTS = dict(
    layer_output=((TOK, 1024), LOW),
    input_grad=((TOK, 1024), LOW),
    grad_in=((8, 4120), WIDE),
    grad_out=((16, 1024), WIDE),
    grad_gu=((8, 4096), WIDE),
    grad_down=((16, 1024), WIDE),
    total=((8, 1792), WIDE),
)
SCRATCH = dict(
    g_small=((4, 4, 4, 16, 128), LOW),
    g_ina=((2, 4, 4, 4, 16, 1024), LOW),
    g_inb=((2, 4, 4, 4, 16, 1024), LOW),
    g_out=((2, 4, 4, 4, 32, 512), LOW),
    g_gu=((2, 4, 4, 4, 16, 1024), LOW),
    g_down=((2, 2, 4, 4, 32, 512), LOW),
    low_small=((4, 4, 4, 16, 128), LOW),
    low_gu=((4, 4, 4, 16, 1024), LOW),
    low_down=((2, 4, 4, 32, 512), LOW),
    small_shard=((8, 128), WIDE),
    heads=((8, 128), WIDE),
    skip=((8, 1536), WIDE),
    cosines=((TOK, 128), WIDE),
    sines=((TOK, 128), WIDE),
    pack=((16, 4224), LOW),
    got=((16, 4224), LOW),
    stage=((16, 1024), LOW),
    small_wide=((1024, 128), WIDE),
    gains=((8, 1024), WIDE),
    taps=((8, 1792), WIDE),
    scale=((8, 1536), WIDE),
    normed=((TOK, 1024), LOW),
    inverse_in=((TOK, 1), WIDE),
    proj=((TOK, 4096), WIDE),
    step_raw=((TOK, 128), WIDE),
    active=((TOK, 1792), WIDE),
    step=((TOK, TOK), WIDE),
    cum=((TOK, TOK), WIDE),
    step_rows=((TOK, TOK), WIDE),
    cum_rows=((TOK, TOK), WIDE),
    turned=((TOK, 640), LOW),
    keys=((2, TOK, 128), LOW),
    values=((2, TOK, 128), LOW),
    mixed=((TOK, 2048), LOW),
    inner=((TOK, TOK), WIDE),
    mixing=((12, 256, TOK), LOW),
    central=((TOK, 1536), WIDE),
    inverse_state=((TOK, 1), WIDE),
    residual=((TOK, 1024), WIDE),
    d_residual=((TOK, 1024), WIDE),
    inverse_ff=((TOK, 1), WIDE),
    both_normed=((256, 1024), LOW),
    both_cotangent=((256, 1024), LOW),
    gate_up=((256, 2048), WIDE),
    hidden=((256, 1024), LOW),
    down_own=((TOK, 1024), WIDE),
    down_part=((TOK, 1024), LOW),
    down_got=((TOK, 1024), LOW),
    back_part=((TOK, 1024), LOW),
    back_got=((TOK, 1024), LOW),
    gu_sum=((2, 16, 1024), WIDE),
    gu_got=((16, 1024), WIDE),
    d_gate=((256, 2048), LOW),
    d_branch=((TOK, 1024), LOW),
    d_state=((TOK, 1536), LOW),
    d_proj=((TOK, 4096), LOW),
    skip_sum=((8, 1536), WIDE),
    d_inner=((TOK, TOK), WIDE),
    d_cum=((TOK, TOK), WIDE),
    flow_rows=((TOK, TOK), WIDE),
    d_step_rows=((TOK, TOK), WIDE),
    vectors=((8, 1792), WIDE),
    left_in=((1024, 256), LOW),
    left_out=((2048, 256), LOW),
    left_gu=((1024, 512), LOW),
    left_down=((1024, 512), LOW),
    right_ina=((256, 1024), LOW),
    right_inb=((256, 1024), LOW),
    right_out=((256, 512), LOW),
    right_gu=((512, 1024), LOW),
    right_down=((512, 512), LOW),
    right_dt=((256, 128), LOW),
    sums=((5, 4, 8, 896), WIDE),
)
BLOCKS = tuple((ROWS[name], COLS[name]) for name in WEIGHTS)
LANDINGS = tuple((3, DEPTH[name], 4) for name in WEIGHTS)
LANDINGS += tuple((3, DEPTH[name]) for name in WEIGHTS)
LANDINGS += tuple({GU: (1, 2), DOWN: (1,)}.get(name, (3,)) for name in WEIGHTS)
ENDS = tuple((ROWS[name], 2048 if name == GU else COLS[name]) for name in WEIGHTS[1:])
SEMS = dict(
    enter=(4, 4), gather=(24, 54), scatter=(18, 30), sums=(5, 5), end=(5, 5), swap=(12, 12), mate=(5, 5),
)


class Plan:
    def __init__(self, refs):
        names = [*INS, *OUTS, *SCRATCH]
        layer = Layer(dict(zip(names, refs)))
        rest = list(refs[len(names) :])
        landings = [[rest.pop(0) for _ in WEIGHTS] for _ in range(3)]
        ends = [None] + [rest.pop(0) for _ in WEIGHTS[1:]]
        ends_got = [None] + [rest.pop(0) for _ in WEIGHTS[1:]]
        sems = {name: (rest.pop(0), rest.pop(0)) for name in SEMS}
        layer.d_wide = layer.gate_up.at[pl.ds(0, 128), :]
        layer.d_active = layer.gate_up.at[pl.ds(128, 128), pl.ds(0, 1792)]
        place = Place()
        arrays = (layer.g_small, layer.g_ina, layer.g_inb, layer.g_out, layer.g_gu, layer.g_down)
        shards = (
            layer.small_shard, layer.in_shard, layer.in_shard, layer.out_shard, layer.gu_shard,
            layer.down_shard,
        )
        grads = (
            layer.low_small, layer.g_gu.at[0], layer.g_gu.at[1], layer.g_out.at[0], layer.low_gu,
            layer.low_down,
        )
        outs = (
            None, layer.grad_in, layer.grad_in, layer.grad_out, layer.grad_gu, layer.grad_down,
        )
        self.place, self.layer, self.grads = place, layer, grads
        self.gather = Gather(place, arrays, *sems["gather"])
        self.enter = Enter(
            place, self.gather, layer.pack, layer.got, layer.stage, shards, sems["enter"]
        )
        self.scatter = Scatter(place, grads, *landings, *sems["scatter"])
        self.sum_all = SumAll(place, layer.sums, *sems["sums"])
        self.end = End(place, ends, ends_got, outs, *sems["end"])
        self.swap = Swap(place, layer, *sems["swap"])
        self.mate = Mate(place, layer, *sems["mate"])

    def last(self, name):
        self.scatter.arrived(name, 2)
        for part, (low, high) in enumerate(PARTS[name]):
            value = self.scatter.add(name, part, 2)
            if name == SMALL:
                mine = jnp.where(self.place.core == 0, value[0:8], value[8:16])
                self.layer.grad_in[:, 4096:4120] = mine[:, 0:24]
            elif name == GU:
                self.layer.gu_sum[:, :, low:high] = value
            else:
                self.end.ends[name][:, low:high] = value
        if name == GU:
            self.mate.start(Mate.GRAD)
        elif name != SMALL:
            self.end.start(name)

    def last_gu(self):
        self.mate.arrived(Mate.GRAD)
        layer, parity, into = self.layer, self.place.parity, self.end.ends[GU]
        for which, value in ((parity, layer.gu_sum[parity]), (1 - parity, layer.gu_got[...])):
            for q in range(2):
                at = pl.ds(pl.multiple_of(1024 * q + 512 * which, 512), 512)
                into[:, at] = value[:, 512 * q : 512 * q + 512]
        self.end.start(GU)


def layer_kernel(*refs):
    plan = Plan(refs)
    place, layer, grads, gather = plan.place, plan.layer, plan.grads, plan.gather
    enter, scatter, sum_all, end, swap = (
        plan.enter, plan.scatter, plan.sum_all, plan.end, plan.swap,
    )
    mate, core = plan.mate, place.core

    def onward(name, phase):
        gather.arrived(name, phase, 0 if gather.direct(name, phase) else 2)
        if phase == 0 or name == SMALL:
            gather.start(name, phase + 1)
        else:
            gather.start_early(name)

    def onward_late(name):
        gather.start_late(name)
        gather.pass_on(name, 0)

    def landed(name):
        gather.arrived(name, 2, 2)
        gather.pass_on(name, 2)

    arrive(place)
    layer.enter()
    enter.run(lambda: meet(place), lambda name: gather.start(name, 0))
    gather.start(SMALL, 0)
    gather.start(OUT, 0)
    gather.start(DOWN, 0)
    layer.tables()
    enter.mate_copy().wait_recv()
    gather.start(GU, 0)
    onward(SMALL, 0)
    onward(INB, 0)
    onward(OUT, 0)
    onward(INA, 0)
    onward(DOWN, 0)
    onward(GU, 0)
    onward(SMALL, 1)
    gather.hand_on(INB, 1, (0,))
    gather.hand_on(INB, 1, (1,))
    gather.hand_on(OUT, 1, (0,))
    gather.hand_on(OUT, 1, (1,))
    gather.hand_on(DOWN, 1, (0,))
    gather.hand_on(DOWN, 1, (1,))
    onward(INA, 1)
    onward_late(INA)
    gather.hand_on(GU, 1, (0,))
    gather.hand_on(GU, 1, (1,))
    onward(INB, 1)
    onward_late(INB)
    gather.share_small()
    gather.hand_on(INA, 2, (0,))
    gather.hand_on(INA, 2, (1,))
    gather.arrived_late(INA, (0,))
    gather.shared_small()
    layer.spread()
    layer.norm_in()
    swap.start_left(INA)
    layer.project_steps()
    onward(OUT, 1)
    onward_late(OUT)
    gather.arrived_late(INA, (1,))
    gather.hand_on(INB, 2, (0,))
    gather.hand_on(INB, 2, (1,))
    gather.arrived_late(INB, (0,))
    gather.arrived_late(INB, (1,))
    onward(DOWN, 1)
    landed(INA)
    layer.project(layer.g_ina, 0, core)
    gather.hand_on(OUT, 2, (0,))
    gather.hand_on(OUT, 2, (1,))
    onward(GU, 1)
    onward_late(GU)
    gather.passed(INA)
    layer.project(layer.g_ina, 0, 1 - core)
    layer.attend()
    gather.arrived_late(OUT, (0,))
    gather.arrived_late(OUT, (1,))
    layer.both_cotangent[0:128, :] = layer.cotangent[...]
    mate.start(Mate.COTANGENT)
    landed(INB)
    layer.project(layer.g_inb, 2048, core)
    gather.hand_on(DOWN, 2, (0,))
    gather.hand_on(DOWN, 2, (1,))
    gather.passed(INB)
    layer.project(layer.g_inb, 2048, 1 - core)
    layer.activate()
    layer.steps()
    landed(OUT)
    layer.mix(0, 6)
    layer.mix(6, 12)
    layer.mix_norm()
    layer.branch_half(core)
    gather.hand_on(GU, 2, (1,))
    gather.passed(OUT)
    layer.branch_half(1 - core)
    layer.branch()
    mate.start(Mate.NORMED)
    layer.turn_left(layer.mixed, layer.left_out, 16)
    swap.start_left(OUT)
    gather.hand_on(GU, 2, (0,))
    onward_late(DOWN)
    mate.arrived(Mate.COTANGENT)
    swap.start_right(DOWN)
    gather.arrived_late(GU, (1,))
    gather.arrived_late(GU, (0,))
    landed(GU)
    gather.arrived_late(DOWN, (0,))
    gather.arrived_late(DOWN, (1,))
    landed(DOWN)
    mate.arrived(Mate.NORMED)
    layer.turn_other()
    swap.start_left(GU)
    layer.feed_half(core)
    gather.passed(GU)
    layer.feed_half(1 - core)
    layer.feed(swap.start_left_rows)
    gather.passed(DOWN)
    layer.back_down()
    swap.start_right(GU)
    layer.back_feed(0)
    mate.start_columns(0)
    layer.back_feed(1)
    mate.start_columns(1)
    swap.arrived(DOWN)
    layer.grad_tall(layer.left_down, layer.right_down, grads[DOWN])
    scatter.start(DOWN, 0)
    layer.back_feed(2)
    mate.start_columns(2)
    layer.back_feed(3)
    mate.start_columns(3)
    swap.arrived(GU)
    layer.grad_wide(layer.left_gu, layer.right_gu, grads[GU])
    scatter.start(GU, 0)
    layer.down()
    mate.start(Mate.DOWN_PART)
    scatter.hand_on(DOWN, 0)
    mate.arrived(Mate.BACK_PART)
    layer.back_residual()
    swap.start_right(OUT)
    layer.back_branch()
    scatter.hand_on(GU, 0)
    gather.finish(OUT)
    swap.arrived(OUT)
    layer.grad_tall(layer.left_out, layer.right_out, grads[OUT])
    scatter.start(OUT, 0)
    layer.back_gated()
    layer.back_attend()
    swap.start_right(INA)
    layer.back_mix(0, 6)
    scatter.relay(DOWN, 0)
    layer.back_mix(6, 12)
    gather.finish(GU)
    swap.arrived(INA)
    layer.grad_wide(layer.left_in, layer.right_ina, grads[INA])
    scatter.start(INA, 0)
    scatter.relay(GU, 0)
    scatter.hand_on(OUT, 0)
    layer.back_steps()
    swap.start_right(SMALL)
    scatter.hand_on(DOWN, 1)
    layer.back_activate()
    swap.start_right(INB)
    mate.arrived(Mate.DOWN_PART)
    layer.down_sum()
    swap.arrived(SMALL)
    layer.grad_wide(layer.left_in, layer.right_dt, grads[SMALL])
    scatter.start(SMALL, 0)
    swap.arrived(INB)
    layer.grad_wide(layer.left_in, layer.right_inb, grads[INB])
    scatter.start(INB, 0)
    layer.back_project(0, 2)
    layer.back_project(2, 4)
    layer.back_input()
    sum_all.begin(layer.vectors)
    scatter.hand_on(GU, 1)
    scatter.hand_on(INA, 0)
    scatter.relay(OUT, 0)
    sum_all.start(1, sum_all.total(0))
    scatter.relay(DOWN, 1)
    scatter.relay(SMALL, 0)
    scatter.hand_on(INB, 0)
    scatter.relay(GU, 1)
    scatter.relay(INA, 0)
    scatter.hand_on(OUT, 1)
    sum_all.start(2, sum_all.total(1))
    plan.last(DOWN)
    scatter.relay(SMALL, 1)
    end.take(DOWN)
    scatter.relay(INB, 0)
    scatter.hand_on(INA, 1)
    plan.last(GU)
    scatter.relay(OUT, 1)
    sum_all.start(3, sum_all.total(2))
    plan.last(SMALL)
    scatter.relay(INA, 1)
    plan.last_gu()
    scatter.relay(INB, 1)
    plan.last(OUT)
    end.take(GU)
    end.take(OUT)
    sum_all.start(4, sum_all.total(3))
    plan.last(INA)
    plan.last(INB)
    end.take(INA)
    end.take(INB)
    sum_all.into(layer.total)
    for name in (SMALL, INA, INB, DOWN):
        gather.finish(name)
    scatter.finish()
    sum_all.finish()
    end.finish()
    swap.finish()
    mate.finish()
    enter.finish()


def finish_kernel(*refs):
    ins, outs = refs[:7], refs[7:]
    for ref, into in zip(ins[:6], outs[:6]):
        into[...] = ref[...]
    me = lax.axis_index("fsdp")
    total = ins[6][...]
    column = lanes((8, 1792))

    def share(size):
        start = me * size
        picked = jnp.where((column >= start) & (column < start + size), total, 0.0)
        folded = picked[:, 0:128]
        for i in range(1, 14):
            folded = folded + picked[:, 128 * i : 128 * i + 128]
        return pltpu.roll(folded, lax.rem(1792 - start, 128), 1)

    outs[6][...] = share(8)[0:2, 0:8]
    outs[7][...] = share(14)[2:7, 0:14]
    outs[8][...] = share(12)[7:8, 0:12]
    outs[9][...] = total[7:8, 1536:1560]
    outs[10][...] = total[7:8, 1664:1688]
    outs[11][...] = total[0:1, 1024:1048]


def local(
    tokens, cotangent, input_weight, output_weight, gate_up_weight, down_weight,
    norm_gains, conv_params, mixer_scale, decay_log, step_bias, mixer_skip_factor,
):
    ins = (
        tokens, cotangent, input_weight, output_weight, gate_up_weight, down_weight, norm_gains,
        conv_params, mixer_scale, decay_log[None], step_bias[None], mixer_skip_factor[None],
    )
    scratch = [pltpu.VMEM(*one) for one in SCRATCH.values()]
    scratch += [pltpu.VMEM(lead + block, LOW) for lead, block in zip(LANDINGS, BLOCKS * 3)]
    scratch += [pltpu.VMEM(block, WIDE) for block in ENDS]
    scratch += [pltpu.VMEM((block[0] // 2, block[1]), WIDE) for block in ENDS]
    scratch += [pltpu.SemaphoreType.DMA((n,)) for counts in SEMS.values() for n in counts]
    whole = pl.BlockSpec(memory_space=pltpu.VMEM)
    results = pl.pallas_call(
        layer_kernel,
        out_shape=[jax.ShapeDtypeStruct(*one) for one in OUTS.values()],
        in_specs=[whole] * len(INS),
        out_specs=[whole] * len(OUTS),
        scratch_shapes=scratch,
        compiler_params=pltpu.CompilerParams(
            collective_id=0, has_side_effects=True, vmem_limit_bytes=127 * 2**19
        ),
        name="layer",
    )(*ins)
    shares = [(2, 8), (5, 14), (1, 12), (1, 24), (1, 24), (1, 24)]
    final = pl.pallas_call(
        finish_kernel,
        out_shape=[jax.ShapeDtypeStruct(*one) for one in list(OUTS.values())[:6]]
        + [jax.ShapeDtypeStruct(one, WIDE) for one in shares],
        in_specs=[whole] * len(OUTS),
        out_specs=[whole] * 12,
        name="finish",
    )(*results)
    return (*final[:9], *(one[0] for one in final[9:]))


def solution(mesh):
    in_specs = (
        P("fsdp", None),
        P("fsdp", None),
        P("fsdp", None),
        P("fsdp", None),
        P("fsdp", None),
        P("fsdp", None),
        P(None, "fsdp"),
        P(None, "fsdp"),
        P(None, "fsdp"),
        P(),
        P(),
        P(),
    )
    out_specs = (
        P("fsdp", None),
        P("fsdp", None),
        P("fsdp", None),
        P("fsdp", None),
        P("fsdp", None),
        P("fsdp", None),
        P(None, "fsdp"),
        P(None, "fsdp"),
        P(None, "fsdp"),
        P(),
        P(),
        P(),
    )
    return jax.shard_map(local, mesh=mesh, in_specs=in_specs, out_specs=out_specs, check_vma=False)
```

```python
import math

import jax
import jax.numpy as jnp
import numpy as np
from jax import lax
from jax.experimental import pallas as pl
from jax.experimental.pallas import tpu as pltpu
from jax.sharding import PartitionSpec as P

HD = 64
MIXER_HEADS = 24
MIXER_HEAD_SIZE = 64
CONVK = 4
MIXER_FEATURES = 1536
TOK = 128
norm_eps = 1e-05
rope_base = 10000.0
masked_value = -1e30

Y, X, Z = range(3)
AXES = (Y, X, Z)
STEPS = (1, 3, 2)
SMALL, INA, INB, OUT, GU, DOWN = range(6)
WEIGHTS = (SMALL, INA, INB, OUT, GU, DOWN)
PAIRED = (GU, DOWN)
ROWS = (16, 16, 16, 32, 16, 32)
COLS = (128, 1024, 1024, 512, 1024, 512)
FIRST = (0, 0, 2048, 0, 0, 0)
DEPTH = (4, 4, 4, 4, 4, 2)
ORDERS = ((X, Y, Z), (Y, Z, X), (Z, X, Y))
PAIR_ORDERS = ((Y, X, Z), (Y, Z, X))
PARTS = (
    ((0, 128),),
    ((0, 256), (256, 640), (640, 1024)),
    ((0, 384), (384, 768), (768, 1024)),
    ((0, 128), (128, 256), (256, 512)),
    ((0, 512), (512, 1024)),
    ((0, 256), (256, 512)),
)
DIRECT = {SMALL: 3, INA: 2}
BACK_DIRECT = {SMALL: 0, INB: 1}


def order_of(name, part):
    return (PAIR_ORDERS if name in PAIRED else ORDERS)[part]


def extent(name, axis):
    return DEPTH[name] if axis == Y else 4


def steps_of(name, axis):
    return (2,) if name in PAIRED and axis == Y else STEPS


def half_columns(name, core):
    return pl.ds(pl.multiple_of(FIRST[name] + core * COLS[name], 512), COLS[name])


class Place:
    def __init__(self):
        me = lax.axis_index("fsdp")
        self.me = me
        self.core = lax.rem(me, 2)
        self.at = [lax.div(me, 32), lax.rem(lax.div(me, 8), 4), lax.rem(lax.div(me, 2), 4)]
        self.sibling = me + 1 - 2 * self.core
        self.parity = lax.rem(self.at[Y], 2)
        self.pair = lax.div(self.at[Y], 2)
        self.mate = me + 32 - 64 * self.parity

    def moved(self, axis, step):
        return lax.rem(self.at[axis] + step, 4)

    def spot(self, name, axis, step):
        if name in PAIRED and axis == Y:
            pair = lax.rem(self.pair + step // 2, 2)
            return pl.ds(2 * pair, 2) if name == GU else pair
        return self.moved(axis, step)

    def peer(self, axis, step):
        at = list(self.at)
        at[axis] = self.moved(axis, step)
        return ((at[Y] * 4 + at[X]) * 4 + at[Z]) * 2 + self.core

    def partners(self):
        return [self.sibling] + [self.peer(axis, step) for axis in AXES for step in STEPS]


def arrive(place):
    for partner in place.partners():
        pl.semaphore_signal(
            pltpu.get_barrier_semaphore(),
            inc=1,
            device_id=(partner,),
            device_id_type=pl.DeviceIdType.MESH,
        )


def meet(place):
    pl.semaphore_wait(pltpu.get_barrier_semaphore(), len(place.partners()))


def push(src, dst, send_sem, recv_sem, device):
    return pltpu.make_async_remote_copy(
        src_ref=src,
        dst_ref=dst,
        send_sem=send_sem,
        recv_sem=recv_sem,
        device_id=(device,),
        device_id_type=pl.DeviceIdType.MESH,
    )


def block_index(where, low, high):
    return tuple(where.get(axis, slice(None)) for axis in AXES) + (
        slice(None),
        pl.ds(low, high - low),
    )


def expect(ref, count, sem, place):
    sizes = [
        (i, j, k)
        for i in range(1, ref.shape[0] + 1)
        for j in range(1, 5)
        for k in range(1, 5)
        if i * j * k == count
    ][0]
    view = ref.at[tuple(pl.ds(0, size) for size in sizes)]
    return push(view, view, sem, sem, place.sibling)


def halved(name, axes, half):
    axis = min(axes)
    size = extent(name, axis) // 2
    return {axis: pl.ds(size * half, size)}


def slab_blocks(name, axes, axis):
    count = 2 if name == GU and axis == Y else 1
    for one in axes:
        count *= extent(name, one)
    return count


class Gather:
    def __init__(self, place, arrays, send_sem, recv_sem):
        self.place, self.arrays = place, arrays
        self.send_sem, self.recv_sem = send_sem, recv_sem

    def ref(self, name):
        if name == SMALL:
            return self.arrays[name]
        return self.arrays[name].at[self.place.core]

    def direct(self, name, phase):
        return phase < DIRECT.get(name, 1)

    def blocks(self, name, phase):
        order = order_of(name, 0)
        if name == SMALL and phase == 2:
            return 8
        return slab_blocks(name, order[:phase], order[phase])

    def send_slot(self, name, phase):
        return self.send_sem.at[4 * name + phase]

    def recv_slot(self, name, phase, kind):
        if self.direct(name, phase):
            kind = 0
        elif kind > 1:
            kind = 2
        if name == SMALL:
            return self.recv_sem.at[phase]
        return self.recv_sem.at[10 * name - 7 + (0, 1, 4)[phase] + kind]

    def slab(self, name, part, phase, step, half=None):
        order = order_of(name, part)
        where = {axis: self.place.spot(name, axis, 0) for axis in order[phase:]}
        where[order[phase]] = self.place.spot(name, order[phase], step)
        if half is not None:
            where |= halved(name, order[:phase], half)
        if name == SMALL and phase == 2:
            where[X] = pl.ds(2 * self.place.core, 2)
        return self.ref(name).at[block_index(where, *PARTS[name][part])]

    def copy(self, name, part, phase, kind, half=None, slot=None):
        axis = order_of(name, part)[phase]
        step, source, handed = (
            [(one, 0, None) for one in steps_of(name, axis)]
            if self.direct(name, phase)
            else ((1, 0, None), (3, 0, None), (1, 3, 0), (3, 1, 1))
        )[kind]
        view = self.slab(name, part, phase, source, handed if half is None else half)
        return push(
            view,
            view,
            self.send_slot(name, phase),
            self.recv_slot(name, phase, kind) if slot is None else slot,
            self.place.peer(axis, step),
        )

    def start(self, name, phase, kinds=(0, 1)):
        if self.direct(name, phase):
            kinds = range(len(steps_of(name, order_of(name, 0)[phase])))
        for kind in kinds:
            for part in range(len(PARTS[name])):
                self.copy(name, part, phase, kind).start()

    def late_slot(self, name, kind):
        return self.recv_sem.at[10 * name + kind]

    def start_early(self, name):
        for kind in (0, 1):
            for part in range(len(PARTS[name])):
                self.copy(name, part, 2, kind, kind).start()

    def start_late(self, name):
        for kind in (0, 1):
            slot = self.late_slot(name, kind)
            for part in range(len(PARTS[name])):
                self.copy(name, part, 2, kind, 1 - kind, slot).start()

    def arrived(self, name, phase, kind=0):
        count = self.blocks(name, phase)
        if self.direct(name, phase):
            count *= len(steps_of(name, order_of(name, 0)[phase]))
        elif phase == 2 and kind < 2:
            count //= 2
        slot = self.recv_slot(name, phase, kind)
        expect(self.ref(name), count, slot, self.place).wait_recv()

    def hand_on(self, name, phase, kinds=(0, 1)):
        for kind in kinds:
            self.arrived(name, phase, kind)
            self.start(name, phase, (kind + 2,))

    def arrived_late(self, name, kinds=(0, 1)):
        for kind in kinds:
            slot = self.late_slot(name, kind)
            expect(self.ref(name), self.blocks(name, 2) // 2, slot, self.place).wait_recv()
            self.pass_on(name, (3, 1)[kind])

    def pass_on(self, name, step):
        for part in range(len(PARTS[name])):
            view = self.slab(name, part, 2, step)
            push(
                view,
                view,
                self.send_slot(name, 3),
                self.recv_sem.at[10 * name + 2],
                self.place.sibling,
            ).start()

    def share_small(self):
        self.arrived(SMALL, 2)
        for step in STEPS:
            view = self.slab(SMALL, 0, 2, step)
            push(
                view, view, self.send_slot(SMALL, 3), self.recv_sem.at[53], self.place.sibling
            ).start()

    def shared_small(self):
        expect(self.ref(SMALL), 24, self.recv_sem.at[53], self.place).wait_recv()

    def passed(self, name):
        count = 16 * DEPTH[name]
        expect(self.ref(name), count, self.recv_sem.at[10 * name + 2], self.place).wait_recv()

    def finish(self, name):
        for phase in range(3):
            count = self.blocks(name, phase)
            if self.direct(name, phase):
                count *= len(steps_of(name, order_of(name, 0)[phase]))
            else:
                count *= 3
            expect(self.ref(name), count, self.send_slot(name, phase), self.place).wait_send()
        slot = self.send_slot(name, 3)
        count = 24 if name == SMALL else 16 * DEPTH[name]
        expect(self.ref(name), count, slot, self.place).wait_send()


def each(count, body):
    for index in range(count):
        body(index)


class Enter:
    COLUMNS = ((INA, 0, 1024), (INB, 1024, 1024), (GU, 2048, 2048), (SMALL, 4096, 128))

    def __init__(self, place, gather, pack, got, stage, shards, sems):
        self.place, self.gather = place, gather
        self.pack, self.got, self.stage, self.shards = pack, got, stage, shards
        self.send_sem, self.recv_sem = sems

    def own(self, name, core):
        at = self.place.at
        first = self.place.pair if name == DOWN else at[Y]
        return self.gather.arrays[name].at[core, first, at[X], at[Z]]

    def copies(self):
        core = self.place.core
        pairs = [(self.pack, self.got)]
        for name in (OUT, DOWN):
            rows = pl.ds(pl.multiple_of(core * 16, 16), 16)
            src = self.shards[name].at[:, half_columns(name, 1 - core)]
            pairs.append((src, self.own(name, 1 - core).at[rows, :]))
        return [
            push(src, dst, self.send_sem.at[i], self.recv_sem.at[i], self.place.sibling)
            for i, (src, dst) in enumerate(pairs)
        ]

    def mate_copy(self):
        return push(
            self.stage,
            self.own(GU, self.place.core),
            self.send_sem.at[3],
            self.recv_sem.at[3],
            self.place.mate,
        )

    def run(self, greet, begin):
        core, at = self.place.core, self.place.at
        wide = jnp.float32
        for name, low, size in self.COLUMNS[:3]:
            first = FIRST[name]
            both = [
                self.shards[name][:, first + size * half : first + size * half + size]
                for half in range(2)
            ]
            both = [one.astype(wide) for one in both]
            self.pack[:, low : low + size] = jnp.concatenate(both, axis=0).astype(jnp.bfloat16)
        small = self.shards[SMALL][...]
        self.pack[:, 4096:4224] = jnp.concatenate([small, small], axis=0).astype(jnp.bfloat16)
        greet()
        copies = self.copies()
        for copy in copies:
            copy.start()
        copies[0].wait_recv()
        for name, low, size in self.COLUMNS:
            mine = self.pack[:, low : low + size].astype(wide)
            other = self.got[:, low : low + size].astype(wide)
            other = jnp.concatenate([other[8:16], other[0:8]], axis=0)
            upper = lax.broadcasted_iota(jnp.int32, (16, size), 0) < 8
            take = upper == (core == 0)
            block = jnp.where(take, mine, other)
            if name == SMALL:
                self.gather.arrays[name][at[Y], at[X], at[Z]] = block.astype(jnp.bfloat16)
            elif name == GU:
                even = jnp.concatenate([block[:, 0:512], block[:, 1024:1536]], axis=1)
                odd = jnp.concatenate([block[:, 512:1024], block[:, 1536:2048]], axis=1)
                first = self.place.parity == 0
                own = jnp.where(first, even, odd).astype(jnp.bfloat16)
                self.own(GU, core)[...] = own
                self.stage[...] = jnp.where(first, odd, even).astype(jnp.bfloat16)
                self.mate_copy().start()
            else:
                self.own(name, core)[...] = block.astype(jnp.bfloat16)
                begin(name)
        for name in (OUT, DOWN):
            rows = pl.ds(pl.multiple_of(core * 16, 16), 16)
            self.own(name, core)[rows, :] = self.shards[name][:, half_columns(name, core)]
        for copy in copies[1:]:
            copy.wait_recv()

    def finish(self):
        for copy in self.copies():
            copy.wait_send()
        self.mate_copy().wait_send()


class Scatter:
    def __init__(self, place, grads, first, second, third, send_sem, recv_sem):
        self.place, self.grads = place, grads
        self.got = (first, second, third)
        self.send_sem, self.recv_sem = send_sem, recv_sem

    def send_slot(self, name, phase):
        return self.send_sem.at[3 * name + phase]

    def recv_slot(self, name, phase, early=False):
        return self.recv_sem.at[5 * name + phase + (3 if early else 0)]

    def direct(self, name, phase):
        return phase >= BACK_DIRECT.get(name, 2)

    def order(self, name, part):
        return order_of(name, part)[::-1]

    def blocks(self, name, phase):
        order = self.order(name, 0)
        return slab_blocks(name, order[phase + 1 :], order[phase])

    def steps(self, name, phase):
        return steps_of(name, self.order(name, 0)[phase])

    def slab(self, name, part, phase, step, half=None):
        order = self.order(name, part)
        where = {axis: self.place.spot(name, axis, 0) for axis in order[:phase]}
        where[order[phase]] = self.place.spot(name, order[phase], step)
        if half is not None:
            where |= halved(name, order[phase + 1 :], half)
        return self.grads[name].at[block_index(where, *PARTS[name][part])]

    def landing(self, name, part, phase, slot, half=None):
        low, high = PARTS[name][part]
        left = self.order(name, part)[phase + 1 :]
        lead = [slice(None)] * len(left)
        if half is not None:
            lead[0] = halved(name, left, half)[min(left)]
        if name == GU and phase == 2:
            lead = [slice(None)]
        return (slot, *lead, slice(None), pl.ds(low, high - low))

    def push(self, name, part, phase, to, source, half, slot, early=False):
        dst = self.got[phase][name].at[self.landing(name, part, phase, slot, half)]
        push(
            self.slab(name, part, phase, source, half),
            dst,
            self.send_slot(name, phase),
            self.recv_slot(name, phase, early),
            self.place.peer(self.order(name, part)[phase], to),
        ).start()

    def start(self, name, phase, parts=None):
        for part in range(len(PARTS[name])) if parts is None else parts:
            if self.direct(name, phase):
                for slot, step in enumerate(self.steps(name, phase)):
                    self.push(name, part, phase, step, step, None, slot)
            else:
                self.push(name, part, phase, 3, 2, 0, 2, True)
                self.push(name, part, phase, 1, 2, 1, 2, True)
                self.push(name, part, phase, 3, 3, 1, 0)
                self.push(name, part, phase, 1, 1, 0, 1)

    def arrived(self, name, phase, early=False):
        count = self.blocks(name, phase)
        if self.direct(name, phase):
            count *= len(self.steps(name, phase))
        elif not early:
            count *= 2
        slot = self.recv_slot(name, phase, early)
        expect(self.grads[name], count, slot, self.place).wait_recv()

    def hand_on(self, name, phase):
        self.arrived(name, phase, True)
        for part in range(len(PARTS[name])):
            for step, half, slot in ((3, 0, 0), (1, 1, 1)):
                own = self.slab(name, part, phase, step, half)
                came = self.got[phase][name].at[self.landing(name, part, phase, 2, half)]

                def body(i):
                    own[i] = (own[i].astype(jnp.float32) + came[i].astype(jnp.float32)).astype(
                        jnp.bfloat16
                    )

                each(own.shape[0], body)
                self.push(name, part, phase, step, step, half, slot)

    def add(self, name, part, phase, pick=()):
        total = self.slab(name, part, phase, 0)[(*pick, Ellipsis)].astype(jnp.float32)
        for slot in range(len(self.steps(name, phase)) if self.direct(name, phase) else 2):
            piece = self.got[phase][name].at[self.landing(name, part, phase, slot)]
            total = total + piece[(*pick, Ellipsis)].astype(jnp.float32)
        return total

    def relay(self, name, phase):
        self.arrived(name, phase)
        for part in range(len(PARTS[name])):
            own = self.slab(name, part, phase, 0)

            def body(i):
                own[i] = self.add(name, part, phase, (i,)).astype(jnp.bfloat16)

            each(own.shape[0], body)
            self.start(name, phase + 1, (part,))

    def finish(self, names, phases):
        for name in names:
            for phase in phases:
                times = len(self.steps(name, phase)) if self.direct(name, phase) else 3
                count = self.blocks(name, phase) * times
                slot = self.send_slot(name, phase)
                expect(self.grads[name], count, slot, self.place).wait_send()


class SumAll:
    def __init__(self, place, got, send_sem, recv_sem):
        self.place, self.got = place, got
        self.send_sem, self.recv_sem = send_sem, recv_sem

    def push(self, src, stage, slot, device):
        dst = self.got.at[stage, slot]
        push(src, dst, self.send_sem.at[stage], self.recv_sem.at[stage], device).start()

    def begin(self, values):
        core, size = self.place.core, self.got.shape[3]
        own = pl.ds(pl.multiple_of(core * size, size), size)
        other = pl.ds(pl.multiple_of((1 - core) * size, size), size)
        self.push(values.at[:, other], 0, core, self.place.sibling)
        self.got[0, core] = values[:, own]

    def start(self, stage, value):
        if stage == 4:
            slot, devices = self.place.core, [self.place.sibling]
        else:
            axis = AXES[stage - 1]
            slot, devices = self.place.at[axis], [self.place.peer(axis, s) for s in STEPS]
        self.got[stage, slot] = value
        for device in devices:
            self.push(self.got.at[stage, slot], stage, slot, device)

    def expect(self, stage):
        view = self.got.at[stage, pl.ds(0, 3 if 0 < stage < 4 else 1)]
        return push(
            view, view, self.send_sem.at[stage], self.recv_sem.at[stage], self.place.sibling
        )

    def total(self, stage):
        self.expect(stage).wait_recv()
        total = self.got[stage, 0]
        for slot in range(1, 4 if stage else 2):
            total = total + self.got[stage, slot]
        return total

    def into(self, ref):
        self.expect(4).wait_recv()
        size = self.got.shape[3]
        for half in range(2):
            ref[:, size * half : size * half + size] = self.got[4, half]

    def finish(self, stages):
        for stage in stages:
            self.expect(stage).wait_send()


class Mate:
    COTANGENT, NORMED, DOWN_PART, BACK_PART, GRAD = range(5)

    def __init__(self, place, layer, send_sem, recv_sem):
        self.place, self.layer = place, layer
        self.send_sem, self.recv_sem = send_sem, recv_sem

    def copy(self, which):
        layer = self.layer
        src, dst = (
            (layer.both_cotangent.at[pl.ds(0, 128)], layer.both_cotangent.at[pl.ds(128, 128)]),
            (layer.both_normed.at[pl.ds(0, 128)], layer.both_normed.at[pl.ds(128, 128)]),
            (layer.down_part, layer.down_got),
            (layer.back_part, layer.back_got),
            (layer.gu_sum.at[1 - self.place.parity], layer.gu_got),
        )[which]
        return push(
            src, dst, self.send_sem.at[which], self.recv_sem.at[which], self.place.mate
        )

    def start(self, which):
        self.copy(which).start()

    def start_columns(self, y):
        at = pl.ds(256 * y, 256)
        push(
            self.layer.back_part.at[:, at],
            self.layer.back_got.at[:, at],
            self.send_sem.at[self.BACK_PART],
            self.recv_sem.at[self.BACK_PART],
            self.place.mate,
        ).start()

    def arrived(self, which):
        self.copy(which).wait_recv()

    def finish(self):
        for which in range(5):
            self.copy(which).wait_send()


class End:
    def __init__(self, place, ends, got, outs, send_sem, recv_sem):
        self.place, self.ends, self.got, self.outs = place, ends, got, outs
        self.send_sem, self.recv_sem = send_sem, recv_sem

    def rows(self, name, core):
        half = ROWS[name] // 2
        return pl.ds(pl.multiple_of(core * half, 8), half)

    def columns(self, name, core):
        if name == GU:
            return pl.ds(pl.multiple_of(core * 2048, 512), 2048)
        return half_columns(name, core)

    def copy(self, name):
        slot = name - 1
        return push(
            self.ends[name].at[self.rows(name, 1 - self.place.core), :],
            self.got[name],
            self.send_sem.at[slot],
            self.recv_sem.at[slot],
            self.place.sibling,
        )

    def start(self, name):
        self.copy(name).start()
        core = self.place.core
        self.outs[name][:, self.columns(name, core)] = self.ends[name][self.rows(name, core), :]

    def take(self, name):
        self.copy(name).wait_recv()
        self.outs[name][:, self.columns(name, 1 - self.place.core)] = self.got[name][...]

    def finish(self):
        for name in WEIGHTS[1:]:
            self.copy(name).wait_send()


LOW, WIDE = jnp.bfloat16, jnp.float32


def dot(left, right):
    return jnp.dot(left, right, preferred_element_type=WIDE)


def dot_back(left, right):
    return lax.dot_general(left, right, (((1,), (1,)), ((), ())), preferred_element_type=WIDE)


def dot_over_rows(left, right):
    return lax.dot_general(left, right, (((0,), (0,)), ((), ())), preferred_element_type=WIDE)


def exact_dot(left, right):
    return jnp.dot(left, right, precision=lax.Precision.HIGHEST, preferred_element_type=WIDE)


def sigmoid(v):
    return 1.0 / (1.0 + jnp.exp(-v))


def tile(index, size):
    return pl.ds(index * size, size)


def lanes(shape):
    return lax.broadcasted_iota(jnp.int32, shape, len(shape) - 1)


def rows_of(shape):
    return lax.broadcasted_iota(jnp.int32, shape, 0)


def pair_stack(value):
    first = lanes(value.shape) < HD
    zero = jnp.zeros_like(value)
    return jnp.concatenate([jnp.where(first, value, zero), jnp.where(first, zero, value)], axis=0)


def pair_join(stacked):
    first = lanes((TOK, 128)) < HD
    return jnp.where(first, stacked[:TOK], stacked[TOK:])


def swap_halves(value):
    first = lax.rem(lanes(value.shape), HD) < HD // 2
    return jnp.where(first, pltpu.roll(value, 128 - HD // 2, 1), pltpu.roll(value, HD // 2, 1))


def doubled(value, which):
    first = lanes(value.shape) < HD
    turned = pltpu.roll(value, HD, 1)
    return jnp.where(first, value, turned) if which == 0 else jnp.where(first, turned, value)


class Layer:
    def __init__(self, refs):
        vars(self).update(refs)


    def enter(self):
        self.vectors[...] = jnp.zeros((8, 1792), WIDE)
        self.skip_sum[...] = jnp.zeros((8, 1536), WIDE)
        self.heads[...] = jnp.zeros((8, 128), WIDE)
        self.heads[0:1, 0:24] = self.decay_log[...]
        self.heads[1:2, 0:24] = self.step_bias[...]
        own = self.small_shard
        own[...] = jnp.zeros((8, 128), WIDE)
        own[0:2, 0:8] = self.norm_gains[...].astype(WIDE)
        own[2:7, 0:14] = self.conv_params[...].astype(WIDE)
        own[7:8, 0:12] = self.mixer_scale[...].astype(WIDE)
        moved = pltpu.roll(own[...], 32, 1)
        own[...] = jnp.zeros((8, 128), WIDE)
        own[:, 0:24] = self.in_shard[:, 4096:4120].astype(WIDE)
        own[...] = own[...] + moved

    def tables(self):
        position = rows_of((TOK, 128)).astype(WIDE)
        column = lax.rem(lanes((TOK, 128)), HD // 2).astype(WIDE)
        angle = position * jnp.exp(column * (-2.0 * math.log(rope_base) / HD))
        sine = jnp.sin(angle)
        first = lax.rem(lanes((TOK, 128)), HD) < HD // 2
        self.cosines[...] = jnp.cos(angle)
        self.sines[...] = jnp.where(first, -sine, sine)
        first = lanes((1, 128)) < HD
        for i in range(12):
            self.skip[0:1, 128 * i : 128 * i + 128] = jnp.where(
                first,
                self.mixer_skip[0:1, 2 * i : 2 * i + 1],
                self.mixer_skip[0:1, 2 * i + 1 : 2 * i + 2],
            )

    def spread(self):
        self.small_wide[...] = self.g_small[...].astype(WIDE).reshape(1024, 128)

        def turned(row):
            got = self.small_wide[pl.ds(row, 128, stride=8), :]
            return jnp.transpose(got)[32:48]

        for group, size, first, count, into in (
            (8, 1024, 0, 2, self.gains),
            (14, 1792, 2, 5, self.taps),
            (12, 1536, 7, 1, self.scale),
        ):
            stacked = jnp.concatenate([turned(first + i) for i in range(count)], axis=0)
            stacked = stacked.astype(LOW)
            for low in range(0, size, 256):
                start = rows_of((128, 256)) * group
                column = lanes((128, 256)) + low
                hot = (column >= start) & (column < start + group)
                index = jnp.sum(jnp.where(hot, start, 0).astype(WIDE), axis=0, keepdims=True)
                within = (lanes((1, 256)) + low).astype(WIDE) - index
                found = dot(stacked, jnp.where(hot, 1.0, 0.0).astype(LOW))
                mask = rows_of((16, 256)).astype(WIDE) == within
                for i in range(count):
                    into[i : i + 1, low : low + 256] = jnp.sum(
                        jnp.where(mask, found[16 * i : 16 * i + 16], 0.0), axis=0, keepdims=True
                    )


    def norm_in(self):
        x = self.tokens[...].astype(WIDE)
        self.inverse_in[...] = lax.rsqrt(jnp.mean(x * x, axis=-1, keepdims=True) + norm_eps)
        normed = x * self.inverse_in[...] * self.gains[0:1, :]
        self.normed[...] = normed.astype(LOW)
        self.left_in[:, 0:128] = jnp.transpose(normed).astype(LOW)

    def project(self, weights, first, half):
        for i in range(2):
            weight = weights[half, :, :, :, :, tile(i, 512)].reshape(1024, 512)
            at = pl.ds(pl.multiple_of(first + half * 1024 + 512 * i, 512), 512)
            self.proj[:, at] = dot(self.normed[...], weight)

    def project_steps(self):
        raw = dot(self.normed[...], self.g_small[...].reshape(1024, 128))
        self.step_raw[...] = jnp.where(lanes((TOK, 128)) < MIXER_HEADS, raw, 0.0)

    def convolved(self, i):
        low = 128 * i
        own = self.proj[:, 2304 + low : 2432 + low]
        row = rows_of((TOK, 128))
        shifted = [own] + [
            jnp.where(row >= k, pltpu.roll(own, k, 0), 0.0) for k in range(1, CONVK)
        ]
        total = self.taps[4:5, low : low + 128]
        for k in range(CONVK):
            total = total + self.taps[3 - k : 4 - k, low : low + 128] * shifted[k]
        return shifted, total

    def activate(self):
        for i in range(14):
            _, total = self.convolved(i)
            active = total * sigmoid(total)
            self.active[:, 128 * i : 128 * i + 128] = active

    def steps(self):
        raw = self.step_raw[...] + self.heads[1:2, :]
        step = jnp.maximum(raw, 0.0) + jnp.log1p(jnp.exp(-jnp.abs(raw)))
        rate = -jnp.exp(self.heads[0:1, :])
        lower = jnp.where(rows_of((TOK, TOK)) >= lanes((TOK, TOK)), 1.0, 0.0)
        total = exact_dot(lower, step * rate)
        self.step[...] = step
        self.cum[...] = total
        self.step_rows[...] = jnp.transpose(step)
        self.cum_rows[...] = jnp.transpose(total)

    def causal(self):
        return rows_of((TOK, TOK)) >= lanes((TOK, TOK))

    def attend(self):
        for i in range(5):
            value = self.proj[:, 128 * i : 128 * i + 128]
            turned = value * self.cosines[...] + swap_halves(value) * self.sines[...]
            self.turned[:, 128 * i : 128 * i + 128] = turned.astype(LOW)
        key = self.turned[:, 512:640].astype(WIDE)
        values = self.proj[:, 640:768]
        for which in range(2):
            self.keys[which] = doubled(key, which).astype(LOW)
            self.values[which] = doubled(values, which).astype(LOW)
        causal = self.causal()
        causal = jnp.concatenate([causal, causal], axis=0)
        for i in range(4):
            queries = pair_stack(self.turned[:, 128 * i : 128 * i + 128])
            scores = dot_back(queries, self.keys[i // 2]) * (1.0 / math.sqrt(HD))
            scores = jnp.where(causal, scores, masked_value)
            power = jnp.exp(scores - jnp.max(scores, axis=-1, keepdims=True))
            probs = power / jnp.sum(power, axis=-1, keepdims=True)
            self.small_wide[tile(i, 256), :] = probs
            self.mixed[:, 128 * i : 128 * i + 128] = pair_join(
                dot(probs.astype(LOW), self.values[i // 2])
            ).astype(LOW)

    def decay(self, head):
        gaps = self.cum[:, head : head + 1] - self.cum_rows[head : head + 1, :]
        return jnp.exp(jnp.where(self.causal(), gaps, masked_value))

    def mix(self, low, high):
        if low == 0:
            self.inner[...] = dot_back(
                self.active[:, 1664:1792].astype(LOW), self.active[:, 1536:1664].astype(LOW)
            )
        inner = self.inner[...]
        square = jnp.zeros((TOK, 1), WIDE) if low == 0 else self.inverse_state[...]
        for i in range(low, high):
            mixing = jnp.concatenate(
                [
                    inner * self.decay(head) * self.step_rows[head : head + 1, :]
                    for head in (2 * i, 2 * i + 1)
                ],
                axis=0,
            ).astype(LOW)
            self.mixing[i] = mixing
            at = slice(128 * i, 128 * i + 128)
            state = pair_join(dot(mixing, self.active[:, at].astype(LOW)))
            central = state + self.skip[0:1, at] * self.active[:, at]
            self.central[:, at] = central
            gate = self.proj[:, 768 + 128 * i : 896 + 128 * i]
            gated = central * (gate * sigmoid(gate))
            square = square + jnp.sum(gated * gated, axis=-1, keepdims=True)
        self.inverse_state[...] = square

    def mix_norm(self):
        inverse = lax.rsqrt(self.inverse_state[...] * (1.0 / MIXER_FEATURES) + norm_eps)
        self.inverse_state[...] = inverse
        for i in range(12):
            at = slice(128 * i, 128 * i + 128)
            gate = self.proj[:, 768 + 128 * i : 896 + 128 * i]
            gated = self.central[:, at] * (gate * sigmoid(gate))
            self.mixed[:, 512 + 128 * i : 640 + 128 * i] = (
                gated * inverse * self.scale[0:1, at]
            ).astype(LOW)

    def turn_left(self, source, into, count):
        for i in range(count):
            block = source[:, 128 * i : 128 * i + 128].astype(WIDE)
            into[128 * i : 128 * i + 128, 0:128] = jnp.transpose(block).astype(LOW)

    def branch_half(self, half):
        at = pl.ds(pl.multiple_of(512 * half, 512), 512)
        self.residual[:, at] = self.tokens[:, at].astype(WIDE) + dot(
            self.mixed[...], self.g_out[half].reshape(2048, 512)
        )

    def branch(self):
        x = self.residual[...]
        self.inverse_ff[...] = lax.rsqrt(jnp.mean(x * x, axis=-1, keepdims=True) + norm_eps)
        normed = x * self.inverse_ff[...] * self.gains[1:2, :]
        self.both_normed[0:128, :] = normed.astype(LOW)
        self.left_gu[:, 0:128] = jnp.transpose(normed).astype(LOW)

    def turn_other(self):
        other = self.both_normed[128:256, :].astype(WIDE)
        self.left_gu[:, 128:256] = jnp.transpose(other).astype(LOW)

    def feed_half(self, half):
        for i in range(2):
            weight = self.g_gu[half, :, :, :, :, tile(i, 512)].reshape(1024, 512)
            at = pl.ds(pl.multiple_of(half * 1024 + 512 * i, 512), 512)
            self.gate_up[:, at] = dot(self.both_normed[...], weight)

    def feed(self, send):
        for i in range(8):
            at = tile(i, 128)
            gate = self.gate_up[:, at]
            hidden = gate * sigmoid(gate) * self.gate_up[:, tile(8 + i, 128)]
            self.hidden[:, at] = hidden.astype(LOW)
            self.left_down[at, 0:256] = jnp.transpose(hidden).astype(LOW)
            if i % 4 == 3:
                send(i // 4)

    def down(self):
        for half in range(2):
            at = tile(half, 512)
            part = dot(self.hidden[...], self.g_down[half].reshape(1024, 512))
            self.down_own[:, at] = self.residual[:, at] + part[0:128]
            self.down_part[:, at] = part[128:256].astype(LOW)

    def down_sum(self):
        self.layer_output[...] = (self.down_own[...] + self.down_got[...].astype(WIDE)).astype(LOW)


    def back_down(self):
        for q in range(2):
            grad = dot_back(
                self.both_cotangent[:, 0:512], self.g_down[0, q].reshape(512, 512)
            ) + dot_back(self.both_cotangent[:, 512:1024], self.g_down[1, q].reshape(512, 512))
            for i in range(4):
                part = grad[:, 128 * i : 128 * i + 128]
                at, up_at = tile(4 * q + i, 128), tile(8 + 4 * q + i, 128)
                gate = self.gate_up[:, at]
                share = sigmoid(gate)
                self.d_gate[:, at] = (
                    part * self.gate_up[:, up_at] * (share * (1.0 + gate * (1.0 - share)))
                ).astype(LOW)
                self.d_gate[:, up_at] = (part * (gate * share)).astype(LOW)

    def norm_back(self, grad, x, inverse, gain):
        turned = x * inverse
        d_gain = jnp.sum(grad * turned, axis=0, keepdims=True)
        scaled = grad * gain
        d_x = inverse * (scaled - turned * jnp.mean(scaled * turned, axis=-1, keepdims=True))
        return d_x, d_gain

    def back_feed(self, y):
        total = dot_back(self.d_gate[:, 0:1024], self.g_gu[0, y].reshape(256, 1024)) + dot_back(
            self.d_gate[:, 1024:2048], self.g_gu[1, y].reshape(256, 1024)
        )
        self.d_wide[:, tile(y, 256)] = total[0:128]
        self.back_part[:, tile(y, 256)] = total[128:256].astype(LOW)

    def back_residual(self):
        grad = self.d_wide[:, 0:1024] + self.back_got[...].astype(WIDE)
        d_x, d_gain = self.norm_back(
            grad, self.residual[...], self.inverse_ff[...], self.gains[1:2, :]
        )
        self.vectors[1:2, 0:1024] = d_gain
        d_residual = self.cotangent[...].astype(WIDE) + d_x
        self.d_residual[...] = d_residual
        self.d_branch[...] = d_residual.astype(LOW)

    def back_branch(self):
        def body(y):
            self.d_wide[:, tile(y, 512)] = dot_back(
                self.d_branch[:, 0:512], self.g_out[0, y].reshape(512, 512)
            ) + dot_back(self.d_branch[:, 512:1024], self.g_out[1, y].reshape(512, 512))

        each(4, body)

    def back_gated(self):
        inverse = self.inverse_state[...]
        mean = jnp.zeros((TOK, 1), WIDE)
        for i in range(12):
            at = slice(128 * i, 128 * i + 128)
            gate = self.proj[:, 768 + 128 * i : 896 + 128 * i]
            gated = self.central[:, at] * (gate * sigmoid(gate))
            grad = self.d_wide[:, 512 + 128 * i : 640 + 128 * i]
            turned = gated * inverse
            self.vectors[7:8, at] = jnp.sum(grad * turned, axis=0, keepdims=True)
            mean = mean + jnp.sum(grad * self.scale[0:1, at] * turned, axis=-1, keepdims=True)
        mean = mean * (1.0 / MIXER_FEATURES)
        for i in range(12):
            at = slice(128 * i, 128 * i + 128)
            gate = self.proj[:, 768 + 128 * i : 896 + 128 * i]
            share = sigmoid(gate)
            open_gate = gate * share
            central = self.central[:, at]
            grad = self.d_wide[:, 512 + 128 * i : 640 + 128 * i]
            d_gated = inverse * (
                grad * self.scale[0:1, at] - central * open_gate * inverse * mean
            )
            d_central = d_gated * open_gate
            self.d_proj[:, 768 + 128 * i : 896 + 128 * i] = (
                d_gated * central * (share * (1.0 + gate * (1.0 - share)))
            ).astype(LOW)
            self.d_state[:, at] = d_central.astype(LOW)
            self.d_active[:, at] = d_central * self.skip[0:1, at]
            self.skip_sum[0:1, at] = jnp.sum(
                d_central * self.active[:, at], axis=0, keepdims=True
            )

    def back_mix(self, low, high):
        inner = self.inner[...]
        lane = lanes((TOK, TOK))
        zero = jnp.zeros((TOK, TOK), WIDE)
        d_inner, d_cum = (zero, zero) if low == 0 else (self.d_inner[...], self.d_cum[...])
        if low == 0:
            self.flow_rows[...] = zero
            self.d_step_rows[...] = zero
        for i in range(low, high):
            at = slice(128 * i, 128 * i + 128)
            stacked = pair_stack(self.d_state[:, at])
            d_mixing = dot_back(stacked, self.active[:, at].astype(LOW))
            self.d_active[:, at] += dot_over_rows(self.mixing[i], stacked)
            for which, head in enumerate((2 * i, 2 * i + 1)):
                grad = d_mixing[TOK * which : TOK * which + TOK]
                decay = self.decay(head)
                step = self.step_rows[head : head + 1, :]
                faded = grad * decay
                d_inner = d_inner + faded * step
                part = faded * inner
                d_step = jnp.sum(part, axis=0, keepdims=True)
                self.d_step_rows[head : head + 1, :] = d_step
                self.flow_rows[head : head + 1, :] = d_step * step
                over = jnp.sum(part * step, axis=-1, keepdims=True)
                d_cum = jnp.where(lane == head, over, d_cum)
        self.d_inner[...] = d_inner
        self.d_cum[...] = d_cum

    def back_steps(self):
        lane = lanes((TOK, TOK))
        d_inner = self.d_inner[...].astype(LOW)
        self.d_active[:, 1664:1792] = dot(d_inner, self.active[:, 1536:1664].astype(LOW))
        self.d_active[:, 1536:1664] = dot_over_rows(d_inner, self.active[:, 1664:1792].astype(LOW))
        d_cum = self.d_cum[...] - jnp.transpose(self.flow_rows[...])
        upper = jnp.where(rows_of((TOK, TOK)) <= lanes((TOK, TOK)), 1.0, 0.0)
        d_rated = exact_dot(upper, d_cum)
        rate = -jnp.exp(self.heads[0:1, :])
        d_step = jnp.transpose(self.d_step_rows[...]) + d_rated * rate
        self.vectors[7:8, 1536:1664] = (
            jnp.sum(d_rated * self.step[...], axis=0, keepdims=True) * rate
        )
        raw = self.step_raw[...] + self.heads[1:2, :]
        d_raw = jnp.where(lane < MIXER_HEADS, d_step * sigmoid(raw), 0.0)
        self.vectors[7:8, 1664:1792] = jnp.sum(d_raw, axis=0, keepdims=True)
        self.right_dt[0:128, :] = d_raw.astype(LOW)
        hot = jnp.where(
            lax.div(rows_of((1536, 128)), MIXER_HEAD_SIZE) == lanes((1536, 128)), 1.0, 0.0
        )
        self.vectors[0:1, 1024:1152] = exact_dot(self.skip_sum[...], hot)[0:1]

    def back_attend(self):
        d_keys, d_values = [], []
        for i in range(4):
            at = slice(128 * i, 128 * i + 128)
            which = i // 2
            d_out = pair_stack(self.d_wide[:, at].astype(LOW))
            d_probs = dot_back(d_out, self.values[which])
            probs = self.small_wide[tile(i, 256), :]
            d_scores = probs * (d_probs - jnp.sum(probs * d_probs, axis=-1, keepdims=True))
            d_raw = (d_scores * (1.0 / math.sqrt(HD))).astype(LOW)
            self.unturn(i, pair_join(dot(d_raw, self.keys[which])))
            d_keys.append(dot_over_rows(d_raw, pair_stack(self.turned[:, at])))
            d_values.append(dot_over_rows(probs.astype(LOW), d_out))
        first = lanes((TOK, 128)) < HD

        def joined(parts):
            one, two = parts[0] + parts[1], parts[2] + parts[3]
            return jnp.where(first, one + pltpu.roll(one, HD, 1), two + pltpu.roll(two, HD, 1))

        self.unturn(4, joined(d_keys))
        self.d_proj[:, 640:768] = joined(d_values).astype(LOW)

    def unturn(self, i, grad):
        self.d_proj[:, 128 * i : 128 * i + 128] = (
            grad * self.cosines[...] - swap_halves(grad) * self.sines[...]
        ).astype(LOW)

    def back_activate(self):
        row = rows_of((TOK, 128))
        for i in range(14):
            at = slice(128 * i, 128 * i + 128)
            shifted, total = self.convolved(i)
            share = sigmoid(total)
            grad = self.d_active[:, at] * (share * (1.0 + total * (1.0 - share)))
            self.vectors[6:7, at] = jnp.sum(grad, axis=0, keepdims=True)
            d_in = self.taps[3:4, at] * grad
            for k in range(CONVK):
                self.vectors[5 - k : 6 - k, at] = jnp.sum(grad * shifted[k], axis=0, keepdims=True)
                if k:
                    later = jnp.where(row < TOK - k, pltpu.roll(grad, TOK - k, 0), 0.0)
                    d_in = d_in + self.taps[3 - k : 4 - k, at] * later
            self.d_proj[:, 2304 + 128 * i : 2432 + 128 * i] = d_in.astype(LOW)

    def back_project(self, low, high):
        small = self.g_small[...].reshape(1024, 128)
        for y in range(low, high):
            total = dot_back(self.right_dt[0:128, :], small[256 * y : 256 * y + 256])
            for half in range(2):
                at = tile(half, 1024)
                total = total + dot_back(self.d_proj[:, at], self.g_ina[half, y].reshape(256, 1024))
                at = tile(2 + half, 1024)
                total = total + dot_back(self.d_proj[:, at], self.g_inb[half, y].reshape(256, 1024))
            self.d_wide[:, tile(y, 256)] = total

    def back_input(self):
        d_x, d_gain = self.norm_back(
            self.d_wide[:, 0:1024],
            self.tokens[...].astype(WIDE),
            self.inverse_in[...],
            self.gains[0:1, :],
        )
        self.vectors[0:1, 0:1024] = d_gain
        self.input_grad[...] = (self.d_residual[...] + d_x).astype(LOW)


    def grad_wide(self, left, right, into):
        width = right.shape[1]
        size = min(width, 512)
        for n in range(width // size):
            for y in range(4):
                block = dot(left[tile(y, 256), :], right[:, tile(n, size)])
                into[y, :, :, :, tile(n, size)] = block.astype(LOW).reshape(4, 4, 16, size)

    def grad_tall(self, left, right, into):
        for y in range(into.shape[0]):
            block = dot(left[tile(y, 512), :], right[...])
            into[y] = block.astype(LOW).reshape(4, 4, 32, 512)


class Swap:
    def __init__(self, place, layer, send_sem, recv_sem):
        self.place, self.layer = place, layer
        self.send_sem, self.recv_sem = send_sem, recv_sem
        self.lefts = (
            None, layer.left_in, None, layer.left_out, layer.left_gu, layer.left_down,
        )
        self.rights = (
            layer.right_dt, layer.right_ina, layer.right_inb, layer.right_out, layer.right_gu,
            layer.right_down,
        )
        self.sources = (
            None, layer.d_proj, layer.d_proj, layer.d_branch, layer.d_gate, layer.both_cotangent,
        )

    def left_copy(self, name):
        ref = self.lefts[name]
        size = ref.shape[1] // 2
        src, dst = ref.at[:, pl.ds(0, size)], ref.at[:, pl.ds(size, size)]
        return push(
            src, dst, self.send_sem.at[name], self.recv_sem.at[name], self.place.sibling
        )

    def right_copy(self, name):
        ref, source = self.rights[name], self.sources[name]
        size = ref.shape[0] // 2
        if source is None:
            src = ref.at[pl.ds(0, size), :]
        else:
            src = source.at[:, half_columns(name, 1 - self.place.core)]
        slot = 6 + name
        return push(
            src,
            ref.at[pl.ds(size, size), :],
            self.send_sem.at[slot],
            self.recv_sem.at[slot],
            self.place.sibling,
        )

    def start_left(self, name):
        self.left_copy(name).start()

    def start_left_rows(self, q):
        ref, rows = self.lefts[DOWN], tile(q, 512)
        push(
            ref.at[rows, pl.ds(0, 256)],
            ref.at[rows, pl.ds(256, 256)],
            self.send_sem.at[DOWN],
            self.recv_sem.at[DOWN],
            self.place.sibling,
        ).start()

    def start_right(self, name):
        ref, source = self.rights[name], self.sources[name]
        if source is not None:
            size = ref.shape[0] // 2
            ref[0:size, :] = source[:, half_columns(name, self.place.core)]
        self.right_copy(name).start()

    def arrived(self, name):
        if self.lefts[name] is not None:
            self.left_copy(name).wait_recv()
        self.right_copy(name).wait_recv()

    def finish(self):
        for name in WEIGHTS:
            self.right_copy(name).wait_send()
            if self.lefts[name] is not None:
                self.left_copy(name).wait_send()


INS = dict(
    tokens=0, cotangent=1, in_shard=2, out_shard=3, gu_shard=4, down_shard=5, norm_gains=6,
    conv_params=7, mixer_scale=8, decay_log=9, step_bias=10, mixer_skip=11,
)
OUTS = dict(
    layer_output=((TOK, 1024), LOW),
    input_grad=((TOK, 1024), LOW),
    grad_in=((8, 4120), WIDE),
    grad_out=((16, 1024), WIDE),
    grad_gu=((8, 4096), WIDE),
    grad_down=((16, 1024), WIDE),
    total=((8, 1792), WIDE),
)
SCRATCH = dict(
    g_small=((4, 4, 4, 16, 128), LOW),
    g_ina=((2, 4, 4, 4, 16, 1024), LOW),
    g_inb=((2, 4, 4, 4, 16, 1024), LOW),
    g_out=((2, 4, 4, 4, 32, 512), LOW),
    g_gu=((2, 4, 4, 4, 16, 1024), LOW),
    g_down=((2, 2, 4, 4, 32, 512), LOW),
    low_small=((4, 4, 4, 16, 128), LOW),
    low_gu=((4, 4, 4, 16, 1024), LOW),
    low_down=((2, 4, 4, 32, 512), LOW),
    small_shard=((8, 128), WIDE),
    heads=((8, 128), WIDE),
    skip=((8, 1536), WIDE),
    cosines=((TOK, 128), WIDE),
    sines=((TOK, 128), WIDE),
    pack=((16, 4224), LOW),
    got=((16, 4224), LOW),
    stage=((16, 1024), LOW),
    small_wide=((1024, 128), WIDE),
    gains=((8, 1024), WIDE),
    taps=((8, 1792), WIDE),
    scale=((8, 1536), WIDE),
    normed=((TOK, 1024), LOW),
    inverse_in=((TOK, 1), WIDE),
    proj=((TOK, 4096), WIDE),
    step_raw=((TOK, 128), WIDE),
    active=((TOK, 1792), WIDE),
    step=((TOK, TOK), WIDE),
    cum=((TOK, TOK), WIDE),
    step_rows=((TOK, TOK), WIDE),
    cum_rows=((TOK, TOK), WIDE),
    turned=((TOK, 640), LOW),
    keys=((2, TOK, 128), LOW),
    values=((2, TOK, 128), LOW),
    mixed=((TOK, 2048), LOW),
    inner=((TOK, TOK), WIDE),
    mixing=((12, 256, TOK), LOW),
    central=((TOK, 1536), WIDE),
    inverse_state=((TOK, 1), WIDE),
    residual=((TOK, 1024), WIDE),
    d_residual=((TOK, 1024), WIDE),
    inverse_ff=((TOK, 1), WIDE),
    both_normed=((256, 1024), LOW),
    both_cotangent=((256, 1024), LOW),
    gate_up=((256, 2048), WIDE),
    hidden=((256, 1024), LOW),
    down_own=((TOK, 1024), WIDE),
    down_part=((TOK, 1024), LOW),
    down_got=((TOK, 1024), LOW),
    back_part=((TOK, 1024), LOW),
    back_got=((TOK, 1024), LOW),
    gu_sum=((2, 16, 1024), WIDE),
    gu_got=((16, 1024), WIDE),
    d_gate=((256, 2048), LOW),
    d_branch=((TOK, 1024), LOW),
    d_state=((TOK, 1536), LOW),
    d_proj=((TOK, 4096), LOW),
    skip_sum=((8, 1536), WIDE),
    d_inner=((TOK, TOK), WIDE),
    d_cum=((TOK, TOK), WIDE),
    flow_rows=((TOK, TOK), WIDE),
    d_step_rows=((TOK, TOK), WIDE),
    vectors=((8, 1792), WIDE),
    left_in=((1024, 256), LOW),
    left_out=((2048, 256), LOW),
    left_gu=((1024, 512), LOW),
    left_down=((1024, 512), LOW),
    right_ina=((256, 1024), LOW),
    right_inb=((256, 1024), LOW),
    right_out=((256, 512), LOW),
    right_gu=((512, 1024), LOW),
    right_down=((512, 512), LOW),
    right_dt=((256, 128), LOW),
    sums=((5, 4, 8, 896), WIDE),
)
BLOCKS = tuple((ROWS[name], COLS[name]) for name in WEIGHTS)
LANDINGS = tuple((3, DEPTH[name], 4) for name in WEIGHTS)
LANDINGS += tuple((3, DEPTH[name]) for name in WEIGHTS)
LANDINGS += tuple({GU: (1, 2), DOWN: (1,)}.get(name, (3,)) for name in WEIGHTS)
ENDS = tuple((ROWS[name], 2048 if name == GU else COLS[name]) for name in WEIGHTS[1:])
SEMS = dict(
    enter=(4, 4), gather=(24, 54), scatter=(18, 30), sums=(5, 5), end=(5, 5), swap=(12, 12), mate=(5, 5),
)


class Plan:
    def __init__(self, refs):
        names = [*INS, *OUTS, *SCRATCH]
        layer = Layer(dict(zip(names, refs)))
        rest = list(refs[len(names) :])
        landings = [[rest.pop(0) for _ in WEIGHTS] for _ in range(3)]
        ends = [None] + [rest.pop(0) for _ in WEIGHTS[1:]]
        ends_got = [None] + [rest.pop(0) for _ in WEIGHTS[1:]]
        sems = {name: (rest.pop(0), rest.pop(0)) for name in SEMS}
        layer.d_wide = layer.gate_up.at[pl.ds(0, 128), :]
        layer.d_active = layer.gate_up.at[pl.ds(128, 128), pl.ds(0, 1792)]
        place = Place()
        arrays = (layer.g_small, layer.g_ina, layer.g_inb, layer.g_out, layer.g_gu, layer.g_down)
        shards = (
            layer.small_shard, layer.in_shard, layer.in_shard, layer.out_shard, layer.gu_shard,
            layer.down_shard,
        )
        grads = (
            layer.low_small, layer.g_gu.at[0], layer.g_gu.at[1], layer.g_out.at[0], layer.low_gu,
            layer.low_down,
        )
        outs = (
            None, layer.grad_in, layer.grad_in, layer.grad_out, layer.grad_gu, layer.grad_down,
        )
        self.place, self.layer, self.grads = place, layer, grads
        self.gather = Gather(place, arrays, *sems["gather"])
        self.enter = Enter(
            place, self.gather, layer.pack, layer.got, layer.stage, shards, sems["enter"]
        )
        self.scatter = Scatter(place, grads, *landings, *sems["scatter"])
        self.sum_all = SumAll(place, layer.sums, *sems["sums"])
        self.end = End(place, ends, ends_got, outs, *sems["end"])
        self.swap = Swap(place, layer, *sems["swap"])
        self.mate = Mate(place, layer, *sems["mate"])

    def last(self, name):
        self.scatter.arrived(name, 2)
        for part, (low, high) in enumerate(PARTS[name]):
            value = self.scatter.add(name, part, 2)
            if name == SMALL:
                mine = jnp.where(self.place.core == 0, value[0:8], value[8:16])
                self.layer.grad_in[:, 4096:4120] = mine[:, 0:24]
            elif name == GU:
                self.layer.gu_sum[:, :, low:high] = value
            else:
                self.end.ends[name][:, low:high] = value
        if name == GU:
            self.mate.start(Mate.GRAD)
        elif name != SMALL:
            self.end.start(name)

    def last_gu(self):
        self.mate.arrived(Mate.GRAD)
        layer, parity, into = self.layer, self.place.parity, self.end.ends[GU]
        for which, value in ((parity, layer.gu_sum[parity]), (1 - parity, layer.gu_got[...])):
            for q in range(2):
                at = pl.ds(pl.multiple_of(1024 * q + 512 * which, 512), 512)
                into[:, at] = value[:, 512 * q : 512 * q + 512]
        self.end.start(GU)


def layer_kernel(*refs):
    plan = Plan(refs)
    place, layer, grads, gather = plan.place, plan.layer, plan.grads, plan.gather
    enter, scatter, sum_all, end, swap = (
        plan.enter, plan.scatter, plan.sum_all, plan.end, plan.swap,
    )
    mate, core = plan.mate, place.core

    def onward(name, phase):
        gather.arrived(name, phase, 0 if gather.direct(name, phase) else 2)
        if phase == 0 or name == SMALL:
            gather.start(name, phase + 1)
        else:
            gather.start_early(name)

    def onward_late(name):
        gather.start_late(name)
        gather.pass_on(name, 0)

    def landed(name):
        gather.arrived(name, 2, 2)
        gather.pass_on(name, 2)

    arrive(place)
    layer.enter()
    enter.run(lambda: meet(place), lambda name: gather.start(name, 0))
    gather.start(SMALL, 0)
    gather.start(OUT, 0)
    gather.start(DOWN, 0)
    layer.tables()
    enter.mate_copy().wait_recv()
    gather.start(GU, 0)
    onward(SMALL, 0)
    onward(INB, 0)
    onward(OUT, 0)
    onward(INA, 0)
    onward(DOWN, 0)
    onward(GU, 0)
    onward(SMALL, 1)
    gather.hand_on(INB, 1, (0,))
    gather.hand_on(INB, 1, (1,))
    gather.hand_on(OUT, 1, (0,))
    gather.hand_on(OUT, 1, (1,))
    gather.hand_on(DOWN, 1, (0,))
    gather.hand_on(DOWN, 1, (1,))
    onward(INA, 1)
    onward_late(INA)
    gather.hand_on(GU, 1, (0,))
    gather.hand_on(GU, 1, (1,))
    onward(INB, 1)
    onward_late(INB)
    gather.share_small()
    gather.hand_on(INA, 2, (0,))
    gather.hand_on(INA, 2, (1,))
    gather.arrived_late(INA, (0,))
    gather.shared_small()
    layer.spread()
    layer.norm_in()
    swap.start_left(INA)
    layer.project_steps()
    onward(OUT, 1)
    onward_late(OUT)
    gather.arrived_late(INA, (1,))
    gather.hand_on(INB, 2, (0,))
    gather.hand_on(INB, 2, (1,))
    gather.arrived_late(INB, (0,))
    gather.arrived_late(INB, (1,))
    onward(DOWN, 1)
    landed(INA)
    layer.project(layer.g_ina, 0, core)
    gather.hand_on(OUT, 2, (0,))
    gather.hand_on(OUT, 2, (1,))
    onward(GU, 1)
    onward_late(GU)
    gather.passed(INA)
    layer.project(layer.g_ina, 0, 1 - core)
    layer.attend()
    gather.arrived_late(OUT, (0,))
    gather.arrived_late(OUT, (1,))
    layer.both_cotangent[0:128, :] = layer.cotangent[...]
    mate.start(Mate.COTANGENT)
    landed(INB)
    layer.project(layer.g_inb, 2048, core)
    gather.hand_on(DOWN, 2, (0,))
    gather.hand_on(DOWN, 2, (1,))
    gather.passed(INB)
    layer.project(layer.g_inb, 2048, 1 - core)
    layer.activate()
    layer.steps()
    landed(OUT)
    layer.mix(0, 6)
    layer.mix(6, 12)
    layer.mix_norm()
    layer.branch_half(core)
    gather.hand_on(GU, 2, (1,))
    gather.passed(OUT)
    layer.branch_half(1 - core)
    layer.branch()
    mate.start(Mate.NORMED)
    layer.turn_left(layer.mixed, layer.left_out, 16)
    swap.start_left(OUT)
    gather.hand_on(GU, 2, (0,))
    onward_late(DOWN)
    mate.arrived(Mate.COTANGENT)
    swap.start_right(DOWN)
    gather.arrived_late(GU, (1,))
    gather.arrived_late(GU, (0,))
    landed(GU)
    gather.arrived_late(DOWN, (0,))
    gather.arrived_late(DOWN, (1,))
    landed(DOWN)
    mate.arrived(Mate.NORMED)
    layer.turn_other()
    swap.start_left(GU)
    layer.feed_half(core)
    gather.passed(GU)
    layer.feed_half(1 - core)
    layer.feed(swap.start_left_rows)
    gather.passed(DOWN)
    layer.back_down()
    swap.start_right(GU)
    layer.back_feed(0)
    mate.start_columns(0)
    layer.back_feed(1)
    mate.start_columns(1)
    swap.arrived(DOWN)
    layer.grad_tall(layer.left_down, layer.right_down, grads[DOWN])
    scatter.start(DOWN, 0)
    layer.back_feed(2)
    mate.start_columns(2)
    layer.back_feed(3)
    mate.start_columns(3)
    swap.arrived(GU)
    layer.grad_wide(layer.left_gu, layer.right_gu, grads[GU])
    scatter.start(GU, 0)
    layer.down()
    mate.start(Mate.DOWN_PART)
    scatter.hand_on(DOWN, 0)
    mate.arrived(Mate.BACK_PART)
    layer.back_residual()
    swap.start_right(OUT)
    layer.back_branch()
    scatter.hand_on(GU, 0)
    gather.finish(OUT)
    swap.arrived(OUT)
    layer.grad_tall(layer.left_out, layer.right_out, grads[OUT])
    scatter.start(OUT, 0)
    layer.back_gated()
    layer.back_attend()
    swap.start_right(INA)
    layer.back_mix(0, 6)
    scatter.relay(DOWN, 0)
    layer.back_mix(6, 12)
    gather.finish(GU)
    swap.arrived(INA)
    layer.grad_wide(layer.left_in, layer.right_ina, grads[INA])
    scatter.start(INA, 0)
    scatter.relay(GU, 0)
    scatter.hand_on(OUT, 0)
    layer.back_steps()
    swap.start_right(SMALL)
    scatter.hand_on(DOWN, 1)
    layer.back_activate()
    swap.start_right(INB)
    mate.arrived(Mate.DOWN_PART)
    layer.down_sum()
    swap.arrived(SMALL)
    layer.grad_wide(layer.left_in, layer.right_dt, grads[SMALL])
    scatter.start(SMALL, 0)
    swap.arrived(INB)
    layer.grad_wide(layer.left_in, layer.right_inb, grads[INB])
    scatter.start(INB, 0)
    layer.back_project(0, 2)
    layer.back_project(2, 4)
    layer.back_input()
    sum_all.begin(layer.vectors)
    scatter.hand_on(GU, 1)
    scatter.hand_on(INA, 0)
    scatter.relay(OUT, 0)
    sum_all.start(1, sum_all.total(0))
    scatter.relay(DOWN, 1)
    scatter.relay(SMALL, 0)
    scatter.hand_on(INB, 0)
    scatter.relay(GU, 1)
    scatter.relay(INA, 0)
    scatter.hand_on(OUT, 1)
    sum_all.start(2, sum_all.total(1))
    plan.last(DOWN)
    scatter.relay(SMALL, 1)
    end.take(DOWN)
    scatter.relay(INB, 0)
    scatter.hand_on(INA, 1)
    plan.last(GU)
    scatter.relay(OUT, 1)
    sum_all.start(3, sum_all.total(2))
    plan.last(SMALL)
    scatter.relay(INA, 1)
    plan.last_gu()
    scatter.relay(INB, 1)
    plan.last(OUT)
    end.take(GU)
    end.take(OUT)
    sum_all.start(4, sum_all.total(3))
    for name in (SMALL, INA, INB, DOWN):
        gather.finish(name)
    enter.finish()
    swap.finish()
    mate.finish()
    sum_all.finish((0, 1, 2))
    scatter.finish((SMALL, OUT, GU, DOWN), (0, 1, 2))
    scatter.finish((INA, INB), (0, 1))
    plan.last(INA)
    plan.last(INB)
    end.take(INA)
    end.take(INB)
    sum_all.into(layer.total)
    scatter.finish((INA, INB), (2,))
    sum_all.finish((3, 4))
    end.finish()


def finish_kernel(*refs):
    ins, outs = refs[:7], refs[7:]
    for ref, into in zip(ins[:6], outs[:6]):
        into[...] = ref[...]
    me = lax.axis_index("fsdp")
    total = ins[6][...]
    column = lanes((8, 1792))

    def share(size):
        start = me * size
        picked = jnp.where((column >= start) & (column < start + size), total, 0.0)
        folded = picked[:, 0:128]
        for i in range(1, 14):
            folded = folded + picked[:, 128 * i : 128 * i + 128]
        return pltpu.roll(folded, lax.rem(1792 - start, 128), 1)

    outs[6][...] = share(8)[0:2, 0:8]
    outs[7][...] = share(14)[2:7, 0:14]
    outs[8][...] = share(12)[7:8, 0:12]
    outs[9][...] = total[7:8, 1536:1560]
    outs[10][...] = total[7:8, 1664:1688]
    outs[11][...] = total[0:1, 1024:1048]


def local(
    tokens, cotangent, input_weight, output_weight, gate_up_weight, down_weight,
    norm_gains, conv_params, mixer_scale, decay_log, step_bias, mixer_skip_factor,
):
    ins = (
        tokens, cotangent, input_weight, output_weight, gate_up_weight, down_weight, norm_gains,
        conv_params, mixer_scale, decay_log[None], step_bias[None], mixer_skip_factor[None],
    )
    scratch = [pltpu.VMEM(*one) for one in SCRATCH.values()]
    scratch += [pltpu.VMEM(lead + block, LOW) for lead, block in zip(LANDINGS, BLOCKS * 3)]
    scratch += [pltpu.VMEM(block, WIDE) for block in ENDS]
    scratch += [pltpu.VMEM((block[0] // 2, block[1]), WIDE) for block in ENDS]
    scratch += [pltpu.SemaphoreType.DMA((n,)) for counts in SEMS.values() for n in counts]
    whole = pl.BlockSpec(memory_space=pltpu.VMEM)
    results = pl.pallas_call(
        layer_kernel,
        out_shape=[jax.ShapeDtypeStruct(*one) for one in OUTS.values()],
        in_specs=[whole] * len(INS),
        out_specs=[whole] * len(OUTS),
        scratch_shapes=scratch,
        compiler_params=pltpu.CompilerParams(
            collective_id=0, has_side_effects=True, vmem_limit_bytes=127 * 2**19
        ),
        name="layer",
    )(*ins)
    shares = [(2, 8), (5, 14), (1, 12), (1, 24), (1, 24), (1, 24)]
    final = pl.pallas_call(
        finish_kernel,
        out_shape=[jax.ShapeDtypeStruct(*one) for one in list(OUTS.values())[:6]]
        + [jax.ShapeDtypeStruct(one, WIDE) for one in shares],
        in_specs=[whole] * len(OUTS),
        out_specs=[whole] * 12,
        name="finish",
    )(*results)
    return (*final[:9], *(one[0] for one in final[9:]))


def solution(mesh):
    in_specs = (
        P("fsdp", None),
        P("fsdp", None),
        P("fsdp", None),
        P("fsdp", None),
        P("fsdp", None),
        P("fsdp", None),
        P(None, "fsdp"),
        P(None, "fsdp"),
        P(None, "fsdp"),
        P(),
        P(),
        P(),
    )
    out_specs = (
        P("fsdp", None),
        P("fsdp", None),
        P("fsdp", None),
        P("fsdp", None),
        P("fsdp", None),
        P("fsdp", None),
        P(None, "fsdp"),
        P(None, "fsdp"),
        P(None, "fsdp"),
        P(),
        P(),
        P(),
    )
    return jax.shard_map(local, mesh=mesh, in_specs=in_specs, out_specs=out_specs, check_vma=False)
```
